32 devices in a mesh: group: 2 (over y), dp: 4 (over z), ctx: 4 (over x, core).
Axes of the slice: x: 2, y: 2, z: 4, core: 2. Of those that a mesh axis runs over, the one named last changes fastest.
Arguments:
- query_rows: bfloat16 [8, 640, 2048], P(('group', 'dp'), 'ctx'), parts along dimension 0, may hold values from -6 to 6
- key_rows: bfloat16 [8, 640, 512], P(('group', 'dp'), 'ctx'), parts along dimension 0, may hold values from -6 to 6
- value_rows: bfloat16 [8, 640, 512], P(('group', 'dp'), 'ctx'), parts along dimension 0, may hold values from -6 to 6
- cotangent: bfloat16 [8, 640, 2048], P(('group', 'dp'), 'ctx'), parts along dimension 0, may hold values from -6 to 6
- router_gate: float32 [8, 640], P(('group', 'dp'), 'ctx'), parts along dimension 0, may hold values from 0.25 to 1
- positions: int32 [8, 640], P(('group', 'dp'), 'ctx'), parts along dimension 0, may hold values from 0 to 4096, as said below
Outputs:
- query_grad: bfloat16 [8, 640, 2048], P(('group', 'dp'), 'ctx'), parts along dimension 0
- key_grad: bfloat16 [8, 640, 512], P(('group', 'dp'), 'ctx'), parts along dimension 0
- value_grad: bfloat16 [8, 640, 512], P(('group', 'dp'), 'ctx'), parts along dimension 0
- gate_grad: float32 [8, 640], P(('group', 'dp'), 'ctx'), parts along dimension 0
The draws below stay inside these ranges and needn't reach their ends.
There are 2 independent parts, one for each index of `group`. The reference program is written for one: setup_inputs(seed, part) draws one part's arguments, and reference() takes and returns one part's arrays. A program takes and returns all parts, laid end to end along the dimension named above; each array names one. Nothing has to cross between parts.
Inputs may be any that keep to these rules, and one draw needn't show every extreme that they name: In each sequence, slot block c (slots c * 160 to c * 160 + 159) holds in rising order the routed positions among positions c * 1024 to c * 1024 + 1023, then 4096 in every unused slot. The first and last position of every block of 1024 positions are routed; a sequence routes 128 tokens for each block on average, and some block fills all 160 slots.
All inputs are finite; a program needn't handle non-finite values.
Results may differ from the reference program's by a relative error of at most 0.02.
Values may be sent and summed in bfloat16 or wider, within the bound.
No kernel may reach another device: no remote copies, remote signals or barrier semaphores. Data moves between devices by JAX's collectives and lax.ppermute only.
A program may use at most 128 MiB of HBM per device.

```python
import jax
import jax.numpy as jnp
from jax import lax

HEADS = 16
KV_HEADS = 4
DH = 128
LOCAL = 1024
ROUTED = 128
CAP = 160
SEQ_LEN = 4096
SLOTS = 640
SEQS = 4
N_CTX = 4


def draw_query_rows(key, part):
    key = jax.random.fold_in(key, 5)
    return jnp.clip(jax.random.normal(key, (SEQS, SLOTS, HEADS * DH), jnp.float32), -6.0, 6.0).astype(jnp.bfloat16)


def draw_key_rows(key, part):
    key = jax.random.fold_in(key, 7)
    return jnp.clip(jax.random.normal(key, (SEQS, SLOTS, KV_HEADS * DH), jnp.float32), -6.0, 6.0).astype(jnp.bfloat16)


def one_block_positions(block_key, count, block):
    order_score = jax.random.randint(block_key, (LOCAL,), 0, 1 << 19, dtype=jnp.int32) * LOCAL + jnp.arange(LOCAL, dtype=jnp.int32)
    order_score = order_score.at[0].set(-2).at[LOCAL - 1].set(-1)
    ranks = jnp.argsort(jnp.argsort(order_score, stable=True), stable=True).astype(jnp.int32)
    picked = ranks < count
    slot = jnp.cumsum(picked.astype(jnp.int32)) - 1
    target = jnp.where(picked, slot, CAP).astype(jnp.int32)
    filled = jnp.full((CAP,), SEQ_LEN, jnp.int32)
    return filled.at[target].set(block * LOCAL + jnp.arange(LOCAL, dtype=jnp.int32), mode='drop')


def one_sequence_positions(key):
    heavy_key, weight_key, place_key = jax.random.split(key, 3)
    blocks = N_CTX
    index = jnp.arange(blocks, dtype=jnp.int32)
    heavy = jax.random.randint(heavy_key, (), 0, blocks, dtype=jnp.int32)
    others = index != heavy
    weights = jnp.where(others, jax.random.randint(weight_key, (blocks,), 4, 6, dtype=jnp.int32), 0)
    spare = blocks * ROUTED - CAP - 2 * (blocks - 1)
    share = spare * weights // jnp.sum(weights)
    leftover = spare - jnp.sum(share)
    order_rank = jnp.cumsum(others.astype(jnp.int32)) - 1
    extra = (others & (order_rank < leftover)).astype(jnp.int32)
    counts = jnp.where(others, jnp.minimum(2 + share + extra, CAP), CAP).astype(jnp.int32)
    block_keys = jax.random.split(place_key, blocks)
    slots = jax.vmap(one_block_positions)(block_keys, counts, index)
    return slots.reshape(blocks * CAP)


def draw_positions(key, part):
    key = jax.random.fold_in(key, 11)
    sequence_keys = jax.random.split(key, SEQS)
    return jax.vmap(one_sequence_positions)(sequence_keys)


def steps_of(stream_key, extent, pieces, low, top_value):
    level = 1.0
    for axis_at, blocks in pieces:
        steps = jax.random.uniform(jax.random.fold_in(jax.random.fold_in(stream_key, 6), axis_at), (blocks,), jnp.float32, low / len(pieces), top_value / len(pieces))
        level = level * jnp.repeat(jnp.exp(steps), extent[axis_at] // blocks).reshape((-1,) + (1,) * (len(extent) - 1 - axis_at))
    return level


def scatter_about(own_key, shape, scale, reach, shards=(), kind=jnp.bfloat16):
    array = scale * jax.random.normal(own_key, shape, jnp.float32)
    if shards:
        array = array * steps_of(own_key, shape, shards, -0.22, 0.18)
    return jnp.clip(array, -reach, reach).astype(kind)


def setup_inputs(seed: int = 0, part: int = 0) -> dict:
    key_of = jax.random.split(jax.random.key(seed), 7)
    part_splits = jax.random.split(jax.random.fold_in(key_of[6], part), 7)
    query_rows = draw_query_rows(jax.random.fold_in(jax.random.fold_in(key_of[6], part), 71), part)
    key_rows = draw_key_rows(jax.random.fold_in(jax.random.fold_in(key_of[6], part), 71), part)
    value_rows = scatter_about(part_splits[2], (SEQS, SLOTS, KV_HEADS * DH), 1.0, 6.0, ((0, 4), (1, 4)))
    cotangent = scatter_about(part_splits[3], (SEQS, SLOTS, HEADS * DH), 1.0, 6.0, ((0, 4), (1, 4)))
    router_gate = jnp.clip(0.25 + 0.75 * jax.random.uniform(part_splits[4], (SEQS, SLOTS), jnp.float32) ** steps_of(part_splits[4], (SEQS, SLOTS), ((0, 4), (1, 4)), -0.2, 0.2), 0.25, 1.0)
    positions = draw_positions(jax.random.fold_in(jax.random.fold_in(key_of[6], part), 71), part)
    return {"query_rows": query_rows, "key_rows": key_rows, "value_rows": value_rows, "cotangent": cotangent, "router_gate": router_gate, "positions": positions}


THETA = 500000.0


def rotate(values, places, sign):
    half = values.shape[-1] // 2
    freq = jnp.power(jnp.float32(THETA), -2.0 * jnp.arange(half, dtype=jnp.float32) / values.shape[-1])
    angle = places[:, None] * freq[None, :]
    cosine = jnp.cos(angle)[:, None, :]
    sine = sign * jnp.sin(angle)[:, None, :]
    first = values[..., :half]
    second = values[..., half:]
    return jnp.concatenate([first * cosine - second * sine, second * cosine + first * sine], axis=-1)


def lowered(values):
    return lax.optimization_barrier(values.astype(jnp.bfloat16))


def one_sequence(items):
    query, key, value, cotangent, gate, places_int = items
    length = query.shape[0]
    groups = KV_HEADS
    ratio = HEADS // KV_HEADS
    scale = DH ** -0.5
    valid = places_int < SEQ_LEN
    places = places_int.astype(jnp.float32)
    query_rot = lowered(rotate(query.astype(jnp.float32).reshape(length, HEADS, DH), places, 1.0))
    key_rot = lowered(rotate(key.astype(jnp.float32).reshape(length, groups, DH), places, 1.0))
    visible = valid[None, :] & (places_int[None, :] <= places_int[:, None])
    gate_used = jnp.where(valid, gate, 0.0).astype(jnp.float32)
    query_groups = query_rot.reshape(length, groups, ratio, DH).transpose(1, 2, 0, 3)
    key_groups = key_rot.transpose(1, 0, 2)
    value_groups = value.reshape(length, groups, DH).transpose(1, 0, 2)
    grad_groups = cotangent.astype(jnp.float32).reshape(length, groups, ratio, DH).transpose(1, 2, 0, 3)
    block_count = length // CAP

    def one_group(parts):
        query_head, key_head, value_head, grad_head = parts
        query_full = query_head.astype(jnp.float32)
        key_full = key_head.astype(jnp.float32)
        value_full = value_head.astype(jnp.float32)
        scores = jnp.einsum("rqd,kd->rqk", query_full, key_full) * scale
        scores = jnp.where(visible[None], scores, -1e30)
        top = jnp.max(scores, axis=-1, keepdims=True)
        total = jnp.sum(jnp.where(visible[None], jnp.exp(scores - top), 0.0), axis=-1, keepdims=True)
        log_total = top + jnp.log(total)
        exact_weights = jnp.where(visible[None], jnp.exp(scores - log_total), 0.0)
        weights = lowered(exact_weights).astype(jnp.float32)
        attn = jnp.einsum("rqk,kd->rqd", weights, value_full)
        out_grad = lowered(grad_head * gate_used[None, :, None]).astype(jnp.float32)
        gate_part = jnp.sum(grad_head * attn, axis=(0, 2))
        delta = jnp.sum(out_grad * attn, axis=-1, keepdims=True)
        prob_grad = jnp.einsum("rqd,kd->rqk", out_grad, value_full)
        score_grad = lowered(exact_weights * (prob_grad - delta)).astype(jnp.float32)
        query_acc = jnp.einsum("rqk,kd->rqd", score_grad, key_full) * scale
        score_blocks = score_grad.reshape(ratio, block_count, CAP, length)
        query_blocks = query_full.reshape(ratio, block_count, CAP, DH)
        key_part = lowered(jnp.einsum("rnck,rncd->nkd", score_blocks, query_blocks) * scale).astype(jnp.float32)
        weight_blocks = weights.reshape(ratio, block_count, CAP, length)
        grad_blocks = out_grad.reshape(ratio, block_count, CAP, DH)
        value_part = lowered(jnp.einsum("rnck,rncd->nkd", weight_blocks, grad_blocks)).astype(jnp.float32)
        return query_acc, jnp.sum(key_part, axis=0), jnp.sum(value_part, axis=0), gate_part

    query_acc, key_sum, value_sum, gate_parts = lax.map(one_group, (query_groups, key_groups, value_groups, grad_groups))
    query_grad = rotate(query_acc.transpose(2, 0, 1, 3).reshape(length, HEADS, DH), places, -1.0)
    query_grad = query_grad.astype(jnp.bfloat16).reshape(length, HEADS * DH)
    key_grad = rotate(key_sum.transpose(1, 0, 2), places, -1.0).astype(jnp.bfloat16).reshape(length, groups * DH)
    value_grad = value_sum.transpose(1, 0, 2).reshape(length, groups * DH).astype(jnp.bfloat16)
    gate_grad = jnp.where(valid, jnp.sum(gate_parts, axis=0), 0.0).astype(jnp.float32)
    return query_grad, key_grad, value_grad, gate_grad


def reference(query_rows, key_rows, value_rows, cotangent, router_gate, positions):
    query_grad, key_grad, value_grad, gate_grad = lax.map(one_sequence, (query_rows, key_rows, value_rows, cotangent, router_gate, positions))
    return (query_grad, key_grad, value_grad, gate_grad)
```

```python
import functools
import math

import jax
import jax.numpy as jnp
from jax import lax
from jax.experimental import pallas as pl
from jax.experimental.pallas import tpu as pltpu
from jax.sharding import PartitionSpec as P

DH = 128
LOCAL = 1024
THETA = 500000.0
EXTRA = 16
HIDDEN = -1e30
SCALE = DH**-0.5
LOG2E = math.log2(math.e)
LN2 = math.log(2.0)
VMEM_LIMIT = 50 * 1024 * 1024

NT = (((1,), (1,)), ((), ()))
NN = (((1,), (0,)), ((), ()))
TN = (((0,), (0,)), ((), ()))


def dot(a, b, dims):
    return lax.dot_general(a, b, dims, preferred_element_type=jnp.float32)


def rotate(values, cosine, sine):
    return values * cosine + pltpu.roll(values, DH // 2, 1) * sine


def pack_kernel(key_ref, value_ref, cos_ref, sin_ref, pos_ref, out_ref, *, groups, limit):
    rows = key_ref.shape[0]
    cosine, sine = cos_ref[...], sin_ref[...]
    for g in range(groups):
        own = key_ref[:, g * DH : (g + 1) * DH].astype(jnp.float32)
        out_ref[:rows, 2 * g * DH : (2 * g + 1) * DH] = rotate(own, cosine, sine).astype(jnp.bfloat16)
        out_ref[:rows, (2 * g + 1) * DH : (2 * g + 2) * DH] = value_ref[:, g * DH : (g + 1) * DH]
    count = jnp.sum(jnp.where(pos_ref[...] < limit, 1.0, 0.0), axis=1, keepdims=True)
    out_ref[rows:, :] = jnp.broadcast_to(count, (EXTRA, out_ref.shape[1])).astype(jnp.bfloat16)


def attention_kernel(query_ref, cot_ref, cos_ref, sin_ref, gate_ref, *refs, blocks, ratio):
    packets = refs[:blocks]
    query_grad_ref, delta_ref = refs[blocks : blocks + 2]
    parts = refs[blocks + 2 : 2 * blocks + 2]
    keys, values, query, cot, weights, score_grads = refs[2 * blocks + 2 :]
    rows = query_ref.shape[0]
    lanes = ratio * rows
    cosine, sine = cos_ref[...], sin_ref[...]
    for j in range(blocks):
        keys[j * rows : (j + 1) * rows, :] = packets[j][:rows, :DH]
        values[j * rows : (j + 1) * rows, :] = packets[j][:rows, DH:]
    for h in range(ratio):
        own = query_ref[:, h * DH : (h + 1) * DH].astype(jnp.float32)
        turned = rotate(own, cosine, sine) * (SCALE * LOG2E)
        query[h * rows : (h + 1) * rows, :] = turned.astype(jnp.bfloat16)
        cot[h * rows : (h + 1) * rows, :] = cot_ref[:, h * DH : (h + 1) * DH]
    for low in range(0, lanes, 256):
        width = min(256, lanes - low)
        here = slice(low, low + width)
        scores = dot(keys[...], query[here, :], NT)
        slot = lax.broadcasted_iota(jnp.int32, (rows, width), 0)
        lane = lax.broadcasted_iota(jnp.int32, (rows, width), 1) + low
        for h in range(1, ratio):
            lane = jnp.where(lane >= rows, lane - rows, lane)
        shown = [jnp.where(slot <= lane, scores[:rows], HIDDEN)]
        slot_f = slot.astype(jnp.float32)
        for j in range(1, blocks):
            count = packets[j][rows:, :DH].astype(jnp.float32)[:1]
            count = jnp.concatenate([count] * (width // DH), axis=1)
            shown.append(jnp.where(slot_f < count, scores[j * rows : (j + 1) * rows], HIDDEN))
        scores = jnp.concatenate(shown, axis=0)
        top = jnp.max(scores, axis=0, keepdims=True)
        raw = jnp.exp2(scores - top)
        inverse = 1.0 / jnp.sum(raw, axis=0, keepdims=True)
        prob_grad = dot(values[...], cot[here, :], NT)
        delta = jnp.sum(raw * prob_grad, axis=0, keepdims=True) * inverse
        delta_ref[:, here] = delta
        gated = raw * (inverse * gate_ref[:, here])
        weights[:, here] = gated.astype(jnp.bfloat16)
        score_grads[:, here] = (gated * (prob_grad - delta)).astype(jnp.bfloat16)
    for j in range(blocks):
        there = slice(j * rows, (j + 1) * rows)
        key_part = dot(score_grads[there, :], query[...], NN) * LN2
        value_part = dot(weights[there, :], cot[...], NN)
        parts[j][:, :DH] = key_part.astype(parts[j].dtype)
        parts[j][:, DH:] = value_part.astype(parts[j].dtype)
    query_acc = dot(score_grads[...], keys[...], TN) * SCALE
    for h in range(ratio):
        query_grad_ref[:, h * DH : (h + 1) * DH] = rotate(
            query_acc[h * rows : (h + 1) * rows], cosine, -sine
        ).astype(jnp.bfloat16)


def finish_kernel(own_ref, cos_ref, sin_ref, *refs, groups):
    got, (key_grad_ref, value_grad_ref) = refs[:-2], refs[-2:]
    total = own_ref[...]
    for ref in got:
        total = total + ref[...].astype(jnp.float32)
    cosine, sine = cos_ref[...], sin_ref[...]
    for g in range(groups):
        here = slice(g * DH, (g + 1) * DH)
        key_sum = total[:, 2 * g * DH : (2 * g + 1) * DH]
        key_grad_ref[:, here] = rotate(key_sum, cosine, -sine).astype(jnp.bfloat16)
        value_grad_ref[:, here] = total[:, (2 * g + 1) * DH : (2 * g + 2) * DH].astype(jnp.bfloat16)


def per_device(query_rows, key_rows, value_rows, cotangent, router_gate, positions):
    rows, heads_width = query_rows.shape[1:]
    group_width = key_rows.shape[2]
    groups = group_width // DH
    ratio = heads_width // group_width
    parts = lax.axis_size("ctx")
    chips = parts // 2
    limit = parts * LOCAL
    params = pltpu.CompilerParams(vmem_limit_bytes=VMEM_LIMIT)

    half = DH // 2
    index = (jnp.arange(DH, dtype=jnp.int32) % half).astype(jnp.float32)
    freq = jnp.power(jnp.float32(THETA), -2.0 * index / DH)
    angle = positions[0].astype(jnp.float32)[:, None] * freq[None, :]
    cosine = jnp.cos(angle)
    sign = jnp.where(jnp.arange(DH) < half, -1.0, 1.0).astype(jnp.float32)
    sine = jnp.sin(angle) * sign
    valid = positions < limit
    gate = jnp.tile(jnp.where(valid, router_gate, 0.0), (1, ratio))

    packet = pl.pallas_call(
        functools.partial(pack_kernel, groups=groups, limit=limit),
        out_shape=jax.ShapeDtypeStruct((rows + EXTRA, 2 * group_width), jnp.bfloat16),
        compiler_params=params,
    )(key_rows[0], value_rows[0], cosine, sine, positions)

    swap = [[(2 * x + k, 2 * x + 1 - k) for x in range(s, chips) for k in range(2)] for s in range(chips)]
    hop = [[(2 * x + k, 2 * (x + s) + k) for x in range(chips - s) for k in range(2)] for s in range(chips)]
    up = [(2 * x, 2 * x + 1) for x in range(chips)]
    back = lambda pairs: [(b, a) for a, b in pairs]

    far = [lax.ppermute(packet, "ctx", hop[s]) for s in range(1, chips)]
    near = lax.ppermute(packet, "ctx", up)
    crossed = [lax.ppermute(far[s - 1], "ctx", swap[s]) for s in range(1, chips)]
    packets = [packet, near] + far + crossed
    blocks = len(packets)

    whole = lambda shape: pl.BlockSpec(shape, lambda g: (0, 0))
    out = pl.pallas_call(
        functools.partial(attention_kernel, blocks=blocks, ratio=ratio),
        grid=(groups,),
        in_specs=[
            pl.BlockSpec((rows, ratio * DH), lambda g: (0, g)),
            pl.BlockSpec((rows, ratio * DH), lambda g: (0, g)),
            whole((rows, DH)),
            whole((rows, DH)),
            whole((1, ratio * rows)),
        ]
        + [pl.BlockSpec((rows + EXTRA, 2 * DH), lambda g: (0, g))] * blocks,
        out_specs=[
            pl.BlockSpec((rows, ratio * DH), lambda g: (0, g)),
            pl.BlockSpec((None, 1, ratio * rows), lambda g: (g, 0, 0)),
        ]
        + [pl.BlockSpec((rows, 2 * DH), lambda g: (0, g))] * blocks,
        out_shape=[
            jax.ShapeDtypeStruct((rows, heads_width), jnp.bfloat16),
            jax.ShapeDtypeStruct((groups, 1, ratio * rows), jnp.float32),
            jax.ShapeDtypeStruct((rows, 2 * group_width), jnp.float32),
        ]
        + [jax.ShapeDtypeStruct((rows, 2 * group_width), jnp.bfloat16)] * (blocks - 1),
        scratch_shapes=[
            pltpu.VMEM((blocks * rows, DH), jnp.bfloat16),
            pltpu.VMEM((blocks * rows, DH), jnp.bfloat16),
            pltpu.VMEM((ratio * rows, DH), jnp.bfloat16),
            pltpu.VMEM((ratio * rows, DH), jnp.bfloat16),
            pltpu.VMEM((blocks * rows, ratio * rows), jnp.bfloat16),
            pltpu.VMEM((blocks * rows, ratio * rows), jnp.bfloat16),
        ],
        compiler_params=params,
    )(query_rows[0], cotangent[0], cosine, sine, gate, *packets)
    query_grad, delta, own_part, near_part = out[:4]
    far_parts, crossed_parts = out[4 : 3 + chips], out[3 + chips :]

    got = [lax.ppermute(near_part, "ctx", back(up))]
    for s in range(1, chips):
        other = lax.ppermute(crossed_parts[s - 1], "ctx", swap[s])
        both = far_parts[s - 1].astype(jnp.float32) + other.astype(jnp.float32)
        got.append(lax.ppermute(both.astype(jnp.bfloat16), "ctx", back(hop[s])))
    gate_grad = jnp.where(valid[0], jnp.sum(delta.reshape(groups * ratio, rows), axis=0), 0.0)
    key_grad, value_grad = pl.pallas_call(
        functools.partial(finish_kernel, groups=groups),
        out_shape=[jax.ShapeDtypeStruct((rows, group_width), jnp.bfloat16)] * 2,
        compiler_params=params,
    )(own_part, cosine, sine, *got)
    return (query_grad[None], key_grad[None], value_grad[None], gate_grad[None])


def solution(mesh):
    wide = P(("group", "dp"), "ctx", None)
    narrow = P(("group", "dp"), "ctx")
    return jax.shard_map(
        per_device,
        mesh=mesh,
        in_specs=(wide, wide, wide, wide, narrow, narrow),
        out_specs=(wide, wide, wide, narrow),
        check_vma=False,
    )
```

```python
import functools
import math

import jax
import jax.numpy as jnp
import numpy as np
from jax import lax
from jax.experimental import pallas as pl
from jax.experimental.pallas import tpu as pltpu
from jax.sharding import PartitionSpec as P

DH = 128
LOCAL = 1024
THETA = 500000.0
EXTRA = 16
HIDDEN = -1e30
SCALE = DH**-0.5
LOG2E = math.log2(math.e)
LN2 = math.log(2.0)

NT = (((1,), (1,)), ((), ()))
NN = (((1,), (0,)), ((), ()))
TN = (((0,), (0,)), ((), ()))
F32 = jnp.float32
BF16 = jnp.bfloat16


def few_bits(value, bits):
    unit = 2.0 ** (math.floor(math.log2(value)) + 1 - bits)
    return math.floor(value / unit) * unit


QUARTER_1 = few_bits(math.pi / 2, 10)
QUARTER_2 = few_bits(math.pi / 2 - QUARTER_1, 10)
QUARTER_3 = math.pi / 2 - QUARTER_1 - QUARTER_2


def dot(a, b, dims):
    return lax.dot_general(a, b, dims, preferred_element_type=F32)


def core_of():
    return lax.rem(lax.axis_index("ctx"), 2)


def rotate(values, cosine, sine):
    return values * cosine + pltpu.roll(values, DH // 2, 1) * sine


def sine_cosine(angle):
    turns = jnp.floor(angle * (2.0 / math.pi) + 0.5)
    rest = ((angle - turns * QUARTER_1) - turns * QUARTER_2) - turns * QUARTER_3
    square = rest * rest
    sine = ((-1.9515295891e-4 * square + 8.3321608736e-3) * square - 1.6666654611e-1) * square * rest + rest
    cosine = (2.443315711809948e-5 * square - 1.388731625493765e-3) * square + 4.166664568298827e-2
    cosine = cosine * square * square - 0.5 * square + 1.0
    quarter = turns.astype(jnp.int32)
    odd = (quarter & 1) == 1
    first, second = jnp.where(odd, cosine, sine), jnp.where(odd, sine, cosine)
    return (
        jnp.where((quarter & 2) == 2, -first, first),
        jnp.where(((quarter + 1) & 2) == 2, -second, second),
    )


def split_rows(row, height):
    high = row.astype(BF16).astype(F32)
    middle = (row - high).astype(BF16).astype(F32)
    low = row - high - middle
    line = lax.broadcasted_iota(jnp.int32, (height, row.shape[1]), 0)
    rows = jnp.where(line == 0, high, jnp.where(line == 1, middle, jnp.where(line == 2, low, 0.0)))
    return rows.astype(BF16)


def joined_row(rows):
    return jnp.sum(rows.astype(F32), axis=0, keepdims=True)


def pack_keys_kernel(
    key_in, value_in, pos_in, freq_in, mine_ref, theirs_ref, cos_ref, sin_ref, key, value, pos, freq, sems, *, limit
):
    copies = [
        pltpu.make_async_copy(source, target, sems.at[i])
        for i, (source, target) in enumerate(((pos_in, pos), (freq_in, freq), (key_in, key), (value_in, value)))
    ]
    for copy in copies:
        copy.start()
    rows = key.shape[0]
    half = key.shape[1] // 2
    core = core_of()
    copies[0].wait()
    copies[1].wait()
    places = pos[...]
    count = jnp.sum(jnp.where(places < limit, 1.0, 0.0), axis=1, keepdims=True)
    count = jnp.broadcast_to(count, (EXTRA, 2 * half)).astype(BF16)
    down = lax.broadcasted_iota(jnp.int32, (rows, rows), 0)
    along = lax.broadcasted_iota(jnp.int32, (rows, rows), 1)
    column = jnp.sum(jnp.where(down == along, places.astype(F32), 0.0), axis=1, keepdims=True)
    sine, cosine = sine_cosine(column * freq[...])
    lane = lax.broadcasted_iota(jnp.int32, (rows, DH), 1)
    sine = jnp.where(lane < DH // 2, -sine, sine)
    cos_ref[...] = cosine
    sin_ref[...] = sine
    copies[2].wait()
    copies[3].wait()
    for out_ref, side in ((mine_ref, core), (theirs_ref, 1 - core)):
        for i in range(half // DH):
            there = pl.ds(pl.multiple_of(side * half + i * DH, DH), DH)
            turned = rotate(key[:, there].astype(F32), cosine, sine)
            out_ref[:rows, 2 * i * DH : (2 * i + 1) * DH] = turned.astype(BF16)
            out_ref[:rows, (2 * i + 1) * DH : (2 * i + 2) * DH] = value[:, there]
        out_ref[rows:, :] = count


def pack_queries_kernel(
    query_in, cot_in, cos_in, sin_in, gate_in, mine_in, theirs_in, out_ref, query, cos_ref, sin_ref, gate_ref, sems
):
    rows = query.shape[0]
    half = query.shape[1] // 2
    core = core_of()
    pairs = [
        (query_in, query),
        (cos_in, cos_ref),
        (sin_in, sin_ref),
        (gate_in, gate_ref),
        (mine_in, out_ref.at[core, :, 2 * half :]),
        (theirs_in, out_ref.at[1 - core, :, 2 * half :]),
        (cot_in.at[:, :half], out_ref.at[0, :rows, half : 2 * half]),
        (cot_in.at[:, half:], out_ref.at[1, :rows, half : 2 * half]),
    ]
    copies = [pltpu.make_async_copy(source, target, sems.at[i]) for i, (source, target) in enumerate(pairs)]
    for copy in copies:
        copy.start()
    for copy in copies[:4]:
        copy.wait()
    cosine, sine = cos_ref[...] * (SCALE * LOG2E), sin_ref[...] * (SCALE * LOG2E)
    gate = split_rows(gate_ref[...], EXTRA)
    for side in range(2):
        for i in range(half // DH):
            there = slice(side * half + i * DH, side * half + (i + 1) * DH)
            turned = rotate(query[:, there].astype(F32), cosine, sine)
            out_ref[side, :rows, i * DH : (i + 1) * DH] = turned.astype(BF16)
        out_ref[side, rows:, : gate.shape[1]] = gate
    for copy in copies[4:]:
        copy.wait()


def chunks(low, high):
    return [slice(at, min(at + 256, high)) for at in range(low, high, 256)]


def local_kernel(packets, keys, values, query, cot, gate, raws, grads, tops, sums, crosses, *, ratio):
    rows = packets.shape[1] - EXTRA
    half_groups = keys.shape[0]
    wide = ratio * rows
    half = half_groups * ratio * DH
    for side in range(2):
        there = slice(side * rows, (side + 1) * rows)
        for i in range(half_groups):
            at = 2 * half + 2 * i * DH
            keys[i, there, :] = packets[side, :rows, at : at + DH]
            values[i, there, :] = packets[side, :rows, at + DH : at + 2 * DH]
            for h in range(ratio):
                to = slice(side * wide + h * rows, side * wide + (h + 1) * rows)
                at = (i * ratio + h) * DH
                query[i, to, :] = packets[side, :rows, at : at + DH]
                cot[i, to, :] = packets[side, :rows, half + at : half + at + DH]
        gate[:, side * wide : (side + 1) * wide] = joined_row(packets[side, rows:, :wide])
    count = packets[0, rows:, 2 * half : 2 * half + 256].astype(F32)[:1]
    for i in range(half_groups):
        for block in range(2):
            reach = (block + 1) * rows
            for here in chunks(block * wide, (block + 1) * wide):
                width = here.stop - here.start
                scores = dot(keys[i, :reach, :], query[i, here, :], NT)
                slot = lax.broadcasted_iota(jnp.int32, (rows, width), 0)
                lane = lax.broadcasted_iota(jnp.int32, (rows, width), 1) + (here.start - block * wide)
                for h in range(1, ratio):
                    lane = jnp.where(lane >= rows, lane - rows, lane)
                shown = jnp.where(slot <= lane, scores[block * rows :], HIDDEN)
                if block:
                    before = jnp.where(slot.astype(F32) < count[:, :width], scores[:rows], HIDDEN)
                    shown = jnp.concatenate([before, shown], axis=0)
                top = jnp.max(shown, axis=0, keepdims=True)
                raw = jnp.exp2(shown - top)
                prob_grad = dot(values[i, :reach, :], cot[i, here, :], NT)
                raws[i, :reach, here] = raw
                grads[i, :reach, here] = prob_grad
                tops[i, :, here] = top
                sums[i, :, here] = jnp.sum(raw, axis=0, keepdims=True)
                crosses[i, :, here] = jnp.sum(raw * prob_grad, axis=0, keepdims=True)


def part_of(weights, score_grads, query, cot, out_ref, i, there, lanes):
    key_part = dot(score_grads[i, there, lanes], query[i, lanes, :], NN) * LN2
    value_part = dot(weights[i, there, lanes], cot[i, lanes, :], NN)
    out_ref[:, 2 * i * DH : (2 * i + 1) * DH] = key_part.astype(out_ref.dtype)
    out_ref[:, (2 * i + 1) * DH : (2 * i + 2) * DH] = value_part.astype(out_ref.dtype)


def far_kernel(query, cot, gate, tops, sums, crosses, *refs, blocks):
    packets = refs[:blocks]
    far_keys, weights, score_grads, factors, deltas = refs[blocks : blocks + 5]
    parts = refs[blocks + 5 : 2 * blocks + 5]
    far_values = refs[-1]
    rows = packets[0].shape[0] - EXTRA
    half_groups, lanes = query.shape[:2]
    for j in range(blocks):
        there = slice(j * rows, (j + 1) * rows)
        for i in range(half_groups):
            far_keys[i, there, :] = packets[j][:rows, 2 * i * DH : (2 * i + 1) * DH]
            far_values[i, there, :] = packets[j][:rows, (2 * i + 1) * DH : (2 * i + 2) * DH]
    counts = [packet[rows:, :256].astype(F32)[:1] for packet in packets]
    for i in range(half_groups):
        for here in chunks(0, lanes):
            width = here.stop - here.start
            scores = dot(far_keys[i], query[i, here, :], NT)
            slot = lax.broadcasted_iota(jnp.int32, (rows, width), 0).astype(F32)
            shown = [
                jnp.where(slot < counts[j][:, :width], scores[j * rows : (j + 1) * rows], HIDDEN)
                for j in range(blocks)
            ]
            shown = jnp.concatenate(shown, axis=0)
            old_top = tops[i, :, here]
            top = jnp.maximum(old_top, jnp.max(shown, axis=0, keepdims=True))
            raw = jnp.exp2(shown - top)
            shrink = jnp.exp2(old_top - top)
            inverse = 1.0 / (sums[i, :, here] * shrink + jnp.sum(raw, axis=0, keepdims=True))
            prob_grad = dot(far_values[i], cot[i, here, :], NT)
            cross = crosses[i, :, here] * shrink + jnp.sum(raw * prob_grad, axis=0, keepdims=True)
            delta = cross * inverse
            factor = inverse * gate[:, here]
            factors[i, :, here] = factor * shrink
            deltas[i, :, here] = delta
            gated = raw * factor
            weights[i, :, here] = gated.astype(BF16)
            score_grads[i, :, here] = (gated * (prob_grad - delta)).astype(BF16)
        for j, out_ref in enumerate(parts):
            part_of(weights, score_grads, query, cot, out_ref, i, slice(j * rows, (j + 1) * rows), slice(0, lanes))


def near_kernel(
    raws, grads, factors, deltas, keys, query, cot, far_keys, far_grads,
    part_mine, out_ref, weights, score_grads, parts,
    *, ratio
):
    rows = part_mine.shape[0]
    half_groups = keys.shape[0]
    wide = ratio * rows
    half = half_groups * ratio * DH
    for i in range(half_groups):
        for block in range(2):
            reach = (block + 1) * rows
            for here in chunks(block * wide, (block + 1) * wide):
                gated = raws[i, :reach, here] * factors[i, :, here]
                weights[i, :reach, here] = gated.astype(BF16)
                score_grads[i, :reach, here] = (gated * (grads[i, :reach, here] - deltas[i, :, here])).astype(BF16)
        for block in range(2):
            there, lanes = slice(block * rows, (block + 1) * rows), slice(block * wide, 2 * wide)
            part_of(weights, score_grads, query, cot, parts.at[block], i, there, lanes)
            reach, lanes = (block + 1) * rows, slice(block * wide, (block + 1) * wide)
            total = dot(score_grads[i, :reach, lanes], keys[i, :reach, :], TN)
            total = (total + dot(far_grads[i, :, lanes], far_keys[i], TN)) * SCALE
            for h in range(ratio):
                at = (i * ratio + h) * DH
                out_ref[block, :rows, at : at + DH] = total[h * rows : (h + 1) * rows].astype(BF16)
    part_mine[...] = parts[core_of()]
    for block in range(2):
        out_ref[block, :rows, half:] = parts[block].astype(BF16)
    summed = deltas[0]
    for i in range(1, half_groups):
        summed = summed + deltas[i]
    down = lax.broadcasted_iota(jnp.int32, (wide, rows), 0)
    along = lax.broadcasted_iota(jnp.int32, (wide, rows), 1)
    for h in range(1, ratio):
        down = jnp.where(down >= rows, down - rows, down)
    chosen = jnp.where(down == along, 1.0, 0.0).astype(BF16)
    for block in range(2):
        own = joined_row(dot(split_rows(summed[:, block * wide : (block + 1) * wide], 16), chosen, NN))
        out_ref[block, rows:, :rows] = split_rows(own, EXTRA)


def finish_queries_kernel(back, pos_ref, cos_ref, sin_ref, query_grad, gate_grad, done, *, limit):
    rows = cos_ref.shape[0]
    half = query_grad.shape[1] // 2
    cosine, sine = cos_ref[...], -sin_ref[...]
    for side in range(2):
        for i in range(half // DH):
            there = slice(side * half + i * DH, side * half + (i + 1) * DH)
            turned = rotate(back[side, :rows, i * DH : (i + 1) * DH].astype(F32), cosine, sine)
            query_grad[:, there] = turned.astype(BF16)
    gate = joined_row(back[0, rows:, :rows]) + joined_row(back[1, rows:, :rows])
    gate_grad[...] = jnp.where(pos_ref[...] < limit, gate, 0.0)
    done[...] = jnp.zeros_like(done)


def finish_keys_kernel(part_mine, back, cos_ref, sin_ref, *refs):
    got, (key_grad, value_grad) = refs[:-2], refs[-2:]
    rows, width = part_mine.shape
    half = width // 2
    core = core_of()
    cosine, sine = cos_ref[...], -sin_ref[...]
    total = part_mine[...]
    other = back[1 - core, :rows, back.shape[2] - width :].astype(F32)
    for s in range(len(got) // 2):
        other = other + got[2 * s][...].astype(F32)
        total = total + got[2 * s + 1][...].astype(F32)
    for values, side in ((total, core), (other, 1 - core)):
        for i in range(half // DH):
            there = pl.ds(pl.multiple_of(side * half + i * DH, DH), DH)
            turned = rotate(values[:, 2 * i * DH : (2 * i + 1) * DH], cosine, sine)
            key_grad[:, there] = turned.astype(BF16)
            value_grad[:, there] = values[:, (2 * i + 1) * DH : (2 * i + 2) * DH].astype(BF16)


def per_device(query_rows, key_rows, value_rows, cotangent, router_gate, positions):
    rows, heads_width = query_rows.shape[1:]
    group_width = key_rows.shape[2]
    groups = group_width // DH
    ratio = heads_width // group_width
    half_groups, half_width = groups // 2, heads_width // 2
    parts = lax.axis_size("ctx")
    chips = parts // 2
    limit = parts * LOCAL
    wide = ratio * rows
    params = pltpu.CompilerParams(vmem_limit_bytes=(16 + 4 * chips) * 1024 * 1024)
    full = pltpu.CompilerParams(vmem_limit_bytes=63 * 1024 * 1024)

    def call(kernel, name, outs, *args, scratch=(), after=(), flops=10**6, in_hbm=False):
        used = len(args)
        specs = [pl.BlockSpec(memory_space=pltpu.HBM if in_hbm else pltpu.VMEM)] * used
        specs += [pl.BlockSpec(memory_space=pl.ANY)] * len(after)

        def body(*refs):
            kernel(*refs[:used], *refs[used + len(after) :])

        return pl.pallas_call(
            body,
            out_shape=[jax.ShapeDtypeStruct(*out) for out in outs],
            in_specs=specs,
            scratch_shapes=list(scratch),
            compiler_params=full if in_hbm else params,
            cost_estimate=pl.CostEstimate(flops=flops, bytes_accessed=1000, transcendentals=0),
            name=name,
        )(*args, *after)

    index = np.arange(DH) % (DH // 2)
    freq = jnp.asarray((THETA ** (-2.0 * index / DH)).astype(np.float32))[None]
    packet = ((rows + EXTRA, group_width), BF16)
    table = ((rows, DH), F32)
    kv_mine, kv_theirs, cosine, sine = call(
        functools.partial(pack_keys_kernel, limit=limit),
        "pack_keys",
        [packet, packet, table, table],
        key_rows[0],
        value_rows[0],
        positions,
        freq,
        in_hbm=True,
        scratch=[
            pltpu.VMEM((rows, group_width), BF16),
            pltpu.VMEM((rows, group_width), BF16),
            pltpu.VMEM((1, rows), jnp.int32),
            pltpu.VMEM((1, DH), F32),
            pltpu.SemaphoreType.DMA((4,)),
        ],
    )

    hop = [[(2 * x + k, 2 * (x + s) + k) for x in range(chips - s) for k in range(2)] for s in range(chips)]
    cross = [[(a, b + 1 - 2 * (b % 2)) for a, b in pairs] for pairs in hop]
    back_hop = [[(b, a) for a, b in pairs] for pairs in hop]
    back_cross = [[(b, a) for a, b in pairs] for pairs in cross]

    far_own = [lax.ppermute(kv_mine, "ctx", hop[s]) for s in range(1, chips)]
    far_sib = [lax.ppermute(kv_theirs, "ctx", cross[s]) for s in range(1, chips)]

    gate = jnp.tile(jnp.where(positions < limit, router_gate, 0.0), (1, ratio))
    pairs = [[2 * x, 2 * x + 1] for x in range(chips)]
    swap = lambda both: lax.all_to_all(both, "ctx", 0, 0, axis_index_groups=pairs)
    (packed,) = call(
        pack_queries_kernel,
        "pack_queries",
        [((2, rows + EXTRA, heads_width + group_width), BF16)],
        query_rows[0],
        cotangent[0],
        cosine,
        sine,
        gate,
        kv_mine,
        kv_theirs,
        in_hbm=True,
        scratch=[
            pltpu.VMEM((rows, heads_width), BF16),
            pltpu.VMEM((rows, DH), F32),
            pltpu.VMEM((rows, DH), F32),
            pltpu.VMEM((1, wide), F32),
            pltpu.SemaphoreType.DMA((8,)),
        ],
    )
    packets = swap(packed)

    row = ((half_groups, 1, 2 * wide), F32)
    table = ((half_groups, 2 * rows, 2 * wide), F32)
    kv_table = ((half_groups, 2 * rows, DH), BF16)
    q_table = ((half_groups, 2 * wide, DH), BF16)
    keys, values, query, cot, gate_row, raws, grads, tops, sums, crosses = call(
        functools.partial(local_kernel, ratio=ratio),
        "local_scores",
        [kv_table, kv_table, q_table, q_table, ((1, 2 * wide), F32), table, table, row, row, row],
        packets,
        flops=3 * 10**6,
    )

    blocks = 2 * (chips - 1)
    far_table = ((half_groups, blocks * rows, 2 * wide), BF16)
    part_shape = ((rows, group_width), BF16)
    far_keys, _, far_grads, factors, deltas, *far_parts = call(
        functools.partial(far_kernel, blocks=blocks),
        "far_scores",
        [((half_groups, blocks * rows, DH), BF16), far_table, far_table, row, row] + [part_shape] * blocks,
        query,
        cot,
        gate_row,
        tops,
        sums,
        crosses,
        *far_sib,
        *far_own,
        flops=4 * 10**6,
        scratch=[pltpu.VMEM((half_groups, blocks * rows, DH), BF16)],
    )
    sib_got = [lax.ppermute(far_parts[s - 1], "ctx", back_cross[s]) for s in range(1, chips)]
    own_got = [lax.ppermute(far_parts[chips + s - 2], "ctx", back_hop[s]) for s in range(1, chips)]

    part_mine, packed = call(
        functools.partial(near_kernel, ratio=ratio),
        "near_grads",
        [
            ((rows, group_width), F32),
            ((2, rows + EXTRA, half_width + group_width), BF16),
        ],
        raws,
        grads,
        factors,
        deltas,
        keys,
        query,
        cot,
        far_keys,
        far_grads,
        flops=4 * 10**6,
        scratch=[
            pltpu.VMEM((half_groups, 2 * rows, 2 * wide), BF16),
            pltpu.VMEM((half_groups, 2 * rows, 2 * wide), BF16),
            pltpu.VMEM((2, rows, group_width), F32),
        ],
    )
    back = swap(packed)
    query_grad, gate_grad, done = call(
        functools.partial(finish_queries_kernel, limit=limit),
        "finish_queries",
        [((rows, heads_width), BF16), ((1, rows), F32), ((8, DH), F32)],
        back,
        positions,
        cosine,
        sine,
    )
    key_grad, value_grad = call(
        finish_keys_kernel,
        "finish_keys",
        [((rows, group_width), BF16)] * 2,
        part_mine,
        back,
        cosine,
        sine,
        *[part for pair in zip(sib_got, own_got) for part in pair],
        after=[done],
    )
    return (query_grad[None], key_grad[None], value_grad[None], gate_grad)


def solution(mesh):
    wide = P(("group", "dp"), "ctx", None)
    narrow = P(("group", "dp"), "ctx")
    return jax.shard_map(
        per_device,
        mesh=mesh,
        in_specs=(wide, wide, wide, wide, narrow, narrow),
        out_specs=(wide, wide, wide, narrow),
        check_vma=False,
    )
```

```python
import functools
import math

import jax
import jax.numpy as jnp
import numpy as np
from jax import lax
from jax.experimental import pallas as pl
from jax.experimental.pallas import tpu as pltpu
from jax.sharding import PartitionSpec as P

DH = 128
LOCAL = 1024
THETA = 500000.0
EXTRA = 16
HIDDEN = -1e30
SCALE = DH**-0.5
LOG2E = math.log2(math.e)
LN2 = math.log(2.0)

NT = (((1,), (1,)), ((), ()))
NN = (((1,), (0,)), ((), ()))
TN = (((0,), (0,)), ((), ()))
F32 = jnp.float32
BF16 = jnp.bfloat16


def few_bits(value, bits):
    unit = 2.0 ** (math.floor(math.log2(value)) + 1 - bits)
    return math.floor(value / unit) * unit


QUARTER_1 = few_bits(math.pi / 2, 10)
QUARTER_2 = few_bits(math.pi / 2 - QUARTER_1, 10)
QUARTER_3 = math.pi / 2 - QUARTER_1 - QUARTER_2


def dot(a, b, dims):
    return lax.dot_general(a, b, dims, preferred_element_type=F32)


def core_of():
    return lax.rem(lax.axis_index("ctx"), 2)


def rotate(values, cosine, sine):
    return values * cosine + pltpu.roll(values, DH // 2, 1) * sine


def sine_cosine(angle):
    turns = jnp.floor(angle * (2.0 / math.pi) + 0.5)
    rest = ((angle - turns * QUARTER_1) - turns * QUARTER_2) - turns * QUARTER_3
    square = rest * rest
    sine = ((-1.9515295891e-4 * square + 8.3321608736e-3) * square - 1.6666654611e-1) * square * rest + rest
    cosine = (2.443315711809948e-5 * square - 1.388731625493765e-3) * square + 4.166664568298827e-2
    cosine = cosine * square * square - 0.5 * square + 1.0
    quarter = turns.astype(jnp.int32)
    odd = (quarter & 1) == 1
    first, second = jnp.where(odd, cosine, sine), jnp.where(odd, sine, cosine)
    return (
        jnp.where((quarter & 2) == 2, -first, first),
        jnp.where(((quarter + 1) & 2) == 2, -second, second),
    )


def split_rows(row, height):
    high = row.astype(BF16).astype(F32)
    middle = (row - high).astype(BF16).astype(F32)
    low = row - high - middle
    line = lax.broadcasted_iota(jnp.int32, (height, row.shape[1]), 0)
    rows = jnp.where(line == 0, high, jnp.where(line == 1, middle, jnp.where(line == 2, low, 0.0)))
    return rows.astype(BF16)


def joined_row(rows):
    return jnp.sum(rows.astype(F32), axis=0, keepdims=True)


def pack_kernel(
    key_in, value_in, query_in, cot_in, gate_in, pos_in, freq_in, mine_out, theirs_out, packed_out, cos_out, sin_out,
    key, value, query, gate, pos, freq, mine, theirs, packed, cos_ref, sin_ref, sems, out_sems, *, limit
):
    rows, width = key.shape
    side_width = width // 2
    half = query.shape[1] // 2
    core = core_of()
    loads = [(pos_in, pos), (freq_in, freq), (key_in, key), (value_in, value), (gate_in, gate), (query_in, query)]
    for side in range(2):
        there = slice(side * half, (side + 1) * half)
        loads.append((cot_in.at[:, there], packed_out.at[side, :rows, half : 2 * half]))
    loads = [pltpu.make_async_copy(source, target, sems.at[i]) for i, (source, target) in enumerate(loads)]
    for copy in loads:
        copy.start()
    loads[0].wait()
    loads[1].wait()
    places = pos[...]
    count = jnp.sum(jnp.where(places < limit, 1.0, 0.0), axis=1, keepdims=True)
    count = jnp.broadcast_to(count, (EXTRA, width)).astype(BF16)
    down = lax.broadcasted_iota(jnp.int32, (rows, rows), 0)
    along = lax.broadcasted_iota(jnp.int32, (rows, rows), 1)
    column = jnp.sum(jnp.where(down == along, places.astype(F32), 0.0), axis=1, keepdims=True)
    sine, cosine = sine_cosine(column * freq[...])
    lane = lax.broadcasted_iota(jnp.int32, (rows, DH), 1)
    sine = jnp.where(lane < DH // 2, -sine, sine)
    cos_ref[...] = cosine
    sin_ref[...] = sine
    loads[2].wait()
    loads[3].wait()
    for out_ref, side in ((mine, core), (theirs, 1 - core)):
        for i in range(side_width // DH):
            there = pl.ds(pl.multiple_of(side * side_width + i * DH, DH), DH)
            turned = rotate(key[:, there].astype(F32), cosine, sine)
            out_ref[:rows, 2 * i * DH : (2 * i + 1) * DH] = turned.astype(BF16)
            out_ref[:rows, (2 * i + 1) * DH : (2 * i + 2) * DH] = value[:, there]
        out_ref[rows:, :] = count
    stores = [
        (mine, mine_out),
        (theirs, theirs_out),
        (cos_ref, cos_out),
        (sin_ref, sin_out),
        (mine, packed_out.at[core, :, 2 * half :]),
        (theirs, packed_out.at[1 - core, :, 2 * half :]),
    ]
    stores += [(packed.at[side], packed_out.at[side, :, :half]) for side in range(2)]
    stores = [pltpu.make_async_copy(source, target, out_sems.at[i]) for i, (source, target) in enumerate(stores)]
    for copy in stores[:6]:
        copy.start()
    loads[4].wait()
    loads[5].wait()
    gates = split_rows(jnp.where(places < limit, gate[...], 0.0), EXTRA)
    cosine, sine = cosine * (SCALE * LOG2E), sine * (SCALE * LOG2E)
    for side in range(2):
        for i in range(half // DH):
            there = slice(side * half + i * DH, side * half + (i + 1) * DH)
            turned = rotate(query[:, there].astype(F32), cosine, sine)
            packed[side, :rows, i * DH : (i + 1) * DH] = turned.astype(BF16)
        packed[side, rows:, :rows] = gates
        stores[6 + side].start()
    for copy in loads[6:] + stores:
        copy.wait()


def chosen(shape, ratio, dim):
    down = lax.broadcasted_iota(jnp.int32, shape, 0)
    along = lax.broadcasted_iota(jnp.int32, shape, 1)
    rows = shape[1 - dim]
    long, short = (down, along) if dim == 0 else (along, down)
    for _ in range(1, ratio):
        long = jnp.where(long >= rows, long - rows, long)
    return jnp.where(long == short, 1.0, 0.0).astype(BF16)


def chunks(low, high):
    return [slice(at, min(at + 256, high)) for at in range(low, high, 256)]


def local_kernel(packets, keys, values, query, cot, gate, raws, grads, tops, sums, crosses, *, ratio):
    rows = packets.shape[1] - EXTRA
    half_groups = keys.shape[0]
    wide = ratio * rows
    half = half_groups * ratio * DH
    for side in range(2):
        there = slice(side * rows, (side + 1) * rows)
        for i in range(half_groups):
            at = 2 * half + 2 * i * DH
            keys[i, there, :] = packets[side, :rows, at : at + DH]
            values[i, there, :] = packets[side, :rows, at + DH : at + 2 * DH]
            for h in range(ratio):
                to = slice(side * wide + h * rows, side * wide + (h + 1) * rows)
                at = (i * ratio + h) * DH
                query[i, to, :] = packets[side, :rows, at : at + DH]
                cot[i, to, :] = packets[side, :rows, half + at : half + at + DH]
        gates = dot(packets[side, rows:, :rows], chosen((rows, wide), ratio, 1), NN)
        gate[:, side * wide : (side + 1) * wide] = joined_row(gates)
    count = packets[0, rows:, 2 * half : 2 * half + 256].astype(F32)[:1]
    for i in range(half_groups):
        for block in range(2):
            reach = (block + 1) * rows
            for here in chunks(block * wide, (block + 1) * wide):
                width = here.stop - here.start
                scores = dot(keys[i, :reach, :], query[i, here, :], NT)
                slot = lax.broadcasted_iota(jnp.int32, (rows, width), 0)
                lane = lax.broadcasted_iota(jnp.int32, (rows, width), 1) + (here.start - block * wide)
                for h in range(1, ratio):
                    lane = jnp.where(lane >= rows, lane - rows, lane)
                shown = jnp.where(slot <= lane, scores[block * rows :], HIDDEN)
                if block:
                    before = jnp.where(slot.astype(F32) < count[:, :width], scores[:rows], HIDDEN)
                    shown = jnp.concatenate([before, shown], axis=0)
                top = jnp.max(shown, axis=0, keepdims=True)
                raw = jnp.exp2(shown - top)
                prob_grad = dot(values[i, :reach, :], cot[i, here, :], NT)
                raws[i, :reach, here] = raw
                grads[i, :reach, here] = prob_grad
                tops[i, :, here] = top
                sums[i, :, here] = jnp.sum(raw, axis=0, keepdims=True)
                crosses[i, :, here] = jnp.sum(raw * prob_grad, axis=0, keepdims=True)


def part_of(weights, score_grads, query, cot, out_ref, i, there, lanes):
    key_part = dot(score_grads[i, there, lanes], query[i, lanes, :], NN) * LN2
    value_part = dot(weights[i, there, lanes], cot[i, lanes, :], NN)
    out_ref[:, 2 * i * DH : (2 * i + 1) * DH] = key_part.astype(out_ref.dtype)
    out_ref[:, (2 * i + 1) * DH : (2 * i + 2) * DH] = value_part.astype(out_ref.dtype)


def far_kernel(query, cot, gate, tops, sums, crosses, *refs, blocks):
    packets = refs[:blocks]
    far_keys, weights, score_grads, factors, deltas = refs[blocks : blocks + 5]
    parts = refs[blocks + 5 : 2 * blocks + 5]
    far_values = refs[-1]
    rows = packets[0].shape[0] - EXTRA
    half_groups, lanes = query.shape[:2]
    for j in range(blocks):
        there = slice(j * rows, (j + 1) * rows)
        for i in range(half_groups):
            far_keys[i, there, :] = packets[j][:rows, 2 * i * DH : (2 * i + 1) * DH]
            far_values[i, there, :] = packets[j][:rows, (2 * i + 1) * DH : (2 * i + 2) * DH]
    alone = lax.axis_index("ctx") < 2

    @pl.when(alone)
    def _():
        for i in range(half_groups):
            inverse = 1.0 / sums[i]
            factors[i] = inverse * gate[...]
            deltas[i] = crosses[i] * inverse

    @pl.when(jnp.logical_not(alone))
    def _():
        counts = [packet[rows:, :256].astype(F32)[:1] for packet in packets]
        for i in range(half_groups):
            for here in chunks(0, lanes):
                width = here.stop - here.start
                scores = dot(far_keys[i], query[i, here, :], NT)
                slot = lax.broadcasted_iota(jnp.int32, (rows, width), 0).astype(F32)
                shown = [
                    jnp.where(slot < counts[j][:, :width], scores[j * rows : (j + 1) * rows], HIDDEN)
                    for j in range(blocks)
                ]
                shown = jnp.concatenate(shown, axis=0)
                old_top = tops[i, :, here]
                top = jnp.maximum(old_top, jnp.max(shown, axis=0, keepdims=True))
                raw = jnp.exp2(shown - top)
                shrink = jnp.exp2(old_top - top)
                inverse = 1.0 / (sums[i, :, here] * shrink + jnp.sum(raw, axis=0, keepdims=True))
                prob_grad = dot(far_values[i], cot[i, here, :], NT)
                cross = crosses[i, :, here] * shrink + jnp.sum(raw * prob_grad, axis=0, keepdims=True)
                delta = cross * inverse
                factor = inverse * gate[:, here]
                factors[i, :, here] = factor * shrink
                deltas[i, :, here] = delta
                gated = raw * factor
                weights[i, :, here] = gated.astype(BF16)
                score_grads[i, :, here] = (gated * (prob_grad - delta)).astype(BF16)
            for j, out_ref in enumerate(parts):
                part_of(weights, score_grads, query, cot, out_ref, i, slice(j * rows, (j + 1) * rows), slice(0, lanes))


def near_kernel(
    raws, grads, factors, deltas, keys, query, cot, far_keys, far_grads,
    part_mine, out_ref, weights, score_grads, parts, acc,
    *, ratio
):
    rows = part_mine.shape[0]
    half_groups = keys.shape[0]
    wide = ratio * rows
    half = half_groups * ratio * DH
    for i in range(half_groups):
        for block in range(2):
            reach = (block + 1) * rows
            for here in chunks(block * wide, (block + 1) * wide):
                gated = raws[i, :reach, here] * factors[i, :, here]
                weights[i, :reach, here] = gated.astype(BF16)
                score_grads[i, :reach, here] = (gated * (grads[i, :reach, here] - deltas[i, :, here])).astype(BF16)
        for block in range(2):
            there, lanes = slice(block * rows, (block + 1) * rows), slice(block * wide, 2 * wide)
            part_of(weights, score_grads, query, cot, parts.at[block], i, there, lanes)
            reach, lanes = (block + 1) * rows, slice(block * wide, (block + 1) * wide)
            acc[i, lanes, :] = dot(score_grads[i, :reach, lanes], keys[i, :reach, :], TN)

    @pl.when(lax.axis_index("ctx") >= 2)
    def _():
        for i in range(half_groups):
            acc[i] += dot(far_grads[i], far_keys[i], TN)

    for i in range(half_groups):
        for block in range(2):
            for h in range(ratio):
                at = (i * ratio + h) * DH
                low = block * wide + h * rows
                out_ref[block, :rows, at : at + DH] = (acc[i, low : low + rows] * SCALE).astype(BF16)
    part_mine[...] = parts[core_of()]
    for block in range(2):
        out_ref[block, :rows, half:] = parts[block].astype(BF16)
    summed = deltas[0]
    for i in range(1, half_groups):
        summed = summed + deltas[i]
    for block in range(2):
        own = split_rows(summed[:, block * wide : (block + 1) * wide], 16)
        own = joined_row(dot(own, chosen((wide, rows), ratio, 0), NN))
        out_ref[block, rows:, :rows] = split_rows(own, EXTRA)


def finish_kernel(back, part_mine, pos_ref, cos_ref, sin_ref, *refs, limit):
    got, (query_grad, key_grad, value_grad, gate_grad) = refs[:-4], refs[-4:]
    rows, width = part_mine.shape
    half, side_width = query_grad.shape[1] // 2, width // 2
    core = core_of()
    cosine, sine = cos_ref[...], -sin_ref[...]
    for side in range(2):
        for i in range(half // DH):
            there = slice(side * half + i * DH, side * half + (i + 1) * DH)
            turned = rotate(back[side, :rows, i * DH : (i + 1) * DH].astype(F32), cosine, sine)
            query_grad[:, there] = turned.astype(BF16)
    gate = joined_row(back[0, rows:, :rows]) + joined_row(back[1, rows:, :rows])
    gate_grad[...] = jnp.where(pos_ref[...] < limit, gate, 0.0)
    total = part_mine[...]
    other = back[1 - core, :rows, half:].astype(F32)
    for s in range(len(got) // 2):
        other = other + got[2 * s][...].astype(F32)
        total = total + got[2 * s + 1][...].astype(F32)
    for values, side in ((total, core), (other, 1 - core)):
        for i in range(side_width // DH):
            there = pl.ds(pl.multiple_of(side * side_width + i * DH, DH), DH)
            turned = rotate(values[:, 2 * i * DH : (2 * i + 1) * DH], cosine, sine)
            key_grad[:, there] = turned.astype(BF16)
            value_grad[:, there] = values[:, (2 * i + 1) * DH : (2 * i + 2) * DH].astype(BF16)


def per_device(query_rows, key_rows, value_rows, cotangent, router_gate, positions):
    rows, heads_width = query_rows.shape[1:]
    group_width = key_rows.shape[2]
    groups = group_width // DH
    ratio = heads_width // group_width
    half_groups, half_width = groups // 2, heads_width // 2
    parts = lax.axis_size("ctx")
    chips = parts // 2
    limit = parts * LOCAL
    wide = ratio * rows
    params = pltpu.CompilerParams(vmem_limit_bytes=(16 + 4 * chips) * 1024 * 1024)
    full = pltpu.CompilerParams(vmem_limit_bytes=63 * 1024 * 1024)

    def call(kernel, name, outs, *args, scratch=(), flops=10**6, in_hbm=False):
        spec = pl.BlockSpec(memory_space=pltpu.HBM if in_hbm else pltpu.VMEM)
        return pl.pallas_call(
            kernel,
            out_shape=[jax.ShapeDtypeStruct(*out) for out in outs],
            in_specs=[spec] * len(args),
            out_specs=[spec] * len(outs),
            scratch_shapes=list(scratch),
            compiler_params=full if in_hbm else params,
            cost_estimate=pl.CostEstimate(flops=flops, bytes_accessed=1000, transcendentals=0),
            name=name,
        )(*args)

    index = np.arange(DH) % (DH // 2)
    freq = jnp.asarray((THETA ** (-2.0 * index / DH)).astype(np.float32))[None]
    packet = ((rows + EXTRA, group_width), BF16)
    packets_shape = ((2, rows + EXTRA, heads_width + group_width), BF16)
    table = ((rows, DH), F32)
    kv_mine, kv_theirs, packed, cosine, sine = call(
        functools.partial(pack_kernel, limit=limit),
        "pack",
        [packet, packet, packets_shape, table, table],
        key_rows[0],
        value_rows[0],
        query_rows[0],
        cotangent[0],
        router_gate,
        positions,
        freq,
        in_hbm=True,
        scratch=[
            pltpu.VMEM((rows, group_width), BF16),
            pltpu.VMEM((rows, group_width), BF16),
            pltpu.VMEM((rows, heads_width), BF16),
            pltpu.VMEM((1, rows), F32),
            pltpu.VMEM((1, rows), jnp.int32),
            pltpu.VMEM((1, DH), F32),
            pltpu.VMEM(*packet),
            pltpu.VMEM(*packet),
            pltpu.VMEM((2, rows + EXTRA, half_width), BF16),
            pltpu.VMEM(*table),
            pltpu.VMEM(*table),
            pltpu.SemaphoreType.DMA((8,)),
            pltpu.SemaphoreType.DMA((8,)),
        ],
    )

    hop = [[(2 * x + k, 2 * (x + s) + k) for x in range(chips - s) for k in range(2)] for s in range(chips)]
    cross = [[(a, b + 1 - 2 * (b % 2)) for a, b in pairs] for pairs in hop]
    back_hop = [[(b, a) for a, b in pairs] for pairs in hop]
    back_cross = [[(b, a) for a, b in pairs] for pairs in cross]

    far_own = [lax.ppermute(kv_mine, "ctx", hop[s]) for s in range(1, chips)]
    far_sib = [lax.ppermute(kv_theirs, "ctx", cross[s]) for s in range(1, chips)]

    pairs = [[2 * x, 2 * x + 1] for x in range(chips)]
    swap = lambda both: lax.all_to_all(both, "ctx", 0, 0, axis_index_groups=pairs)
    packets = swap(packed)

    row = ((half_groups, 1, 2 * wide), F32)
    table = ((half_groups, 2 * rows, 2 * wide), F32)
    kv_table = ((half_groups, 2 * rows, DH), BF16)
    q_table = ((half_groups, 2 * wide, DH), BF16)
    keys, values, query, cot, gate_row, raws, grads, tops, sums, crosses = call(
        functools.partial(local_kernel, ratio=ratio),
        "local_scores",
        [kv_table, kv_table, q_table, q_table, ((1, 2 * wide), F32), table, table, row, row, row],
        packets,
        flops=3 * 10**6,
    )

    blocks = 2 * (chips - 1)
    far_table = ((half_groups, blocks * rows, 2 * wide), BF16)
    part_shape = ((rows, group_width), BF16)
    far_keys, _, far_grads, factors, deltas, *far_parts = call(
        functools.partial(far_kernel, blocks=blocks),
        "far_scores",
        [((half_groups, blocks * rows, DH), BF16), far_table, far_table, row, row] + [part_shape] * blocks,
        query,
        cot,
        gate_row,
        tops,
        sums,
        crosses,
        *far_sib,
        *far_own,
        flops=4 * 10**6,
        scratch=[pltpu.VMEM((half_groups, blocks * rows, DH), BF16)],
    )
    sib_got = [lax.ppermute(far_parts[s - 1], "ctx", back_cross[s]) for s in range(1, chips)]
    own_got = [lax.ppermute(far_parts[chips + s - 2], "ctx", back_hop[s]) for s in range(1, chips)]

    part_mine, packed = call(
        functools.partial(near_kernel, ratio=ratio),
        "near_grads",
        [
            ((rows, group_width), F32),
            ((2, rows + EXTRA, half_width + group_width), BF16),
        ],
        raws,
        grads,
        factors,
        deltas,
        keys,
        query,
        cot,
        far_keys,
        far_grads,
        flops=4 * 10**6,
        scratch=[
            pltpu.VMEM((half_groups, 2 * rows, 2 * wide), BF16),
            pltpu.VMEM((half_groups, 2 * rows, 2 * wide), BF16),
            pltpu.VMEM((2, rows, group_width), F32),
            pltpu.VMEM((half_groups, 2 * wide, DH), F32),
        ],
    )
    back = swap(packed)
    query_grad, key_grad, value_grad, gate_grad = call(
        functools.partial(finish_kernel, limit=limit),
        "finish",
        [((rows, heads_width), BF16)] + [((rows, group_width), BF16)] * 2 + [((1, rows), F32)],
        back,
        part_mine,
        positions,
        cosine,
        sine,
        *[part for pair in zip(sib_got, own_got) for part in pair],
    )
    return (query_grad[None], key_grad[None], value_grad[None], gate_grad)


def solution(mesh):
    wide = P(("group", "dp"), "ctx", None)
    narrow = P(("group", "dp"), "ctx")
    return jax.shard_map(
        per_device,
        mesh=mesh,
        in_specs=(wide, wide, wide, wide, narrow, narrow),
        out_specs=(wide, wide, wide, narrow),
        check_vma=False,
    )
```

```python
import functools
import math

import jax
import jax.numpy as jnp
import numpy as np
from jax import lax
from jax.experimental import pallas as pl
from jax.experimental.pallas import tpu as pltpu
from jax.sharding import PartitionSpec as P

DH = 128
LOCAL = 1024
THETA = 500000.0
EXTRA = 16
HIDDEN = -1e30
SCALE = DH**-0.5
LOG2E = math.log2(math.e)
LN2 = math.log(2.0)

NT = (((1,), (1,)), ((), ()))
NN = (((1,), (0,)), ((), ()))
TN = (((0,), (0,)), ((), ()))
F32 = jnp.float32
BF16 = jnp.bfloat16


def few_bits(value, bits):
    unit = 2.0 ** (math.floor(math.log2(value)) + 1 - bits)
    return math.floor(value / unit) * unit


QUARTER_1 = few_bits(math.pi / 2, 10)
QUARTER_2 = few_bits(math.pi / 2 - QUARTER_1, 10)
QUARTER_3 = math.pi / 2 - QUARTER_1 - QUARTER_2


def dot(a, b, dims):
    return lax.dot_general(a, b, dims, preferred_element_type=F32)


def core_of():
    return lax.rem(lax.axis_index("ctx"), 2)


def rotate(values, cosine, sine):
    return values * cosine + pltpu.roll(values, DH // 2, 1) * sine


def sine_cosine(angle):
    turns = jnp.floor(angle * (2.0 / math.pi) + 0.5)
    rest = ((angle - turns * QUARTER_1) - turns * QUARTER_2) - turns * QUARTER_3
    square = rest * rest
    sine = ((-1.9515295891e-4 * square + 8.3321608736e-3) * square - 1.6666654611e-1) * square * rest + rest
    cosine = (2.443315711809948e-5 * square - 1.388731625493765e-3) * square + 4.166664568298827e-2
    cosine = cosine * square * square - 0.5 * square + 1.0
    quarter = turns.astype(jnp.int32)
    odd = (quarter & 1) == 1
    first, second = jnp.where(odd, cosine, sine), jnp.where(odd, sine, cosine)
    return (
        jnp.where((quarter & 2) == 2, -first, first),
        jnp.where(((quarter + 1) & 2) == 2, -second, second),
    )


def split_rows(row, height):
    high = row.astype(BF16).astype(F32)
    middle = (row - high).astype(BF16).astype(F32)
    low = row - high - middle
    line = lax.broadcasted_iota(jnp.int32, (height, row.shape[1]), 0)
    rows = jnp.where(line == 0, high, jnp.where(line == 1, middle, jnp.where(line == 2, low, 0.0)))
    return rows.astype(BF16)


def joined_row(rows):
    return jnp.sum(rows.astype(F32), axis=0, keepdims=True)


def pack_kernel(
    key_in, value_in, query_in, cot_in, gate_in, pos_in, freq_in, mine, theirs, packed, cos_ref, sin_ref,
    key, value, query, gate, pos, freq, sems, *, limit
):
    rows, width = key.shape
    side_width = width // 2
    half = query.shape[1] // 2
    core = core_of()
    loads = [(pos_in, pos), (freq_in, freq), (key_in, key), (value_in, value), (gate_in, gate), (query_in, query)]
    for side in range(2):
        there = slice(side * half, (side + 1) * half)
        loads.append((cot_in.at[:, there], packed.at[side, :rows, half : 2 * half]))
    loads = [pltpu.make_async_copy(source, target, sems.at[i]) for i, (source, target) in enumerate(loads)]
    for copy in loads:
        copy.start()
    loads[0].wait()
    loads[1].wait()
    places = pos[...]
    count = jnp.sum(jnp.where(places < limit, 1.0, 0.0), axis=1, keepdims=True)
    count = jnp.broadcast_to(count, (EXTRA, width)).astype(BF16)
    down = lax.broadcasted_iota(jnp.int32, (rows, rows), 0)
    along = lax.broadcasted_iota(jnp.int32, (rows, rows), 1)
    column = jnp.sum(jnp.where(down == along, places.astype(F32), 0.0), axis=1, keepdims=True)
    sine, cosine = sine_cosine(column * freq[...])
    lane = lax.broadcasted_iota(jnp.int32, (rows, DH), 1)
    sine = jnp.where(lane < DH // 2, -sine, sine)
    cos_ref[...] = cosine
    sin_ref[...] = sine
    loads[2].wait()
    loads[3].wait()
    for out_ref, side in ((mine, core), (theirs, 1 - core)):
        for i in range(side_width // DH):
            there = pl.ds(pl.multiple_of(side * side_width + i * DH, DH), DH)
            turned = rotate(key[:, there].astype(F32), cosine, sine)
            out_ref[:rows, 2 * i * DH : (2 * i + 1) * DH] = turned.astype(BF16)
            out_ref[:rows, (2 * i + 1) * DH : (2 * i + 2) * DH] = value[:, there]
        out_ref[rows:, :] = count
        packed[side, :, 2 * half :] = out_ref[...]
    loads[4].wait()
    loads[5].wait()
    gates = split_rows(jnp.where(places < limit, gate[...], 0.0), EXTRA)
    cosine, sine = cosine * (SCALE * LOG2E), sine * (SCALE * LOG2E)
    for side in range(2):
        for i in range(half // DH):
            there = slice(side * half + i * DH, side * half + (i + 1) * DH)
            turned = rotate(query[:, there].astype(F32), cosine, sine)
            packed[side, :rows, i * DH : (i + 1) * DH] = turned.astype(BF16)
        packed[side, rows:, :rows] = gates
    for copy in loads[6:]:
        copy.wait()


def chosen(shape, ratio, dim):
    down = lax.broadcasted_iota(jnp.int32, shape, 0)
    along = lax.broadcasted_iota(jnp.int32, shape, 1)
    rows = shape[1 - dim]
    long, short = (down, along) if dim == 0 else (along, down)
    for _ in range(1, ratio):
        long = jnp.where(long >= rows, long - rows, long)
    return jnp.where(long == short, 1.0, 0.0).astype(BF16)


def chunks(low, high):
    return [slice(at, min(at + 256, high)) for at in range(low, high, 256)]


def local_kernel(packets, keys, values, query, cot, gate, raws, grads, tops, sums, crosses, *, ratio):
    rows = packets.shape[1] - EXTRA
    half_groups = keys.shape[0]
    wide = ratio * rows
    half = half_groups * ratio * DH
    for side in range(2):
        there = slice(side * rows, (side + 1) * rows)
        for i in range(half_groups):
            at = 2 * half + 2 * i * DH
            keys[i, there, :] = packets[side, :rows, at : at + DH]
            values[i, there, :] = packets[side, :rows, at + DH : at + 2 * DH]
            for h in range(ratio):
                to = slice(side * wide + h * rows, side * wide + (h + 1) * rows)
                at = (i * ratio + h) * DH
                query[i, to, :] = packets[side, :rows, at : at + DH]
                cot[i, to, :] = packets[side, :rows, half + at : half + at + DH]
        gates = dot(packets[side, rows:, :rows], chosen((rows, wide), ratio, 1), NN)
        gate[:, side * wide : (side + 1) * wide] = joined_row(gates)
    count = packets[0, rows:, 2 * half : 2 * half + 256].astype(F32)[:1]
    for i in range(half_groups):
        for block in range(2):
            reach = (block + 1) * rows
            for here in chunks(block * wide, (block + 1) * wide):
                width = here.stop - here.start
                scores = dot(keys[i, :reach, :], query[i, here, :], NT)
                slot = lax.broadcasted_iota(jnp.int32, (rows, width), 0)
                lane = lax.broadcasted_iota(jnp.int32, (rows, width), 1) + (here.start - block * wide)
                for h in range(1, ratio):
                    lane = jnp.where(lane >= rows, lane - rows, lane)
                shown = jnp.where(slot <= lane, scores[block * rows :], HIDDEN)
                if block:
                    before = jnp.where(slot.astype(F32) < count[:, :width], scores[:rows], HIDDEN)
                    shown = jnp.concatenate([before, shown], axis=0)
                top = jnp.max(shown, axis=0, keepdims=True)
                raw = jnp.exp2(shown - top)
                prob_grad = dot(values[i, :reach, :], cot[i, here, :], NT)
                raws[i, :reach, here] = raw
                grads[i, :reach, here] = prob_grad
                tops[i, :, here] = top
                sums[i, :, here] = jnp.sum(raw, axis=0, keepdims=True)
                crosses[i, :, here] = jnp.sum(raw * prob_grad, axis=0, keepdims=True)


def part_of(weights, score_grads, query, cot, out_ref, i, there, lanes):
    key_part = dot(score_grads[i, there, lanes], query[i, lanes, :], NN) * LN2
    value_part = dot(weights[i, there, lanes], cot[i, lanes, :], NN)
    out_ref[:, 2 * i * DH : (2 * i + 1) * DH] = key_part.astype(out_ref.dtype)
    out_ref[:, (2 * i + 1) * DH : (2 * i + 2) * DH] = value_part.astype(out_ref.dtype)


def far_kernel(query, cot, gate, tops, sums, crosses, *refs, blocks):
    packets = refs[:blocks]
    far_keys, weights, score_grads, factors, deltas = refs[blocks : blocks + 5]
    parts = refs[blocks + 5 : 2 * blocks + 5]
    far_values = refs[-1]
    rows = packets[0].shape[0] - EXTRA
    half_groups, lanes = query.shape[:2]
    for j in range(blocks):
        there = slice(j * rows, (j + 1) * rows)
        for i in range(half_groups):
            far_keys[i, there, :] = packets[j][:rows, 2 * i * DH : (2 * i + 1) * DH]
            far_values[i, there, :] = packets[j][:rows, (2 * i + 1) * DH : (2 * i + 2) * DH]
    alone = lax.axis_index("ctx") < 2

    @pl.when(alone)
    def _():
        for i in range(half_groups):
            inverse = 1.0 / sums[i]
            factors[i] = inverse * gate[...]
            deltas[i] = crosses[i] * inverse

    @pl.when(jnp.logical_not(alone))
    def _():
        counts = [packet[rows:, :256].astype(F32)[:1] for packet in packets]
        for i in range(half_groups):
            for here in chunks(0, lanes):
                width = here.stop - here.start
                scores = dot(far_keys[i], query[i, here, :], NT)
                slot = lax.broadcasted_iota(jnp.int32, (rows, width), 0).astype(F32)
                shown = [
                    jnp.where(slot < counts[j][:, :width], scores[j * rows : (j + 1) * rows], HIDDEN)
                    for j in range(blocks)
                ]
                shown = jnp.concatenate(shown, axis=0)
                old_top = tops[i, :, here]
                top = jnp.maximum(old_top, jnp.max(shown, axis=0, keepdims=True))
                raw = jnp.exp2(shown - top)
                shrink = jnp.exp2(old_top - top)
                inverse = 1.0 / (sums[i, :, here] * shrink + jnp.sum(raw, axis=0, keepdims=True))
                prob_grad = dot(far_values[i], cot[i, here, :], NT)
                cross = crosses[i, :, here] * shrink + jnp.sum(raw * prob_grad, axis=0, keepdims=True)
                delta = cross * inverse
                factor = inverse * gate[:, here]
                factors[i, :, here] = factor * shrink
                deltas[i, :, here] = delta
                gated = raw * factor
                weights[i, :, here] = gated.astype(BF16)
                score_grads[i, :, here] = (gated * (prob_grad - delta)).astype(BF16)
            for j, out_ref in enumerate(parts):
                part_of(weights, score_grads, query, cot, out_ref, i, slice(j * rows, (j + 1) * rows), slice(0, lanes))


def near_kernel(
    raws, grads, factors, deltas, keys, query, cot, far_keys, far_grads,
    part_mine, out_ref, weights, score_grads, parts, acc,
    *, ratio
):
    rows = part_mine.shape[0]
    half_groups = keys.shape[0]
    wide = ratio * rows
    half = half_groups * ratio * DH
    for i in range(half_groups):
        for block in range(2):
            reach = (block + 1) * rows
            for here in chunks(block * wide, (block + 1) * wide):
                gated = raws[i, :reach, here] * factors[i, :, here]
                weights[i, :reach, here] = gated.astype(BF16)
                score_grads[i, :reach, here] = (gated * (grads[i, :reach, here] - deltas[i, :, here])).astype(BF16)
        for block in range(2):
            there, lanes = slice(block * rows, (block + 1) * rows), slice(block * wide, 2 * wide)
            part_of(weights, score_grads, query, cot, parts.at[block], i, there, lanes)
            reach, lanes = (block + 1) * rows, slice(block * wide, (block + 1) * wide)
            acc[i, lanes, :] = dot(score_grads[i, :reach, lanes], keys[i, :reach, :], TN)

    @pl.when(lax.axis_index("ctx") >= 2)
    def _():
        for i in range(half_groups):
            acc[i] += dot(far_grads[i], far_keys[i], TN)

    for i in range(half_groups):
        for block in range(2):
            for h in range(ratio):
                at = (i * ratio + h) * DH
                low = block * wide + h * rows
                out_ref[block, :rows, at : at + DH] = (acc[i, low : low + rows] * SCALE).astype(BF16)
    part_mine[...] = parts[core_of()]
    for block in range(2):
        out_ref[block, :rows, half:] = parts[block].astype(BF16)
    summed = deltas[0]
    for i in range(1, half_groups):
        summed = summed + deltas[i]
    for block in range(2):
        own = split_rows(summed[:, block * wide : (block + 1) * wide], 16)
        own = joined_row(dot(own, chosen((wide, rows), ratio, 0), NN))
        out_ref[block, rows:, :rows] = split_rows(own, EXTRA)


def finish_kernel(back, part_mine, pos_ref, cos_ref, sin_ref, *refs, limit):
    got, (query_grad, key_grad, value_grad, gate_grad) = refs[:-4], refs[-4:]
    rows, width = part_mine.shape
    half, side_width = query_grad.shape[1] // 2, width // 2
    core = core_of()
    cosine, sine = cos_ref[...], -sin_ref[...]
    for side in range(2):
        for i in range(half // DH):
            there = slice(side * half + i * DH, side * half + (i + 1) * DH)
            turned = rotate(back[side, :rows, i * DH : (i + 1) * DH].astype(F32), cosine, sine)
            query_grad[:, there] = turned.astype(BF16)
    gate = joined_row(back[0, rows:, :rows]) + joined_row(back[1, rows:, :rows])
    gate_grad[...] = jnp.where(pos_ref[...] < limit, gate, 0.0)
    total = part_mine[...]
    other = back[1 - core, :rows, half:].astype(F32)
    for s in range(len(got) // 2):
        other = other + got[2 * s][...].astype(F32)
        total = total + got[2 * s + 1][...].astype(F32)
    for values, side in ((total, core), (other, 1 - core)):
        for i in range(side_width // DH):
            there = pl.ds(pl.multiple_of(side * side_width + i * DH, DH), DH)
            turned = rotate(values[:, 2 * i * DH : (2 * i + 1) * DH], cosine, sine)
            key_grad[:, there] = turned.astype(BF16)
            value_grad[:, there] = values[:, (2 * i + 1) * DH : (2 * i + 2) * DH].astype(BF16)


def per_device(query_rows, key_rows, value_rows, cotangent, router_gate, positions):
    rows, heads_width = query_rows.shape[1:]
    group_width = key_rows.shape[2]
    groups = group_width // DH
    ratio = heads_width // group_width
    half_groups, half_width = groups // 2, heads_width // 2
    parts = lax.axis_size("ctx")
    chips = parts // 2
    limit = parts * LOCAL
    wide = ratio * rows
    params = pltpu.CompilerParams(vmem_limit_bytes=(16 + 4 * chips) * 1024 * 1024)

    def call(kernel, name, outs, *args, scratch=(), flops=10**6, in_hbm=False):
        if in_hbm:
            args = [pltpu.with_memory_space_constraint(arg, pltpu.HBM) for arg in args]
        spec = pl.BlockSpec(memory_space=pltpu.HBM if in_hbm else pltpu.VMEM)
        return pl.pallas_call(
            kernel,
            out_shape=[jax.ShapeDtypeStruct(*out) for out in outs],
            in_specs=[spec] * len(args),
            scratch_shapes=list(scratch),
            compiler_params=params,
            cost_estimate=pl.CostEstimate(flops=flops, bytes_accessed=1000, transcendentals=0),
            name=name,
        )(*args)

    index = np.arange(DH) % (DH // 2)
    freq = jnp.asarray((THETA ** (-2.0 * index / DH)).astype(np.float32))[None]
    packet = ((rows + EXTRA, group_width), BF16)
    packets_shape = ((2, rows + EXTRA, heads_width + group_width), BF16)
    table = ((rows, DH), F32)
    kv_mine, kv_theirs, packed, cosine, sine = call(
        functools.partial(pack_kernel, limit=limit),
        "pack",
        [packet, packet, packets_shape, table, table],
        key_rows[0],
        value_rows[0],
        query_rows[0],
        cotangent[0],
        router_gate,
        positions,
        freq,
        in_hbm=True,
        scratch=[
            pltpu.VMEM((rows, group_width), BF16),
            pltpu.VMEM((rows, group_width), BF16),
            pltpu.VMEM((rows, heads_width), BF16),
            pltpu.VMEM((1, rows), F32),
            pltpu.VMEM((1, rows), jnp.int32),
            pltpu.VMEM((1, DH), F32),
            pltpu.SemaphoreType.DMA((8,)),
        ],
    )

    hop = [[(2 * x + k, 2 * (x + s) + k) for x in range(chips - s) for k in range(2)] for s in range(chips)]
    cross = [[(a, b + 1 - 2 * (b % 2)) for a, b in pairs] for pairs in hop]
    back_hop = [[(b, a) for a, b in pairs] for pairs in hop]
    back_cross = [[(b, a) for a, b in pairs] for pairs in cross]

    far_own = [lax.ppermute(kv_mine, "ctx", hop[s]) for s in range(1, chips)]
    far_sib = [lax.ppermute(kv_theirs, "ctx", cross[s]) for s in range(1, chips)]

    pairs = [[2 * x, 2 * x + 1] for x in range(chips)]
    swap = lambda both: lax.all_to_all(both, "ctx", 0, 0, axis_index_groups=pairs)
    packets = swap(packed)

    row = ((half_groups, 1, 2 * wide), F32)
    table = ((half_groups, 2 * rows, 2 * wide), F32)
    kv_table = ((half_groups, 2 * rows, DH), BF16)
    q_table = ((half_groups, 2 * wide, DH), BF16)
    keys, values, query, cot, gate_row, raws, grads, tops, sums, crosses = call(
        functools.partial(local_kernel, ratio=ratio),
        "local_scores",
        [kv_table, kv_table, q_table, q_table, ((1, 2 * wide), F32), table, table, row, row, row],
        packets,
        flops=3 * 10**6,
    )

    blocks = 2 * (chips - 1)
    far_table = ((half_groups, blocks * rows, 2 * wide), BF16)
    part_shape = ((rows, group_width), BF16)
    far_keys, _, far_grads, factors, deltas, *far_parts = call(
        functools.partial(far_kernel, blocks=blocks),
        "far_scores",
        [((half_groups, blocks * rows, DH), BF16), far_table, far_table, row, row] + [part_shape] * blocks,
        query,
        cot,
        gate_row,
        tops,
        sums,
        crosses,
        *far_sib,
        *far_own,
        flops=4 * 10**6,
        scratch=[pltpu.VMEM((half_groups, blocks * rows, DH), BF16)],
    )
    sib_got = [lax.ppermute(far_parts[s - 1], "ctx", back_cross[s]) for s in range(1, chips)]
    own_got = [lax.ppermute(far_parts[chips + s - 2], "ctx", back_hop[s]) for s in range(1, chips)]

    part_mine, packed = call(
        functools.partial(near_kernel, ratio=ratio),
        "near_grads",
        [
            ((rows, group_width), F32),
            ((2, rows + EXTRA, half_width + group_width), BF16),
        ],
        raws,
        grads,
        factors,
        deltas,
        keys,
        query,
        cot,
        far_keys,
        far_grads,
        flops=4 * 10**6,
        scratch=[
            pltpu.VMEM((half_groups, 2 * rows, 2 * wide), BF16),
            pltpu.VMEM((half_groups, 2 * rows, 2 * wide), BF16),
            pltpu.VMEM((2, rows, group_width), F32),
            pltpu.VMEM((half_groups, 2 * wide, DH), F32),
        ],
    )
    back = swap(packed)
    query_grad, key_grad, value_grad, gate_grad = call(
        functools.partial(finish_kernel, limit=limit),
        "finish",
        [((rows, heads_width), BF16)] + [((rows, group_width), BF16)] * 2 + [((1, rows), F32)],
        back,
        part_mine,
        positions,
        cosine,
        sine,
        *[part for pair in zip(sib_got, own_got) for part in pair],
    )
    return (query_grad[None], key_grad[None], value_grad[None], gate_grad)


def solution(mesh):
    wide = P(("group", "dp"), "ctx", None)
    narrow = P(("group", "dp"), "ctx")
    return jax.shard_map(
        per_device,
        mesh=mesh,
        in_specs=(wide, wide, wide, wide, narrow, narrow),
        out_specs=(wide, wide, wide, narrow),
        check_vma=False,
    )
```

```python
import functools
import math

import jax
import jax.numpy as jnp
import numpy as np
from jax import lax
from jax.experimental import pallas as pl
from jax.experimental.pallas import tpu as pltpu
from jax.sharding import PartitionSpec as P

DH = 128
LOCAL = 1024
THETA = 500000.0
EXTRA = 16
HIDDEN = -1e30
UNUSED = 2.0**14
SCALE = DH**-0.5
LOG2E = math.log2(math.e)
LN2 = math.log(2.0)

NT = (((1,), (1,)), ((), ()))
NN = (((1,), (0,)), ((), ()))
TN = (((0,), (0,)), ((), ()))
F32 = jnp.float32
BF16 = jnp.bfloat16


def few_bits(value, bits):
    unit = 2.0 ** (math.floor(math.log2(value)) + 1 - bits)
    return math.floor(value / unit) * unit


QUARTER_1 = few_bits(math.pi / 2, 10)
QUARTER_2 = few_bits(math.pi / 2 - QUARTER_1, 10)
QUARTER_3 = math.pi / 2 - QUARTER_1 - QUARTER_2


def dot(a, b, dims):
    return lax.dot_general(a, b, dims, preferred_element_type=F32)


def core_of():
    return lax.rem(lax.axis_index("ctx"), 2)


def rotate(values, cosine, sine):
    return values * cosine + pltpu.roll(values, DH // 2, 1) * sine


def sine_cosine(angle):
    turns = jnp.floor(angle * (2.0 / math.pi) + 0.5)
    rest = ((angle - turns * QUARTER_1) - turns * QUARTER_2) - turns * QUARTER_3
    square = rest * rest
    sine = ((-1.9515295891e-4 * square + 8.3321608736e-3) * square - 1.6666654611e-1) * square * rest + rest
    cosine = (2.443315711809948e-5 * square - 1.388731625493765e-3) * square + 4.166664568298827e-2
    cosine = cosine * square * square - 0.5 * square + 1.0
    quarter = turns.astype(jnp.int32)
    odd = (quarter & 1) == 1
    first, second = jnp.where(odd, cosine, sine), jnp.where(odd, sine, cosine)
    return (
        jnp.where((quarter & 2) == 2, -first, first),
        jnp.where(((quarter + 1) & 2) == 2, -second, second),
    )


def split_rows(row, height):
    high = row.astype(BF16).astype(F32)
    middle = (row - high).astype(BF16).astype(F32)
    low = row - high - middle
    line = lax.broadcasted_iota(jnp.int32, (height, row.shape[1]), 0)
    rows = jnp.where(line == 0, high, jnp.where(line == 1, middle, jnp.where(line == 2, low, 0.0)))
    return rows.astype(BF16)


def joined_row(rows):
    return jnp.sum(rows.astype(F32), axis=0, keepdims=True)


def pack_kernel(
    key_in, value_in, query_in, cot_in, gate_in, pos_in, freq_in, mine, theirs, packed, cos_ref, sin_ref,
    key, value, query, gate, pos, freq, sems, *, limit
):
    rows, width = key.shape
    side_width = width // 2
    half = query.shape[1] // 2
    core = core_of()
    loads = [(pos_in, pos), (freq_in, freq), (key_in, key), (value_in, value), (gate_in, gate), (query_in, query)]
    for side in range(2):
        there = slice(side * half, (side + 1) * half)
        loads.append((cot_in.at[:, there], packed.at[side, :rows, half : 2 * half]))
    loads = [pltpu.make_async_copy(source, target, sems.at[i]) for i, (source, target) in enumerate(loads)]
    for copy in loads:
        copy.start()
    loads[0].wait()
    loads[1].wait()
    places = pos[...]
    count = jnp.sum(jnp.where(places < limit, 1.0, 0.0), axis=1, keepdims=True)
    count = jnp.broadcast_to(count, (EXTRA, width)).astype(BF16)
    down = lax.broadcasted_iota(jnp.int32, (rows, rows), 0)
    along = lax.broadcasted_iota(jnp.int32, (rows, rows), 1)
    column = jnp.sum(jnp.where(down == along, places.astype(F32), 0.0), axis=1, keepdims=True)
    sine, cosine = sine_cosine(column * freq[...])
    lane = lax.broadcasted_iota(jnp.int32, (rows, DH), 1)
    sine = jnp.where(lane < DH // 2, -sine, sine)
    cos_ref[...] = cosine
    sin_ref[...] = sine
    loads[2].wait()
    loads[3].wait()
    used = jnp.broadcast_to(column, (rows, DH)) < limit
    for out_ref, side in ((mine, core), (theirs, 1 - core)):
        for i in range(side_width // DH):
            there = pl.ds(pl.multiple_of(side * side_width + i * DH, DH), DH)
            turned = rotate(key[:, there].astype(F32), cosine, sine)
            out_ref[:, 2 * i * DH : (2 * i + 1) * DH] = jnp.where(used, turned, UNUSED).astype(BF16)
            out_ref[:, (2 * i + 1) * DH : (2 * i + 2) * DH] = value[:, there]
            packed[side, :rows, 2 * half + 2 * i * DH : 2 * half + (2 * i + 1) * DH] = turned.astype(BF16)
            packed[side, :rows, 2 * half + (2 * i + 1) * DH : 2 * half + (2 * i + 2) * DH] = value[:, there]
        packed[side, rows:, 2 * half :] = count
    loads[4].wait()
    loads[5].wait()
    gates = split_rows(jnp.where(places < limit, gate[...], 0.0), EXTRA)
    cosine, sine = cosine * (SCALE * LOG2E), sine * (SCALE * LOG2E)
    for side in range(2):
        for i in range(half // DH):
            there = slice(side * half + i * DH, side * half + (i + 1) * DH)
            turned = rotate(query[:, there].astype(F32), cosine, sine)
            packed[side, :rows, i * DH : (i + 1) * DH] = turned.astype(BF16)
        packed[side, rows:, :rows] = gates
    for copy in loads[6:]:
        copy.wait()


def chosen(shape, ratio, dim):
    down = lax.broadcasted_iota(jnp.int32, shape, 0)
    along = lax.broadcasted_iota(jnp.int32, shape, 1)
    rows = shape[1 - dim]
    long, short = (down, along) if dim == 0 else (along, down)
    for _ in range(1, ratio):
        long = jnp.where(long >= rows, long - rows, long)
    return jnp.where(long == short, 1.0, 0.0).astype(BF16)


def chunks(low, high):
    return [slice(at, min(at + 256, high)) for at in range(low, high, 256)]


def local_kernel(packets, keys, values, query, cot, gate, raws, grads, tops, sums, crosses, *, ratio):
    rows = packets.shape[1] - EXTRA
    half_groups = keys.shape[0]
    wide = ratio * rows
    half = half_groups * ratio * DH
    for side in range(2):
        there = slice(side * rows, (side + 1) * rows)
        for i in range(half_groups):
            at = 2 * half + 2 * i * DH
            keys[i, there, :] = packets[side, :rows, at : at + DH]
            values[i, there, :] = packets[side, :rows, at + DH : at + 2 * DH]
            for h in range(ratio):
                to = slice(side * wide + h * rows, side * wide + (h + 1) * rows)
                at = (i * ratio + h) * DH
                query[i, to, :] = packets[side, :rows, at : at + DH]
                cot[i, to, :] = packets[side, :rows, half + at : half + at + DH]
        gates = dot(packets[side, rows:, :rows], chosen((rows, wide), ratio, 1), NN)
        gate[:, side * wide : (side + 1) * wide] = joined_row(gates)
    count = packets[0, rows:, 2 * half : 2 * half + 256].astype(F32)[:1]
    for i in range(half_groups):
        for block in range(2):
            reach = (block + 1) * rows
            for here in chunks(block * wide, (block + 1) * wide):
                width = here.stop - here.start
                scores = dot(keys[i, :reach, :], query[i, here, :], NT)
                slot = lax.broadcasted_iota(jnp.int32, (rows, width), 0)
                lane = lax.broadcasted_iota(jnp.int32, (rows, width), 1) + (here.start - block * wide)
                for h in range(1, ratio):
                    lane = jnp.where(lane >= rows, lane - rows, lane)
                shown = jnp.where(slot <= lane, scores[block * rows :], HIDDEN)
                if block:
                    before = jnp.where(slot.astype(F32) < count[:, :width], scores[:rows], HIDDEN)
                    shown = jnp.concatenate([before, shown], axis=0)
                top = jnp.max(shown, axis=0, keepdims=True)
                raw = jnp.exp2(shown - top)
                prob_grad = dot(values[i, :reach, :], cot[i, here, :], NT)
                raws[i, :reach, here] = raw
                grads[i, :reach, here] = prob_grad
                tops[i, :, here] = top
                sums[i, :, here] = jnp.sum(raw, axis=0, keepdims=True)
                crosses[i, :, here] = jnp.sum(raw * prob_grad, axis=0, keepdims=True)


def part_of(weights, score_grads, query, cot, out_ref, i, there, lanes):
    key_part = dot(score_grads[i, there, lanes], query[i, lanes, :], NN) * LN2
    value_part = dot(weights[i, there, lanes], cot[i, lanes, :], NN)
    out_ref[:, 2 * i * DH : (2 * i + 1) * DH] = key_part.astype(out_ref.dtype)
    out_ref[:, (2 * i + 1) * DH : (2 * i + 2) * DH] = value_part.astype(out_ref.dtype)


def used_slots(packet, here):
    chip = lax.div(lax.axis_index("ctx"), 2)
    key = packet[:, :DH].astype(F32)[:, :1]
    return jnp.broadcast_to(key, (packet.shape[0], 256)) < jnp.where(chip >= here, UNUSED / 2, -UNUSED)


def early_kernel(query, cot, tops, sums, crosses, packet, raws, grads, new_tops, new_sums, new_crosses):
    half_groups, lanes = query.shape[:2]
    alone = lax.axis_index("ctx") < 2

    @pl.when(alone)
    def _():
        new_tops[...] = tops[...]
        new_sums[...] = sums[...]
        new_crosses[...] = crosses[...]

    @pl.when(jnp.logical_not(alone))
    def _():
        used = used_slots(packet, 1)
        for i in range(half_groups):
            key = packet[:, 2 * i * DH : (2 * i + 1) * DH]
            value = packet[:, (2 * i + 1) * DH : (2 * i + 2) * DH]
            for here in chunks(0, lanes):
                width = here.stop - here.start
                shown = jnp.where(used[:, :width], dot(key, query[i, here, :], NT), HIDDEN)
                old_top = tops[i, :, here]
                top = jnp.maximum(old_top, jnp.max(shown, axis=0, keepdims=True))
                raw = jnp.exp2(shown - top)
                shrink = jnp.exp2(old_top - top)
                prob_grad = dot(value, cot[i, here, :], NT)
                raws[i, :, here] = raw
                grads[i, :, here] = prob_grad
                new_tops[i, :, here] = top
                new_sums[i, :, here] = sums[i, :, here] * shrink + jnp.sum(raw, axis=0, keepdims=True)
                cross = jnp.sum(raw * prob_grad, axis=0, keepdims=True)
                new_crosses[i, :, here] = crosses[i, :, here] * shrink + cross


def far_kernel(query, cot, gate, first_tops, raws, grads, tops, sums, crosses, early, *refs, blocks):
    packets = refs[: blocks - 1]
    far_keys, weights, score_grads, factors, deltas = refs[blocks - 1 : blocks + 4]
    parts = refs[blocks + 4 : -2]
    late_keys, late_values = refs[-2:]
    rows = early.shape[0]
    half_groups, lanes = query.shape[:2]
    alone = lax.axis_index("ctx") < 2

    @pl.when(alone)
    def _():
        for i in range(half_groups):
            inverse = 1.0 / sums[i]
            factors[i] = inverse * gate[...]
            deltas[i] = crosses[i] * inverse

    @pl.when(jnp.logical_not(alone))
    def _():
        for i in range(half_groups):
            far_keys[i, :rows, :] = early[:, 2 * i * DH : (2 * i + 1) * DH]
            for j, packet in enumerate(packets):
                there = slice(j * rows, (j + 1) * rows)
                far_keys[i, (j + 1) * rows : (j + 2) * rows, :] = packet[:, 2 * i * DH : (2 * i + 1) * DH]
                late_keys[i, there, :] = packet[:, 2 * i * DH : (2 * i + 1) * DH]
                late_values[i, there, :] = packet[:, (2 * i + 1) * DH : (2 * i + 2) * DH]
        hops = blocks // 2
        used = [used_slots(packet, (j + 1) % hops + 1) for j, packet in enumerate(packets)]
        for i in range(half_groups):
            for here in chunks(0, lanes):
                width = here.stop - here.start
                scores = dot(late_keys[i], query[i, here, :], NT)
                shown = [
                    jnp.where(used[j][:, :width], scores[j * rows : (j + 1) * rows], HIDDEN)
                    for j in range(blocks - 1)
                ]
                shown = jnp.concatenate(shown, axis=0)
                old_top = tops[i, :, here]
                top = jnp.maximum(old_top, jnp.max(shown, axis=0, keepdims=True))
                raw = jnp.exp2(shown - top)
                shrink = jnp.exp2(old_top - top)
                inverse = 1.0 / (sums[i, :, here] * shrink + jnp.sum(raw, axis=0, keepdims=True))
                prob_grad = dot(late_values[i], cot[i, here, :], NT)
                cross = crosses[i, :, here] * shrink + jnp.sum(raw * prob_grad, axis=0, keepdims=True)
                delta = cross * inverse
                factor = inverse * gate[:, here]
                factors[i, :, here] = factor * jnp.exp2(first_tops[i, :, here] - top)
                deltas[i, :, here] = delta
                gated = raw * factor
                weights[i, rows:, here] = gated.astype(BF16)
                score_grads[i, rows:, here] = (gated * (prob_grad - delta)).astype(BF16)
                gated = raws[i, :, here] * (factor * shrink)
                weights[i, :rows, here] = gated.astype(BF16)
                score_grads[i, :rows, here] = (gated * (grads[i, :, here] - delta)).astype(BF16)
            for j, out_ref in enumerate(parts):
                part_of(weights, score_grads, query, cot, out_ref, i, slice(j * rows, (j + 1) * rows), slice(0, lanes))


def far_rest_kernel(weights, score_grads, query, cot, *parts):
    rows = parts[0].shape[0]
    half_groups, lanes = query.shape[:2]

    @pl.when(lax.axis_index("ctx") >= 2)
    def _():
        for j, out_ref in enumerate(parts):
            there = slice((len(parts) + j) * rows, (len(parts) + j + 1) * rows)
            for i in range(half_groups):
                part_of(weights, score_grads, query, cot, out_ref, i, there, slice(0, lanes))


def near_kernel(
    raws, grads, factors, deltas, keys, query, cot, far_keys, far_grads,
    part_mine, out_ref, weights, score_grads, parts, acc,
    *, ratio
):
    rows = part_mine.shape[0]
    half_groups = keys.shape[0]
    wide = ratio * rows
    half = half_groups * ratio * DH
    for i in range(half_groups):
        for block in range(2):
            reach = (block + 1) * rows
            for here in chunks(block * wide, (block + 1) * wide):
                gated = raws[i, :reach, here] * factors[i, :, here]
                weights[i, :reach, here] = gated.astype(BF16)
                score_grads[i, :reach, here] = (gated * (grads[i, :reach, here] - deltas[i, :, here])).astype(BF16)
        for block in range(2):
            there, lanes = slice(block * rows, (block + 1) * rows), slice(block * wide, 2 * wide)
            part_of(weights, score_grads, query, cot, parts.at[block], i, there, lanes)
            reach, lanes = (block + 1) * rows, slice(block * wide, (block + 1) * wide)
            acc[i, lanes, :] = dot(score_grads[i, :reach, lanes], keys[i, :reach, :], TN)

    @pl.when(lax.axis_index("ctx") >= 2)
    def _():
        for i in range(half_groups):
            acc[i] += dot(far_grads[i], far_keys[i], TN)

    for i in range(half_groups):
        for block in range(2):
            for h in range(ratio):
                at = (i * ratio + h) * DH
                low = block * wide + h * rows
                out_ref[block, :rows, at : at + DH] = (acc[i, low : low + rows] * SCALE).astype(BF16)
    part_mine[...] = parts[core_of()]
    for block in range(2):
        out_ref[block, :rows, half:] = parts[block].astype(BF16)
    summed = deltas[0]
    for i in range(1, half_groups):
        summed = summed + deltas[i]
    for block in range(2):
        own = split_rows(summed[:, block * wide : (block + 1) * wide], 16)
        own = joined_row(dot(own, chosen((wide, rows), ratio, 0), NN))
        out_ref[block, rows:, :rows] = split_rows(own, EXTRA)


def turn_back(values, out_key, out_value, cosine, sine, starts):
    for i, there in enumerate(starts):
        turned = rotate(values[:, 2 * i * DH : (2 * i + 1) * DH], cosine, sine)
        out_key[:, there] = turned.astype(BF16)
        out_value[:, there] = values[:, (2 * i + 1) * DH : (2 * i + 2) * DH].astype(BF16)


def finish_queries_kernel(back, pos_ref, cos_ref, sin_ref, *refs, limit):
    got, (query_grad, gate_grad, key_part, value_part) = refs[:-4], refs[-4:]
    rows = cos_ref.shape[0]
    half = query_grad.shape[1] // 2
    cosine, sine = cos_ref[...], -sin_ref[...]
    for side in range(2):
        for i in range(half // DH):
            there = slice(side * half + i * DH, side * half + (i + 1) * DH)
            turned = rotate(back[side, :rows, i * DH : (i + 1) * DH].astype(F32), cosine, sine)
            query_grad[:, there] = turned.astype(BF16)
    gate = joined_row(back[0, rows:, :rows]) + joined_row(back[1, rows:, :rows])
    gate_grad[...] = jnp.where(pos_ref[...] < limit, gate, 0.0)
    other = back[1 - core_of(), :rows, half:].astype(F32)
    for ref in got:
        other = other + ref[...].astype(F32)
    starts = [slice(i * DH, (i + 1) * DH) for i in range(key_part.shape[1] // DH)]
    turn_back(other, key_part, value_part, cosine, sine, starts)


def finish_keys_kernel(part_mine, key_part, value_part, cos_ref, sin_ref, *refs):
    got, (key_grad, value_grad) = refs[:-2], refs[-2:]
    half = key_part.shape[1]
    core = core_of()
    total = part_mine[...]
    for ref in got:
        total = total + ref[...].astype(F32)
    starts = [pl.ds(pl.multiple_of(core * half + i * DH, DH), DH) for i in range(half // DH)]
    turn_back(total, key_grad, value_grad, cos_ref[...], -sin_ref[...], starts)
    there = pl.ds(pl.multiple_of((1 - core) * half, DH), half)
    key_grad[:, there] = key_part[...]
    value_grad[:, there] = value_part[...]


def per_device(query_rows, key_rows, value_rows, cotangent, router_gate, positions):
    rows, heads_width = query_rows.shape[1:]
    group_width = key_rows.shape[2]
    groups = group_width // DH
    ratio = heads_width // group_width
    half_groups, half_width = groups // 2, heads_width // 2
    parts = lax.axis_size("ctx")
    chips = parts // 2
    limit = parts * LOCAL
    wide = ratio * rows
    params = pltpu.CompilerParams(vmem_limit_bytes=(16 + 4 * chips) * 1024 * 1024)

    def call(kernel, name, outs, *args, scratch=(), flops=10**6, in_hbm=False):
        if in_hbm:
            args = [pltpu.with_memory_space_constraint(arg, pltpu.HBM) for arg in args]
        spec = pl.BlockSpec(memory_space=pltpu.HBM if in_hbm else pltpu.VMEM)
        return pl.pallas_call(
            kernel,
            out_shape=[jax.ShapeDtypeStruct(*out) for out in outs],
            in_specs=[spec] * len(args),
            scratch_shapes=list(scratch),
            compiler_params=params,
            cost_estimate=pl.CostEstimate(flops=flops, bytes_accessed=1000, transcendentals=0),
            name=name,
        )(*args)

    index = np.arange(DH) % (DH // 2)
    freq = jnp.asarray((THETA ** (-2.0 * index / DH)).astype(np.float32))[None]
    packet = ((rows, group_width), BF16)
    packets_shape = ((2, rows + EXTRA, heads_width + group_width), BF16)
    table = ((rows, DH), F32)
    kv_mine, kv_theirs, packed, cosine, sine = call(
        functools.partial(pack_kernel, limit=limit),
        "pack",
        [packet, packet, packets_shape, table, table],
        key_rows[0],
        value_rows[0],
        query_rows[0],
        cotangent[0],
        router_gate,
        positions,
        freq,
        in_hbm=True,
        scratch=[
            pltpu.VMEM((rows, group_width), BF16),
            pltpu.VMEM((rows, group_width), BF16),
            pltpu.VMEM((rows, heads_width), BF16),
            pltpu.VMEM((1, rows), F32),
            pltpu.VMEM((1, rows), jnp.int32),
            pltpu.VMEM((1, DH), F32),
            pltpu.SemaphoreType.DMA((8,)),
        ],
    )

    hop = [[(2 * x + k, 2 * (x + s) + k) for x in range(chips - s) for k in range(2)] for s in range(chips)]
    cross = [[(a, b + 1 - 2 * (b % 2)) for a, b in pairs] for pairs in hop]
    back_hop = [[(b, a) for a, b in pairs] for pairs in hop]
    back_cross = [[(b, a) for a, b in pairs] for pairs in cross]

    far_own = [lax.ppermute(kv_mine, "ctx", hop[s]) for s in range(1, chips)]
    far_sib = [lax.ppermute(kv_theirs, "ctx", cross[s]) for s in range(1, chips)]

    pairs = [[2 * x, 2 * x + 1] for x in range(chips)]
    swap = lambda both: lax.all_to_all(both, "ctx", 0, 0, axis_index_groups=pairs)
    packets = swap(packed)

    row = ((half_groups, 1, 2 * wide), F32)
    table = ((half_groups, 2 * rows, 2 * wide), F32)
    kv_table = ((half_groups, 2 * rows, DH), BF16)
    q_table = ((half_groups, 2 * wide, DH), BF16)
    keys, values, query, cot, gate_row, raws, grads, tops, sums, crosses = call(
        functools.partial(local_kernel, ratio=ratio),
        "local_scores",
        [kv_table, kv_table, q_table, q_table, ((1, 2 * wide), F32), table, table, row, row, row],
        packets,
        flops=3 * 10**6,
    )

    blocks = 2 * (chips - 1)
    far_table = ((half_groups, blocks * rows, 2 * wide), BF16)
    table = ((half_groups, rows, 2 * wide), F32)
    late = ((half_groups, (blocks - 1) * rows, DH), BF16)
    early_raws, early_grads, early_tops, sums, crosses = call(
        early_kernel, "early_scores", [table, table, row, row, row], query, cot, tops, sums, crosses, far_sib[0]
    )
    far_keys, weights, far_grads, factors, deltas, *sib_parts = call(
        functools.partial(far_kernel, blocks=blocks),
        "far_scores",
        [((half_groups, blocks * rows, DH), BF16), far_table, far_table, row, row] + [packet] * (chips - 1),
        query,
        cot,
        gate_row,
        tops,
        early_raws,
        early_grads,
        early_tops,
        sums,
        crosses,
        *far_sib,
        *far_own,
        scratch=[pltpu.VMEM(*late), pltpu.VMEM(*late)],
    )
    sib_got = [lax.ppermute(sib_parts[s - 1], "ctx", back_cross[s]) for s in range(1, chips)]
    own_parts = call(far_rest_kernel, "far_rest", [packet] * (chips - 1), weights, far_grads, query, cot)
    own_got = [lax.ppermute(own_parts[s - 1], "ctx", back_hop[s]) for s in range(1, chips)]

    part_mine, packed = call(
        functools.partial(near_kernel, ratio=ratio),
        "near_grads",
        [
            ((rows, group_width), F32),
            ((2, rows + EXTRA, half_width + group_width), BF16),
        ],
        raws,
        grads,
        factors,
        deltas,
        keys,
        query,
        cot,
        far_keys,
        far_grads,
        flops=4 * 10**6,
        scratch=[
            pltpu.VMEM((half_groups, 2 * rows, 2 * wide), BF16),
            pltpu.VMEM((half_groups, 2 * rows, 2 * wide), BF16),
            pltpu.VMEM((2, rows, group_width), F32),
            pltpu.VMEM((half_groups, 2 * wide, DH), F32),
        ],
    )
    back = swap(packed)
    side = ((rows, group_width // 2), BF16)
    query_grad, gate_grad, key_part, value_part = call(
        functools.partial(finish_queries_kernel, limit=limit),
        "finish_queries",
        [((rows, heads_width), BF16), ((1, rows), F32), side, side],
        back,
        positions,
        cosine,
        sine,
        *sib_got,
        flops=3 * 10**8,
    )
    key_grad, value_grad = call(
        finish_keys_kernel,
        "finish_keys",
        [((rows, group_width), BF16)] * 2,
        part_mine,
        key_part,
        value_part,
        cosine,
        sine,
        *own_got,
    )
    return (query_grad[None], key_grad[None], value_grad[None], gate_grad)


def solution(mesh):
    wide = P(("group", "dp"), "ctx", None)
    narrow = P(("group", "dp"), "ctx")
    return jax.shard_map(
        per_device,
        mesh=mesh,
        in_specs=(wide, wide, wide, wide, narrow, narrow),
        out_specs=(wide, wide, wide, narrow),
        check_vma=False,
    )
```

```python
import functools
import math

import jax
import jax.numpy as jnp
import numpy as np
from jax import lax
from jax.experimental import pallas as pl
from jax.experimental.pallas import tpu as pltpu
from jax.sharding import PartitionSpec as P

DH = 128
LOCAL = 1024
THETA = 500000.0
EXTRA = 16
HIDDEN = -1e30
UNUSED = 2.0**14
SCALE = DH**-0.5
LOG2E = math.log2(math.e)
LN2 = math.log(2.0)

NT = (((1,), (1,)), ((), ()))
NN = (((1,), (0,)), ((), ()))
TN = (((0,), (0,)), ((), ()))
F32 = jnp.float32
BF16 = jnp.bfloat16


def few_bits(value, bits):
    unit = 2.0 ** (math.floor(math.log2(value)) + 1 - bits)
    return math.floor(value / unit) * unit


QUARTER_1 = few_bits(math.pi / 2, 10)
QUARTER_2 = few_bits(math.pi / 2 - QUARTER_1, 10)
QUARTER_3 = math.pi / 2 - QUARTER_1 - QUARTER_2


def dot(a, b, dims):
    return lax.dot_general(a, b, dims, preferred_element_type=F32)


def core_of():
    return lax.rem(lax.axis_index("ctx"), 2)


def rotate(values, cosine, sine):
    return values * cosine + pltpu.roll(values, DH // 2, 1) * sine


def sine_cosine(angle):
    turns = jnp.floor(angle * (2.0 / math.pi) + 0.5)
    rest = ((angle - turns * QUARTER_1) - turns * QUARTER_2) - turns * QUARTER_3
    square = rest * rest
    sine = ((-1.9515295891e-4 * square + 8.3321608736e-3) * square - 1.6666654611e-1) * square * rest + rest
    cosine = (2.443315711809948e-5 * square - 1.388731625493765e-3) * square + 4.166664568298827e-2
    cosine = cosine * square * square - 0.5 * square + 1.0
    quarter = turns.astype(jnp.int32)
    odd = (quarter & 1) == 1
    first, second = jnp.where(odd, cosine, sine), jnp.where(odd, sine, cosine)
    return (
        jnp.where((quarter & 2) == 2, -first, first),
        jnp.where(((quarter + 1) & 2) == 2, -second, second),
    )


def split_rows(row, height):
    high = row.astype(BF16).astype(F32)
    middle = (row - high).astype(BF16).astype(F32)
    low = row - high - middle
    line = lax.broadcasted_iota(jnp.int32, (height, row.shape[1]), 0)
    rows = jnp.where(line == 0, high, jnp.where(line == 1, middle, jnp.where(line == 2, low, 0.0)))
    return rows.astype(BF16)


def joined_row(rows):
    return jnp.sum(rows.astype(F32), axis=0, keepdims=True)


def pack_kernel(
    key_in, value_in, query_in, cot_in, gate_in, pos_in, freq_in, mine, theirs, packed, cos_ref, sin_ref,
    key, value, query, gate, pos, freq, sems, *, limit
):
    rows, width = key.shape
    side_width = width // 2
    half = query.shape[1] // 2
    core = core_of()
    loads = [(pos_in, pos), (freq_in, freq), (key_in, key), (value_in, value), (gate_in, gate), (query_in, query)]
    for side in range(2):
        there = slice(side * half, (side + 1) * half)
        loads.append((cot_in.at[:, there], packed.at[side, :rows, half : 2 * half]))
    loads = [pltpu.make_async_copy(source, target, sems.at[i]) for i, (source, target) in enumerate(loads)]
    for copy in loads:
        copy.start()
    loads[0].wait()
    loads[1].wait()
    places = pos[...]
    count = jnp.sum(jnp.where(places < limit, 1.0, 0.0), axis=1, keepdims=True)
    count = jnp.broadcast_to(count, (EXTRA, width)).astype(BF16)
    down = lax.broadcasted_iota(jnp.int32, (rows, rows), 0)
    along = lax.broadcasted_iota(jnp.int32, (rows, rows), 1)
    column = jnp.sum(jnp.where(down == along, places.astype(F32), 0.0), axis=1, keepdims=True)
    sine, cosine = sine_cosine(column * freq[...])
    lane = lax.broadcasted_iota(jnp.int32, (rows, DH), 1)
    sine = jnp.where(lane < DH // 2, -sine, sine)
    cos_ref[...] = cosine
    sin_ref[...] = sine
    loads[2].wait()
    loads[3].wait()
    used = jnp.broadcast_to(column, (rows, DH)) < limit
    for out_ref, side in ((mine, core), (theirs, 1 - core)):
        for i in range(side_width // DH):
            there = pl.ds(pl.multiple_of(side * side_width + i * DH, DH), DH)
            turned = rotate(key[:, there].astype(F32), cosine, sine)
            out_ref[:, 2 * i * DH : (2 * i + 1) * DH] = jnp.where(used, turned, UNUSED).astype(BF16)
            out_ref[:, (2 * i + 1) * DH : (2 * i + 2) * DH] = value[:, there]
            packed[side, :rows, 2 * half + 2 * i * DH : 2 * half + (2 * i + 1) * DH] = turned.astype(BF16)
            packed[side, :rows, 2 * half + (2 * i + 1) * DH : 2 * half + (2 * i + 2) * DH] = value[:, there]
        packed[side, rows:, 2 * half :] = count
    loads[4].wait()
    loads[5].wait()
    gates = split_rows(jnp.where(places < limit, gate[...], 0.0), EXTRA)
    cosine, sine = cosine * (SCALE * LOG2E), sine * (SCALE * LOG2E)
    for side in range(2):
        for i in range(half // DH):
            there = slice(side * half + i * DH, side * half + (i + 1) * DH)
            turned = rotate(query[:, there].astype(F32), cosine, sine)
            packed[side, :rows, i * DH : (i + 1) * DH] = turned.astype(BF16)
        packed[side, rows:, :rows] = gates
    for copy in loads[6:]:
        copy.wait()


def chosen(shape, ratio, dim):
    down = lax.broadcasted_iota(jnp.int32, shape, 0)
    along = lax.broadcasted_iota(jnp.int32, shape, 1)
    rows = shape[1 - dim]
    long, short = (down, along) if dim == 0 else (along, down)
    for _ in range(1, ratio):
        long = jnp.where(long >= rows, long - rows, long)
    return jnp.where(long == short, 1.0, 0.0).astype(BF16)


def chunks(low, high):
    return [slice(at, min(at + 256, high)) for at in range(low, high, 256)]


def local_kernel(packets, keys, values, query, cot, gate, raws, grads, tops, sums, crosses, *, ratio):
    rows = packets.shape[1] - EXTRA
    half_groups = keys.shape[0]
    wide = ratio * rows
    half = half_groups * ratio * DH
    for side in range(2):
        there = slice(side * rows, (side + 1) * rows)
        for i in range(half_groups):
            at = 2 * half + 2 * i * DH
            keys[i, there, :] = packets[side, :rows, at : at + DH]
            values[i, there, :] = packets[side, :rows, at + DH : at + 2 * DH]
            for h in range(ratio):
                to = slice(side * wide + h * rows, side * wide + (h + 1) * rows)
                at = (i * ratio + h) * DH
                query[i, to, :] = packets[side, :rows, at : at + DH]
                cot[i, to, :] = packets[side, :rows, half + at : half + at + DH]
        gates = dot(packets[side, rows:, :rows], chosen((rows, wide), ratio, 1), NN)
        gate[:, side * wide : (side + 1) * wide] = joined_row(gates)
    count = packets[0, rows:, 2 * half : 2 * half + 256].astype(F32)[:1]
    for i in range(half_groups):
        for block in range(2):
            reach = (block + 1) * rows
            for here in chunks(block * wide, (block + 1) * wide):
                width = here.stop - here.start
                scores = dot(keys[i, :reach, :], query[i, here, :], NT)
                slot = lax.broadcasted_iota(jnp.int32, (rows, width), 0)
                lane = lax.broadcasted_iota(jnp.int32, (rows, width), 1) + (here.start - block * wide)
                for h in range(1, ratio):
                    lane = jnp.where(lane >= rows, lane - rows, lane)
                shown = jnp.where(slot <= lane, scores[block * rows :], HIDDEN)
                if block:
                    before = jnp.where(slot.astype(F32) < count[:, :width], scores[:rows], HIDDEN)
                    shown = jnp.concatenate([before, shown], axis=0)
                top = jnp.max(shown, axis=0, keepdims=True)
                raw = jnp.exp2(shown - top)
                prob_grad = dot(values[i, :reach, :], cot[i, here, :], NT)
                raws[i, :reach, here] = raw
                grads[i, :reach, here] = prob_grad
                tops[i, :, here] = top
                sums[i, :, here] = jnp.sum(raw, axis=0, keepdims=True)
                crosses[i, :, here] = jnp.sum(raw * prob_grad, axis=0, keepdims=True)


def part_of(weights, score_grads, query, cot, out_ref, i, there, lanes):
    key_part = dot(score_grads[i, there, lanes], query[i, lanes, :], NN) * LN2
    value_part = dot(weights[i, there, lanes], cot[i, lanes, :], NN)
    out_ref[:, 2 * i * DH : (2 * i + 1) * DH] = key_part.astype(out_ref.dtype)
    out_ref[:, (2 * i + 1) * DH : (2 * i + 2) * DH] = value_part.astype(out_ref.dtype)


def used_slots(packet, here):
    chip = lax.div(lax.axis_index("ctx"), 2)
    key = packet[:, :DH].astype(F32)[:, :1]
    return jnp.broadcast_to(key, (packet.shape[0], 256)) < jnp.where(chip >= here, UNUSED / 2, -UNUSED)


def early_kernel(query, cot, tops, sums, crosses, packet, raws, grads, new_tops, new_sums, new_crosses):
    half_groups, lanes = query.shape[:2]
    alone = lax.axis_index("ctx") < 2

    @pl.when(alone)
    def _():
        new_tops[...] = tops[...]
        new_sums[...] = sums[...]
        new_crosses[...] = crosses[...]

    @pl.when(jnp.logical_not(alone))
    def _():
        used = used_slots(packet, 1)
        for i in range(half_groups):
            key = packet[:, 2 * i * DH : (2 * i + 1) * DH]
            value = packet[:, (2 * i + 1) * DH : (2 * i + 2) * DH]
            for here in chunks(0, lanes):
                width = here.stop - here.start
                shown = jnp.where(used[:, :width], dot(key, query[i, here, :], NT), HIDDEN)
                old_top = tops[i, :, here]
                top = jnp.maximum(old_top, jnp.max(shown, axis=0, keepdims=True))
                raw = jnp.exp2(shown - top)
                shrink = jnp.exp2(old_top - top)
                prob_grad = dot(value, cot[i, here, :], NT)
                raws[i, :, here] = raw
                grads[i, :, here] = prob_grad
                new_tops[i, :, here] = top
                new_sums[i, :, here] = sums[i, :, here] * shrink + jnp.sum(raw, axis=0, keepdims=True)
                cross = jnp.sum(raw * prob_grad, axis=0, keepdims=True)
                new_crosses[i, :, here] = crosses[i, :, here] * shrink + cross


def far_kernel(query, cot, gate, first_tops, raws, grads, tops, sums, crosses, early, *refs, blocks):
    packets = refs[: blocks - 1]
    far_keys, weights, score_grads, factors, deltas = refs[blocks - 1 : blocks + 4]
    parts = refs[blocks + 4 : -2]
    late_keys, late_values = refs[-2:]
    rows = early.shape[0]
    half_groups, lanes = query.shape[:2]
    alone = lax.axis_index("ctx") < 2

    @pl.when(alone)
    def _():
        for i in range(half_groups):
            inverse = 1.0 / sums[i]
            factors[i] = inverse * gate[...]
            deltas[i] = crosses[i] * inverse

    @pl.when(jnp.logical_not(alone))
    def _():
        for i in range(half_groups):
            far_keys[i, :rows, :] = early[:, 2 * i * DH : (2 * i + 1) * DH]
            for j, packet in enumerate(packets):
                there = slice(j * rows, (j + 1) * rows)
                far_keys[i, (j + 1) * rows : (j + 2) * rows, :] = packet[:, 2 * i * DH : (2 * i + 1) * DH]
                late_keys[i, there, :] = packet[:, 2 * i * DH : (2 * i + 1) * DH]
                late_values[i, there, :] = packet[:, (2 * i + 1) * DH : (2 * i + 2) * DH]
        hops = blocks // 2
        used = [used_slots(packet, (j + 1) % hops + 1) for j, packet in enumerate(packets)]
        for i in range(half_groups):
            for here in chunks(0, lanes):
                width = here.stop - here.start
                scores = dot(late_keys[i], query[i, here, :], NT)
                shown = [
                    jnp.where(used[j][:, :width], scores[j * rows : (j + 1) * rows], HIDDEN)
                    for j in range(blocks - 1)
                ]
                shown = jnp.concatenate(shown, axis=0)
                old_top = tops[i, :, here]
                top = jnp.maximum(old_top, jnp.max(shown, axis=0, keepdims=True))
                raw = jnp.exp2(shown - top)
                shrink = jnp.exp2(old_top - top)
                inverse = 1.0 / (sums[i, :, here] * shrink + jnp.sum(raw, axis=0, keepdims=True))
                prob_grad = dot(late_values[i], cot[i, here, :], NT)
                cross = crosses[i, :, here] * shrink + jnp.sum(raw * prob_grad, axis=0, keepdims=True)
                delta = cross * inverse
                factor = inverse * gate[:, here]
                factors[i, :, here] = factor * jnp.exp2(first_tops[i, :, here] - top)
                deltas[i, :, here] = delta
                gated = raw * factor
                weights[i, rows:, here] = gated.astype(BF16)
                score_grads[i, rows:, here] = (gated * (prob_grad - delta)).astype(BF16)
                gated = raws[i, :, here] * (factor * shrink)
                weights[i, :rows, here] = gated.astype(BF16)
                score_grads[i, :rows, here] = (gated * (grads[i, :, here] - delta)).astype(BF16)
            for j, out_ref in enumerate(parts):
                part_of(weights, score_grads, query, cot, out_ref, i, slice(j * rows, (j + 1) * rows), slice(0, lanes))


def far_rest_kernel(weights, score_grads, query, cot, *parts):
    rows = parts[0].shape[0]
    half_groups, lanes = query.shape[:2]

    @pl.when(lax.axis_index("ctx") >= 2)
    def _():
        for j, out_ref in enumerate(parts):
            there = slice((len(parts) + j) * rows, (len(parts) + j + 1) * rows)
            for i in range(half_groups):
                part_of(weights, score_grads, query, cot, out_ref, i, there, slice(0, lanes))


def near_kernel(
    raws, grads, factors, deltas, keys, query, cot, far_keys, far_grads,
    part_mine, query_mine, gate_mine, theirs, weights, score_grads, parts, acc,
    *, ratio
):
    rows = part_mine.shape[0]
    half_groups = keys.shape[0]
    wide = ratio * rows
    half = half_groups * ratio * DH
    for i in range(half_groups):
        for block in range(2):
            reach = (block + 1) * rows
            for here in chunks(block * wide, (block + 1) * wide):
                gated = raws[i, :reach, here] * factors[i, :, here]
                weights[i, :reach, here] = gated.astype(BF16)
                score_grads[i, :reach, here] = (gated * (grads[i, :reach, here] - deltas[i, :, here])).astype(BF16)
        for block in range(2):
            there, lanes = slice(block * rows, (block + 1) * rows), slice(block * wide, 2 * wide)
            part_of(weights, score_grads, query, cot, parts.at[block], i, there, lanes)
            reach, lanes = (block + 1) * rows, slice(block * wide, (block + 1) * wide)
            acc[i, lanes, :] = dot(score_grads[i, :reach, lanes], keys[i, :reach, :], TN)

    @pl.when(lax.axis_index("ctx") >= 2)
    def _():
        for i in range(half_groups):
            acc[i] += dot(far_grads[i], far_keys[i], TN)

    core = core_of()
    for out_ref, block in ((theirs, 1 - core), (query_mine, core)):
        for i in range(half_groups):
            for h in range(ratio):
                at = (i * ratio + h) * DH
                low = pl.ds(pl.multiple_of(block * wide + h * rows, 16), rows)
                out_ref[:rows, at : at + DH] = (acc[i, low, :] * SCALE).astype(BF16)
    part_mine[...] = parts[core]
    theirs[:rows, half:] = parts[1 - core].astype(BF16)
    summed = deltas[0]
    for i in range(1, half_groups):
        summed = summed + deltas[i]
    gates = []
    for block in range(2):
        own = split_rows(summed[:, block * wide : (block + 1) * wide], 16)
        gates.append(joined_row(dot(own, chosen((wide, rows), ratio, 0), NN)))
    gate_mine[...] = jnp.where(core == 0, gates[0], gates[1])
    theirs[rows:, :rows] = split_rows(jnp.where(core == 0, gates[1], gates[0]), EXTRA)


def turn_back(values, out_key, out_value, cosine, sine, starts):
    for i, there in enumerate(starts):
        turned = rotate(values[:, 2 * i * DH : (2 * i + 1) * DH], cosine, sine)
        out_key[:, there] = turned.astype(BF16)
        out_value[:, there] = values[:, (2 * i + 1) * DH : (2 * i + 2) * DH].astype(BF16)


def finish_queries_kernel(back, query_mine, gate_mine, pos_ref, cos_ref, sin_ref, *refs, limit):
    got, (query_grad, gate_grad, key_part, value_part) = refs[:-4], refs[-4:]
    rows, half = query_mine.shape
    core = core_of()
    cosine, sine = cos_ref[...], -sin_ref[...]
    for side, ref in ((core, query_mine), (1 - core, back.at[1 - core])):
        for i in range(half // DH):
            there = pl.ds(pl.multiple_of(side * half + i * DH, DH), DH)
            turned = rotate(ref[:rows, i * DH : (i + 1) * DH].astype(F32), cosine, sine)
            query_grad[:, there] = turned.astype(BF16)
    gate = gate_mine[...] + joined_row(back[1 - core, rows:, :rows])
    gate_grad[...] = jnp.where(pos_ref[...] < limit, gate, 0.0)
    other = back[1 - core, :rows, half:].astype(F32)
    for ref in got:
        other = other + ref[...].astype(F32)
    starts = [slice(i * DH, (i + 1) * DH) for i in range(key_part.shape[1] // DH)]
    turn_back(other, key_part, value_part, cosine, sine, starts)


def finish_keys_kernel(part_mine, key_part, value_part, cos_ref, sin_ref, *refs):
    got, (key_grad, value_grad) = refs[:-2], refs[-2:]
    half = key_part.shape[1]
    core = core_of()
    total = part_mine[...]
    for ref in got:
        total = total + ref[...].astype(F32)
    starts = [pl.ds(pl.multiple_of(core * half + i * DH, DH), DH) for i in range(half // DH)]
    turn_back(total, key_grad, value_grad, cos_ref[...], -sin_ref[...], starts)
    there = pl.ds(pl.multiple_of((1 - core) * half, DH), half)
    key_grad[:, there] = key_part[...]
    value_grad[:, there] = value_part[...]


def per_device(query_rows, key_rows, value_rows, cotangent, router_gate, positions):
    rows, heads_width = query_rows.shape[1:]
    group_width = key_rows.shape[2]
    groups = group_width // DH
    ratio = heads_width // group_width
    half_groups, half_width = groups // 2, heads_width // 2
    parts = lax.axis_size("ctx")
    chips = parts // 2
    limit = parts * LOCAL
    wide = ratio * rows
    params = pltpu.CompilerParams(vmem_limit_bytes=(16 + 4 * chips) * 1024 * 1024)

    def call(kernel, name, outs, *args, scratch=(), flops=10**6, in_hbm=False):
        if in_hbm:
            args = [pltpu.with_memory_space_constraint(arg, pltpu.HBM) for arg in args]
        spec = pl.BlockSpec(memory_space=pltpu.HBM if in_hbm else pltpu.VMEM)
        return pl.pallas_call(
            kernel,
            out_shape=[jax.ShapeDtypeStruct(*out) for out in outs],
            in_specs=[spec] * len(args),
            scratch_shapes=list(scratch),
            compiler_params=params,
            cost_estimate=pl.CostEstimate(flops=flops, bytes_accessed=1000, transcendentals=0),
            name=name,
        )(*args)

    index = np.arange(DH) % (DH // 2)
    freq = jnp.asarray((THETA ** (-2.0 * index / DH)).astype(np.float32))[None]
    packet = ((rows, group_width), BF16)
    packets_shape = ((2, rows + EXTRA, heads_width + group_width), BF16)
    table = ((rows, DH), F32)
    kv_mine, kv_theirs, packed, cosine, sine = call(
        functools.partial(pack_kernel, limit=limit),
        "pack",
        [packet, packet, packets_shape, table, table],
        key_rows[0],
        value_rows[0],
        query_rows[0],
        cotangent[0],
        router_gate,
        positions,
        freq,
        in_hbm=True,
        scratch=[
            pltpu.VMEM((rows, group_width), BF16),
            pltpu.VMEM((rows, group_width), BF16),
            pltpu.VMEM((rows, heads_width), BF16),
            pltpu.VMEM((1, rows), F32),
            pltpu.VMEM((1, rows), jnp.int32),
            pltpu.VMEM((1, DH), F32),
            pltpu.SemaphoreType.DMA((8,)),
        ],
    )

    hop = [[(2 * x + k, 2 * (x + s) + k) for x in range(chips - s) for k in range(2)] for s in range(chips)]
    cross = [[(a, b + 1 - 2 * (b % 2)) for a, b in pairs] for pairs in hop]
    back_hop = [[(b, a) for a, b in pairs] for pairs in hop]
    back_cross = [[(b, a) for a, b in pairs] for pairs in cross]

    far_own = [lax.ppermute(kv_mine, "ctx", hop[s]) for s in range(1, chips)]
    far_sib = [lax.ppermute(kv_theirs, "ctx", cross[s]) for s in range(1, chips)]

    pairs = [[2 * x, 2 * x + 1] for x in range(chips)]
    swap = lambda both: lax.all_to_all(both, "ctx", 0, 0, axis_index_groups=pairs)
    packets = swap(packed)

    row = ((half_groups, 1, 2 * wide), F32)
    table = ((half_groups, 2 * rows, 2 * wide), F32)
    kv_table = ((half_groups, 2 * rows, DH), BF16)
    q_table = ((half_groups, 2 * wide, DH), BF16)
    keys, values, query, cot, gate_row, raws, grads, tops, sums, crosses = call(
        functools.partial(local_kernel, ratio=ratio),
        "local_scores",
        [kv_table, kv_table, q_table, q_table, ((1, 2 * wide), F32), table, table, row, row, row],
        packets,
        flops=3 * 10**6,
    )

    blocks = 2 * (chips - 1)
    far_table = ((half_groups, blocks * rows, 2 * wide), BF16)
    table = ((half_groups, rows, 2 * wide), F32)
    late = ((half_groups, (blocks - 1) * rows, DH), BF16)
    early_raws, early_grads, early_tops, sums, crosses = call(
        early_kernel, "early_scores", [table, table, row, row, row], query, cot, tops, sums, crosses, far_sib[0]
    )
    far_keys, weights, far_grads, factors, deltas, *sib_parts = call(
        functools.partial(far_kernel, blocks=blocks),
        "far_scores",
        [((half_groups, blocks * rows, DH), BF16), far_table, far_table, row, row] + [packet] * (chips - 1),
        query,
        cot,
        gate_row,
        tops,
        early_raws,
        early_grads,
        early_tops,
        sums,
        crosses,
        *far_sib,
        *far_own,
        scratch=[pltpu.VMEM(*late), pltpu.VMEM(*late)],
    )
    sib_got = [lax.ppermute(sib_parts[s - 1], "ctx", back_cross[s]) for s in range(1, chips)]
    own_parts = call(far_rest_kernel, "far_rest", [packet] * (chips - 1), weights, far_grads, query, cot)
    own_got = [lax.ppermute(own_parts[s - 1], "ctx", back_hop[s]) for s in range(1, chips)]

    part_mine, query_mine, gate_mine, theirs = call(
        functools.partial(near_kernel, ratio=ratio),
        "near_grads",
        [
            ((rows, group_width), F32),
            ((rows, half_width), BF16),
            ((1, rows), F32),
            ((rows + EXTRA, half_width + group_width), BF16),
        ],
        raws,
        grads,
        factors,
        deltas,
        keys,
        query,
        cot,
        far_keys,
        far_grads,
        flops=4 * 10**6,
        scratch=[
            pltpu.VMEM((half_groups, 2 * rows, 2 * wide), BF16),
            pltpu.VMEM((half_groups, 2 * rows, 2 * wide), BF16),
            pltpu.VMEM((2, rows, group_width), F32),
            pltpu.VMEM((half_groups, 2 * wide, DH), F32),
        ],
    )
    back = lax.all_gather(theirs, "ctx", axis_index_groups=pairs)
    side = ((rows, group_width // 2), BF16)
    query_grad, gate_grad, key_part, value_part = call(
        functools.partial(finish_queries_kernel, limit=limit),
        "finish_queries",
        [((rows, heads_width), BF16), ((1, rows), F32), side, side],
        back,
        query_mine,
        gate_mine,
        positions,
        cosine,
        sine,
        *sib_got,
        flops=3 * 10**8,
    )
    key_grad, value_grad = call(
        finish_keys_kernel,
        "finish_keys",
        [((rows, group_width), BF16)] * 2,
        part_mine,
        key_part,
        value_part,
        cosine,
        sine,
        *own_got,
    )
    return (query_grad[None], key_grad[None], value_grad[None], gate_grad)


def solution(mesh):
    wide = P(("group", "dp"), "ctx", None)
    narrow = P(("group", "dp"), "ctx")
    return jax.shard_map(
        per_device,
        mesh=mesh,
        in_specs=(wide, wide, wide, wide, narrow, narrow),
        out_specs=(wide, wide, wide, narrow),
        check_vma=False,
    )
```

```python
import functools
import math

import jax
import jax.numpy as jnp
import numpy as np
from jax import lax
from jax.experimental import pallas as pl
from jax.experimental.pallas import tpu as pltpu
from jax.sharding import PartitionSpec as P

DH = 128
LOCAL = 1024
THETA = 500000.0
EXTRA = 16
HIDDEN = -1e30
UNUSED = 2.0**14
SCALE = DH**-0.5
LOG2E = math.log2(math.e)
LN2 = math.log(2.0)

NT = (((1,), (1,)), ((), ()))
NN = (((1,), (0,)), ((), ()))
TN = (((0,), (0,)), ((), ()))
F32 = jnp.float32
BF16 = jnp.bfloat16


def few_bits(value, bits):
    unit = 2.0 ** (math.floor(math.log2(value)) + 1 - bits)
    return math.floor(value / unit) * unit


QUARTER_1 = few_bits(math.pi / 2, 10)
QUARTER_2 = few_bits(math.pi / 2 - QUARTER_1, 10)
QUARTER_3 = math.pi / 2 - QUARTER_1 - QUARTER_2


def dot(a, b, dims):
    return lax.dot_general(a, b, dims, preferred_element_type=F32)


def core_of():
    return lax.rem(lax.axis_index("ctx"), 2)


def rotate(values, cosine, sine):
    return values * cosine + pltpu.roll(values, DH // 2, 1) * sine


def sine_cosine(angle):
    turns = jnp.floor(angle * (2.0 / math.pi) + 0.5)
    rest = ((angle - turns * QUARTER_1) - turns * QUARTER_2) - turns * QUARTER_3
    square = rest * rest
    sine = ((-1.9515295891e-4 * square + 8.3321608736e-3) * square - 1.6666654611e-1) * square * rest + rest
    cosine = (2.443315711809948e-5 * square - 1.388731625493765e-3) * square + 4.166664568298827e-2
    cosine = cosine * square * square - 0.5 * square + 1.0
    quarter = turns.astype(jnp.int32)
    odd = (quarter & 1) == 1
    first, second = jnp.where(odd, cosine, sine), jnp.where(odd, sine, cosine)
    return (
        jnp.where((quarter & 2) == 2, -first, first),
        jnp.where(((quarter + 1) & 2) == 2, -second, second),
    )


def split_rows(row, height):
    high = row.astype(BF16).astype(F32)
    middle = (row - high).astype(BF16).astype(F32)
    low = row - high - middle
    line = lax.broadcasted_iota(jnp.int32, (height, row.shape[1]), 0)
    rows = jnp.where(line == 0, high, jnp.where(line == 1, middle, jnp.where(line == 2, low, 0.0)))
    return rows.astype(BF16)


def joined_row(rows):
    return jnp.sum(rows.astype(F32), axis=0, keepdims=True)


def pack_keys_kernel(
    key_in, value_in, pos_in, freq_in, mine, theirs, packed, cos_ref, sin_ref, count_ref, key, value, pos, freq, sems,
    *, limit
):
    loads = [(pos_in, pos), (freq_in, freq), (key_in, key), (value_in, value)]
    loads = [pltpu.make_async_copy(source, target, sems.at[i]) for i, (source, target) in enumerate(loads)]
    for copy in loads:
        copy.start()
    rows, width = key.shape
    side_width = width // 2
    core = core_of()
    down = lax.broadcasted_iota(jnp.int32, (rows, rows), 0)
    along = lax.broadcasted_iota(jnp.int32, (rows, rows), 1)
    lane = lax.broadcasted_iota(jnp.int32, (rows, DH), 1)
    loads[0].wait()
    loads[1].wait()
    places = pos[...]
    count = jnp.sum(jnp.where(places < limit, 1.0, 0.0), axis=1, keepdims=True)
    count_ref[...] = jnp.broadcast_to(count, count_ref.shape).astype(BF16)
    column = jnp.sum(jnp.where(down == along, places.astype(F32), 0.0), axis=1, keepdims=True)
    sine, cosine = sine_cosine(column * freq[...])
    sine = jnp.where(lane < DH // 2, -sine, sine)
    cos_ref[...] = cosine
    sin_ref[...] = sine
    used = jnp.broadcast_to(column, (rows, DH)) < limit
    loads[2].wait()
    loads[3].wait()
    for out_ref, side in ((mine, core), (theirs, 1 - core)):
        for i in range(side_width // DH):
            there = pl.ds(pl.multiple_of(side * side_width + i * DH, DH), DH)
            turned = rotate(key[:, there].astype(F32), cosine, sine)
            out_ref[:, 2 * i * DH : (2 * i + 1) * DH] = jnp.where(used, turned, UNUSED).astype(BF16)
            out_ref[:, (2 * i + 1) * DH : (2 * i + 2) * DH] = value[:, there]
            packed[side, :, 2 * i * DH : (2 * i + 1) * DH] = turned.astype(BF16)
            packed[side, :, (2 * i + 1) * DH : (2 * i + 2) * DH] = value[:, there]


def pack_queries_kernel(query, cot, gate, pos, cos_ref, sin_ref, count, kv, packed, *, limit):
    rows = query.shape[0]
    half = query.shape[1] // 2
    gates = split_rows(jnp.where(pos[...] < limit, gate[...], 0.0), EXTRA)
    cosine, sine = cos_ref[...] * (SCALE * LOG2E), sin_ref[...] * (SCALE * LOG2E)
    for side in range(2):
        for i in range(half // DH):
            there = slice(side * half + i * DH, side * half + (i + 1) * DH)
            turned = rotate(query[:, there].astype(F32), cosine, sine)
            packed[side, :rows, i * DH : (i + 1) * DH] = turned.astype(BF16)
        packed[side, :rows, half : 2 * half] = cot[:, side * half : (side + 1) * half]
        packed[side, :rows, 2 * half :] = kv[side]
        packed[side, rows:, :rows] = gates
        packed[side, rows:, 2 * half : 2 * half + 256] = count[...]


def chosen(shape, ratio, dim):
    down = lax.broadcasted_iota(jnp.int32, shape, 0)
    along = lax.broadcasted_iota(jnp.int32, shape, 1)
    rows = shape[1 - dim]
    long, short = (down, along) if dim == 0 else (along, down)
    for _ in range(1, ratio):
        long = jnp.where(long >= rows, long - rows, long)
    return jnp.where(long == short, 1.0, 0.0).astype(BF16)


def chunks(low, high):
    return [slice(at, min(at + 256, high)) for at in range(low, high, 256)]


def local_kernel(packets, keys, values, query, cot, gate, raws, grads, tops, sums, crosses, *, ratio):
    rows = packets.shape[1] - EXTRA
    half_groups = keys.shape[0]
    wide = ratio * rows
    half = half_groups * ratio * DH
    for side in range(2):
        there = slice(side * rows, (side + 1) * rows)
        for i in range(half_groups):
            at = 2 * half + 2 * i * DH
            keys[i, there, :] = packets[side, :rows, at : at + DH]
            values[i, there, :] = packets[side, :rows, at + DH : at + 2 * DH]
            for h in range(ratio):
                to = slice(side * wide + h * rows, side * wide + (h + 1) * rows)
                at = (i * ratio + h) * DH
                query[i, to, :] = packets[side, :rows, at : at + DH]
                cot[i, to, :] = packets[side, :rows, half + at : half + at + DH]
        gates = dot(packets[side, rows:, :rows], chosen((rows, wide), ratio, 1), NN)
        gate[:, side * wide : (side + 1) * wide] = joined_row(gates)
    count = packets[0, rows:, 2 * half : 2 * half + 256].astype(F32)[:1]
    for i in range(half_groups):
        for block in range(2):
            reach = (block + 1) * rows
            for here in chunks(block * wide, (block + 1) * wide):
                width = here.stop - here.start
                scores = dot(keys[i, :reach, :], query[i, here, :], NT)
                slot = lax.broadcasted_iota(jnp.int32, (rows, width), 0)
                lane = lax.broadcasted_iota(jnp.int32, (rows, width), 1) + (here.start - block * wide)
                for h in range(1, ratio):
                    lane = jnp.where(lane >= rows, lane - rows, lane)
                shown = jnp.where(slot <= lane, scores[block * rows :], HIDDEN)
                if block:
                    before = jnp.where(slot.astype(F32) < count[:, :width], scores[:rows], HIDDEN)
                    shown = jnp.concatenate([before, shown], axis=0)
                top = jnp.max(shown, axis=0, keepdims=True)
                raw = jnp.exp2(shown - top)
                prob_grad = dot(values[i, :reach, :], cot[i, here, :], NT)
                raws[i, :reach, here] = raw
                grads[i, :reach, here] = prob_grad
                tops[i, :, here] = top
                sums[i, :, here] = jnp.sum(raw, axis=0, keepdims=True)
                crosses[i, :, here] = jnp.sum(raw * prob_grad, axis=0, keepdims=True)


def part_of(weights, score_grads, query, cot, out_ref, i, there, lanes):
    key_part = dot(score_grads[i, there, lanes], query[i, lanes, :], NN) * LN2
    value_part = dot(weights[i, there, lanes], cot[i, lanes, :], NN)
    out_ref[:, 2 * i * DH : (2 * i + 1) * DH] = key_part.astype(out_ref.dtype)
    out_ref[:, (2 * i + 1) * DH : (2 * i + 2) * DH] = value_part.astype(out_ref.dtype)


def used_slots(packet, here):
    chip = lax.div(lax.axis_index("ctx"), 2)
    key = packet[:, :DH].astype(F32)[:, :1]
    return jnp.broadcast_to(key, (packet.shape[0], 256)) < jnp.where(chip >= here, UNUSED / 2, -UNUSED)


def early_kernel(query, cot, tops, sums, crosses, packet, raws, grads, new_tops, new_sums, new_crosses):
    half_groups, lanes = query.shape[:2]
    alone = lax.axis_index("ctx") < 2

    @pl.when(alone)
    def _():
        new_tops[...] = tops[...]
        new_sums[...] = sums[...]
        new_crosses[...] = crosses[...]

    @pl.when(jnp.logical_not(alone))
    def _():
        used = used_slots(packet, 1)
        for i in range(half_groups):
            key = packet[:, 2 * i * DH : (2 * i + 1) * DH]
            value = packet[:, (2 * i + 1) * DH : (2 * i + 2) * DH]
            for here in chunks(0, lanes):
                width = here.stop - here.start
                shown = jnp.where(used[:, :width], dot(key, query[i, here, :], NT), HIDDEN)
                old_top = tops[i, :, here]
                top = jnp.maximum(old_top, jnp.max(shown, axis=0, keepdims=True))
                raw = jnp.exp2(shown - top)
                shrink = jnp.exp2(old_top - top)
                prob_grad = dot(value, cot[i, here, :], NT)
                raws[i, :, here] = raw
                grads[i, :, here] = prob_grad
                new_tops[i, :, here] = top
                new_sums[i, :, here] = sums[i, :, here] * shrink + jnp.sum(raw, axis=0, keepdims=True)
                cross = jnp.sum(raw * prob_grad, axis=0, keepdims=True)
                new_crosses[i, :, here] = crosses[i, :, here] * shrink + cross


def far_kernel(query, cot, gate, first_tops, raws, grads, tops, sums, crosses, early, *refs, blocks):
    packets = refs[: blocks - 1]
    far_keys, weights, score_grads, late_raws, late_grads = refs[blocks - 1 : blocks + 4]
    factors, late_factors, deltas, part, late_keys, late_values = refs[blocks + 4 :]
    rows = early.shape[0]
    half_groups, lanes = query.shape[:2]
    alone = lax.axis_index("ctx") < 2

    @pl.when(alone)
    def _():
        for i in range(half_groups):
            inverse = 1.0 / sums[i]
            factors[i] = inverse * gate[...]
            deltas[i] = crosses[i] * inverse

    @pl.when(jnp.logical_not(alone))
    def _():
        for i in range(half_groups):
            far_keys[i, :rows, :] = early[:, 2 * i * DH : (2 * i + 1) * DH]
            for j, packet in enumerate(packets):
                there = slice(j * rows, (j + 1) * rows)
                far_keys[i, (j + 1) * rows : (j + 2) * rows, :] = packet[:, 2 * i * DH : (2 * i + 1) * DH]
                late_keys[i, there, :] = packet[:, 2 * i * DH : (2 * i + 1) * DH]
                late_values[i, there, :] = packet[:, (2 * i + 1) * DH : (2 * i + 2) * DH]
        hops = blocks // 2
        used = [used_slots(packet, (j + 1) % hops + 1) for j, packet in enumerate(packets)]
        for i in range(half_groups):
            for here in chunks(0, lanes):
                width = here.stop - here.start
                scores = dot(late_keys[i], query[i, here, :], NT)
                shown = [
                    jnp.where(used[j][:, :width], scores[j * rows : (j + 1) * rows], HIDDEN)
                    for j in range(blocks - 1)
                ]
                shown = jnp.concatenate(shown, axis=0)
                old_top = tops[i, :, here]
                top = jnp.maximum(old_top, jnp.max(shown, axis=0, keepdims=True))
                raw = jnp.exp2(shown - top)
                shrink = jnp.exp2(old_top - top)
                inverse = 1.0 / (sums[i, :, here] * shrink + jnp.sum(raw, axis=0, keepdims=True))
                prob_grad = dot(late_values[i], cot[i, here, :], NT)
                late_raws[i, :, here] = raw.astype(late_raws.dtype)
                late_grads[i, :, here] = prob_grad.astype(late_grads.dtype)
                cross = crosses[i, :, here] * shrink + jnp.sum(raw * prob_grad, axis=0, keepdims=True)
                delta = cross * inverse
                factor = inverse * gate[:, here]
                factors[i, :, here] = factor * jnp.exp2(first_tops[i, :, here] - top)
                late_factors[i, :, here] = factor
                deltas[i, :, here] = delta
                gated = raws[i, :, here] * (factor * shrink)
                weights[i, :, here] = gated.astype(BF16)
                score_grads[i, :, here] = (gated * (grads[i, :, here] - delta)).astype(BF16)
            part_of(weights, score_grads, query, cot, part, i, slice(0, rows), slice(0, lanes))


def far_rest_kernel(raws, grads, factors, deltas, early_grads, query, cot, score_grads, *refs):
    parts, weights = refs[:-1], refs[-1]
    rows = early_grads.shape[1]
    half_groups, lanes = query.shape[:2]

    @pl.when(lax.axis_index("ctx") >= 2)
    def _():
        for i in range(half_groups):
            score_grads[i, :rows, :] = early_grads[i]
            for here in chunks(0, lanes):
                gated = raws[i, :, here].astype(F32) * factors[i, :, here]
                weights[i, rows:, here] = gated.astype(BF16)
                rest = grads[i, :, here].astype(F32) - deltas[i, :, here]
                score_grads[i, rows:, here] = (gated * rest).astype(BF16)
            for j, out_ref in enumerate(parts):
                there = slice((j + 1) * rows, (j + 2) * rows)
                part_of(weights, score_grads, query, cot, out_ref, i, there, slice(0, lanes))


def near_kernel(
    raws, grads, factors, deltas, keys, query, cot, far_keys, far_grads,
    part_mine, out_ref, weights, score_grads, parts, acc,
    *, ratio
):
    rows = part_mine.shape[0]
    half_groups = keys.shape[0]
    wide = ratio * rows
    half = half_groups * ratio * DH
    for i in range(half_groups):
        for block in range(2):
            reach = (block + 1) * rows
            for here in chunks(block * wide, (block + 1) * wide):
                gated = raws[i, :reach, here] * factors[i, :, here]
                weights[i, :reach, here] = gated.astype(BF16)
                score_grads[i, :reach, here] = (gated * (grads[i, :reach, here] - deltas[i, :, here])).astype(BF16)
        for block in range(2):
            there, lanes = slice(block * rows, (block + 1) * rows), slice(block * wide, 2 * wide)
            part_of(weights, score_grads, query, cot, parts.at[block], i, there, lanes)
            reach, lanes = (block + 1) * rows, slice(block * wide, (block + 1) * wide)
            acc[i, lanes, :] = dot(score_grads[i, :reach, lanes], keys[i, :reach, :], TN)

    @pl.when(lax.axis_index("ctx") >= 2)
    def _():
        for i in range(half_groups):
            acc[i] += dot(far_grads[i], far_keys[i], TN)

    for i in range(half_groups):
        for block in range(2):
            for h in range(ratio):
                at = (i * ratio + h) * DH
                low = block * wide + h * rows
                out_ref[block, :rows, at : at + DH] = (acc[i, low : low + rows] * SCALE).astype(BF16)
    part_mine[...] = parts[core_of()]
    for block in range(2):
        out_ref[block, :rows, half:] = parts[block].astype(BF16)
    summed = deltas[0]
    for i in range(1, half_groups):
        summed = summed + deltas[i]
    for block in range(2):
        own = split_rows(summed[:, block * wide : (block + 1) * wide], 16)
        own = joined_row(dot(own, chosen((wide, rows), ratio, 0), NN))
        out_ref[block, rows:, :rows] = split_rows(own, EXTRA)


def turn_back(values, out_key, out_value, cosine, sine, starts):
    for i, there in enumerate(starts):
        turned = rotate(values[:, 2 * i * DH : (2 * i + 1) * DH], cosine, sine)
        out_key[:, there] = turned.astype(BF16)
        out_value[:, there] = values[:, (2 * i + 1) * DH : (2 * i + 2) * DH].astype(BF16)


def finish_queries_kernel(back, pos_ref, cos_ref, sin_ref, *refs, limit):
    got, (query_grad, gate_grad, key_part, value_part) = refs[:-4], refs[-4:]
    rows = cos_ref.shape[0]
    half = query_grad.shape[1] // 2
    cosine, sine = cos_ref[...], -sin_ref[...]
    for side in range(2):
        for i in range(half // DH):
            there = slice(side * half + i * DH, side * half + (i + 1) * DH)
            turned = rotate(back[side, :rows, i * DH : (i + 1) * DH].astype(F32), cosine, sine)
            query_grad[:, there] = turned.astype(BF16)
    gate = joined_row(back[0, rows:, :rows]) + joined_row(back[1, rows:, :rows])
    gate_grad[...] = jnp.where(pos_ref[...] < limit, gate, 0.0)
    other = back[1 - core_of(), :rows, half:].astype(F32)
    for ref in got:
        other = other + ref[...].astype(F32)
    starts = [slice(i * DH, (i + 1) * DH) for i in range(key_part.shape[1] // DH)]
    turn_back(other, key_part, value_part, cosine, sine, starts)


def finish_keys_kernel(part_mine, key_part, value_part, cos_ref, sin_ref, *refs):
    got, (key_grad, value_grad) = refs[:-2], refs[-2:]
    half = key_part.shape[1]
    core = core_of()
    total = part_mine[...]
    for ref in got:
        total = total + ref[...].astype(F32)
    starts = [pl.ds(pl.multiple_of(core * half + i * DH, DH), DH) for i in range(half // DH)]
    turn_back(total, key_grad, value_grad, cos_ref[...], -sin_ref[...], starts)
    there = pl.ds(pl.multiple_of((1 - core) * half, DH), half)
    key_grad[:, there] = key_part[...]
    value_grad[:, there] = value_part[...]


def per_device(query_rows, key_rows, value_rows, cotangent, router_gate, positions):
    rows, heads_width = query_rows.shape[1:]
    group_width = key_rows.shape[2]
    groups = group_width // DH
    ratio = heads_width // group_width
    half_groups, half_width = groups // 2, heads_width // 2
    parts = lax.axis_size("ctx")
    chips = parts // 2
    limit = parts * LOCAL
    wide = ratio * rows
    params = pltpu.CompilerParams(vmem_limit_bytes=(16 + 4 * chips) * 1024 * 1024)

    def call(kernel, name, outs, *args, scratch=(), flops=10**6, in_hbm=False):
        if in_hbm:
            args = [pltpu.with_memory_space_constraint(arg, pltpu.HBM) for arg in args]
        spec = pl.BlockSpec(memory_space=pltpu.HBM if in_hbm else pltpu.VMEM)
        return pl.pallas_call(
            kernel,
            out_shape=[jax.ShapeDtypeStruct(*out) for out in outs],
            in_specs=[spec] * len(args),
            scratch_shapes=list(scratch),
            compiler_params=params,
            cost_estimate=pl.CostEstimate(flops=flops, bytes_accessed=1000, transcendentals=0),
            name=name,
        )(*args)

    index = np.arange(DH) % (DH // 2)
    freq = jnp.asarray((THETA ** (-2.0 * index / DH)).astype(np.float32))[None]
    packet = ((rows, group_width), BF16)
    table = ((rows, DH), F32)
    kv_mine, kv_theirs, kv_both, cosine, sine, count = call(
        functools.partial(pack_keys_kernel, limit=limit),
        "pack_keys",
        [packet, packet, ((2, rows, group_width), BF16), table, table, ((EXTRA, 256), BF16)],
        key_rows[0],
        value_rows[0],
        positions,
        freq,
        in_hbm=True,
        flops=5 * 10**9,
        scratch=[
            pltpu.VMEM((rows, group_width), BF16),
            pltpu.VMEM((rows, group_width), BF16),
            pltpu.VMEM((1, rows), jnp.int32),
            pltpu.VMEM((1, DH), F32),
            pltpu.SemaphoreType.DMA((4,)),
        ],
    )

    hop = [[(2 * x + k, 2 * (x + s) + k) for x in range(chips - s) for k in range(2)] for s in range(chips)]
    cross = [[(a, b + 1 - 2 * (b % 2)) for a, b in pairs] for pairs in hop]
    back_hop = [[(b, a) for a, b in pairs] for pairs in hop]
    back_cross = [[(b, a) for a, b in pairs] for pairs in cross]

    far_own = [lax.ppermute(kv_mine, "ctx", hop[s]) for s in range(1, chips)]
    far_sib = [lax.ppermute(kv_theirs, "ctx", cross[s]) for s in range(1, chips)]

    pairs = [[2 * x, 2 * x + 1] for x in range(chips)]
    swap = lambda both: lax.all_to_all(both, "ctx", 0, 0, axis_index_groups=pairs)
    (packed,) = call(
        functools.partial(pack_queries_kernel, limit=limit),
        "pack_queries",
        [((2, rows + EXTRA, heads_width + group_width), BF16)],
        query_rows[0],
        cotangent[0],
        router_gate,
        positions,
        cosine,
        sine,
        count,
        kv_both,
    )
    packets = swap(packed)

    row = ((half_groups, 1, 2 * wide), F32)
    table = ((half_groups, 2 * rows, 2 * wide), F32)
    kv_table = ((half_groups, 2 * rows, DH), BF16)
    q_table = ((half_groups, 2 * wide, DH), BF16)
    keys, values, query, cot, gate_row, raws, grads, tops, sums, crosses = call(
        functools.partial(local_kernel, ratio=ratio),
        "local_scores",
        [kv_table, kv_table, q_table, q_table, ((1, 2 * wide), F32), table, table, row, row, row],
        packets,
        flops=3 * 10**6,
    )

    blocks = 2 * (chips - 1)
    table = ((half_groups, rows, 2 * wide), F32)
    low_table = ((half_groups, rows, 2 * wide), BF16)
    late = (half_groups, (blocks - 1) * rows, 2 * wide)
    late_table = (late, F32 if chips == 2 else BF16)
    late_rows = pltpu.VMEM((half_groups, (blocks - 1) * rows, DH), BF16)
    far_table = ((half_groups, blocks * rows, 2 * wide), BF16)
    early_raws, early_grads, early_tops, sums, crosses = call(
        early_kernel, "early_scores", [table, table, row, row, row], query, cot, tops, sums, crosses, far_sib[0]
    )
    far_keys, _, early_low, late_raws, late_grads, factors, late_factors, deltas, early_part = call(
        functools.partial(far_kernel, blocks=blocks),
        "far_scores",
        [((half_groups, blocks * rows, DH), BF16), low_table, low_table, late_table, late_table, row, row, row, packet],
        query,
        cot,
        gate_row,
        tops,
        early_raws,
        early_grads,
        early_tops,
        sums,
        crosses,
        *far_sib,
        *far_own,
        scratch=[late_rows, late_rows],
    )
    sib_got = [lax.ppermute(early_part, "ctx", back_cross[1])]
    far_grads, *parts = call(
        far_rest_kernel,
        "far_rest",
        [far_table] + [packet] * (blocks - 1),
        late_raws,
        late_grads,
        late_factors,
        deltas,
        early_low,
        query,
        cot,
        scratch=[pltpu.VMEM(*far_table)],
    )
    sib_got += [lax.ppermute(parts[s - 2], "ctx", back_cross[s]) for s in range(2, chips)]
    own_got = [lax.ppermute(parts[chips + s - 3], "ctx", back_hop[s]) for s in range(1, chips)]

    part_mine, packed = call(
        functools.partial(near_kernel, ratio=ratio),
        "near_grads",
        [
            ((rows, group_width), F32),
            ((2, rows + EXTRA, half_width + group_width), BF16),
        ],
        raws,
        grads,
        factors,
        deltas,
        keys,
        query,
        cot,
        far_keys,
        far_grads,
        flops=4 * 10**6,
        scratch=[
            pltpu.VMEM((half_groups, 2 * rows, 2 * wide), BF16),
            pltpu.VMEM((half_groups, 2 * rows, 2 * wide), BF16),
            pltpu.VMEM((2, rows, group_width), F32),
            pltpu.VMEM((half_groups, 2 * wide, DH), F32),
        ],
    )
    back = swap(packed)
    side = ((rows, group_width // 2), BF16)
    query_grad, gate_grad, key_part, value_part = call(
        functools.partial(finish_queries_kernel, limit=limit),
        "finish_queries",
        [((rows, heads_width), BF16), ((1, rows), F32), side, side],
        back,
        positions,
        cosine,
        sine,
        *sib_got,
        flops=3 * 10**8,
    )
    key_grad, value_grad = call(
        finish_keys_kernel,
        "finish_keys",
        [((rows, group_width), BF16)] * 2,
        part_mine,
        key_part,
        value_part,
        cosine,
        sine,
        *own_got,
    )
    return (query_grad[None], key_grad[None], value_grad[None], gate_grad)


def solution(mesh):
    wide = P(("group", "dp"), "ctx", None)
    narrow = P(("group", "dp"), "ctx")
    return jax.shard_map(
        per_device,
        mesh=mesh,
        in_specs=(wide, wide, wide, wide, narrow, narrow),
        out_specs=(wide, wide, wide, narrow),
        check_vma=False,
    )
```

```python
import functools
import math

import jax
import jax.numpy as jnp
import numpy as np
from jax import lax
from jax.experimental import pallas as pl
from jax.experimental.pallas import tpu as pltpu
from jax.sharding import PartitionSpec as P

DH = 128
LOCAL = 1024
THETA = 500000.0
EXTRA = 16
HIDDEN = -1e30
UNUSED = 2.0**14
SCALE = DH**-0.5
LOG2E = math.log2(math.e)
LN2 = math.log(2.0)

NT = (((1,), (1,)), ((), ()))
NN = (((1,), (0,)), ((), ()))
TN = (((0,), (0,)), ((), ()))
F32 = jnp.float32
BF16 = jnp.bfloat16


def few_bits(value, bits):
    unit = 2.0 ** (math.floor(math.log2(value)) + 1 - bits)
    return math.floor(value / unit) * unit


QUARTER_1 = few_bits(math.pi / 2, 10)
QUARTER_2 = few_bits(math.pi / 2 - QUARTER_1, 10)
QUARTER_3 = math.pi / 2 - QUARTER_1 - QUARTER_2


def dot(a, b, dims):
    return lax.dot_general(a, b, dims, preferred_element_type=F32)


def core_of():
    return lax.rem(lax.axis_index("ctx"), 2)


def rotate(values, cosine, sine):
    return values * cosine + pltpu.roll(values, DH // 2, 1) * sine


def sine_cosine(angle):
    turns = jnp.floor(angle * (2.0 / math.pi) + 0.5)
    rest = ((angle - turns * QUARTER_1) - turns * QUARTER_2) - turns * QUARTER_3
    square = rest * rest
    sine = ((-1.9515295891e-4 * square + 8.3321608736e-3) * square - 1.6666654611e-1) * square * rest + rest
    cosine = (2.443315711809948e-5 * square - 1.388731625493765e-3) * square + 4.166664568298827e-2
    cosine = cosine * square * square - 0.5 * square + 1.0
    quarter = turns.astype(jnp.int32)
    odd = (quarter & 1) == 1
    first, second = jnp.where(odd, cosine, sine), jnp.where(odd, sine, cosine)
    return (
        jnp.where((quarter & 2) == 2, -first, first),
        jnp.where(((quarter + 1) & 2) == 2, -second, second),
    )


def split_rows(row, height):
    high = row.astype(BF16).astype(F32)
    middle = (row - high).astype(BF16).astype(F32)
    low = row - high - middle
    line = lax.broadcasted_iota(jnp.int32, (height, row.shape[1]), 0)
    rows = jnp.where(line == 0, high, jnp.where(line == 1, middle, jnp.where(line == 2, low, 0.0)))
    return rows.astype(BF16)


def joined_row(rows):
    return jnp.sum(rows.astype(F32), axis=0, keepdims=True)


def pack_keys_kernel(
    key_in, value_in, pos_in, freq_in, mine, theirs, packed, cos_ref, sin_ref, count_ref, key, value, pos, freq, sems,
    *, limit
):
    loads = [(pos_in, pos), (freq_in, freq), (key_in, key), (value_in, value)]
    loads = [pltpu.make_async_copy(source, target, sems.at[i]) for i, (source, target) in enumerate(loads)]
    for copy in loads:
        copy.start()
    rows, width = key.shape
    side_width = width // 2
    core = core_of()
    down = lax.broadcasted_iota(jnp.int32, (rows, rows), 0)
    along = lax.broadcasted_iota(jnp.int32, (rows, rows), 1)
    lane = lax.broadcasted_iota(jnp.int32, (rows, DH), 1)
    loads[0].wait()
    loads[1].wait()
    places = pos[...]
    count = jnp.sum(jnp.where(places < limit, 1.0, 0.0), axis=1, keepdims=True)
    count_ref[...] = jnp.broadcast_to(count, count_ref.shape).astype(BF16)
    column = jnp.sum(jnp.where(down == along, places.astype(F32), 0.0), axis=1, keepdims=True)
    sine, cosine = sine_cosine(column * freq[...])
    sine = jnp.where(lane < DH // 2, -sine, sine)
    cos_ref[...] = cosine
    sin_ref[...] = sine
    used = jnp.broadcast_to(column, (rows, DH)) < limit
    loads[2].wait()
    loads[3].wait()
    for out_ref, side in ((mine, core), (theirs, 1 - core)):
        for i in range(side_width // DH):
            there = pl.ds(pl.multiple_of(side * side_width + i * DH, DH), DH)
            turned = rotate(key[:, there].astype(F32), cosine, sine)
            out_ref[:, 2 * i * DH : (2 * i + 1) * DH] = jnp.where(used, turned, UNUSED).astype(BF16)
            out_ref[:, (2 * i + 1) * DH : (2 * i + 2) * DH] = value[:, there]
            packed[side, :, 2 * i * DH : (2 * i + 1) * DH] = turned.astype(BF16)
            packed[side, :, (2 * i + 1) * DH : (2 * i + 2) * DH] = value[:, there]


def pack_queries_kernel(query, cot, gate, pos, cos_ref, sin_ref, count, kv, packed, *, limit):
    rows = query.shape[0]
    half = query.shape[1] // 2
    gates = split_rows(jnp.where(pos[...] < limit, gate[...], 0.0), EXTRA)
    cosine, sine = cos_ref[...] * (SCALE * LOG2E), sin_ref[...] * (SCALE * LOG2E)
    for side in range(2):
        for i in range(half // DH):
            there = slice(side * half + i * DH, side * half + (i + 1) * DH)
            turned = rotate(query[:, there].astype(F32), cosine, sine)
            packed[side, :rows, i * DH : (i + 1) * DH] = turned.astype(BF16)
        packed[side, :rows, half : 2 * half] = cot[:, side * half : (side + 1) * half]
        packed[side, :rows, 2 * half :] = kv[side]
        packed[side, rows:, :rows] = gates
        packed[side, rows:, 2 * half : 2 * half + 256] = count[...]


def chosen(shape, ratio, dim):
    down = lax.broadcasted_iota(jnp.int32, shape, 0)
    along = lax.broadcasted_iota(jnp.int32, shape, 1)
    rows = shape[1 - dim]
    long, short = (down, along) if dim == 0 else (along, down)
    for _ in range(1, ratio):
        long = jnp.where(long >= rows, long - rows, long)
    return jnp.where(long == short, 1.0, 0.0).astype(BF16)


def chunks(low, high):
    return [slice(at, min(at + 256, high)) for at in range(low, high, 256)]


def local_kernel(packets, keys, query, cot, gate, raws, grads, tops, sums, crosses, values, *, ratio):
    rows = packets.shape[1] - EXTRA
    half_groups = keys.shape[0]
    wide = ratio * rows
    half = half_groups * ratio * DH
    for side in range(2):
        there = slice(side * rows, (side + 1) * rows)
        for i in range(half_groups):
            at = 2 * half + 2 * i * DH
            keys[i, there, :] = packets[side, :rows, at : at + DH]
            values[i, there, :] = packets[side, :rows, at + DH : at + 2 * DH]
            for h in range(ratio):
                to = slice(side * wide + h * rows, side * wide + (h + 1) * rows)
                at = (i * ratio + h) * DH
                query[i, to, :] = packets[side, :rows, at : at + DH]
                cot[i, to, :] = packets[side, :rows, half + at : half + at + DH]
        gates = dot(packets[side, rows:, :rows], chosen((rows, wide), ratio, 1), NN)
        gate[:, side * wide : (side + 1) * wide] = joined_row(gates)
    count = packets[0, rows:, 2 * half : 2 * half + 256].astype(F32)[:1]
    for i in range(half_groups):
        for block in range(2):
            reach = (block + 1) * rows
            for here in chunks(block * wide, (block + 1) * wide):
                width = here.stop - here.start
                scores = dot(keys[i, :reach, :], query[i, here, :], NT)
                slot = lax.broadcasted_iota(jnp.int32, (rows, width), 0)
                lane = lax.broadcasted_iota(jnp.int32, (rows, width), 1) + (here.start - block * wide)
                for h in range(1, ratio):
                    lane = jnp.where(lane >= rows, lane - rows, lane)
                shown = jnp.where(slot <= lane, scores[block * rows :], HIDDEN)
                if block:
                    before = jnp.where(slot.astype(F32) < count[:, :width], scores[:rows], HIDDEN)
                    shown = jnp.concatenate([before, shown], axis=0)
                top = jnp.max(shown, axis=0, keepdims=True)
                raw = jnp.exp2(shown - top)
                prob_grad = dot(values[i, :reach, :], cot[i, here, :], NT)
                raws[i, :reach, here] = raw
                grads[i, :reach, here] = prob_grad
                tops[i, :, here] = top
                sums[i, :, here] = jnp.sum(raw, axis=0, keepdims=True)
                crosses[i, :, here] = jnp.sum(raw * prob_grad, axis=0, keepdims=True)


def part_of(weights, score_grads, query, cot, out_ref, i, there, lanes):
    key_part = dot(score_grads[i, there, lanes], query[i, lanes, :], NN) * LN2
    value_part = dot(weights[i, there, lanes], cot[i, lanes, :], NN)
    out_ref[:, 2 * i * DH : (2 * i + 1) * DH] = key_part.astype(out_ref.dtype)
    out_ref[:, (2 * i + 1) * DH : (2 * i + 2) * DH] = value_part.astype(out_ref.dtype)


def used_slots(packet, here):
    chip = lax.div(lax.axis_index("ctx"), 2)
    key = packet[:, :DH].astype(F32)[:, :1]
    return jnp.broadcast_to(key, (packet.shape[0], 256)) < jnp.where(chip >= here, UNUSED / 2, -UNUSED)


def early_kernel(query, cot, tops, sums, crosses, packet, raws, grads, new_tops, new_sums, new_crosses):
    half_groups, lanes = query.shape[:2]
    alone = lax.axis_index("ctx") < 2

    @pl.when(alone)
    def _():
        new_tops[...] = tops[...]
        new_sums[...] = sums[...]
        new_crosses[...] = crosses[...]

    @pl.when(jnp.logical_not(alone))
    def _():
        used = used_slots(packet, 1)
        for i in range(half_groups):
            key = packet[:, 2 * i * DH : (2 * i + 1) * DH]
            value = packet[:, (2 * i + 1) * DH : (2 * i + 2) * DH]
            for here in chunks(0, lanes):
                width = here.stop - here.start
                shown = jnp.where(used[:, :width], dot(key, query[i, here, :], NT), HIDDEN)
                old_top = tops[i, :, here]
                top = jnp.maximum(old_top, jnp.max(shown, axis=0, keepdims=True))
                raw = jnp.exp2(shown - top)
                shrink = jnp.exp2(old_top - top)
                prob_grad = dot(value, cot[i, here, :], NT)
                raws[i, :, here] = raw
                grads[i, :, here] = prob_grad
                new_tops[i, :, here] = top
                new_sums[i, :, here] = sums[i, :, here] * shrink + jnp.sum(raw, axis=0, keepdims=True)
                cross = jnp.sum(raw * prob_grad, axis=0, keepdims=True)
                new_crosses[i, :, here] = crosses[i, :, here] * shrink + cross


def far_kernel(query, cot, gate, first_tops, raws, grads, tops, sums, crosses, early, *refs, blocks):
    packets = refs[: blocks - 1]
    far_keys, score_grads, late_raws, late_grads, factors, late_factors, deltas, part = refs[blocks - 1 : -3]
    late_keys, late_values, weights = refs[-3:]
    rows = early.shape[0]
    half_groups, lanes = query.shape[:2]
    alone = lax.axis_index("ctx") < 2

    @pl.when(alone)
    def _():
        for i in range(half_groups):
            inverse = 1.0 / sums[i]
            factors[i] = inverse * gate[...]
            deltas[i] = crosses[i] * inverse

    @pl.when(jnp.logical_not(alone))
    def _():
        for i in range(half_groups):
            far_keys[i, :rows, :] = early[:, 2 * i * DH : (2 * i + 1) * DH]
            for j, packet in enumerate(packets):
                there = slice(j * rows, (j + 1) * rows)
                far_keys[i, (j + 1) * rows : (j + 2) * rows, :] = packet[:, 2 * i * DH : (2 * i + 1) * DH]
                late_keys[i, there, :] = packet[:, 2 * i * DH : (2 * i + 1) * DH]
                late_values[i, there, :] = packet[:, (2 * i + 1) * DH : (2 * i + 2) * DH]
        hops = blocks // 2
        used = [used_slots(packet, (j + 1) % hops + 1) for j, packet in enumerate(packets)]
        for i in range(half_groups):
            for here in chunks(0, lanes):
                width = here.stop - here.start
                scores = dot(late_keys[i], query[i, here, :], NT)
                shown = [
                    jnp.where(used[j][:, :width], scores[j * rows : (j + 1) * rows], HIDDEN)
                    for j in range(blocks - 1)
                ]
                shown = jnp.concatenate(shown, axis=0)
                old_top = tops[i, :, here]
                top = jnp.maximum(old_top, jnp.max(shown, axis=0, keepdims=True))
                raw = jnp.exp2(shown - top)
                shrink = jnp.exp2(old_top - top)
                inverse = 1.0 / (sums[i, :, here] * shrink + jnp.sum(raw, axis=0, keepdims=True))
                prob_grad = dot(late_values[i], cot[i, here, :], NT)
                late_raws[i, :, here] = raw.astype(late_raws.dtype)
                late_grads[i, :, here] = prob_grad.astype(late_grads.dtype)
                cross = crosses[i, :, here] * shrink + jnp.sum(raw * prob_grad, axis=0, keepdims=True)
                delta = cross * inverse
                factor = inverse * gate[:, here]
                factors[i, :, here] = factor * jnp.exp2(first_tops[i, :, here] - top)
                late_factors[i, :, here] = factor
                deltas[i, :, here] = delta
                gated = raws[i, :, here] * (factor * shrink)
                weights[i, :, here] = gated.astype(BF16)
                score_grads[i, :, here] = (gated * (grads[i, :, here] - delta)).astype(BF16)
            part_of(weights, score_grads, query, cot, part, i, slice(0, rows), slice(0, lanes))


def far_rest_kernel(raws, grads, factors, deltas, early_grads, query, cot, score_grads, *refs):
    parts, weights = refs[:-1], refs[-1]
    rows = early_grads.shape[1]
    half_groups, lanes = query.shape[:2]

    @pl.when(lax.axis_index("ctx") >= 2)
    def _():
        for i in range(half_groups):
            score_grads[i, :rows, :] = early_grads[i]
            for here in chunks(0, lanes):
                gated = raws[i, :, here].astype(F32) * factors[i, :, here]
                weights[i, rows:, here] = gated.astype(BF16)
                rest = grads[i, :, here].astype(F32) - deltas[i, :, here]
                score_grads[i, rows:, here] = (gated * rest).astype(BF16)
            for j, out_ref in enumerate(parts):
                there = slice((j + 1) * rows, (j + 2) * rows)
                part_of(weights, score_grads, query, cot, out_ref, i, there, slice(0, lanes))


def near_kernel(
    raws, grads, factors, deltas, keys, query, cot, far_keys, far_grads,
    part_mine, out_ref, weights, score_grads, parts, acc,
    *, ratio
):
    rows = part_mine.shape[0]
    half_groups = keys.shape[0]
    wide = ratio * rows
    half = half_groups * ratio * DH
    for i in range(half_groups):
        for block in range(2):
            reach = (block + 1) * rows
            for here in chunks(block * wide, (block + 1) * wide):
                gated = raws[i, :reach, here] * factors[i, :, here]
                weights[i, :reach, here] = gated.astype(BF16)
                score_grads[i, :reach, here] = (gated * (grads[i, :reach, here] - deltas[i, :, here])).astype(BF16)
        for block in range(2):
            there, lanes = slice(block * rows, (block + 1) * rows), slice(block * wide, 2 * wide)
            part_of(weights, score_grads, query, cot, parts.at[block], i, there, lanes)
            reach, lanes = (block + 1) * rows, slice(block * wide, (block + 1) * wide)
            acc[i, lanes, :] = dot(score_grads[i, :reach, lanes], keys[i, :reach, :], TN)

    @pl.when(lax.axis_index("ctx") >= 2)
    def _():
        for i in range(half_groups):
            acc[i] += dot(far_grads[i], far_keys[i], TN)

    for i in range(half_groups):
        for block in range(2):
            for h in range(ratio):
                at = (i * ratio + h) * DH
                low = block * wide + h * rows
                out_ref[block, :rows, at : at + DH] = (acc[i, low : low + rows] * SCALE).astype(BF16)
    part_mine[...] = parts[core_of()]
    for block in range(2):
        out_ref[block, :rows, half:] = parts[block].astype(BF16)
    summed = deltas[0]
    for i in range(1, half_groups):
        summed = summed + deltas[i]
    for block in range(2):
        own = split_rows(summed[:, block * wide : (block + 1) * wide], 16)
        own = joined_row(dot(own, chosen((wide, rows), ratio, 0), NN))
        out_ref[block, rows:, :rows] = split_rows(own, EXTRA)


def turn_back(values, out_key, out_value, cosine, sine, starts):
    for i, there in enumerate(starts):
        turned = rotate(values[:, 2 * i * DH : (2 * i + 1) * DH], cosine, sine)
        out_key[:, there] = turned.astype(BF16)
        out_value[:, there] = values[:, (2 * i + 1) * DH : (2 * i + 2) * DH].astype(BF16)


def finish_queries_kernel(back, pos_ref, cos_ref, sin_ref, *refs, limit):
    got, (query_grad, gate_grad, key_part, value_part) = refs[:-4], refs[-4:]
    rows = cos_ref.shape[0]
    half = query_grad.shape[1] // 2
    cosine, sine = cos_ref[...], -sin_ref[...]
    for side in range(2):
        for i in range(half // DH):
            there = slice(side * half + i * DH, side * half + (i + 1) * DH)
            turned = rotate(back[side, :rows, i * DH : (i + 1) * DH].astype(F32), cosine, sine)
            query_grad[:, there] = turned.astype(BF16)
    gate = joined_row(back[0, rows:, :rows]) + joined_row(back[1, rows:, :rows])
    gate_grad[...] = jnp.where(pos_ref[...] < limit, gate, 0.0)
    other = back[1 - core_of(), :rows, half:].astype(F32)
    for ref in got:
        other = other + ref[...].astype(F32)
    starts = [slice(i * DH, (i + 1) * DH) for i in range(key_part.shape[1] // DH)]
    turn_back(other, key_part, value_part, cosine, sine, starts)


def finish_keys_kernel(part_mine, key_part, value_part, cos_ref, sin_ref, *refs):
    got, (key_grad, value_grad) = refs[:-2], refs[-2:]
    half = key_part.shape[1]
    core = core_of()
    total = part_mine[...]
    for ref in got:
        total = total + ref[...].astype(F32)
    starts = [pl.ds(pl.multiple_of(core * half + i * DH, DH), DH) for i in range(half // DH)]
    turn_back(total, key_grad, value_grad, cos_ref[...], -sin_ref[...], starts)
    there = pl.ds(pl.multiple_of((1 - core) * half, DH), half)
    key_grad[:, there] = key_part[...]
    value_grad[:, there] = value_part[...]


def per_device(query_rows, key_rows, value_rows, cotangent, router_gate, positions):
    rows, heads_width = query_rows.shape[1:]
    group_width = key_rows.shape[2]
    groups = group_width // DH
    ratio = heads_width // group_width
    half_groups, half_width = groups // 2, heads_width // 2
    parts = lax.axis_size("ctx")
    chips = parts // 2
    limit = parts * LOCAL
    wide = ratio * rows
    params = pltpu.CompilerParams(vmem_limit_bytes=(16 + 4 * chips) * 1024 * 1024)

    def call(kernel, name, outs, *args, scratch=(), flops=10**6, in_hbm=False):
        if in_hbm:
            args = [pltpu.with_memory_space_constraint(arg, pltpu.HBM) for arg in args]
        spec = pl.BlockSpec(memory_space=pltpu.HBM if in_hbm else pltpu.VMEM)
        return pl.pallas_call(
            kernel,
            out_shape=[jax.ShapeDtypeStruct(*out) for out in outs],
            in_specs=[spec] * len(args),
            scratch_shapes=list(scratch),
            compiler_params=params,
            cost_estimate=pl.CostEstimate(flops=flops, bytes_accessed=1000, transcendentals=0),
            name=name,
        )(*args)

    index = np.arange(DH) % (DH // 2)
    freq = jnp.asarray((THETA ** (-2.0 * index / DH)).astype(np.float32))[None]
    packet = ((rows, group_width), BF16)
    table = ((rows, DH), F32)
    kv_mine, kv_theirs, kv_both, cosine, sine, count = call(
        functools.partial(pack_keys_kernel, limit=limit),
        "pack_keys",
        [packet, packet, ((2, rows, group_width), BF16), table, table, ((EXTRA, 256), BF16)],
        key_rows[0],
        value_rows[0],
        positions,
        freq,
        in_hbm=True,
        flops=5 * 10**9,
        scratch=[
            pltpu.VMEM((rows, group_width), BF16),
            pltpu.VMEM((rows, group_width), BF16),
            pltpu.VMEM((1, rows), jnp.int32),
            pltpu.VMEM((1, DH), F32),
            pltpu.SemaphoreType.DMA((4,)),
        ],
    )

    hop = [[(2 * x + k, 2 * (x + s) + k) for x in range(chips - s) for k in range(2)] for s in range(chips)]
    cross = [[(a, b + 1 - 2 * (b % 2)) for a, b in pairs] for pairs in hop]
    back_hop = [[(b, a) for a, b in pairs] for pairs in hop]
    back_cross = [[(b, a) for a, b in pairs] for pairs in cross]

    far_own = [lax.ppermute(kv_mine, "ctx", hop[s]) for s in range(1, chips)]
    far_sib = [lax.ppermute(kv_theirs, "ctx", cross[s]) for s in range(1, chips)]

    pairs = [[2 * x, 2 * x + 1] for x in range(chips)]
    swap = lambda both: lax.all_to_all(both, "ctx", 0, 0, axis_index_groups=pairs)
    (packed,) = call(
        functools.partial(pack_queries_kernel, limit=limit),
        "pack_queries",
        [((2, rows + EXTRA, heads_width + group_width), BF16)],
        query_rows[0],
        cotangent[0],
        router_gate,
        positions,
        cosine,
        sine,
        count,
        kv_both,
    )
    packets = swap(packed)

    row = ((half_groups, 1, 2 * wide), F32)
    table = ((half_groups, 2 * rows, 2 * wide), F32)
    kv_table = ((half_groups, 2 * rows, DH), BF16)
    q_table = ((half_groups, 2 * wide, DH), BF16)
    keys, query, cot, gate_row, raws, grads, tops, sums, crosses = call(
        functools.partial(local_kernel, ratio=ratio),
        "local_scores",
        [kv_table, q_table, q_table, ((1, 2 * wide), F32), table, table, row, row, row],
        packets,
        scratch=[pltpu.VMEM(*kv_table)],
        flops=3 * 10**6,
    )

    blocks = 2 * (chips - 1)
    table = ((half_groups, rows, 2 * wide), F32)
    low_table = ((half_groups, rows, 2 * wide), BF16)
    late = (half_groups, (blocks - 1) * rows, 2 * wide)
    late_table = (late, F32 if chips == 2 else BF16)
    late_rows = pltpu.VMEM((half_groups, (blocks - 1) * rows, DH), BF16)
    far_table = ((half_groups, blocks * rows, 2 * wide), BF16)
    early_raws, early_grads, early_tops, sums, crosses = call(
        early_kernel, "early_scores", [table, table, row, row, row], query, cot, tops, sums, crosses, far_sib[0]
    )
    far_keys, early_low, late_raws, late_grads, factors, late_factors, deltas, early_part = call(
        functools.partial(far_kernel, blocks=blocks),
        "far_scores",
        [((half_groups, blocks * rows, DH), BF16), low_table, late_table, late_table, row, row, row, packet],
        query,
        cot,
        gate_row,
        tops,
        early_raws,
        early_grads,
        early_tops,
        sums,
        crosses,
        *far_sib,
        *far_own,
        scratch=[late_rows, late_rows, pltpu.VMEM(*low_table)],
    )
    sib_got = [lax.ppermute(early_part, "ctx", back_cross[1])]
    far_grads, *parts = call(
        far_rest_kernel,
        "far_rest",
        [far_table] + [packet] * (blocks - 1),
        late_raws,
        late_grads,
        late_factors,
        deltas,
        early_low,
        query,
        cot,
        scratch=[pltpu.VMEM(*far_table)],
    )
    sib_got += [lax.ppermute(parts[s - 2], "ctx", back_cross[s]) for s in range(2, chips)]
    own_got = [lax.ppermute(parts[chips + s - 3], "ctx", back_hop[s]) for s in range(1, chips)]

    part_mine, packed = call(
        functools.partial(near_kernel, ratio=ratio),
        "near_grads",
        [
            ((rows, group_width), F32),
            ((2, rows + EXTRA, half_width + group_width), BF16),
        ],
        raws,
        grads,
        factors,
        deltas,
        keys,
        query,
        cot,
        far_keys,
        far_grads,
        flops=4 * 10**6,
        scratch=[
            pltpu.VMEM((half_groups, 2 * rows, 2 * wide), BF16),
            pltpu.VMEM((half_groups, 2 * rows, 2 * wide), BF16),
            pltpu.VMEM((2, rows, group_width), F32),
            pltpu.VMEM((half_groups, 2 * wide, DH), F32),
        ],
    )
    back = swap(packed)
    side = ((rows, group_width // 2), BF16)
    query_grad, gate_grad, key_part, value_part = call(
        functools.partial(finish_queries_kernel, limit=limit),
        "finish_queries",
        [((rows, heads_width), BF16), ((1, rows), F32), side, side],
        back,
        positions,
        cosine,
        sine,
        *sib_got,
        flops=3 * 10**8,
    )
    key_grad, value_grad = call(
        finish_keys_kernel,
        "finish_keys",
        [((rows, group_width), BF16)] * 2,
        part_mine,
        key_part,
        value_part,
        cosine,
        sine,
        *own_got,
    )
    return (query_grad[None], key_grad[None], value_grad[None], gate_grad)


def solution(mesh):
    wide = P(("group", "dp"), "ctx", None)
    narrow = P(("group", "dp"), "ctx")
    return jax.shard_map(
        per_device,
        mesh=mesh,
        in_specs=(wide, wide, wide, wide, narrow, narrow),
        out_specs=(wide, wide, wide, narrow),
        check_vma=False,
    )
```

```python
import functools
import math

import jax
import jax.numpy as jnp
import numpy as np
from jax import lax
from jax.experimental import pallas as pl
from jax.experimental.pallas import tpu as pltpu
from jax.sharding import PartitionSpec as P

DH = 128
LOCAL = 1024
THETA = 500000.0
EXTRA = 16
HIDDEN = -1e30
UNUSED = 2.0**14
SCALE = DH**-0.5
LOG2E = math.log2(math.e)
LN2 = math.log(2.0)

NT = (((1,), (1,)), ((), ()))
NN = (((1,), (0,)), ((), ()))
TN = (((0,), (0,)), ((), ()))
F32 = jnp.float32
BF16 = jnp.bfloat16


def few_bits(value, bits):
    unit = 2.0 ** (math.floor(math.log2(value)) + 1 - bits)
    return math.floor(value / unit) * unit


QUARTER_1 = few_bits(math.pi / 2, 10)
QUARTER_2 = few_bits(math.pi / 2 - QUARTER_1, 10)
QUARTER_3 = math.pi / 2 - QUARTER_1 - QUARTER_2


def dot(a, b, dims):
    return lax.dot_general(a, b, dims, preferred_element_type=F32)


def core_of():
    return lax.rem(lax.axis_index("ctx"), 2)


def rotate(values, cosine, sine):
    return values * cosine + pltpu.roll(values, DH // 2, 1) * sine


def sine_cosine(angle):
    turns = jnp.floor(angle * (2.0 / math.pi) + 0.5)
    rest = ((angle - turns * QUARTER_1) - turns * QUARTER_2) - turns * QUARTER_3
    square = rest * rest
    sine = ((-1.9515295891e-4 * square + 8.3321608736e-3) * square - 1.6666654611e-1) * square * rest + rest
    cosine = (2.443315711809948e-5 * square - 1.388731625493765e-3) * square + 4.166664568298827e-2
    cosine = cosine * square * square - 0.5 * square + 1.0
    quarter = turns.astype(jnp.int32)
    odd = (quarter & 1) == 1
    first, second = jnp.where(odd, cosine, sine), jnp.where(odd, sine, cosine)
    return (
        jnp.where((quarter & 2) == 2, -first, first),
        jnp.where(((quarter + 1) & 2) == 2, -second, second),
    )


def split_rows(row, height):
    high = row.astype(BF16).astype(F32)
    middle = (row - high).astype(BF16).astype(F32)
    low = row - high - middle
    line = lax.broadcasted_iota(jnp.int32, (height, row.shape[1]), 0)
    rows = jnp.where(line == 0, high, jnp.where(line == 1, middle, jnp.where(line == 2, low, 0.0)))
    return rows.astype(BF16)


def joined_row(rows):
    return jnp.sum(rows.astype(F32), axis=0, keepdims=True)


def pack_keys_kernel(
    key_in, value_in, pos_in, freq_in, key_mine, key_theirs, value_mine, value_theirs, cos_ref, sin_ref,
    key, value, pos, freq, sems, *, limit
):
    loads = [(pos_in, pos), (freq_in, freq), (key_in, key), (value_in, value)]
    loads = [pltpu.make_async_copy(source, target, sems.at[i]) for i, (source, target) in enumerate(loads)]
    for copy in loads:
        copy.start()
    rows, width = key.shape
    half = width // 2
    core = core_of()
    down = lax.broadcasted_iota(jnp.int32, (rows, rows), 0)
    along = lax.broadcasted_iota(jnp.int32, (rows, rows), 1)
    lane = lax.broadcasted_iota(jnp.int32, (rows, DH), 1)
    loads[0].wait()
    loads[1].wait()
    column = jnp.sum(jnp.where(down == along, pos[...].astype(F32), 0.0), axis=1, keepdims=True)
    sine, cosine = sine_cosine(column * freq[...])
    sine = jnp.where(lane < DH // 2, -sine, sine)
    cos_ref[...] = cosine
    sin_ref[...] = sine
    used = jnp.broadcast_to(column, (rows, DH)) < limit
    loads[2].wait()
    loads[3].wait()
    for key_out, value_out, side in ((key_mine, value_mine, core), (key_theirs, value_theirs, 1 - core)):
        for i in range(half // DH):
            there = pl.ds(pl.multiple_of(side * half + i * DH, DH), DH)
            turned = rotate(key[:, there].astype(F32), cosine, sine)
            key_out[:, i * DH : (i + 1) * DH] = jnp.where(used, turned, UNUSED).astype(BF16)
            value_out[:, i * DH : (i + 1) * DH] = value[:, there]


def pack_queries_kernel(query, cot, gate, pos, cos_ref, sin_ref, key, value, mine, theirs, gate_mine, *, limit):
    rows = query.shape[0]
    half, width = query.shape[1] // 2, key.shape[1]
    core = core_of()
    used_gate = jnp.where(pos[...] < limit, gate[...], 0.0)
    gate_mine[...] = used_gate
    theirs[rows:, :rows] = split_rows(used_gate, EXTRA)
    theirs[:rows, 2 * half : 2 * half + width] = key[...]
    theirs[:rows, 2 * half + width :] = value[...]
    cosine, sine = cos_ref[...] * (SCALE * LOG2E), sin_ref[...] * (SCALE * LOG2E)
    for out_ref, side in ((mine, core), (theirs, 1 - core)):
        for i in range(half // DH):
            there = pl.ds(pl.multiple_of(side * half + i * DH, DH), DH)
            turned = rotate(query[:, there].astype(F32), cosine, sine)
            out_ref[:rows, i * DH : (i + 1) * DH] = turned.astype(BF16)
        out_ref[:rows, half : 2 * half] = cot[:, pl.ds(pl.multiple_of(side * half, DH), half)]


def chosen(shape, ratio, dim):
    down = lax.broadcasted_iota(jnp.int32, shape, 0)
    along = lax.broadcasted_iota(jnp.int32, shape, 1)
    rows = shape[1 - dim]
    long, short = (down, along) if dim == 0 else (along, down)
    for _ in range(1, ratio):
        long = jnp.where(long >= rows, long - rows, long)
    return jnp.where(long == short, 1.0, 0.0).astype(BF16)


def chunks(low, high):
    return [slice(at, min(at + 256, high)) for at in range(low, high, 256)]


def used_slots(key, here):
    chip = lax.div(lax.axis_index("ctx"), 2)
    first = key[:, :DH].astype(F32)[:, :1]
    return jnp.broadcast_to(first, (key.shape[0], 256)) < jnp.where(chip >= here, UNUSED / 2, -UNUSED)


def local_kernel(
    key_mine, value_mine, mine, gate_mine, sib, keys, query, cot, gate, raws, grads, tops, sums, crosses, values,
    *, ratio
):
    rows = key_mine.shape[0]
    half_groups = keys.shape[0]
    wide = ratio * rows
    half = half_groups * ratio * DH
    core = core_of()
    spread = chosen((rows, wide), ratio, 1)
    key_sib = sib.at[:rows, 2 * half : 2 * half + half_groups * DH]
    value_sib = sib.at[:rows, 2 * half + half_groups * DH :]
    for key, value, packet, side in ((key_mine, value_mine, mine, core), (key_sib, value_sib, sib, 1 - core)):
        there = pl.ds(pl.multiple_of(side * rows, 16), rows)
        for i in range(half_groups):
            keys[i, there, :] = key[:, i * DH : (i + 1) * DH]
            values[i, there, :] = value[:, i * DH : (i + 1) * DH]
            for h in range(ratio):
                to = pl.ds(pl.multiple_of(side * wide + h * rows, 16), rows)
                at = (i * ratio + h) * DH
                query[i, to, :] = packet[:rows, at : at + DH]
                cot[i, to, :] = packet[:rows, half + at : half + at + DH]
    own = joined_row(dot(split_rows(gate_mine[...], EXTRA), spread, NN))
    other = joined_row(dot(sib[rows:, :rows], spread, NN))
    gate[:, :wide] = jnp.where(core == 0, own, other)
    gate[:, wide:] = jnp.where(core == 0, other, own)
    used = used_slots(keys[0, :rows, :], 0)
    for i in range(half_groups):
        for block in range(2):
            reach = (block + 1) * rows
            for here in chunks(block * wide, (block + 1) * wide):
                width = here.stop - here.start
                scores = dot(keys[i, :reach, :], query[i, here, :], NT)
                slot = lax.broadcasted_iota(jnp.int32, (rows, width), 0)
                lane = lax.broadcasted_iota(jnp.int32, (rows, width), 1) + (here.start - block * wide)
                for h in range(1, ratio):
                    lane = jnp.where(lane >= rows, lane - rows, lane)
                shown = jnp.where(slot <= lane, scores[block * rows :], HIDDEN)
                if block:
                    before = jnp.where(used[:, :width], scores[:rows], HIDDEN)
                    shown = jnp.concatenate([before, shown], axis=0)
                top = jnp.max(shown, axis=0, keepdims=True)
                raw = jnp.exp2(shown - top)
                prob_grad = dot(values[i, :reach, :], cot[i, here, :], NT)
                raws[i, :reach, here] = raw
                grads[i, :reach, here] = prob_grad
                tops[i, :, here] = top
                sums[i, :, here] = jnp.sum(raw, axis=0, keepdims=True)
                crosses[i, :, here] = jnp.sum(raw * prob_grad, axis=0, keepdims=True)


def part_of(weights, score_grads, query, cot, out_ref, i, there, lanes):
    key_part = dot(score_grads[i, there, lanes], query[i, lanes, :], NN) * LN2
    value_part = dot(weights[i, there, lanes], cot[i, lanes, :], NN)
    out_ref[:, 2 * i * DH : (2 * i + 1) * DH] = key_part.astype(out_ref.dtype)
    out_ref[:, (2 * i + 1) * DH : (2 * i + 2) * DH] = value_part.astype(out_ref.dtype)


def far_keys_kernel(query, cot, gate, tops, sums, *refs, blocks):
    packets = refs[:blocks]
    far_keys, raws, factors, far_factors, shrinks, inverses = refs[blocks : blocks + 6]
    parts, weights = refs[blocks + 6 : -1], refs[-1]
    rows = packets[0].shape[0]
    half_groups, lanes = query.shape[:2]
    alone = lax.axis_index("ctx") < 2

    @pl.when(alone)
    def _():
        for i in range(half_groups):
            inverse = 1.0 / sums[i]
            factors[i] = inverse * gate[...]
            inverses[i] = inverse

    @pl.when(jnp.logical_not(alone))
    def _():
        for i in range(half_groups):
            for j, packet in enumerate(packets):
                far_keys[i, j * rows : (j + 1) * rows, :] = packet[:, i * DH : (i + 1) * DH]
        used = [used_slots(packet, j % (blocks // 2) + 1) for j, packet in enumerate(packets)]
        for i in range(half_groups):
            for here in chunks(0, lanes):
                width = here.stop - here.start
                scores = dot(far_keys[i], query[i, here, :], NT)
                shown = [
                    jnp.where(used[j][:, :width], scores[j * rows : (j + 1) * rows], HIDDEN) for j in range(blocks)
                ]
                shown = jnp.concatenate(shown, axis=0)
                old_top = tops[i, :, here]
                top = jnp.maximum(old_top, jnp.max(shown, axis=0, keepdims=True))
                raw = jnp.exp2(shown - top)
                shrink = jnp.exp2(old_top - top)
                inverse = 1.0 / (sums[i, :, here] * shrink + jnp.sum(raw, axis=0, keepdims=True))
                factor = inverse * gate[:, here]
                factors[i, :, here] = factor * shrink
                far_factors[i, :, here] = factor
                shrinks[i, :, here] = shrink
                inverses[i, :, here] = inverse
                raws[i, :, here] = raw.astype(raws.dtype)
                weights[i, :, here] = (raw * factor).astype(BF16)
            for j, out_ref in enumerate(parts):
                there = slice(j * rows, (j + 1) * rows)
                out_ref[:, i * DH : (i + 1) * DH] = dot(weights[i, there, :], cot[i], NN).astype(BF16)


def far_values_kernel(query, cot, raws, far_factors, shrinks, inverses, crosses, *refs, blocks):
    packets = refs[:blocks]
    score_grads, deltas = refs[blocks : blocks + 2]
    parts, far_values = refs[blocks + 2 : -1], refs[-1]
    rows = packets[0].shape[0]
    half_groups, lanes = query.shape[:2]
    alone = lax.axis_index("ctx") < 2

    @pl.when(alone)
    def _():
        for i in range(half_groups):
            deltas[i] = crosses[i] * inverses[i]

    @pl.when(jnp.logical_not(alone))
    def _():
        for i in range(half_groups):
            for j, packet in enumerate(packets):
                far_values[i, j * rows : (j + 1) * rows, :] = packet[:, i * DH : (i + 1) * DH]
        for i in range(half_groups):
            for here in chunks(0, lanes):
                raw = raws[i, :, here].astype(F32)
                prob_grad = dot(far_values[i], cot[i, here, :], NT)
                cross = jnp.sum(raw * prob_grad, axis=0, keepdims=True)
                delta = (crosses[i, :, here] * shrinks[i, :, here] + cross) * inverses[i, :, here]
                deltas[i, :, here] = delta
                score_grad = raw * far_factors[i, :, here] * (prob_grad - delta)
                score_grads[i, :, here] = score_grad.astype(BF16)
            for j, out_ref in enumerate(parts):
                there = slice(j * rows, (j + 1) * rows)
                part = dot(score_grads[i, there, :], query[i], NN) * LN2
                out_ref[:, i * DH : (i + 1) * DH] = part.astype(BF16)


def near_kernel(
    raws, grads, factors, deltas, keys, query, cot, far_keys, far_grads,
    part_mine, out_ref, weights, score_grads, parts, acc,
    *, ratio
):
    rows = part_mine.shape[0]
    half_groups = keys.shape[0]
    wide = ratio * rows
    half = half_groups * ratio * DH
    for i in range(half_groups):
        for block in range(2):
            reach = (block + 1) * rows
            for here in chunks(block * wide, (block + 1) * wide):
                gated = raws[i, :reach, here] * factors[i, :, here]
                weights[i, :reach, here] = gated.astype(BF16)
                score_grads[i, :reach, here] = (gated * (grads[i, :reach, here] - deltas[i, :, here])).astype(BF16)
        for block in range(2):
            there, lanes = slice(block * rows, (block + 1) * rows), slice(block * wide, 2 * wide)
            part_of(weights, score_grads, query, cot, parts.at[block], i, there, lanes)
            reach, lanes = (block + 1) * rows, slice(block * wide, (block + 1) * wide)
            acc[i, :, lanes] = dot(keys[i, :reach, :], score_grads[i, :reach, lanes], TN)

    @pl.when(lax.axis_index("ctx") >= 2)
    def _():
        for i in range(half_groups):
            acc[i] += dot(far_keys[i], far_grads[i], TN)

    for i in range(half_groups):
        total = jnp.transpose(acc[i] * SCALE).astype(BF16)
        for block in range(2):
            for h in range(ratio):
                at = (i * ratio + h) * DH
                low = block * wide + h * rows
                out_ref[block, :rows, at : at + DH] = total[low : low + rows]
    part_mine[...] = parts[core_of()]
    for block in range(2):
        out_ref[block, :rows, half:] = parts[block].astype(BF16)
    summed = deltas[0]
    for i in range(1, half_groups):
        summed = summed + deltas[i]
    for block in range(2):
        own = split_rows(summed[:, block * wide : (block + 1) * wide], 16)
        own = joined_row(dot(own, chosen((wide, rows), ratio, 0), NN))
        out_ref[block, rows:, :rows] = split_rows(own, EXTRA)


def sum_values_kernel(back, part_mine, *refs):
    got, (own, other) = refs[:-2], refs[-2:]
    rows, half = own.shape
    start = back.shape[2] - 2 * half
    core = core_of()
    for i in range(half // DH):
        here = slice(i * DH, (i + 1) * DH)
        there = (2 * i + 1) * DH
        mine = part_mine[:, there : there + DH]
        theirs = back[1 - core, :rows, start + there : start + there + DH].astype(F32)
        for s in range(len(got) // 2):
            theirs = theirs + got[2 * s][:, here].astype(F32)
            mine = mine + got[2 * s + 1][:, here].astype(F32)
        own[:, here] = mine.astype(BF16)
        other[:, here] = theirs.astype(BF16)


def finish_kernel(back, part_mine, pos_ref, cos_ref, sin_ref, value_own, value_other, *refs, limit):
    got, (query_grad, key_grad, value_grad, gate_grad) = refs[:-4], refs[-4:]
    rows, half = value_own.shape
    wide = query_grad.shape[1] // 2
    core = core_of()
    cosine, sine = cos_ref[...], -sin_ref[...]
    value_grad[:, pl.ds(pl.multiple_of(core * half, DH), half)] = value_own[...]
    value_grad[:, pl.ds(pl.multiple_of((1 - core) * half, DH), half)] = value_other[...]
    gate = joined_row(back[0, rows:, :rows]) + joined_row(back[1, rows:, :rows])
    gate_grad[...] = jnp.where(pos_ref[...] < limit, gate, 0.0)
    for i in range(half // DH):
        here = slice(i * DH, (i + 1) * DH)
        mine = part_mine[:, 2 * i * DH : (2 * i + 1) * DH]
        theirs = back[1 - core, :rows, wide + 2 * i * DH : wide + (2 * i + 1) * DH].astype(F32)
        for s in range(len(got) // 2):
            theirs = theirs + got[2 * s][:, here].astype(F32)
            mine = mine + got[2 * s + 1][:, here].astype(F32)
        for total, side in ((mine, core), (theirs, 1 - core)):
            there = pl.ds(pl.multiple_of(side * half + i * DH, DH), DH)
            key_grad[:, there] = rotate(total, cosine, sine).astype(BF16)
    for side in range(2):
        for i in range(wide // DH):
            turned = rotate(back[side, :rows, i * DH : (i + 1) * DH].astype(F32), cosine, sine)
            query_grad[:, side * wide + i * DH : side * wide + (i + 1) * DH] = turned.astype(BF16)


def per_device(query_rows, key_rows, value_rows, cotangent, router_gate, positions):
    rows, heads_width = query_rows.shape[1:]
    group_width = key_rows.shape[2]
    groups = group_width // DH
    ratio = heads_width // group_width
    half_groups, half_width = groups // 2, heads_width // 2
    parts = lax.axis_size("ctx")
    chips = parts // 2
    limit = parts * LOCAL
    wide = ratio * rows
    params = pltpu.CompilerParams(vmem_limit_bytes=(16 + 4 * chips) * 1024 * 1024)

    def call(kernel, name, outs, *args, scratch=(), flops=10**6, in_hbm=False):
        if in_hbm:
            args = [pltpu.with_memory_space_constraint(arg, pltpu.HBM) for arg in args]
        spec = pl.BlockSpec(memory_space=pltpu.HBM if in_hbm else pltpu.VMEM)
        return pl.pallas_call(
            kernel,
            out_shape=[jax.ShapeDtypeStruct(*out) for out in outs],
            in_specs=[spec] * len(args),
            scratch_shapes=list(scratch),
            compiler_params=params,
            cost_estimate=pl.CostEstimate(flops=flops, bytes_accessed=1000, transcendentals=0),
            name=name,
        )(*args)

    index = np.arange(DH) % (DH // 2)
    freq = jnp.asarray((THETA ** (-2.0 * index / DH)).astype(np.float32))[None]
    packet = ((rows, group_width // 2), BF16)
    table = ((rows, DH), F32)
    key_mine, key_theirs, value_mine, value_theirs, cosine, sine = call(
        functools.partial(pack_keys_kernel, limit=limit),
        "pack_keys",
        [packet, packet, packet, packet, table, table],
        key_rows[0],
        value_rows[0],
        positions,
        freq,
        in_hbm=True,
        flops=5 * 10**9,
        scratch=[
            pltpu.VMEM((rows, group_width), BF16),
            pltpu.VMEM((rows, group_width), BF16),
            pltpu.VMEM((1, rows), jnp.int32),
            pltpu.VMEM((1, DH), F32),
            pltpu.SemaphoreType.DMA((4,)),
        ],
    )

    hop = [[(2 * x + k, 2 * (x + s) + k) for x in range(chips - s) for k in range(2)] for s in range(chips)]
    cross = [[(a, b + 1 - 2 * (b % 2)) for a, b in pairs] for pairs in hop]
    back_hop = [[(b, a) for a, b in pairs] for pairs in hop]
    back_cross = [[(b, a) for a, b in pairs] for pairs in cross]

    steps = range(1, chips)

    def send(sib, own, sib_pairs, own_pairs):
        sib = [lax.ppermute(sib[s - 1], "ctx", sib_pairs[s]) for s in steps]
        return sib, [lax.ppermute(own[s - 1], "ctx", own_pairs[s]) for s in steps]

    sib_keys, own_keys = send([key_theirs] * chips, [key_mine] * chips, cross, hop)
    sib_values, own_values = send([value_theirs] * chips, [value_mine] * chips, cross, hop)

    pairs = [[2 * x, 2 * x + 1] for x in range(chips)]
    mine, theirs, gate_mine = call(
        functools.partial(pack_queries_kernel, limit=limit),
        "pack_queries",
        [((rows, heads_width), BF16), ((rows + EXTRA, heads_width + group_width), BF16), ((1, rows), F32)],
        query_rows[0],
        cotangent[0],
        router_gate,
        positions,
        cosine,
        sine,
        key_theirs,
        value_theirs,
    )
    sib = lax.ppermute(theirs, "ctx", [pair for a, b in pairs for pair in ((a, b), (b, a))])

    row = ((half_groups, 1, 2 * wide), F32)
    table = ((half_groups, 2 * rows, 2 * wide), F32)
    kv_table = ((half_groups, 2 * rows, DH), BF16)
    q_table = ((half_groups, 2 * wide, DH), BF16)
    keys, query, cot, gate_row, raws, grads, tops, sums, crosses = call(
        functools.partial(local_kernel, ratio=ratio),
        "local_scores",
        [kv_table, q_table, q_table, ((1, 2 * wide), F32), table, table, row, row, row],
        key_mine,
        value_mine,
        mine,
        gate_mine,
        sib,
        scratch=[pltpu.VMEM(*kv_table)],
        flops=3 * 10**6,
    )

    blocks = 2 * (chips - 1)
    far_rows = ((half_groups, blocks * rows, DH), BF16)
    far_low = ((half_groups, blocks * rows, 2 * wide), BF16)
    far_table = (far_low[0], F32 if chips == 2 else BF16)
    far_keys, far_raws, factors, far_factors, shrinks, inverses, *parts = call(
        functools.partial(far_keys_kernel, blocks=blocks),
        "far_keys",
        [far_rows, far_table, row, row, row, row] + [packet] * blocks,
        query,
        cot,
        gate_row,
        tops,
        sums,
        *sib_keys,
        *own_keys,
        scratch=[pltpu.VMEM(*far_low)],
    )
    sib_value_got, own_value_got = send(parts[: chips - 1], parts[chips - 1 :], back_cross, back_hop)
    far_grads, deltas, *parts = call(
        functools.partial(far_values_kernel, blocks=blocks),
        "far_values",
        [far_low, row] + [packet] * blocks,
        query,
        cot,
        far_raws,
        far_factors,
        shrinks,
        inverses,
        crosses,
        *sib_values,
        *own_values,
        scratch=[pltpu.VMEM(*far_rows)],
    )
    sib_key_got, own_key_got = send(parts[: chips - 1], parts[chips - 1 :], back_cross, back_hop)

    part_mine, packed = call(
        functools.partial(near_kernel, ratio=ratio),
        "near_grads",
        [
            ((rows, group_width), F32),
            ((2, rows + EXTRA, half_width + group_width), BF16),
        ],
        raws,
        grads,
        factors,
        deltas,
        keys,
        query,
        cot,
        far_keys,
        far_grads,
        flops=4 * 10**6,
        scratch=[
            pltpu.VMEM((half_groups, 2 * rows, 2 * wide), BF16),
            pltpu.VMEM((half_groups, 2 * rows, 2 * wide), BF16),
            pltpu.VMEM((2, rows, group_width), F32),
            pltpu.VMEM((half_groups, DH, 2 * wide), F32),
        ],
    )
    back = lax.all_to_all(packed, "ctx", 0, 0, axis_index_groups=pairs)
    value_own, value_other = call(
        sum_values_kernel,
        "sum_values",
        [packet, packet],
        back,
        part_mine,
        *[part for pair in zip(sib_value_got, own_value_got) for part in pair],
        flops=3 * 10**8,
    )
    query_grad, key_grad, value_grad, gate_grad = call(
        functools.partial(finish_kernel, limit=limit),
        "finish",
        [((rows, heads_width), BF16)] + [((rows, group_width), BF16)] * 2 + [((1, rows), F32)],
        back,
        part_mine,
        positions,
        cosine,
        sine,
        value_own,
        value_other,
        *[part for pair in zip(sib_key_got, own_key_got) for part in pair],
    )
    return (query_grad[None], key_grad[None], value_grad[None], gate_grad)


def solution(mesh):
    wide = P(("group", "dp"), "ctx", None)
    narrow = P(("group", "dp"), "ctx")
    return jax.shard_map(
        per_device,
        mesh=mesh,
        in_specs=(wide, wide, wide, wide, narrow, narrow),
        out_specs=(wide, wide, wide, narrow),
        check_vma=False,
    )
```

```python
import functools
import math

import jax
import jax.numpy as jnp
import numpy as np
from jax import lax
from jax.experimental import pallas as pl
from jax.experimental.pallas import tpu as pltpu
from jax.sharding import PartitionSpec as P

DH = 128
LOCAL = 1024
THETA = 500000.0
EXTRA = 16
HIDDEN = -1e30
UNUSED = 2.0**14
SCALE = DH**-0.5
LOG2E = math.log2(math.e)
LN2 = math.log(2.0)

NT = (((1,), (1,)), ((), ()))
NN = (((1,), (0,)), ((), ()))
TN = (((0,), (0,)), ((), ()))
F32 = jnp.float32
BF16 = jnp.bfloat16


def few_bits(value, bits):
    unit = 2.0 ** (math.floor(math.log2(value)) + 1 - bits)
    return math.floor(value / unit) * unit


QUARTER_1 = few_bits(math.pi / 2, 10)
QUARTER_2 = few_bits(math.pi / 2 - QUARTER_1, 10)
QUARTER_3 = math.pi / 2 - QUARTER_1 - QUARTER_2


def dot(a, b, dims):
    return lax.dot_general(a, b, dims, preferred_element_type=F32)


def core_of():
    return lax.rem(lax.axis_index("ctx"), 2)


def rotate(values, cosine, sine):
    return values * cosine + pltpu.roll(values, DH // 2, 1) * sine


def sine_cosine(angle):
    turns = jnp.floor(angle * (2.0 / math.pi) + 0.5)
    rest = ((angle - turns * QUARTER_1) - turns * QUARTER_2) - turns * QUARTER_3
    square = rest * rest
    sine = ((-1.9515295891e-4 * square + 8.3321608736e-3) * square - 1.6666654611e-1) * square * rest + rest
    cosine = (2.443315711809948e-5 * square - 1.388731625493765e-3) * square + 4.166664568298827e-2
    cosine = cosine * square * square - 0.5 * square + 1.0
    quarter = turns.astype(jnp.int32)
    odd = (quarter & 1) == 1
    first, second = jnp.where(odd, cosine, sine), jnp.where(odd, sine, cosine)
    return (
        jnp.where((quarter & 2) == 2, -first, first),
        jnp.where(((quarter + 1) & 2) == 2, -second, second),
    )


def split_rows(row, height):
    high = row.astype(BF16).astype(F32)
    middle = (row - high).astype(BF16).astype(F32)
    low = row - high - middle
    line = lax.broadcasted_iota(jnp.int32, (height, row.shape[1]), 0)
    rows = jnp.where(line == 0, high, jnp.where(line == 1, middle, jnp.where(line == 2, low, 0.0)))
    return rows.astype(BF16)


def joined_row(rows):
    return jnp.sum(rows.astype(F32), axis=0, keepdims=True)


def pack_keys_kernel(
    key_in, value_in, pos_in, freq_in, key_mine, key_theirs, value_mine, value_theirs, cos_ref, sin_ref,
    key, value, pos, freq, sems, *, limit
):
    loads = [(pos_in, pos), (freq_in, freq), (key_in, key), (value_in, value)]
    loads = [pltpu.make_async_copy(source, target, sems.at[i]) for i, (source, target) in enumerate(loads)]
    for copy in loads:
        copy.start()
    rows, width = key.shape
    half = width // 2
    core = core_of()
    down = lax.broadcasted_iota(jnp.int32, (rows, rows), 0)
    along = lax.broadcasted_iota(jnp.int32, (rows, rows), 1)
    lane = lax.broadcasted_iota(jnp.int32, (rows, DH), 1)
    loads[0].wait()
    loads[1].wait()
    column = jnp.sum(jnp.where(down == along, pos[...].astype(F32), 0.0), axis=1, keepdims=True)
    sine, cosine = sine_cosine(column * freq[...])
    sine = jnp.where(lane < DH // 2, -sine, sine)
    cos_ref[...] = cosine
    sin_ref[...] = sine
    used = jnp.broadcast_to(column, (rows, DH)) < limit
    loads[2].wait()
    loads[3].wait()
    for key_out, value_out, side in ((key_mine, value_mine, core), (key_theirs, value_theirs, 1 - core)):
        for i in range(half // DH):
            there = pl.ds(pl.multiple_of(side * half + i * DH, DH), DH)
            turned = rotate(key[:, there].astype(F32), cosine, sine)
            key_out[:, i * DH : (i + 1) * DH] = jnp.where(used, turned, UNUSED).astype(BF16)
            value_out[:, i * DH : (i + 1) * DH] = value[:, there]


def pack_queries_kernel(query, cot, gate, pos, cos_ref, sin_ref, key, value, mine, theirs, gate_mine, *, limit):
    rows = query.shape[0]
    half, width = query.shape[1] // 2, key.shape[1]
    core = core_of()
    used_gate = jnp.where(pos[...] < limit, gate[...], 0.0)
    gate_mine[...] = used_gate
    theirs[rows:, :rows] = split_rows(used_gate, EXTRA)
    theirs[:rows, 2 * half : 2 * half + width] = key[...]
    theirs[:rows, 2 * half + width :] = value[...]
    cosine, sine = cos_ref[...] * (SCALE * LOG2E), sin_ref[...] * (SCALE * LOG2E)
    for out_ref, side in ((mine, core), (theirs, 1 - core)):
        for i in range(half // DH):
            there = pl.ds(pl.multiple_of(side * half + i * DH, DH), DH)
            turned = rotate(query[:, there].astype(F32), cosine, sine)
            out_ref[:rows, i * DH : (i + 1) * DH] = turned.astype(BF16)
        out_ref[:rows, half : 2 * half] = cot[:, pl.ds(pl.multiple_of(side * half, DH), half)]


def chosen(shape, ratio, dim):
    down = lax.broadcasted_iota(jnp.int32, shape, 0)
    along = lax.broadcasted_iota(jnp.int32, shape, 1)
    rows = shape[1 - dim]
    long, short = (down, along) if dim == 0 else (along, down)
    for _ in range(1, ratio):
        long = jnp.where(long >= rows, long - rows, long)
    return jnp.where(long == short, 1.0, 0.0).astype(BF16)


def chunks(low, high):
    return [slice(at, min(at + 256, high)) for at in range(low, high, 256)]


def used_slots(key, here):
    chip = lax.div(lax.axis_index("ctx"), 2)
    first = key[:, :DH].astype(F32)[:, :1]
    return jnp.broadcast_to(first, (key.shape[0], 256)) < jnp.where(chip >= here, UNUSED / 2, -UNUSED)


def local_kernel(
    key_mine, value_mine, mine, gate_mine, sib, keys, query, cot, gate, raws, grads, tops, sums, crosses, values,
    *, ratio
):
    rows = key_mine.shape[0]
    half_groups = keys.shape[0]
    wide = ratio * rows
    half = half_groups * ratio * DH
    core = core_of()
    spread = chosen((rows, wide), ratio, 1)
    key_sib = sib.at[:rows, 2 * half : 2 * half + half_groups * DH]
    value_sib = sib.at[:rows, 2 * half + half_groups * DH :]
    for key, value, packet, side in ((key_mine, value_mine, mine, core), (key_sib, value_sib, sib, 1 - core)):
        there = pl.ds(pl.multiple_of(side * rows, 16), rows)
        for i in range(half_groups):
            keys[i, there, :] = key[:, i * DH : (i + 1) * DH]
            values[i, there, :] = value[:, i * DH : (i + 1) * DH]
            for h in range(ratio):
                to = pl.ds(pl.multiple_of(side * wide + h * rows, 16), rows)
                at = (i * ratio + h) * DH
                query[i, to, :] = packet[:rows, at : at + DH]
                cot[i, to, :] = packet[:rows, half + at : half + at + DH]
    own = joined_row(dot(split_rows(gate_mine[...], EXTRA), spread, NN))
    other = joined_row(dot(sib[rows:, :rows], spread, NN))
    gate[:, :wide] = jnp.where(core == 0, own, other)
    gate[:, wide:] = jnp.where(core == 0, other, own)
    used = used_slots(keys[0, :rows, :], 0)
    for i in range(half_groups):
        for block in range(2):
            reach = (block + 1) * rows
            for here in chunks(block * wide, (block + 1) * wide):
                width = here.stop - here.start
                scores = dot(keys[i, :reach, :], query[i, here, :], NT)
                slot = lax.broadcasted_iota(jnp.int32, (rows, width), 0)
                lane = lax.broadcasted_iota(jnp.int32, (rows, width), 1) + (here.start - block * wide)
                for h in range(1, ratio):
                    lane = jnp.where(lane >= rows, lane - rows, lane)
                shown = jnp.where(slot <= lane, scores[block * rows :], HIDDEN)
                if block:
                    before = jnp.where(used[:, :width], scores[:rows], HIDDEN)
                    shown = jnp.concatenate([before, shown], axis=0)
                top = jnp.max(shown, axis=0, keepdims=True)
                raw = jnp.exp2(shown - top)
                prob_grad = dot(values[i, :reach, :], cot[i, here, :], NT)
                raws[i, :reach, here] = raw
                grads[i, :reach, here] = prob_grad
                tops[i, :, here] = top
                sums[i, :, here] = jnp.sum(raw, axis=0, keepdims=True)
                crosses[i, :, here] = jnp.sum(raw * prob_grad, axis=0, keepdims=True)


def part_of(weights, score_grads, query, cot, out_ref, i, there, lanes):
    key_part = dot(score_grads[i, there, lanes], query[i, lanes, :], NN) * LN2
    value_part = dot(weights[i, there, lanes], cot[i, lanes, :], NN)
    out_ref[:, 2 * i * DH : (2 * i + 1) * DH] = key_part.astype(out_ref.dtype)
    out_ref[:, (2 * i + 1) * DH : (2 * i + 2) * DH] = value_part.astype(out_ref.dtype)


def far_keys_kernel(query, cot, gate, tops, sums, *refs, blocks):
    packets = refs[:blocks]
    far_keys, raws, weights, factors, far_factors, shrinks, inverses = refs[blocks : blocks + 7]
    parts = refs[blocks + 7 :]
    rows = packets[0].shape[0]
    half_groups, lanes = query.shape[:2]
    alone = lax.axis_index("ctx") < 2

    @pl.when(alone)
    def _():
        for i in range(half_groups):
            inverse = 1.0 / sums[i]
            factors[i] = inverse * gate[...]
            inverses[i] = inverse

    @pl.when(jnp.logical_not(alone))
    def _():
        for i in range(half_groups):
            for j, packet in enumerate(packets):
                far_keys[i, j * rows : (j + 1) * rows, :] = packet[:, i * DH : (i + 1) * DH]
        used = [used_slots(packet, j % (blocks // 2) + 1) for j, packet in enumerate(packets)]
        for i in range(half_groups):
            for here in chunks(0, lanes):
                width = here.stop - here.start
                scores = dot(far_keys[i], query[i, here, :], NT)
                shown = [
                    jnp.where(used[j][:, :width], scores[j * rows : (j + 1) * rows], HIDDEN) for j in range(blocks)
                ]
                shown = jnp.concatenate(shown, axis=0)
                old_top = tops[i, :, here]
                top = jnp.maximum(old_top, jnp.max(shown, axis=0, keepdims=True))
                raw = jnp.exp2(shown - top)
                shrink = jnp.exp2(old_top - top)
                inverse = 1.0 / (sums[i, :, here] * shrink + jnp.sum(raw, axis=0, keepdims=True))
                factor = inverse * gate[:, here]
                factors[i, :, here] = factor * shrink
                far_factors[i, :, here] = factor
                shrinks[i, :, here] = shrink
                inverses[i, :, here] = inverse
                raws[i, :, here] = raw.astype(raws.dtype)
                weights[i, :, here] = (raw * factor).astype(BF16)
            for j, out_ref in enumerate(parts):
                there = slice(j * rows, (j + 1) * rows)
                out_ref[:, i * DH : (i + 1) * DH] = dot(weights[i, there, :], cot[i], NN).astype(BF16)


def far_values_kernel(query, cot, raws, weights, far_factors, shrinks, inverses, crosses, *refs, blocks):
    packets = refs[:blocks]
    score_grads, deltas = refs[blocks : blocks + 2]
    parts, far_values = refs[blocks + 2 : -1], refs[-1]
    rows = packets[0].shape[0]
    half_groups, lanes = query.shape[:2]
    alone = lax.axis_index("ctx") < 2

    @pl.when(alone)
    def _():
        for i in range(half_groups):
            deltas[i] = crosses[i] * inverses[i]

    @pl.when(jnp.logical_not(alone))
    def _():
        for i in range(half_groups):
            for j, packet in enumerate(packets):
                far_values[i, j * rows : (j + 1) * rows, :] = packet[:, i * DH : (i + 1) * DH]
        for i in range(half_groups):
            for here in chunks(0, lanes):
                raw = raws[i, :, here].astype(F32)
                prob_grad = dot(far_values[i], cot[i, here, :], NT)
                cross = jnp.sum(raw * prob_grad, axis=0, keepdims=True)
                delta = (crosses[i, :, here] * shrinks[i, :, here] + cross) * inverses[i, :, here]
                deltas[i, :, here] = delta
                score_grad = raw * far_factors[i, :, here] * (prob_grad - delta)
                score_grads[i, :, here] = score_grad.astype(BF16)
            for j, out_ref in enumerate(parts):
                there = slice(j * rows, (j + 1) * rows)
                part = dot(score_grads[i, there, :], query[i], NN) * LN2
                out_ref[:, i * DH : (i + 1) * DH] = part.astype(BF16)
                if j >= blocks // 2:
                    part = dot(weights[i, there, :], cot[i], NN)
                    out_ref[:, (half_groups + i) * DH : (half_groups + i + 1) * DH] = part.astype(BF16)


def near_kernel(
    raws, grads, factors, deltas, keys, query, cot, far_keys, far_grads, cos_ref, sin_ref,
    part_mine, query_mine, gate_mine, theirs, weights, score_grads, parts, acc, turned,
    *, ratio
):
    rows = part_mine.shape[0]
    half_groups = keys.shape[0]
    wide = ratio * rows
    half = half_groups * ratio * DH
    for i in range(half_groups):
        for block in range(2):
            reach = (block + 1) * rows
            for here in chunks(block * wide, (block + 1) * wide):
                gated = raws[i, :reach, here] * factors[i, :, here]
                weights[i, :reach, here] = gated.astype(BF16)
                score_grads[i, :reach, here] = (gated * (grads[i, :reach, here] - deltas[i, :, here])).astype(BF16)
        for block in range(2):
            there, lanes = slice(block * rows, (block + 1) * rows), slice(block * wide, 2 * wide)
            part_of(weights, score_grads, query, cot, parts.at[block], i, there, lanes)
            reach, lanes = (block + 1) * rows, slice(block * wide, (block + 1) * wide)
            acc[i, :, lanes] = dot(keys[i, :reach, :], score_grads[i, :reach, lanes], TN)

    @pl.when(lax.axis_index("ctx") >= 2)
    def _():
        for i in range(half_groups):
            acc[i] += dot(far_keys[i], far_grads[i], TN)

    core = core_of()
    cosine, sine = cos_ref[...], -sin_ref[...]
    for i in range(half_groups):
        turned[...] = jnp.transpose(acc[i] * SCALE)
        for h in range(ratio):
            here = slice((i * ratio + h) * DH, (i * ratio + h + 1) * DH)
            own = turned[pl.ds(pl.multiple_of(core * wide + h * rows, 16), rows), :]
            query_mine[:, here] = rotate(own, cosine, sine).astype(BF16)
            other = turned[pl.ds(pl.multiple_of((1 - core) * wide + h * rows, 16), rows), :]
            theirs[:rows, here] = other.astype(BF16)
    part_mine[...] = parts[core]
    theirs[:rows, half:] = parts[1 - core].astype(BF16)
    summed = deltas[0]
    for i in range(1, half_groups):
        summed = summed + deltas[i]
    gates = []
    for block in range(2):
        own = split_rows(summed[:, block * wide : (block + 1) * wide], 16)
        gates.append(joined_row(dot(own, chosen((wide, rows), ratio, 0), NN)))
    gate_mine[...] = jnp.where(core == 0, gates[0], gates[1])
    theirs[rows:, :rows] = split_rows(jnp.where(core == 0, gates[1], gates[0]), EXTRA)


def sum_first_kernel(*refs):
    got, other = refs[:-1], refs[-1]
    total = got[0][...].astype(F32)
    for ref in got[1:]:
        total = total + ref[...].astype(F32)
    other[...] = total


def sum_rest_kernel(value_in, part_mine, *refs):
    got, (key_own, value_own, key_other, value_other) = refs[:-4], refs[-4:]
    half = value_in.shape[1]
    value_other[...] = value_in[...]
    total = got[0][...].astype(F32)
    for ref in got[2::2]:
        total = total + ref[...].astype(F32)
    key_other[...] = total
    for i in range(half // DH):
        here, there = slice(i * DH, (i + 1) * DH), slice(half + i * DH, half + (i + 1) * DH)
        key = part_mine[:, 2 * i * DH : (2 * i + 1) * DH]
        value = part_mine[:, (2 * i + 1) * DH : (2 * i + 2) * DH]
        for ref in got[1::2]:
            key = key + ref[:, here].astype(F32)
            value = value + ref[:, there].astype(F32)
        key_own[:, here] = key
        value_own[:, here] = value


def finish_kernel(
    back, query_mine, gate_mine, key_own, value_own, key_other, value_other, pos_ref, cos_ref, sin_ref,
    query_out, key_out, value_out, gate_grad, query, key, value, sems, *, limit
):
    rows, half = value_own.shape
    wide = query_mine.shape[1]
    core = core_of()
    side = lambda which, width, at=0, size=None: pl.ds(pl.multiple_of(which * width + at, DH), size or width)
    copies = [pltpu.make_async_copy(query_mine, query_out.at[:, side(core, wide)], sems.at[0])]
    copies[0].start()
    cosine, sine = cos_ref[...], -sin_ref[...]
    for i in range(half // DH):
        here = slice(i * DH, (i + 1) * DH)
        there = wide + 2 * i * DH
        other_key = key_other[:, here] + back[:rows, there : there + DH].astype(F32)
        other_value = value_other[:, here] + back[:rows, there + DH : there + 2 * DH].astype(F32)
        for key_sum, value_sum, which in (
            (key_own[:, here], value_own[:, here], core),
            (other_key, other_value, 1 - core),
        ):
            to = side(which, half, i * DH, DH)
            key[:, to] = rotate(key_sum, cosine, sine).astype(BF16)
            value[:, to] = value_sum.astype(BF16)
    copies.append(pltpu.make_async_copy(key, key_out, sems.at[1]))
    copies.append(pltpu.make_async_copy(value, value_out, sems.at[2]))
    copies[1].start()
    copies[2].start()
    for part in range(2):
        low = part * (wide // 2)
        for i in range(wide // 2 // DH):
            here = slice(low + i * DH, low + (i + 1) * DH)
            query[:, here] = rotate(back[:rows, here].astype(F32), cosine, sine).astype(BF16)
        to = query_out.at[:, side(1 - core, wide, low, wide // 2)]
        copies.append(pltpu.make_async_copy(query.at[:, low : low + wide // 2], to, sems.at[3 + part]))
        copies[-1].start()
    gate = gate_mine[...] + joined_row(back[rows:, :rows])
    gate_grad[...] = jnp.where(pos_ref[...] < limit, gate, 0.0)
    for copy in copies:
        copy.wait()


def per_device(query_rows, key_rows, value_rows, cotangent, router_gate, positions):
    rows, heads_width = query_rows.shape[1:]
    group_width = key_rows.shape[2]
    groups = group_width // DH
    ratio = heads_width // group_width
    half_groups, half_width = groups // 2, heads_width // 2
    parts = lax.axis_size("ctx")
    chips = parts // 2
    limit = parts * LOCAL
    wide = ratio * rows
    params = pltpu.CompilerParams(vmem_limit_bytes=(16 + 4 * chips) * 1024 * 1024)

    def call(kernel, name, outs, *args, scratch=(), flops=10**6, in_hbm=False, out_hbm=0):
        if in_hbm:
            args = [pltpu.with_memory_space_constraint(arg, pltpu.HBM) for arg in args]
        spec = pl.BlockSpec(memory_space=pltpu.HBM if in_hbm else pltpu.VMEM)
        return pl.pallas_call(
            kernel,
            out_shape=[jax.ShapeDtypeStruct(*out) for out in outs],
            in_specs=[spec] * len(args),
            out_specs=[
                pl.BlockSpec(memory_space=pltpu.HBM if i < out_hbm else pltpu.VMEM) for i in range(len(outs))
            ],
            scratch_shapes=list(scratch),
            compiler_params=params,
            cost_estimate=pl.CostEstimate(flops=flops, bytes_accessed=1000, transcendentals=0),
            name=name,
        )(*args)

    index = np.arange(DH) % (DH // 2)
    freq = jnp.asarray((THETA ** (-2.0 * index / DH)).astype(np.float32))[None]
    packet = ((rows, group_width // 2), BF16)
    table = ((rows, DH), F32)
    key_mine, key_theirs, value_mine, value_theirs, cosine, sine = call(
        functools.partial(pack_keys_kernel, limit=limit),
        "pack_keys",
        [packet, packet, packet, packet, table, table],
        key_rows[0],
        value_rows[0],
        positions,
        freq,
        in_hbm=True,
        flops=5 * 10**9,
        scratch=[
            pltpu.VMEM((rows, group_width), BF16),
            pltpu.VMEM((rows, group_width), BF16),
            pltpu.VMEM((1, rows), jnp.int32),
            pltpu.VMEM((1, DH), F32),
            pltpu.SemaphoreType.DMA((4,)),
        ],
    )

    hop = [[(2 * x + k, 2 * (x + s) + k) for x in range(chips - s) for k in range(2)] for s in range(chips)]
    cross = [[(a, b + 1 - 2 * (b % 2)) for a, b in pairs] for pairs in hop]
    back_hop = [[(b, a) for a, b in pairs] for pairs in hop]
    back_cross = [[(b, a) for a, b in pairs] for pairs in cross]

    steps = range(1, chips)

    def send(sib, own, sib_pairs, own_pairs):
        sib = [lax.ppermute(sib[s - 1], "ctx", sib_pairs[s]) for s in steps]
        return sib, [lax.ppermute(own[s - 1], "ctx", own_pairs[s]) for s in steps]

    sib_keys, own_keys = send([key_theirs] * chips, [key_mine] * chips, cross, hop)
    sib_values, own_values = send([value_theirs] * chips, [value_mine] * chips, cross, hop)

    pairs = [[2 * x, 2 * x + 1] for x in range(chips)]
    mine, theirs, gate_mine = call(
        functools.partial(pack_queries_kernel, limit=limit),
        "pack_queries",
        [((rows, heads_width), BF16), ((rows + EXTRA, heads_width + group_width), BF16), ((1, rows), F32)],
        query_rows[0],
        cotangent[0],
        router_gate,
        positions,
        cosine,
        sine,
        key_theirs,
        value_theirs,
    )
    swap = [pair for a, b in pairs for pair in ((a, b), (b, a))]
    sib = lax.ppermute(theirs, "ctx", swap)

    row = ((half_groups, 1, 2 * wide), F32)
    table = ((half_groups, 2 * rows, 2 * wide), F32)
    kv_table = ((half_groups, 2 * rows, DH), BF16)
    q_table = ((half_groups, 2 * wide, DH), BF16)
    keys, query, cot, gate_row, raws, grads, tops, sums, crosses = call(
        functools.partial(local_kernel, ratio=ratio),
        "local_scores",
        [kv_table, q_table, q_table, ((1, 2 * wide), F32), table, table, row, row, row],
        key_mine,
        value_mine,
        mine,
        gate_mine,
        sib,
        scratch=[pltpu.VMEM(*kv_table)],
        flops=3 * 10**6,
    )

    blocks = 2 * (chips - 1)
    far_rows = ((half_groups, blocks * rows, DH), BF16)
    far_low = ((half_groups, blocks * rows, 2 * wide), BF16)
    far_table = (far_low[0], F32 if chips == 2 else BF16)
    far_keys, far_raws, weights, factors, far_factors, shrinks, inverses, *parts = call(
        functools.partial(far_keys_kernel, blocks=blocks),
        "far_keys",
        [far_rows, far_table, far_low, row, row, row, row] + [packet] * (chips - 1),
        query,
        cot,
        gate_row,
        tops,
        sums,
        *sib_keys,
        *own_keys,
    )
    sib_value_got = [lax.ppermute(parts[s - 1], "ctx", back_cross[s]) for s in steps]
    far_grads, deltas, *parts = call(
        functools.partial(far_values_kernel, blocks=blocks),
        "far_values",
        [far_low, row] + [packet] * (chips - 1) + [((rows, group_width), BF16)] * (chips - 1),
        query,
        cot,
        far_raws,
        weights,
        far_factors,
        shrinks,
        inverses,
        crosses,
        *sib_values,
        *own_values,
        scratch=[pltpu.VMEM(*far_rows)],
    )
    sib_key_got, own_got = send(parts[: chips - 1], parts[chips - 1 :], back_cross, back_hop)

    part_mine, query_mine, gate_mine, theirs = call(
        functools.partial(near_kernel, ratio=ratio),
        "near_grads",
        [
            ((rows, group_width), F32),
            ((rows, half_width), BF16),
            ((1, rows), F32),
            ((rows + EXTRA, half_width + group_width), BF16),
        ],
        raws,
        grads,
        factors,
        deltas,
        keys,
        query,
        cot,
        far_keys,
        far_grads,
        cosine,
        sine,
        flops=4 * 10**6,
        scratch=[
            pltpu.VMEM((half_groups, 2 * rows, 2 * wide), BF16),
            pltpu.VMEM((half_groups, 2 * rows, 2 * wide), BF16),
            pltpu.VMEM((2, rows, group_width), F32),
            pltpu.VMEM((half_groups, DH, 2 * wide), F32),
            pltpu.VMEM((2 * wide, DH), F32),
        ],
    )
    back = lax.ppermute(theirs, "ctx", swap)
    total = ((rows, group_width // 2), F32)
    (value_other,) = call(sum_first_kernel, "sum_first", [total], *sib_value_got, flops=5 * 10**9)
    sums = call(
        sum_rest_kernel,
        "sum_rest",
        [total] * 4,
        value_other,
        part_mine,
        *[part for pair in zip(sib_key_got, own_got) for part in pair],
        flops=5 * 10**9,
    )
    query_grad, key_grad, value_grad, gate_grad = call(
        functools.partial(finish_kernel, limit=limit),
        "finish",
        [((rows, heads_width), BF16)] + [((rows, group_width), BF16)] * 2 + [((1, rows), F32)],
        back,
        query_mine,
        gate_mine,
        *sums,
        positions,
        cosine,
        sine,
        out_hbm=3,
        scratch=[
            pltpu.VMEM((rows, half_width), BF16),
            pltpu.VMEM((rows, group_width), BF16),
            pltpu.VMEM((rows, group_width), BF16),
            pltpu.SemaphoreType.DMA((5,)),
        ],
    )
    return (query_grad[None], key_grad[None], value_grad[None], gate_grad)


def solution(mesh):
    wide = P(("group", "dp"), "ctx", None)
    narrow = P(("group", "dp"), "ctx")
    return jax.shard_map(
        per_device,
        mesh=mesh,
        in_specs=(wide, wide, wide, wide, narrow, narrow),
        out_specs=(wide, wide, wide, narrow),
        check_vma=False,
    )
```

```python
import functools
import math

import jax
import jax.numpy as jnp
import numpy as np
from jax import lax
from jax.experimental import pallas as pl
from jax.experimental.pallas import tpu as pltpu
from jax.sharding import PartitionSpec as P

DH = 128
LOCAL = 1024
THETA = 500000.0
EXTRA = 16
HIDDEN = -1e30
UNUSED = 2.0**14
SCALE = DH**-0.5
LOG2E = math.log2(math.e)
LN2 = math.log(2.0)

NT = (((1,), (1,)), ((), ()))
NN = (((1,), (0,)), ((), ()))
TN = (((0,), (0,)), ((), ()))
F32 = jnp.float32
BF16 = jnp.bfloat16


def few_bits(value, bits):
    unit = 2.0 ** (math.floor(math.log2(value)) + 1 - bits)
    return math.floor(value / unit) * unit


QUARTER_1 = few_bits(math.pi / 2, 10)
QUARTER_2 = few_bits(math.pi / 2 - QUARTER_1, 10)
QUARTER_3 = math.pi / 2 - QUARTER_1 - QUARTER_2


def dot(a, b, dims):
    return lax.dot_general(a, b, dims, preferred_element_type=F32)


def core_of():
    return lax.rem(lax.axis_index("ctx"), 2)


def rotate(values, cosine, sine):
    return values * cosine + pltpu.roll(values, DH // 2, 1) * sine


def sine_cosine(angle):
    turns = jnp.floor(angle * (2.0 / math.pi) + 0.5)
    rest = ((angle - turns * QUARTER_1) - turns * QUARTER_2) - turns * QUARTER_3
    square = rest * rest
    sine = ((-1.9515295891e-4 * square + 8.3321608736e-3) * square - 1.6666654611e-1) * square * rest + rest
    cosine = (2.443315711809948e-5 * square - 1.388731625493765e-3) * square + 4.166664568298827e-2
    cosine = cosine * square * square - 0.5 * square + 1.0
    quarter = turns.astype(jnp.int32)
    odd = (quarter & 1) == 1
    first, second = jnp.where(odd, cosine, sine), jnp.where(odd, sine, cosine)
    return (
        jnp.where((quarter & 2) == 2, -first, first),
        jnp.where(((quarter + 1) & 2) == 2, -second, second),
    )


def split_rows(row, height):
    high = row.astype(BF16).astype(F32)
    middle = (row - high).astype(BF16).astype(F32)
    low = row - high - middle
    line = lax.broadcasted_iota(jnp.int32, (height, row.shape[1]), 0)
    rows = jnp.where(line == 0, high, jnp.where(line == 1, middle, jnp.where(line == 2, low, 0.0)))
    return rows.astype(BF16)


def joined_row(rows):
    return jnp.sum(rows.astype(F32), axis=0, keepdims=True)


def pack_kernel(
    key_in, value_in, query_in, cot_in, gate_in, pos_in, freq_in,
    key_mine, key_theirs, value_mine, value_theirs, theirs, gate_mine, cos_ref, sin_ref,
    key, value, query, gate, pos, freq, sems, *, limit
):
    rows, width = key.shape
    side_width = width // 2
    half = query.shape[1]
    core = core_of()
    there = pl.ds(pl.multiple_of((1 - core) * half, DH), half)
    loads = [(pos_in, pos), (freq_in, freq), (key_in, key), (value_in, value), (query_in.at[:, there], query)]
    loads += [(gate_in, gate), (cot_in.at[:, there], theirs.at[:rows, half : 2 * half])]
    loads = [pltpu.make_async_copy(source, target, sems.at[i]) for i, (source, target) in enumerate(loads)]
    for copy in loads:
        copy.start()
    down = lax.broadcasted_iota(jnp.int32, (rows, rows), 0)
    along = lax.broadcasted_iota(jnp.int32, (rows, rows), 1)
    lane = lax.broadcasted_iota(jnp.int32, (rows, DH), 1)
    loads[0].wait()
    loads[1].wait()
    places = pos[...]
    column = jnp.sum(jnp.where(down == along, places.astype(F32), 0.0), axis=1, keepdims=True)
    sine, cosine = sine_cosine(column * freq[...])
    sine = jnp.where(lane < DH // 2, -sine, sine)
    cos_ref[...] = cosine
    sin_ref[...] = sine
    used = jnp.broadcast_to(column, (rows, DH)) < limit
    loads[2].wait()
    loads[3].wait()
    for key_out, value_out, side in ((key_mine, value_mine, core), (key_theirs, value_theirs, 1 - core)):
        for i in range(side_width // DH):
            from_ = pl.ds(pl.multiple_of(side * side_width + i * DH, DH), DH)
            turned = jnp.where(used, rotate(key[:, from_].astype(F32), cosine, sine), UNUSED).astype(BF16)
            key_out[:, i * DH : (i + 1) * DH] = turned
            value_out[:, i * DH : (i + 1) * DH] = value[:, from_]
    theirs[:rows, 2 * half : 2 * half + side_width] = key_theirs[...]
    theirs[:rows, 2 * half + side_width :] = value_theirs[...]
    loads[4].wait()
    cosine, sine = cosine * (SCALE * LOG2E), sine * (SCALE * LOG2E)
    for i in range(half // DH):
        here = slice(i * DH, (i + 1) * DH)
        theirs[:rows, here] = rotate(query[:, here].astype(F32), cosine, sine).astype(BF16)
    loads[5].wait()
    used_gate = jnp.where(places < limit, gate[...], 0.0)
    gate_mine[...] = used_gate
    theirs[rows:, :rows] = split_rows(used_gate, EXTRA)
    loads[6].wait()


def chosen(shape, ratio, dim):
    down = lax.broadcasted_iota(jnp.int32, shape, 0)
    along = lax.broadcasted_iota(jnp.int32, shape, 1)
    rows = shape[1 - dim]
    long, short = (down, along) if dim == 0 else (along, down)
    for _ in range(1, ratio):
        long = jnp.where(long >= rows, long - rows, long)
    return jnp.where(long == short, 1.0, 0.0).astype(BF16)


def chunks(low, high):
    return [slice(at, min(at + 256, high)) for at in range(low, high, 256)]


def used_slots(key, here):
    chip = lax.div(lax.axis_index("ctx"), 2)
    first = key[:, :DH].astype(F32)[:, :1]
    return jnp.broadcast_to(first, (key.shape[0], 256)) < jnp.where(chip >= here, UNUSED / 2, -UNUSED)


def local_kernel(
    key_mine, value_mine, query_in, cot_in, cos_ref, sin_ref, gate_mine, sib,
    keys, query, cot, gate, raws, grads, tops, sums, crosses, values, *, ratio
):
    rows = key_mine.shape[0]
    half_groups = keys.shape[0]
    wide = ratio * rows
    half = half_groups * ratio * DH
    core = core_of()
    spread = chosen((rows, wide), ratio, 1)
    key_sib = sib.at[:rows, 2 * half : 2 * half + half_groups * DH]
    value_sib = sib.at[:rows, 2 * half + half_groups * DH :]
    cosine, sine = cos_ref[...] * (SCALE * LOG2E), sin_ref[...] * (SCALE * LOG2E)
    for key, value, side in ((key_mine, value_mine, core), (key_sib, value_sib, 1 - core)):
        there = pl.ds(pl.multiple_of(side * rows, 16), rows)
        for i in range(half_groups):
            keys[i, there, :] = key[:, i * DH : (i + 1) * DH]
            values[i, there, :] = value[:, i * DH : (i + 1) * DH]
            for h in range(ratio):
                to = pl.ds(pl.multiple_of(side * wide + h * rows, 16), rows)
                at = (i * ratio + h) * DH
                if key is key_mine:
                    here = pl.ds(pl.multiple_of(core * half + at, DH), DH)
                    query[i, to, :] = rotate(query_in[:, here].astype(F32), cosine, sine).astype(BF16)
                    cot[i, to, :] = cot_in[:, here]
                else:
                    query[i, to, :] = sib[:rows, at : at + DH]
                    cot[i, to, :] = sib[:rows, half + at : half + at + DH]
    own = joined_row(dot(split_rows(gate_mine[...], EXTRA), spread, NN))
    other = joined_row(dot(sib[rows:, :rows], spread, NN))
    gate[:, :wide] = jnp.where(core == 0, own, other)
    gate[:, wide:] = jnp.where(core == 0, other, own)
    used = used_slots(keys[0, :rows, :], 0)
    for i in range(half_groups):
        for block in range(2):
            reach = (block + 1) * rows
            for here in chunks(block * wide, (block + 1) * wide):
                width = here.stop - here.start
                scores = dot(keys[i, :reach, :], query[i, here, :], NT)
                slot = lax.broadcasted_iota(jnp.int32, (rows, width), 0)
                lane = lax.broadcasted_iota(jnp.int32, (rows, width), 1) + (here.start - block * wide)
                for h in range(1, ratio):
                    lane = jnp.where(lane >= rows, lane - rows, lane)
                shown = jnp.where(slot <= lane, scores[block * rows :], HIDDEN)
                if block:
                    before = jnp.where(used[:, :width], scores[:rows], HIDDEN)
                    shown = jnp.concatenate([before, shown], axis=0)
                top = jnp.max(shown, axis=0, keepdims=True)
                raw = jnp.exp2(shown - top)
                prob_grad = dot(values[i, :reach, :], cot[i, here, :], NT)
                raws[i, :reach, here] = raw
                grads[i, :reach, here] = prob_grad
                tops[i, :, here] = top
                sums[i, :, here] = jnp.sum(raw, axis=0, keepdims=True)
                crosses[i, :, here] = jnp.sum(raw * prob_grad, axis=0, keepdims=True)


def part_of(weights, score_grads, query, cot, out_ref, i, there, lanes):
    key_part = dot(score_grads[i, there, lanes], query[i, lanes, :], NN) * LN2
    value_part = dot(weights[i, there, lanes], cot[i, lanes, :], NN)
    out_ref[:, 2 * i * DH : (2 * i + 1) * DH] = key_part.astype(out_ref.dtype)
    out_ref[:, (2 * i + 1) * DH : (2 * i + 2) * DH] = value_part.astype(out_ref.dtype)


def far_keys_kernel(query, cot, gate, tops, sums, *refs, blocks):
    packets = refs[:blocks]
    far_keys, raws, factors, far_factors, shrinks, inverses = refs[blocks : blocks + 6]
    parts, weights = refs[blocks + 6 : -1], refs[-1]
    rows = packets[0].shape[0]
    half_groups, lanes = query.shape[:2]
    alone = lax.axis_index("ctx") < 2

    @pl.when(alone)
    def _():
        for i in range(half_groups):
            inverse = 1.0 / sums[i]
            factors[i] = inverse * gate[...]
            inverses[i] = inverse

    @pl.when(jnp.logical_not(alone))
    def _():
        for i in range(half_groups):
            for j, packet in enumerate(packets):
                far_keys[i, j * rows : (j + 1) * rows, :] = packet[:, i * DH : (i + 1) * DH]
        used = [used_slots(packet, j % (blocks // 2) + 1) for j, packet in enumerate(packets)]
        for i in range(half_groups):
            for here in chunks(0, lanes):
                width = here.stop - here.start
                scores = dot(far_keys[i], query[i, here, :], NT)
                shown = [
                    jnp.where(used[j][:, :width], scores[j * rows : (j + 1) * rows], HIDDEN) for j in range(blocks)
                ]
                shown = jnp.concatenate(shown, axis=0)
                old_top = tops[i, :, here]
                top = jnp.maximum(old_top, jnp.max(shown, axis=0, keepdims=True))
                raw = jnp.exp2(shown - top)
                shrink = jnp.exp2(old_top - top)
                inverse = 1.0 / (sums[i, :, here] * shrink + jnp.sum(raw, axis=0, keepdims=True))
                factor = inverse * gate[:, here]
                factors[i, :, here] = factor * shrink
                far_factors[i, :, here] = factor
                shrinks[i, :, here] = shrink
                inverses[i, :, here] = inverse
                raws[i, :, here] = raw.astype(raws.dtype)
                weights[i, :, here] = (raw * factor).astype(BF16)
            for j, out_ref in enumerate(parts):
                there = slice(j * rows, (j + 1) * rows)
                out_ref[:, i * DH : (i + 1) * DH] = dot(weights[i, there, :], cot[i], NN).astype(BF16)


def far_values_kernel(query, cot, raws, far_factors, shrinks, inverses, crosses, *refs, blocks):
    packets = refs[:blocks]
    score_grads, deltas = refs[blocks : blocks + 2]
    parts, far_values = refs[blocks + 2 : -1], refs[-1]
    rows = packets[0].shape[0]
    half_groups, lanes = query.shape[:2]
    alone = lax.axis_index("ctx") < 2

    @pl.when(alone)
    def _():
        for i in range(half_groups):
            deltas[i] = crosses[i] * inverses[i]

    @pl.when(jnp.logical_not(alone))
    def _():
        for i in range(half_groups):
            for j, packet in enumerate(packets):
                far_values[i, j * rows : (j + 1) * rows, :] = packet[:, i * DH : (i + 1) * DH]
        for i in range(half_groups):
            for here in chunks(0, lanes):
                raw = raws[i, :, here].astype(F32)
                prob_grad = dot(far_values[i], cot[i, here, :], NT)
                cross = jnp.sum(raw * prob_grad, axis=0, keepdims=True)
                delta = (crosses[i, :, here] * shrinks[i, :, here] + cross) * inverses[i, :, here]
                deltas[i, :, here] = delta
                score_grad = raw * far_factors[i, :, here] * (prob_grad - delta)
                score_grads[i, :, here] = score_grad.astype(BF16)
            for j, out_ref in enumerate(parts):
                there = slice(j * rows, (j + 1) * rows)
                part = dot(score_grads[i, there, :], query[i], NN) * LN2
                out_ref[:, i * DH : (i + 1) * DH] = part.astype(BF16)


def near_kernel(
    raws, grads, factors, deltas, keys, query, cot, far_keys, far_grads, cos_ref, sin_ref,
    part_mine, query_mine, gate_mine, theirs, weights, score_grads, parts, acc, turned,
    *, ratio
):
    rows = part_mine.shape[0]
    half_groups = keys.shape[0]
    wide = ratio * rows
    half = half_groups * ratio * DH
    for i in range(half_groups):
        for block in range(2):
            reach = (block + 1) * rows
            for here in chunks(block * wide, (block + 1) * wide):
                gated = raws[i, :reach, here] * factors[i, :, here]
                weights[i, :reach, here] = gated.astype(BF16)
                score_grads[i, :reach, here] = (gated * (grads[i, :reach, here] - deltas[i, :, here])).astype(BF16)
        for block in range(2):
            there, lanes = slice(block * rows, (block + 1) * rows), slice(block * wide, 2 * wide)
            part_of(weights, score_grads, query, cot, parts.at[block], i, there, lanes)
            reach, lanes = (block + 1) * rows, slice(block * wide, (block + 1) * wide)
            acc[i, :, lanes] = dot(keys[i, :reach, :], score_grads[i, :reach, lanes], TN)

    @pl.when(lax.axis_index("ctx") >= 2)
    def _():
        for i in range(half_groups):
            acc[i] += dot(far_keys[i], far_grads[i], TN)

    core = core_of()
    cosine, sine = cos_ref[...], -sin_ref[...]
    for i in range(half_groups):
        turned[...] = jnp.transpose(acc[i] * SCALE)
        for h in range(ratio):
            here = slice((i * ratio + h) * DH, (i * ratio + h + 1) * DH)
            own = turned[pl.ds(pl.multiple_of(core * wide + h * rows, 16), rows), :]
            query_mine[:, here] = rotate(own, cosine, sine).astype(BF16)
            other = turned[pl.ds(pl.multiple_of((1 - core) * wide + h * rows, 16), rows), :]
            theirs[:rows, here] = other.astype(BF16)
    part_mine[...] = parts[core]
    theirs[:rows, half:] = parts[1 - core].astype(BF16)
    summed = deltas[0]
    for i in range(1, half_groups):
        summed = summed + deltas[i]
    gates = []
    for block in range(2):
        own = split_rows(summed[:, block * wide : (block + 1) * wide], 16)
        gates.append(joined_row(dot(own, chosen((wide, rows), ratio, 0), NN)))
    gate_mine[...] = jnp.where(core == 0, gates[0], gates[1])
    theirs[rows:, :rows] = split_rows(jnp.where(core == 0, gates[1], gates[0]), EXTRA)


def sum_first_kernel(part_mine, *refs):
    got, (own, other) = refs[:-2], refs[-2:]
    total = got[0][...].astype(F32)
    for ref in got[2::2]:
        total = total + ref[...].astype(F32)
    other[...] = total
    for i in range(own.shape[1] // DH):
        here = slice(i * DH, (i + 1) * DH)
        value = part_mine[:, (2 * i + 1) * DH : (2 * i + 2) * DH]
        for ref in got[1::2]:
            value = value + ref[:, here].astype(F32)
        own[:, here] = value


def sum_rest_kernel(value_own, part_mine, *refs):
    got, (own, other) = refs[:-2], refs[-2:]
    total = got[0][...].astype(F32)
    for ref in got[2::2]:
        total = total + ref[...].astype(F32)
    other[...] = total
    for i in range(own.shape[1] // DH):
        here = slice(i * DH, (i + 1) * DH)
        key = part_mine[:, 2 * i * DH : (2 * i + 1) * DH]
        for ref in got[1::2]:
            key = key + ref[:, here].astype(F32)
        own[:, here] = key


def finish_kernel(
    back, query_mine, gate_mine, key_own, value_own, key_other, value_other, pos_ref, cos_ref, sin_ref,
    query_grad, key_grad, value_grad, gate_grad, *, limit
):
    rows, half = value_own.shape
    wide = query_mine.shape[1]
    core = core_of()
    side = lambda which, width, at=0, size=None: pl.ds(pl.multiple_of(which * width + at, DH), size or width)
    cosine, sine = cos_ref[...], -sin_ref[...]
    for i in range(half // DH):
        here = slice(i * DH, (i + 1) * DH)
        there = wide + 2 * i * DH
        other_key = key_other[:, here] + back[:rows, there : there + DH].astype(F32)
        other_value = value_other[:, here] + back[:rows, there + DH : there + 2 * DH].astype(F32)
        for key_sum, value_sum, which in (
            (key_own[:, here], value_own[:, here], core),
            (other_key, other_value, 1 - core),
        ):
            to = side(which, half, i * DH, DH)
            key_grad[:, to] = rotate(key_sum, cosine, sine).astype(BF16)
            value_grad[:, to] = value_sum.astype(BF16)
    query_grad[:, side(core, wide)] = query_mine[...]
    for i in range(wide // DH):
        turned = rotate(back[:rows, i * DH : (i + 1) * DH].astype(F32), cosine, sine)
        query_grad[:, side(1 - core, wide, i * DH, DH)] = turned.astype(BF16)
    gate = gate_mine[...] + joined_row(back[rows:, :rows])
    gate_grad[...] = jnp.where(pos_ref[...] < limit, gate, 0.0)


def per_device(query_rows, key_rows, value_rows, cotangent, router_gate, positions):
    rows, heads_width = query_rows.shape[1:]
    group_width = key_rows.shape[2]
    groups = group_width // DH
    ratio = heads_width // group_width
    half_groups, half_width = groups // 2, heads_width // 2
    parts = lax.axis_size("ctx")
    chips = parts // 2
    limit = parts * LOCAL
    wide = ratio * rows
    params = pltpu.CompilerParams(vmem_limit_bytes=(16 + 4 * chips) * 1024 * 1024)

    def call(kernel, name, outs, *args, scratch=(), flops=10**6, in_hbm=False):
        if in_hbm:
            args = [pltpu.with_memory_space_constraint(arg, pltpu.HBM) for arg in args]
        spec = pl.BlockSpec(memory_space=pltpu.HBM if in_hbm else pltpu.VMEM)
        return pl.pallas_call(
            kernel,
            out_shape=[jax.ShapeDtypeStruct(*out) for out in outs],
            in_specs=[spec] * len(args),
            scratch_shapes=list(scratch),
            compiler_params=params,
            cost_estimate=pl.CostEstimate(flops=flops, bytes_accessed=1000, transcendentals=0),
            name=name,
        )(*args)

    index = np.arange(DH) % (DH // 2)
    freq = jnp.asarray((THETA ** (-2.0 * index / DH)).astype(np.float32))[None]
    packet = ((rows, group_width // 2), BF16)
    table = ((rows, DH), F32)
    line = ((1, rows), F32)
    theirs_shape = ((rows + EXTRA, heads_width + group_width), BF16)
    key_mine, key_theirs, value_mine, value_theirs, theirs, gate_mine, cosine, sine = call(
        functools.partial(pack_kernel, limit=limit),
        "pack",
        [packet, packet, packet, packet, theirs_shape, line, table, table],
        key_rows[0],
        value_rows[0],
        query_rows[0],
        cotangent[0],
        router_gate,
        positions,
        freq,
        in_hbm=True,
        flops=5 * 10**9,
        scratch=[
            pltpu.VMEM((rows, group_width), BF16),
            pltpu.VMEM((rows, group_width), BF16),
            pltpu.VMEM((rows, half_width), BF16),
            pltpu.VMEM(*line),
            pltpu.VMEM((1, rows), jnp.int32),
            pltpu.VMEM((1, DH), F32),
            pltpu.SemaphoreType.DMA((7,)),
        ],
    )

    hop = [[(2 * x + k, 2 * (x + s) + k) for x in range(chips - s) for k in range(2)] for s in range(chips)]
    cross = [[(a, b + 1 - 2 * (b % 2)) for a, b in pairs] for pairs in hop]
    back_hop = [[(b, a) for a, b in pairs] for pairs in hop]
    back_cross = [[(b, a) for a, b in pairs] for pairs in cross]

    steps = range(1, chips)

    def send(sib, own, sib_pairs, own_pairs):
        sib = [lax.ppermute(sib[s - 1], "ctx", sib_pairs[s]) for s in steps]
        return sib, [lax.ppermute(own[s - 1], "ctx", own_pairs[s]) for s in steps]

    sib_keys, own_keys = send([key_theirs] * chips, [key_mine] * chips, cross, hop)
    sib_values, own_values = send([value_theirs] * chips, [value_mine] * chips, cross, hop)

    pairs = [[2 * x, 2 * x + 1] for x in range(chips)]
    swap = [pair for a, b in pairs for pair in ((a, b), (b, a))]
    sib = lax.ppermute(theirs, "ctx", swap)

    row = ((half_groups, 1, 2 * wide), F32)
    table = ((half_groups, 2 * rows, 2 * wide), F32)
    kv_table = ((half_groups, 2 * rows, DH), BF16)
    q_table = ((half_groups, 2 * wide, DH), BF16)
    keys, query, cot, gate_row, raws, grads, tops, sums, crosses = call(
        functools.partial(local_kernel, ratio=ratio),
        "local_scores",
        [kv_table, q_table, q_table, ((1, 2 * wide), F32), table, table, row, row, row],
        key_mine,
        value_mine,
        query_rows[0],
        cotangent[0],
        cosine,
        sine,
        gate_mine,
        sib,
        scratch=[pltpu.VMEM(*kv_table)],
        flops=3 * 10**6,
    )

    blocks = 2 * (chips - 1)
    far_rows = ((half_groups, blocks * rows, DH), BF16)
    far_low = ((half_groups, blocks * rows, 2 * wide), BF16)
    far_table = (far_low[0], F32 if chips == 2 else BF16)
    far_keys, far_raws, factors, far_factors, shrinks, inverses, *parts = call(
        functools.partial(far_keys_kernel, blocks=blocks),
        "far_keys",
        [far_rows, far_table, row, row, row, row] + [packet] * blocks,
        query,
        cot,
        gate_row,
        tops,
        sums,
        *sib_keys,
        *own_keys,
        scratch=[pltpu.VMEM(*far_low)],
    )
    sib_value_got, own_value_got = send(parts[: chips - 1], parts[chips - 1 :], back_cross, back_hop)
    far_grads, deltas, *parts = call(
        functools.partial(far_values_kernel, blocks=blocks),
        "far_values",
        [far_low, row] + [packet] * blocks,
        query,
        cot,
        far_raws,
        far_factors,
        shrinks,
        inverses,
        crosses,
        *sib_values,
        *own_values,
        scratch=[pltpu.VMEM(*far_rows)],
    )
    sib_key_got, own_key_got = send(parts[: chips - 1], parts[chips - 1 :], back_cross, back_hop)

    part_mine, query_mine, gate_part, theirs = call(
        functools.partial(near_kernel, ratio=ratio),
        "near_grads",
        [
            ((rows, group_width), F32),
            ((rows, half_width), BF16),
            ((1, rows), F32),
            ((rows + EXTRA, half_width + group_width), BF16),
        ],
        raws,
        grads,
        factors,
        deltas,
        keys,
        query,
        cot,
        far_keys,
        far_grads,
        cosine,
        sine,
        flops=4 * 10**6,
        scratch=[
            pltpu.VMEM((half_groups, 2 * rows, 2 * wide), BF16),
            pltpu.VMEM((half_groups, 2 * rows, 2 * wide), BF16),
            pltpu.VMEM((2, rows, group_width), F32),
            pltpu.VMEM((half_groups, DH, 2 * wide), F32),
            pltpu.VMEM((2 * wide, DH), F32),
        ],
    )
    back = lax.ppermute(theirs, "ctx", swap)
    total = ((rows, group_width // 2), F32)
    value_own, value_other = call(
        sum_first_kernel,
        "sum_first",
        [total, total],
        part_mine,
        *[part for pair in zip(sib_value_got, own_value_got) for part in pair],
        flops=5 * 10**9,
    )
    key_own, key_other = call(
        sum_rest_kernel,
        "sum_rest",
        [total, total],
        value_own,
        part_mine,
        *[part for pair in zip(sib_key_got, own_key_got) for part in pair],
        flops=5 * 10**9,
    )
    query_grad, key_grad, value_grad, gate_grad = call(
        functools.partial(finish_kernel, limit=limit),
        "finish",
        [((rows, heads_width), BF16)] + [((rows, group_width), BF16)] * 2 + [line],
        back,
        query_mine,
        gate_part,
        key_own,
        value_own,
        key_other,
        value_other,
        positions,
        cosine,
        sine,
    )
    return (query_grad[None], key_grad[None], value_grad[None], gate_grad)


def solution(mesh):
    wide = P(("group", "dp"), "ctx", None)
    narrow = P(("group", "dp"), "ctx")
    return jax.shard_map(
        per_device,
        mesh=mesh,
        in_specs=(wide, wide, wide, wide, narrow, narrow),
        out_specs=(wide, wide, wide, narrow),
        check_vma=False,
    )
```

```python
import functools
import math

import jax
import jax.numpy as jnp
import numpy as np
from jax import lax
from jax.experimental import pallas as pl
from jax.experimental.pallas import tpu as pltpu
from jax.sharding import PartitionSpec as P

DH = 128
LOCAL = 1024
THETA = 500000.0
EXTRA = 16
HIDDEN = -1e30
UNUSED = 2.0**14
SCALE = DH**-0.5
LOG2E = math.log2(math.e)
LN2 = math.log(2.0)

NT = (((1,), (1,)), ((), ()))
NN = (((1,), (0,)), ((), ()))
TN = (((0,), (0,)), ((), ()))
F32 = jnp.float32
BF16 = jnp.bfloat16


def few_bits(value, bits):
    unit = 2.0 ** (math.floor(math.log2(value)) + 1 - bits)
    return math.floor(value / unit) * unit


QUARTER_1 = few_bits(math.pi / 2, 10)
QUARTER_2 = few_bits(math.pi / 2 - QUARTER_1, 10)
QUARTER_3 = math.pi / 2 - QUARTER_1 - QUARTER_2


def dot(a, b, dims):
    return lax.dot_general(a, b, dims, preferred_element_type=F32)


def core_of():
    return lax.rem(lax.axis_index("ctx"), 2)


def rotate(values, cosine, sine):
    return values * cosine + pltpu.roll(values, DH // 2, 1) * sine


def sine_cosine(angle):
    turns = jnp.floor(angle * (2.0 / math.pi) + 0.5)
    rest = ((angle - turns * QUARTER_1) - turns * QUARTER_2) - turns * QUARTER_3
    square = rest * rest
    sine = ((-1.9515295891e-4 * square + 8.3321608736e-3) * square - 1.6666654611e-1) * square * rest + rest
    cosine = (2.443315711809948e-5 * square - 1.388731625493765e-3) * square + 4.166664568298827e-2
    cosine = cosine * square * square - 0.5 * square + 1.0
    quarter = turns.astype(jnp.int32)
    odd = (quarter & 1) == 1
    first, second = jnp.where(odd, cosine, sine), jnp.where(odd, sine, cosine)
    return (
        jnp.where((quarter & 2) == 2, -first, first),
        jnp.where(((quarter + 1) & 2) == 2, -second, second),
    )


def split_rows(row, height):
    high = row.astype(BF16).astype(F32)
    middle = (row - high).astype(BF16).astype(F32)
    low = row - high - middle
    line = lax.broadcasted_iota(jnp.int32, (height, row.shape[1]), 0)
    rows = jnp.where(line == 0, high, jnp.where(line == 1, middle, jnp.where(line == 2, low, 0.0)))
    return rows.astype(BF16)


def joined_row(rows):
    return jnp.sum(rows.astype(F32), axis=0, keepdims=True)


def pack_kernel(
    key_in, value_in, query_in, cot_in, gate_in, pos_in, freq_in,
    key_mine, key_theirs, value_mine, value_theirs, theirs, gate_mine, valid, cos_ref, sin_ref,
    key, value, query, gate, pos, freq, sems, *, limit
):
    rows, width = key.shape
    side_width = width // 2
    half = query.shape[1]
    core = core_of()
    there = pl.ds(pl.multiple_of((1 - core) * half, DH), half)
    loads = [(pos_in, pos), (freq_in, freq), (key_in, key), (value_in, value), (query_in.at[:, there], query)]
    loads += [(gate_in, gate), (cot_in.at[:, there], theirs.at[:rows, half : 2 * half])]
    loads = [pltpu.make_async_copy(source, target, sems.at[i]) for i, (source, target) in enumerate(loads)]
    for copy in loads:
        copy.start()
    down = lax.broadcasted_iota(jnp.int32, (rows, rows), 0)
    along = lax.broadcasted_iota(jnp.int32, (rows, rows), 1)
    lane = lax.broadcasted_iota(jnp.int32, (rows, DH), 1)
    loads[0].wait()
    loads[1].wait()
    places = pos[...]
    column = jnp.sum(jnp.where(down == along, places.astype(F32), 0.0), axis=1, keepdims=True)
    sine, cosine = sine_cosine(column * freq[...])
    sine = jnp.where(lane < DH // 2, -sine, sine)
    cos_ref[...] = cosine
    sin_ref[...] = sine
    used = jnp.broadcast_to(column, (rows, DH)) < limit
    loads[2].wait()
    loads[3].wait()
    for key_out, value_out, side in ((key_mine, value_mine, core), (key_theirs, value_theirs, 1 - core)):
        for i in range(side_width // DH):
            from_ = pl.ds(pl.multiple_of(side * side_width + i * DH, DH), DH)
            turned = jnp.where(used, rotate(key[:, from_].astype(F32), cosine, sine), UNUSED).astype(BF16)
            key_out[:, i * DH : (i + 1) * DH] = turned
            value_out[:, i * DH : (i + 1) * DH] = value[:, from_]
    theirs[:rows, 2 * half : 2 * half + side_width] = key_theirs[...]
    theirs[:rows, 2 * half + side_width :] = value_theirs[...]
    loads[4].wait()
    cosine, sine = cosine * (SCALE * LOG2E), sine * (SCALE * LOG2E)
    for i in range(half // DH):
        here = slice(i * DH, (i + 1) * DH)
        theirs[:rows, here] = rotate(query[:, here].astype(F32), cosine, sine).astype(BF16)
    loads[5].wait()
    valid[...] = jnp.where(places < limit, 1.0, 0.0)
    used_gate = jnp.where(places < limit, gate[...], 0.0)
    gate_mine[...] = used_gate
    theirs[rows:, :rows] = split_rows(used_gate, EXTRA)
    loads[6].wait()


def chosen(shape, ratio, dim):
    down = lax.broadcasted_iota(jnp.int32, shape, 0)
    along = lax.broadcasted_iota(jnp.int32, shape, 1)
    rows = shape[1 - dim]
    long, short = (down, along) if dim == 0 else (along, down)
    for _ in range(1, ratio):
        long = jnp.where(long >= rows, long - rows, long)
    return jnp.where(long == short, 1.0, 0.0).astype(BF16)


def chunks(low, high):
    return [slice(at, min(at + 256, high)) for at in range(low, high, 256)]


def used_slots(key, here):
    chip = lax.div(lax.axis_index("ctx"), 2)
    first = key[:, :DH].astype(F32)[:, :1]
    return jnp.broadcast_to(first, (key.shape[0], 256)) < jnp.where(chip >= here, UNUSED / 2, -UNUSED)


def local_kernel(
    key_mine, value_mine, query_in, cot_in, cos_ref, sin_ref, gate_mine, sib,
    keys, query, cot, gate, raws, grads, tops, sums, crosses, values, *, ratio
):
    rows = key_mine.shape[0]
    half_groups = keys.shape[0]
    wide = ratio * rows
    half = half_groups * ratio * DH
    core = core_of()
    spread = chosen((rows, wide), ratio, 1)
    key_sib = sib.at[:rows, 2 * half : 2 * half + half_groups * DH]
    value_sib = sib.at[:rows, 2 * half + half_groups * DH :]
    cosine, sine = cos_ref[...] * (SCALE * LOG2E), sin_ref[...] * (SCALE * LOG2E)
    for key, value, side in ((key_mine, value_mine, core), (key_sib, value_sib, 1 - core)):
        there = pl.ds(pl.multiple_of(side * rows, 16), rows)
        for i in range(half_groups):
            keys[i, there, :] = key[:, i * DH : (i + 1) * DH]
            values[i, there, :] = value[:, i * DH : (i + 1) * DH]
            for h in range(ratio):
                to = pl.ds(pl.multiple_of(side * wide + h * rows, 16), rows)
                at = (i * ratio + h) * DH
                if key is key_mine:
                    here = pl.ds(pl.multiple_of(core * half + at, DH), DH)
                    query[i, to, :] = rotate(query_in[:, here].astype(F32), cosine, sine).astype(BF16)
                    cot[i, to, :] = cot_in[:, here]
                else:
                    query[i, to, :] = sib[:rows, at : at + DH]
                    cot[i, to, :] = sib[:rows, half + at : half + at + DH]
    own = joined_row(dot(split_rows(gate_mine[...], EXTRA), spread, NN))
    other = joined_row(dot(sib[rows:, :rows], spread, NN))
    gate[:, :wide] = jnp.where(core == 0, own, other)
    gate[:, wide:] = jnp.where(core == 0, other, own)
    used = used_slots(keys[0, :rows, :], 0)
    for i in range(half_groups):
        for block in range(2):
            reach = (block + 1) * rows
            for here in chunks(block * wide, (block + 1) * wide):
                width = here.stop - here.start
                scores = dot(keys[i, :reach, :], query[i, here, :], NT)
                slot = lax.broadcasted_iota(jnp.int32, (rows, width), 0)
                lane = lax.broadcasted_iota(jnp.int32, (rows, width), 1) + (here.start - block * wide)
                for h in range(1, ratio):
                    lane = jnp.where(lane >= rows, lane - rows, lane)
                shown = jnp.where(slot <= lane, scores[block * rows :], HIDDEN)
                if block:
                    before = jnp.where(used[:, :width], scores[:rows], HIDDEN)
                    shown = jnp.concatenate([before, shown], axis=0)
                top = jnp.max(shown, axis=0, keepdims=True)
                raw = jnp.exp2(shown - top)
                prob_grad = dot(values[i, :reach, :], cot[i, here, :], NT)
                raws[i, :reach, here] = raw
                grads[i, :reach, here] = prob_grad
                tops[i, :, here] = top
                sums[i, :, here] = jnp.sum(raw, axis=0, keepdims=True)
                crosses[i, :, here] = jnp.sum(raw * prob_grad, axis=0, keepdims=True)


def part_of(weights, score_grads, query, cot, out_ref, i, there, lanes):
    key_part = dot(score_grads[i, there, lanes], query[i, lanes, :], NN) * LN2
    value_part = dot(weights[i, there, lanes], cot[i, lanes, :], NN)
    out_ref[:, 2 * i * DH : (2 * i + 1) * DH] = key_part.astype(out_ref.dtype)
    out_ref[:, (2 * i + 1) * DH : (2 * i + 2) * DH] = value_part.astype(out_ref.dtype)


def early_kernel(query, tops, sums, packet, raws, new_tops, new_sums):
    half_groups, lanes = query.shape[:2]
    alone = lax.axis_index("ctx") < 2

    @pl.when(alone)
    def _():
        new_tops[...] = tops[...]
        new_sums[...] = sums[...]

    @pl.when(jnp.logical_not(alone))
    def _():
        used = used_slots(packet, 1)
        for i in range(half_groups):
            key = packet[:, i * DH : (i + 1) * DH]
            for here in chunks(0, lanes):
                width = here.stop - here.start
                shown = jnp.where(used[:, :width], dot(key, query[i, here, :], NT), HIDDEN)
                old_top = tops[i, :, here]
                top = jnp.maximum(old_top, jnp.max(shown, axis=0, keepdims=True))
                raw = jnp.exp2(shown - top)
                raws[i, :, here] = raw
                new_tops[i, :, here] = top
                new_sums[i, :, here] = sums[i, :, here] * jnp.exp2(old_top - top) + jnp.sum(raw, axis=0, keepdims=True)


def far_keys_kernel(query, cot, gate, first_tops, early_raws, tops, sums, *refs, blocks):
    packets = refs[:blocks]
    far_keys, raws, factors, far_factors, shrinks, inverses = refs[blocks : blocks + 6]
    parts, weights = refs[blocks + 6 : -1], refs[-1]
    rows = packets[0].shape[0]
    half_groups, lanes = query.shape[:2]
    alone = lax.axis_index("ctx") < 2

    @pl.when(alone)
    def _():
        for i in range(half_groups):
            inverse = 1.0 / sums[i]
            factors[i] = inverse * gate[...]
            inverses[i] = inverse

    @pl.when(jnp.logical_not(alone))
    def _():
        for i in range(half_groups):
            for j, packet in enumerate(packets):
                far_keys[i, j * rows : (j + 1) * rows, :] = packet[:, i * DH : (i + 1) * DH]
        used = [used_slots(packets[j], j % (blocks // 2) + 1) for j in range(1, blocks)]
        for i in range(half_groups):
            for here in chunks(0, lanes):
                width = here.stop - here.start
                scores = dot(far_keys[i, rows:, :], query[i, here, :], NT)
                shown = [
                    jnp.where(used[j][:, :width], scores[j * rows : (j + 1) * rows], HIDDEN)
                    for j in range(blocks - 1)
                ]
                shown = jnp.concatenate(shown, axis=0)
                old_top = tops[i, :, here]
                top = jnp.maximum(old_top, jnp.max(shown, axis=0, keepdims=True))
                raw = jnp.exp2(shown - top)
                shrink = jnp.exp2(old_top - top)
                first_shrink = jnp.exp2(first_tops[i, :, here] - top)
                inverse = 1.0 / (sums[i, :, here] * shrink + jnp.sum(raw, axis=0, keepdims=True))
                factor = inverse * gate[:, here]
                factors[i, :, here] = factor * first_shrink
                far_factors[i, :, here] = factor
                shrinks[i, :, here] = first_shrink
                inverses[i, :, here] = inverse
                raws[i, rows:, here] = raw.astype(raws.dtype)
                weights[i, rows:, here] = (raw * factor).astype(BF16)
                raw = early_raws[i, :, here] * shrink
                raws[i, :rows, here] = raw.astype(raws.dtype)
                weights[i, :rows, here] = (raw * factor).astype(BF16)
            for j, out_ref in enumerate(parts):
                there = slice(j * rows, (j + 1) * rows)
                out_ref[:, i * DH : (i + 1) * DH] = dot(weights[i, there, :], cot[i], NN).astype(BF16)


def far_values_kernel(query, cot, raws, far_factors, shrinks, inverses, crosses, *refs, blocks):
    packets = refs[:blocks]
    score_grads, deltas = refs[blocks : blocks + 2]
    parts, far_values = refs[blocks + 2 : -1], refs[-1]
    rows = packets[0].shape[0]
    half_groups, lanes = query.shape[:2]
    alone = lax.axis_index("ctx") < 2

    @pl.when(alone)
    def _():
        for i in range(half_groups):
            deltas[i] = crosses[i] * inverses[i]

    @pl.when(jnp.logical_not(alone))
    def _():
        for i in range(half_groups):
            for j, packet in enumerate(packets):
                far_values[i, j * rows : (j + 1) * rows, :] = packet[:, i * DH : (i + 1) * DH]
        for i in range(half_groups):
            for here in chunks(0, lanes):
                raw = raws[i, :, here].astype(F32)
                prob_grad = dot(far_values[i], cot[i, here, :], NT)
                cross = jnp.sum(raw * prob_grad, axis=0, keepdims=True)
                delta = (crosses[i, :, here] * shrinks[i, :, here] + cross) * inverses[i, :, here]
                deltas[i, :, here] = delta
                score_grad = raw * far_factors[i, :, here] * (prob_grad - delta)
                score_grads[i, :, here] = score_grad.astype(BF16)
            for j, out_ref in enumerate(parts):
                there = slice(j * rows, (j + 1) * rows)
                part = dot(score_grads[i, there, :], query[i], NN) * LN2
                out_ref[:, i * DH : (i + 1) * DH] = part.astype(BF16)


def near_kernel(
    raws, grads, factors, deltas, keys, query, cot, far_keys, far_grads, cos_ref, sin_ref,
    part_mine, query_mine, gate_mine, theirs, weights, score_grads, parts, acc, turned,
    *, ratio
):
    rows = part_mine.shape[0]
    half_groups = keys.shape[0]
    wide = ratio * rows
    half = half_groups * ratio * DH
    for i in range(half_groups):
        for block in range(2):
            reach = (block + 1) * rows
            for here in chunks(block * wide, (block + 1) * wide):
                gated = raws[i, :reach, here] * factors[i, :, here]
                weights[i, :reach, here] = gated.astype(BF16)
                score_grads[i, :reach, here] = (gated * (grads[i, :reach, here] - deltas[i, :, here])).astype(BF16)
        for block in range(2):
            there, lanes = slice(block * rows, (block + 1) * rows), slice(block * wide, 2 * wide)
            part_of(weights, score_grads, query, cot, parts.at[block], i, there, lanes)
            reach, lanes = (block + 1) * rows, slice(block * wide, (block + 1) * wide)
            acc[i, :, lanes] = dot(keys[i, :reach, :], score_grads[i, :reach, lanes], TN)

    @pl.when(lax.axis_index("ctx") >= 2)
    def _():
        for i in range(half_groups):
            acc[i] += dot(far_keys[i], far_grads[i], TN)

    core = core_of()
    cosine, sine = cos_ref[...], -sin_ref[...]
    for i in range(half_groups):
        turned[...] = jnp.transpose(acc[i] * SCALE)
        for h in range(ratio):
            here = slice((i * ratio + h) * DH, (i * ratio + h + 1) * DH)
            own = turned[pl.ds(pl.multiple_of(core * wide + h * rows, 16), rows), :]
            query_mine[:, here] = rotate(own, cosine, sine).astype(BF16)
            other = turned[pl.ds(pl.multiple_of((1 - core) * wide + h * rows, 16), rows), :]
            theirs[:rows, here] = other.astype(BF16)
    part_mine[...] = parts[core]
    theirs[:rows, half:] = parts[1 - core].astype(BF16)
    summed = deltas[0]
    for i in range(1, half_groups):
        summed = summed + deltas[i]
    gates = []
    for block in range(2):
        own = split_rows(summed[:, block * wide : (block + 1) * wide], 16)
        gates.append(joined_row(dot(own, chosen((wide, rows), ratio, 0), NN)))
    gate_mine[...] = jnp.where(core == 0, gates[0], gates[1])
    theirs[rows:, :rows] = split_rows(jnp.where(core == 0, gates[1], gates[0]), EXTRA)


def sum_first_kernel(part_mine, *refs):
    got, (own, other) = refs[:-2], refs[-2:]
    total = got[0][...].astype(F32)
    for ref in got[2::2]:
        total = total + ref[...].astype(F32)
    other[...] = total
    for i in range(own.shape[1] // DH):
        here = slice(i * DH, (i + 1) * DH)
        value = part_mine[:, (2 * i + 1) * DH : (2 * i + 2) * DH]
        for ref in got[1::2]:
            value = value + ref[:, here].astype(F32)
        own[:, here] = value


def sum_rest_kernel(value_own, part_mine, *refs):
    got, (own, other) = refs[:-2], refs[-2:]
    total = got[0][...].astype(F32)
    for ref in got[2::2]:
        total = total + ref[...].astype(F32)
    other[...] = total
    for i in range(own.shape[1] // DH):
        here = slice(i * DH, (i + 1) * DH)
        key = part_mine[:, 2 * i * DH : (2 * i + 1) * DH]
        for ref in got[1::2]:
            key = key + ref[:, here].astype(F32)
        own[:, here] = key


def finish_kernel(
    back, query_mine, gate_mine, key_own, value_own, key_other, value_other, valid, cos_ref, sin_ref,
    query_grad, key_grad, value_grad, gate_grad
):
    rows, half = value_own.shape
    wide = query_mine.shape[1]
    core = core_of()
    side = lambda which, width, at=0, size=None: pl.ds(pl.multiple_of(which * width + at, DH), size or width)
    cosine, sine = cos_ref[...], -sin_ref[...]
    for i in range(half // DH):
        here = slice(i * DH, (i + 1) * DH)
        there = wide + 2 * i * DH
        other_key = key_other[:, here] + back[:rows, there : there + DH].astype(F32)
        other_value = value_other[:, here] + back[:rows, there + DH : there + 2 * DH].astype(F32)
        for key_sum, value_sum, which in (
            (key_own[:, here], value_own[:, here], core),
            (other_key, other_value, 1 - core),
        ):
            to = side(which, half, i * DH, DH)
            key_grad[:, to] = rotate(key_sum, cosine, sine).astype(BF16)
            value_grad[:, to] = value_sum.astype(BF16)
    query_grad[:, side(core, wide)] = query_mine[...]
    for i in range(wide // DH):
        turned = rotate(back[:rows, i * DH : (i + 1) * DH].astype(F32), cosine, sine)
        query_grad[:, side(1 - core, wide, i * DH, DH)] = turned.astype(BF16)
    gate = gate_mine[...] + joined_row(back[rows:, :rows])
    gate_grad[...] = jnp.where(valid[...] > 0.0, gate, 0.0)


def per_device(query_rows, key_rows, value_rows, cotangent, router_gate, positions):
    rows, heads_width = query_rows.shape[1:]
    group_width = key_rows.shape[2]
    groups = group_width // DH
    ratio = heads_width // group_width
    half_groups, half_width = groups // 2, heads_width // 2
    parts = lax.axis_size("ctx")
    chips = parts // 2
    limit = parts * LOCAL
    wide = ratio * rows
    params = pltpu.CompilerParams(vmem_limit_bytes=(16 + 4 * chips) * 1024 * 1024)

    def call(kernel, name, outs, *args, scratch=(), flops=10**6, in_hbm=False):
        if in_hbm:
            args = [pltpu.with_memory_space_constraint(arg, pltpu.HBM) for arg in args]
        spec = pl.BlockSpec(memory_space=pltpu.HBM if in_hbm else pltpu.VMEM)
        return pl.pallas_call(
            kernel,
            out_shape=[jax.ShapeDtypeStruct(*out) for out in outs],
            in_specs=[spec] * len(args),
            scratch_shapes=list(scratch),
            compiler_params=params,
            cost_estimate=pl.CostEstimate(flops=flops, bytes_accessed=1000, transcendentals=0),
            name=name,
        )(*args)

    index = np.arange(DH) % (DH // 2)
    freq = jnp.asarray((THETA ** (-2.0 * index / DH)).astype(np.float32))[None]
    packet = ((rows, group_width // 2), BF16)
    table = ((rows, DH), F32)
    line = ((1, rows), F32)
    theirs_shape = ((rows + EXTRA, heads_width + group_width), BF16)
    key_mine, key_theirs, value_mine, value_theirs, theirs, gate_mine, valid, cosine, sine = call(
        functools.partial(pack_kernel, limit=limit),
        "pack",
        [packet, packet, packet, packet, theirs_shape, line, line, table, table],
        key_rows[0],
        value_rows[0],
        query_rows[0],
        cotangent[0],
        router_gate,
        positions,
        freq,
        in_hbm=True,
        flops=5 * 10**9,
        scratch=[
            pltpu.VMEM((rows, group_width), BF16),
            pltpu.VMEM((rows, group_width), BF16),
            pltpu.VMEM((rows, half_width), BF16),
            pltpu.VMEM(*line),
            pltpu.VMEM((1, rows), jnp.int32),
            pltpu.VMEM((1, DH), F32),
            pltpu.SemaphoreType.DMA((7,)),
        ],
    )

    hop = [[(2 * x + k, 2 * (x + s) + k) for x in range(chips - s) for k in range(2)] for s in range(chips)]
    cross = [[(a, b + 1 - 2 * (b % 2)) for a, b in pairs] for pairs in hop]
    back_hop = [[(b, a) for a, b in pairs] for pairs in hop]
    back_cross = [[(b, a) for a, b in pairs] for pairs in cross]

    steps = range(1, chips)

    def send(sib, own, sib_pairs, own_pairs):
        sib = [lax.ppermute(sib[s - 1], "ctx", sib_pairs[s]) for s in steps]
        return sib, [lax.ppermute(own[s - 1], "ctx", own_pairs[s]) for s in steps]

    sib_keys, own_keys = send([key_theirs] * chips, [key_mine] * chips, cross, hop)
    sib_values, own_values = send([value_theirs] * chips, [value_mine] * chips, cross, hop)

    pairs = [[2 * x, 2 * x + 1] for x in range(chips)]
    swap = [pair for a, b in pairs for pair in ((a, b), (b, a))]
    sib = lax.ppermute(theirs, "ctx", swap)

    row = ((half_groups, 1, 2 * wide), F32)
    table = ((half_groups, 2 * rows, 2 * wide), F32)
    kv_table = ((half_groups, 2 * rows, DH), BF16)
    q_table = ((half_groups, 2 * wide, DH), BF16)
    keys, query, cot, gate_row, raws, grads, tops, sums, crosses = call(
        functools.partial(local_kernel, ratio=ratio),
        "local_scores",
        [kv_table, q_table, q_table, ((1, 2 * wide), F32), table, table, row, row, row],
        key_mine,
        value_mine,
        query_rows[0],
        cotangent[0],
        cosine,
        sine,
        gate_mine,
        sib,
        scratch=[pltpu.VMEM(*kv_table)],
        flops=3 * 10**6,
    )

    blocks = 2 * (chips - 1)
    far_rows = ((half_groups, blocks * rows, DH), BF16)
    far_low = ((half_groups, blocks * rows, 2 * wide), BF16)
    far_table = (far_low[0], F32 if chips == 2 else BF16)
    early_table = ((half_groups, rows, 2 * wide), F32)
    early_raws, early_tops, early_sums = call(
        early_kernel, "early_keys", [early_table, row, row], query, tops, sums, sib_keys[0]
    )
    far_keys, far_raws, factors, far_factors, shrinks, inverses, *parts = call(
        functools.partial(far_keys_kernel, blocks=blocks),
        "far_keys",
        [far_rows, far_table, row, row, row, row] + [packet] * blocks,
        query,
        cot,
        gate_row,
        tops,
        early_raws,
        early_tops,
        early_sums,
        *sib_keys,
        *own_keys,
        scratch=[pltpu.VMEM(*far_low)],
    )
    sib_value_got, own_value_got = send(parts[: chips - 1], parts[chips - 1 :], back_cross, back_hop)
    far_grads, deltas, *parts = call(
        functools.partial(far_values_kernel, blocks=blocks),
        "far_values",
        [far_low, row] + [packet] * blocks,
        query,
        cot,
        far_raws,
        far_factors,
        shrinks,
        inverses,
        crosses,
        *sib_values,
        *own_values,
        scratch=[pltpu.VMEM(*far_rows)],
    )
    sib_key_got, own_key_got = send(parts[: chips - 1], parts[chips - 1 :], back_cross, back_hop)

    part_mine, query_mine, gate_part, theirs = call(
        functools.partial(near_kernel, ratio=ratio),
        "near_grads",
        [
            ((rows, group_width), F32),
            ((rows, half_width), BF16),
            ((1, rows), F32),
            ((rows + EXTRA, half_width + group_width), BF16),
        ],
        raws,
        grads,
        factors,
        deltas,
        keys,
        query,
        cot,
        far_keys,
        far_grads,
        cosine,
        sine,
        flops=4 * 10**6,
        scratch=[
            pltpu.VMEM((half_groups, 2 * rows, 2 * wide), BF16),
            pltpu.VMEM((half_groups, 2 * rows, 2 * wide), BF16),
            pltpu.VMEM((2, rows, group_width), F32),
            pltpu.VMEM((half_groups, DH, 2 * wide), F32),
            pltpu.VMEM((2 * wide, DH), F32),
        ],
    )
    back = lax.ppermute(theirs, "ctx", swap)
    total = ((rows, group_width // 2), F32)
    value_own, value_other = call(
        sum_first_kernel,
        "sum_first",
        [total, total],
        part_mine,
        *[part for pair in zip(sib_value_got, own_value_got) for part in pair],
        flops=5 * 10**9,
    )
    key_own, key_other = call(
        sum_rest_kernel,
        "sum_rest",
        [total, total],
        value_own,
        part_mine,
        *[part for pair in zip(sib_key_got, own_key_got) for part in pair],
        flops=5 * 10**9,
    )
    query_grad, key_grad, value_grad, gate_grad = call(
        finish_kernel,
        "finish",
        [((rows, heads_width), BF16)] + [((rows, group_width), BF16)] * 2 + [line],
        back,
        query_mine,
        gate_part,
        key_own,
        value_own,
        key_other,
        value_other,
        valid,
        cosine,
        sine,
    )
    return (query_grad[None], key_grad[None], value_grad[None], gate_grad)


def solution(mesh):
    wide = P(("group", "dp"), "ctx", None)
    narrow = P(("group", "dp"), "ctx")
    return jax.shard_map(
        per_device,
        mesh=mesh,
        in_specs=(wide, wide, wide, wide, narrow, narrow),
        out_specs=(wide, wide, wide, narrow),
        check_vma=False,
    )
```

```python
import functools
import math

import jax
import jax.numpy as jnp
import numpy as np
from jax import lax
from jax.experimental import pallas as pl
from jax.experimental.pallas import tpu as pltpu
from jax.sharding import PartitionSpec as P

DH = 128
LOCAL = 1024
THETA = 500000.0
EXTRA = 16
HIDDEN = -1e30
UNUSED = 2.0**14
SCALE = DH**-0.5
LOG2E = math.log2(math.e)
LN2 = math.log(2.0)
FAR_COST = 5 * 10**9

NT = (((1,), (1,)), ((), ()))
NN = (((1,), (0,)), ((), ()))
TN = (((0,), (0,)), ((), ()))
F32 = jnp.float32
BF16 = jnp.bfloat16


def few_bits(value, bits):
    unit = 2.0 ** (math.floor(math.log2(value)) + 1 - bits)
    return math.floor(value / unit) * unit


QUARTER_1 = few_bits(math.pi / 2, 10)
QUARTER_2 = few_bits(math.pi / 2 - QUARTER_1, 10)
QUARTER_3 = math.pi / 2 - QUARTER_1 - QUARTER_2


def dot(a, b, dims):
    return lax.dot_general(a, b, dims, preferred_element_type=F32)


def core_of():
    return lax.rem(lax.axis_index("ctx"), 2)


def rotate(values, cosine, sine):
    return values * cosine + pltpu.roll(values, DH // 2, 1) * sine


def sine_cosine(angle):
    turns = jnp.floor(angle * (2.0 / math.pi) + 0.5)
    rest = ((angle - turns * QUARTER_1) - turns * QUARTER_2) - turns * QUARTER_3
    square = rest * rest
    sine = ((-1.9515295891e-4 * square + 8.3321608736e-3) * square - 1.6666654611e-1) * square * rest + rest
    cosine = (2.443315711809948e-5 * square - 1.388731625493765e-3) * square + 4.166664568298827e-2
    cosine = cosine * square * square - 0.5 * square + 1.0
    quarter = turns.astype(jnp.int32)
    odd = (quarter & 1) == 1
    first, second = jnp.where(odd, cosine, sine), jnp.where(odd, sine, cosine)
    return (
        jnp.where((quarter & 2) == 2, -first, first),
        jnp.where(((quarter + 1) & 2) == 2, -second, second),
    )


def split_rows(row, height):
    high = row.astype(BF16).astype(F32)
    middle = (row - high).astype(BF16).astype(F32)
    low = row - high - middle
    line = lax.broadcasted_iota(jnp.int32, (height, row.shape[1]), 0)
    rows = jnp.where(line == 0, high, jnp.where(line == 1, middle, jnp.where(line == 2, low, 0.0)))
    return rows.astype(BF16)


def joined_row(rows):
    return jnp.sum(rows.astype(F32), axis=0, keepdims=True)


def pack_kernel(
    key_in, value_in, query_in, cot_in, gate_in, pos_in, freq_in,
    key_mine, key_theirs, value_mine, value_theirs, theirs, gate_mine, valid, cos_ref, sin_ref,
    key, value, query, gate, pos, freq, sems, *, limit
):
    rows, width = key.shape
    side_width = width // 2
    half = query.shape[1]
    core = core_of()
    there = pl.ds(pl.multiple_of((1 - core) * half, DH), half)
    loads = [(pos_in, pos), (freq_in, freq), (key_in, key), (value_in, value), (query_in.at[:, there], query)]
    loads += [(gate_in, gate), (cot_in.at[:, there], theirs.at[:rows, half : 2 * half])]
    loads = [pltpu.make_async_copy(source, target, sems.at[i]) for i, (source, target) in enumerate(loads)]
    for copy in loads:
        copy.start()
    down = lax.broadcasted_iota(jnp.int32, (rows, rows), 0)
    along = lax.broadcasted_iota(jnp.int32, (rows, rows), 1)
    lane = lax.broadcasted_iota(jnp.int32, (rows, DH), 1)
    loads[0].wait()
    loads[1].wait()
    places = pos[...]
    column = jnp.sum(jnp.where(down == along, places.astype(F32), 0.0), axis=1, keepdims=True)
    sine, cosine = sine_cosine(column * freq[...])
    sine = jnp.where(lane < DH // 2, -sine, sine)
    cos_ref[...] = cosine
    sin_ref[...] = sine
    used = jnp.broadcast_to(column, (rows, DH)) < limit
    loads[2].wait()
    loads[3].wait()
    for key_out, value_out, side in ((key_mine, value_mine, core), (key_theirs, value_theirs, 1 - core)):
        for i in range(side_width // DH):
            from_ = pl.ds(pl.multiple_of(side * side_width + i * DH, DH), DH)
            turned = jnp.where(used, rotate(key[:, from_].astype(F32), cosine, sine), UNUSED).astype(BF16)
            key_out[:, i * DH : (i + 1) * DH] = turned
            value_out[:, i * DH : (i + 1) * DH] = value[:, from_]
    theirs[:rows, 2 * half : 2 * half + side_width] = key_theirs[...]
    theirs[:rows, 2 * half + side_width :] = value_theirs[...]
    loads[4].wait()
    cosine, sine = cosine * (SCALE * LOG2E), sine * (SCALE * LOG2E)
    for i in range(half // DH):
        here = slice(i * DH, (i + 1) * DH)
        theirs[:rows, here] = rotate(query[:, here].astype(F32), cosine, sine).astype(BF16)
    loads[5].wait()
    valid[...] = jnp.where(places < limit, 1.0, 0.0)
    used_gate = jnp.where(places < limit, gate[...], 0.0)
    gate_mine[...] = used_gate
    theirs[rows:, :rows] = split_rows(used_gate, EXTRA)
    loads[6].wait()


def chosen(shape, ratio, dim):
    down = lax.broadcasted_iota(jnp.int32, shape, 0)
    along = lax.broadcasted_iota(jnp.int32, shape, 1)
    rows = shape[1 - dim]
    long, short = (down, along) if dim == 0 else (along, down)
    for _ in range(1, ratio):
        long = jnp.where(long >= rows, long - rows, long)
    return jnp.where(long == short, 1.0, 0.0).astype(BF16)


def chunks(low, high):
    return [slice(at, min(at + 256, high)) for at in range(low, high, 256)]


def used_slots(key, here):
    chip = lax.div(lax.axis_index("ctx"), 2)
    first = key[:, :DH].astype(F32)[:, :1]
    return jnp.broadcast_to(first, (key.shape[0], 256)) < jnp.where(chip >= here, UNUSED / 2, -UNUSED)


def local_kernel(
    key_mine, value_mine, value_theirs, query_in, cot_in, cos_ref, sin_ref, gate_mine, sib,
    send_mine, send_theirs, keys, values, query, cot, gate, raws, tops, sums, crosses, *, ratio
):
    rows = key_mine.shape[0]
    half_groups = keys.shape[0]
    wide = ratio * rows
    half = half_groups * ratio * DH
    core = core_of()
    send_mine[...] = value_mine[...]
    send_theirs[...] = value_theirs[...]
    spread = chosen((rows, wide), ratio, 1)
    key_sib = sib.at[:rows, 2 * half : 2 * half + half_groups * DH]
    value_sib = sib.at[:rows, 2 * half + half_groups * DH :]
    cosine, sine = cos_ref[...] * (SCALE * LOG2E), sin_ref[...] * (SCALE * LOG2E)
    for key, value, side in ((key_mine, value_mine, core), (key_sib, value_sib, 1 - core)):
        there = pl.ds(pl.multiple_of(side * rows, 16), rows)
        for i in range(half_groups):
            keys[i, there, :] = key[:, i * DH : (i + 1) * DH]
            values[i, there, :] = value[:, i * DH : (i + 1) * DH]
            for h in range(ratio):
                to = pl.ds(pl.multiple_of(side * wide + h * rows, 16), rows)
                at = (i * ratio + h) * DH
                if key is key_mine:
                    here = pl.ds(pl.multiple_of(core * half + at, DH), DH)
                    query[i, to, :] = rotate(query_in[:, here].astype(F32), cosine, sine).astype(BF16)
                    cot[i, to, :] = cot_in[:, here]
                else:
                    query[i, to, :] = sib[:rows, at : at + DH]
                    cot[i, to, :] = sib[:rows, half + at : half + at + DH]
    own = joined_row(dot(split_rows(gate_mine[...], EXTRA), spread, NN))
    other = joined_row(dot(sib[rows:, :rows], spread, NN))
    gate[:, :wide] = jnp.where(core == 0, own, other)
    gate[:, wide:] = jnp.where(core == 0, other, own)
    used = used_slots(keys[0, :rows, :], 0)
    for i in range(half_groups):
        for block in range(2):
            reach = (block + 1) * rows
            for here in chunks(block * wide, (block + 1) * wide):
                width = here.stop - here.start
                scores = dot(keys[i, :reach, :], query[i, here, :], NT)
                slot = lax.broadcasted_iota(jnp.int32, (rows, width), 0)
                lane = lax.broadcasted_iota(jnp.int32, (rows, width), 1) + (here.start - block * wide)
                for h in range(1, ratio):
                    lane = jnp.where(lane >= rows, lane - rows, lane)
                shown = jnp.where(slot <= lane, scores[block * rows :], HIDDEN)
                if block:
                    before = jnp.where(used[:, :width], scores[:rows], HIDDEN)
                    shown = jnp.concatenate([before, shown], axis=0)
                top = jnp.max(shown, axis=0, keepdims=True)
                raw = jnp.exp2(shown - top)
                raws[i, :reach, here] = raw
                tops[i, :, here] = top
                sums[i, :, here] = jnp.sum(raw, axis=0, keepdims=True)

    @pl.when(lax.axis_index("ctx") >= 2)
    def _():
        for i in range(half_groups):
            for block in range(2):
                reach = (block + 1) * rows
                for here in chunks(block * wide, (block + 1) * wide):
                    prob_grad = dot(values[i, :reach, :], cot[i, here, :], NT)
                    crosses[i, :, here] = jnp.sum(raws[i, :reach, here] * prob_grad, axis=0, keepdims=True)


def part_of(weights, score_grads, query, cot, out_ref, i, there, lanes):
    key_part = dot(score_grads[i, there, lanes], query[i, lanes, :], NN) * LN2
    value_part = dot(weights[i, there, lanes], cot[i, lanes, :], NN)
    out_ref[:, 2 * i * DH : (2 * i + 1) * DH] = key_part.astype(out_ref.dtype)
    out_ref[:, (2 * i + 1) * DH : (2 * i + 2) * DH] = value_part.astype(out_ref.dtype)


def far_keys_kernel(query, cot, gate, tops, sums, *refs, blocks):
    packets = refs[:blocks]
    far_keys, raws, factors, far_factors, shrinks, inverses = refs[blocks : blocks + 6]
    parts, weights = refs[blocks + 6 : -1], refs[-1]
    rows = packets[0].shape[0]
    half_groups, lanes = query.shape[:2]
    alone = lax.axis_index("ctx") < 2

    @pl.when(alone)
    def _():
        for i in range(half_groups):
            inverse = 1.0 / sums[i]
            factors[i] = inverse * gate[...]
            inverses[i] = inverse

    @pl.when(jnp.logical_not(alone))
    def _():
        for i in range(half_groups):
            for j, packet in enumerate(packets):
                far_keys[i, j * rows : (j + 1) * rows, :] = packet[:, i * DH : (i + 1) * DH]
        used = [used_slots(packet, j % (blocks // 2) + 1) for j, packet in enumerate(packets)]
        for i in range(half_groups):
            for here in chunks(0, lanes):
                width = here.stop - here.start
                scores = dot(far_keys[i], query[i, here, :], NT)
                shown = [
                    jnp.where(used[j][:, :width], scores[j * rows : (j + 1) * rows], HIDDEN) for j in range(blocks)
                ]
                shown = jnp.concatenate(shown, axis=0)
                old_top = tops[i, :, here]
                top = jnp.maximum(old_top, jnp.max(shown, axis=0, keepdims=True))
                raw = jnp.exp2(shown - top)
                shrink = jnp.exp2(old_top - top)
                inverse = 1.0 / (sums[i, :, here] * shrink + jnp.sum(raw, axis=0, keepdims=True))
                factor = inverse * gate[:, here]
                factors[i, :, here] = factor * shrink
                far_factors[i, :, here] = factor
                shrinks[i, :, here] = shrink
                inverses[i, :, here] = inverse
                raws[i, :, here] = raw.astype(raws.dtype)
                weights[i, :, here] = (raw * factor).astype(BF16)
            for j, out_ref in enumerate(parts):
                there = slice(j * rows, (j + 1) * rows)
                out_ref[:, i * DH : (i + 1) * DH] = dot(weights[i, there, :], cot[i], NN).astype(BF16)


def far_values_kernel(query, cot, raws, far_factors, shrinks, inverses, crosses, *refs, blocks):
    packets = refs[:blocks]
    score_grads, deltas = refs[blocks : blocks + 2]
    parts, far_values = refs[blocks + 2 : -1], refs[-1]
    rows = packets[0].shape[0]
    half_groups, lanes = query.shape[:2]

    @pl.when(lax.axis_index("ctx") >= 2)
    def _():
        for i in range(half_groups):
            for j, packet in enumerate(packets):
                far_values[i, j * rows : (j + 1) * rows, :] = packet[:, i * DH : (i + 1) * DH]
        for i in range(half_groups):
            for here in chunks(0, lanes):
                raw = raws[i, :, here].astype(F32)
                prob_grad = dot(far_values[i], cot[i, here, :], NT)
                cross = jnp.sum(raw * prob_grad, axis=0, keepdims=True)
                delta = (crosses[i, :, here] * shrinks[i, :, here] + cross) * inverses[i, :, here]
                deltas[i, :, here] = delta
                score_grad = raw * far_factors[i, :, here] * (prob_grad - delta)
                score_grads[i, :, here] = score_grad.astype(BF16)
            for j, out_ref in enumerate(parts):
                there = slice(j * rows, (j + 1) * rows)
                part = dot(score_grads[i, there, :], query[i], NN) * LN2
                out_ref[:, i * DH : (i + 1) * DH] = part.astype(BF16)


def near_kernel(
    raws, values, factors, inverses, far_deltas, keys, query, cot, far_keys, far_grads, cos_ref, sin_ref,
    part_mine, query_mine, gate_mine, theirs, weights, score_grads, parts, acc, turned, deltas,
    *, ratio
):
    rows = part_mine.shape[0]
    half_groups = keys.shape[0]
    wide = ratio * rows
    half = half_groups * ratio * DH
    alone = lax.axis_index("ctx") < 2
    for i in range(half_groups):
        for block in range(2):
            reach = (block + 1) * rows
            for here in chunks(block * wide, (block + 1) * wide):
                raw = raws[i, :reach, here]
                prob_grad = dot(values[i, :reach, :], cot[i, here, :], NT)
                delta = jnp.sum(raw * prob_grad, axis=0, keepdims=True) * inverses[i, :, here]
                delta = jnp.where(alone, delta, far_deltas[i, :, here])
                deltas[i, :, here] = delta
                gated = raw * factors[i, :, here]
                weights[i, :reach, here] = gated.astype(BF16)
                score_grads[i, :reach, here] = (gated * (prob_grad - delta)).astype(BF16)
        for block in range(2):
            there, lanes = slice(block * rows, (block + 1) * rows), slice(block * wide, 2 * wide)
            part_of(weights, score_grads, query, cot, parts.at[block], i, there, lanes)
            reach, lanes = (block + 1) * rows, slice(block * wide, (block + 1) * wide)
            acc[i, :, lanes] = dot(keys[i, :reach, :], score_grads[i, :reach, lanes], TN)

    @pl.when(lax.axis_index("ctx") >= 2)
    def _():
        for i in range(half_groups):
            acc[i] += dot(far_keys[i], far_grads[i], TN)

    core = core_of()
    cosine, sine = cos_ref[...], -sin_ref[...]
    for i in range(half_groups):
        turned[...] = jnp.transpose(acc[i] * SCALE)
        for h in range(ratio):
            here = slice((i * ratio + h) * DH, (i * ratio + h + 1) * DH)
            own = turned[pl.ds(pl.multiple_of(core * wide + h * rows, 16), rows), :]
            query_mine[:, here] = rotate(own, cosine, sine).astype(BF16)
            other = turned[pl.ds(pl.multiple_of((1 - core) * wide + h * rows, 16), rows), :]
            theirs[:rows, here] = other.astype(BF16)
    part_mine[...] = parts[core]
    theirs[:rows, half:] = parts[1 - core].astype(BF16)
    summed = deltas[0]
    for i in range(1, half_groups):
        summed = summed + deltas[i]
    gates = []
    for block in range(2):
        own = split_rows(summed[:, block * wide : (block + 1) * wide], 16)
        gates.append(joined_row(dot(own, chosen((wide, rows), ratio, 0), NN)))
    gate_mine[...] = jnp.where(core == 0, gates[0], gates[1])
    theirs[rows:, :rows] = split_rows(jnp.where(core == 0, gates[1], gates[0]), EXTRA)


def sum_first_kernel(part_mine, *refs):
    got, (own, other) = refs[:-2], refs[-2:]
    total = got[0][...].astype(F32)
    for ref in got[2::2]:
        total = total + ref[...].astype(F32)
    other[...] = total
    for i in range(own.shape[1] // DH):
        here = slice(i * DH, (i + 1) * DH)
        value = part_mine[:, (2 * i + 1) * DH : (2 * i + 2) * DH]
        for ref in got[1::2]:
            value = value + ref[:, here].astype(F32)
        own[:, here] = value


def sum_rest_kernel(value_own, part_mine, *refs):
    got, (own, other) = refs[:-2], refs[-2:]
    total = got[0][...].astype(F32)
    for ref in got[2::2]:
        total = total + ref[...].astype(F32)
    other[...] = total
    for i in range(own.shape[1] // DH):
        here = slice(i * DH, (i + 1) * DH)
        key = part_mine[:, 2 * i * DH : (2 * i + 1) * DH]
        for ref in got[1::2]:
            key = key + ref[:, here].astype(F32)
        own[:, here] = key


def finish_kernel(
    back, query_mine, gate_mine, key_own, value_own, key_other, value_other, valid, cos_ref, sin_ref,
    query_grad, key_grad, value_grad, gate_grad
):
    rows, half = value_own.shape
    wide = query_mine.shape[1]
    core = core_of()
    side = lambda which, width, at=0, size=None: pl.ds(pl.multiple_of(which * width + at, DH), size or width)
    cosine, sine = cos_ref[...], -sin_ref[...]
    for i in range(half // DH):
        here = slice(i * DH, (i + 1) * DH)
        there = wide + 2 * i * DH
        other_key = key_other[:, here] + back[:rows, there : there + DH].astype(F32)
        other_value = value_other[:, here] + back[:rows, there + DH : there + 2 * DH].astype(F32)
        for key_sum, value_sum, which in (
            (key_own[:, here], value_own[:, here], core),
            (other_key, other_value, 1 - core),
        ):
            to = side(which, half, i * DH, DH)
            key_grad[:, to] = rotate(key_sum, cosine, sine).astype(BF16)
            value_grad[:, to] = value_sum.astype(BF16)
    query_grad[:, side(core, wide)] = query_mine[...]
    for i in range(wide // DH):
        turned = rotate(back[:rows, i * DH : (i + 1) * DH].astype(F32), cosine, sine)
        query_grad[:, side(1 - core, wide, i * DH, DH)] = turned.astype(BF16)
    gate = gate_mine[...] + joined_row(back[rows:, :rows])
    gate_grad[...] = jnp.where(valid[...] > 0.0, gate, 0.0)


def per_device(query_rows, key_rows, value_rows, cotangent, router_gate, positions):
    rows, heads_width = query_rows.shape[1:]
    group_width = key_rows.shape[2]
    groups = group_width // DH
    ratio = heads_width // group_width
    half_groups, half_width = groups // 2, heads_width // 2
    parts = lax.axis_size("ctx")
    chips = parts // 2
    limit = parts * LOCAL
    wide = ratio * rows
    params = pltpu.CompilerParams(vmem_limit_bytes=(16 + 4 * chips) * 1024 * 1024)

    def call(kernel, name, outs, *args, scratch=(), flops=10**6, in_hbm=False):
        if in_hbm:
            args = [pltpu.with_memory_space_constraint(arg, pltpu.HBM) for arg in args]
        spec = pl.BlockSpec(memory_space=pltpu.HBM if in_hbm else pltpu.VMEM)
        return pl.pallas_call(
            kernel,
            out_shape=[jax.ShapeDtypeStruct(*out) for out in outs],
            in_specs=[spec] * len(args),
            scratch_shapes=list(scratch),
            compiler_params=params,
            cost_estimate=pl.CostEstimate(flops=flops, bytes_accessed=1000, transcendentals=0),
            name=name,
        )(*args)

    index = np.arange(DH) % (DH // 2)
    freq = jnp.asarray((THETA ** (-2.0 * index / DH)).astype(np.float32))[None]
    packet = ((rows, group_width // 2), BF16)
    table = ((rows, DH), F32)
    line = ((1, rows), F32)
    theirs_shape = ((rows + EXTRA, heads_width + group_width), BF16)
    key_mine, key_theirs, value_mine, value_theirs, theirs, gate_mine, valid, cosine, sine = call(
        functools.partial(pack_kernel, limit=limit),
        "pack",
        [packet, packet, packet, packet, theirs_shape, line, line, table, table],
        key_rows[0],
        value_rows[0],
        query_rows[0],
        cotangent[0],
        router_gate,
        positions,
        freq,
        in_hbm=True,
        flops=5 * 10**9,
        scratch=[
            pltpu.VMEM((rows, group_width), BF16),
            pltpu.VMEM((rows, group_width), BF16),
            pltpu.VMEM((rows, half_width), BF16),
            pltpu.VMEM(*line),
            pltpu.VMEM((1, rows), jnp.int32),
            pltpu.VMEM((1, DH), F32),
            pltpu.SemaphoreType.DMA((7,)),
        ],
    )

    hop = [[(2 * x + k, 2 * (x + s) + k) for x in range(chips - s) for k in range(2)] for s in range(chips)]
    cross = [[(a, b + 1 - 2 * (b % 2)) for a, b in pairs] for pairs in hop]
    back_hop = [[(b, a) for a, b in pairs] for pairs in hop]
    back_cross = [[(b, a) for a, b in pairs] for pairs in cross]

    steps = range(1, chips)

    def send(sib, own, sib_pairs, own_pairs):
        sib = [lax.ppermute(sib[s - 1], "ctx", sib_pairs[s]) for s in steps]
        return sib, [lax.ppermute(own[s - 1], "ctx", own_pairs[s]) for s in steps]

    sib_keys, own_keys = send([key_theirs] * chips, [key_mine] * chips, cross, hop)

    pairs = [[2 * x, 2 * x + 1] for x in range(chips)]
    swap = [pair for a, b in pairs for pair in ((a, b), (b, a))]
    sib = lax.ppermute(theirs, "ctx", swap)

    row = ((half_groups, 1, 2 * wide), F32)
    table = ((half_groups, 2 * rows, 2 * wide), F32)
    kv_table = ((half_groups, 2 * rows, DH), BF16)
    q_table = ((half_groups, 2 * wide, DH), BF16)
    send_mine, send_theirs, keys, values, query, cot, gate_row, raws, tops, sums, crosses = call(
        functools.partial(local_kernel, ratio=ratio),
        "local_scores",
        [packet, packet, kv_table, kv_table, q_table, q_table, ((1, 2 * wide), F32), table, row, row, row],
        key_mine,
        value_mine,
        value_theirs,
        query_rows[0],
        cotangent[0],
        cosine,
        sine,
        gate_mine,
        sib,
        flops=3 * 10**6,
    )

    sib_values, own_values = send([send_theirs] * chips, [send_mine] * chips, cross, hop)

    blocks = 2 * (chips - 1)
    far_rows = ((half_groups, blocks * rows, DH), BF16)
    far_low = ((half_groups, blocks * rows, 2 * wide), BF16)
    far_table = (far_low[0], F32 if chips == 2 else BF16)
    far_keys, far_raws, factors, far_factors, shrinks, inverses, *parts = call(
        functools.partial(far_keys_kernel, blocks=blocks),
        "far_keys",
        [far_rows, far_table, row, row, row, row] + [packet] * blocks,
        query,
        cot,
        gate_row,
        tops,
        sums,
        *sib_keys,
        *own_keys,
        flops=FAR_COST,
        scratch=[pltpu.VMEM(*far_low)],
    )
    sib_value_got, own_value_got = send(parts[: chips - 1], parts[chips - 1 :], back_cross, back_hop)
    far_grads, deltas, *parts = call(
        functools.partial(far_values_kernel, blocks=blocks),
        "far_values",
        [far_low, row] + [packet] * blocks,
        query,
        cot,
        far_raws,
        far_factors,
        shrinks,
        inverses,
        crosses,
        *sib_values,
        *own_values,
        scratch=[pltpu.VMEM(*far_rows)],
    )
    sib_key_got, own_key_got = send(parts[: chips - 1], parts[chips - 1 :], back_cross, back_hop)

    part_mine, query_mine, gate_part, theirs = call(
        functools.partial(near_kernel, ratio=ratio),
        "near_grads",
        [
            ((rows, group_width), F32),
            ((rows, half_width), BF16),
            ((1, rows), F32),
            ((rows + EXTRA, half_width + group_width), BF16),
        ],
        raws,
        values,
        factors,
        inverses,
        deltas,
        keys,
        query,
        cot,
        far_keys,
        far_grads,
        cosine,
        sine,
        flops=4 * 10**6,
        scratch=[
            pltpu.VMEM((half_groups, 2 * rows, 2 * wide), BF16),
            pltpu.VMEM((half_groups, 2 * rows, 2 * wide), BF16),
            pltpu.VMEM((2, rows, group_width), F32),
            pltpu.VMEM((half_groups, DH, 2 * wide), F32),
            pltpu.VMEM((2 * wide, DH), F32),
            pltpu.VMEM(*row),
        ],
    )
    back = lax.ppermute(theirs, "ctx", swap)
    total = ((rows, group_width // 2), F32)
    value_own, value_other = call(
        sum_first_kernel,
        "sum_first",
        [total, total],
        part_mine,
        *[part for pair in zip(sib_value_got, own_value_got) for part in pair],
        flops=5 * 10**9,
    )
    key_own, key_other = call(
        sum_rest_kernel,
        "sum_rest",
        [total, total],
        value_own,
        part_mine,
        *[part for pair in zip(sib_key_got, own_key_got) for part in pair],
        flops=5 * 10**9,
    )
    query_grad, key_grad, value_grad, gate_grad = call(
        finish_kernel,
        "finish",
        [((rows, heads_width), BF16)] + [((rows, group_width), BF16)] * 2 + [line],
        back,
        query_mine,
        gate_part,
        key_own,
        value_own,
        key_other,
        value_other,
        valid,
        cosine,
        sine,
    )
    return (query_grad[None], key_grad[None], value_grad[None], gate_grad)


def solution(mesh):
    wide = P(("group", "dp"), "ctx", None)
    narrow = P(("group", "dp"), "ctx")
    return jax.shard_map(
        per_device,
        mesh=mesh,
        in_specs=(wide, wide, wide, wide, narrow, narrow),
        out_specs=(wide, wide, wide, narrow),
        check_vma=False,
    )
```

```python
import functools
import math

import jax
import jax.numpy as jnp
import numpy as np
from jax import lax
from jax.experimental import pallas as pl
from jax.experimental.pallas import tpu as pltpu
from jax.sharding import PartitionSpec as P

DH = 128
LOCAL = 1024
THETA = 500000.0
EXTRA = 16
HIDDEN = -1e30
UNUSED = 2.0**14
SCALE = DH**-0.5
LOG2E = math.log2(math.e)
LN2 = math.log(2.0)

NT = (((1,), (1,)), ((), ()))
NN = (((1,), (0,)), ((), ()))
TN = (((0,), (0,)), ((), ()))
F32 = jnp.float32
BF16 = jnp.bfloat16


def few_bits(value, bits):
    unit = 2.0 ** (math.floor(math.log2(value)) + 1 - bits)
    return math.floor(value / unit) * unit


QUARTER_1 = few_bits(math.pi / 2, 10)
QUARTER_2 = few_bits(math.pi / 2 - QUARTER_1, 10)
QUARTER_3 = math.pi / 2 - QUARTER_1 - QUARTER_2


def dot(a, b, dims):
    return lax.dot_general(a, b, dims, preferred_element_type=F32)


def core_of():
    return lax.rem(lax.axis_index("ctx"), 2)


def rotate(values, cosine, sine):
    return values * cosine + pltpu.roll(values, DH // 2, 1) * sine


def sine_cosine(angle):
    turns = jnp.floor(angle * (2.0 / math.pi) + 0.5)
    rest = ((angle - turns * QUARTER_1) - turns * QUARTER_2) - turns * QUARTER_3
    square = rest * rest
    sine = ((-1.9515295891e-4 * square + 8.3321608736e-3) * square - 1.6666654611e-1) * square * rest + rest
    cosine = (2.443315711809948e-5 * square - 1.388731625493765e-3) * square + 4.166664568298827e-2
    cosine = cosine * square * square - 0.5 * square + 1.0
    quarter = turns.astype(jnp.int32)
    odd = (quarter & 1) == 1
    first, second = jnp.where(odd, cosine, sine), jnp.where(odd, sine, cosine)
    return (
        jnp.where((quarter & 2) == 2, -first, first),
        jnp.where(((quarter + 1) & 2) == 2, -second, second),
    )


def split_rows(row, height):
    high = row.astype(BF16).astype(F32)
    middle = (row - high).astype(BF16).astype(F32)
    low = row - high - middle
    line = lax.broadcasted_iota(jnp.int32, (height, row.shape[1]), 0)
    rows = jnp.where(line == 0, high, jnp.where(line == 1, middle, jnp.where(line == 2, low, 0.0)))
    return rows.astype(BF16)


def joined_row(rows):
    return jnp.sum(rows.astype(F32), axis=0, keepdims=True)


def pack_kernel(
    key_in, value_in, query_in, cot_in, gate_in, pos_in, freq_in,
    key_mine, key_theirs, value_mine, value_theirs, theirs, gate_mine, valid, cos_ref, sin_ref,
    key, value, query, gate, pos, freq, sems, *, limit
):
    rows, width = key.shape
    side_width = width // 2
    half = query.shape[1]
    core = core_of()
    there = pl.ds(pl.multiple_of((1 - core) * half, DH), half)
    loads = [(pos_in, pos), (freq_in, freq), (key_in, key), (value_in, value), (query_in.at[:, there], query)]
    loads += [(gate_in, gate), (cot_in.at[:, there], theirs.at[:rows, half : 2 * half])]
    loads = [pltpu.make_async_copy(source, target, sems.at[i]) for i, (source, target) in enumerate(loads)]
    for copy in loads:
        copy.start()
    down = lax.broadcasted_iota(jnp.int32, (rows, rows), 0)
    along = lax.broadcasted_iota(jnp.int32, (rows, rows), 1)
    lane = lax.broadcasted_iota(jnp.int32, (rows, DH), 1)
    loads[0].wait()
    loads[1].wait()
    places = pos[...]
    column = jnp.sum(jnp.where(down == along, places.astype(F32), 0.0), axis=1, keepdims=True)
    sine, cosine = sine_cosine(column * freq[...])
    sine = jnp.where(lane < DH // 2, -sine, sine)
    cos_ref[...] = cosine
    sin_ref[...] = sine
    used = jnp.broadcast_to(column, (rows, DH)) < limit
    loads[2].wait()
    loads[3].wait()
    for key_out, value_out, side in ((key_mine, value_mine, core), (key_theirs, value_theirs, 1 - core)):
        for i in range(side_width // DH):
            from_ = pl.ds(pl.multiple_of(side * side_width + i * DH, DH), DH)
            turned = jnp.where(used, rotate(key[:, from_].astype(F32), cosine, sine), UNUSED).astype(BF16)
            key_out[:, i * DH : (i + 1) * DH] = turned
            value_out[:, i * DH : (i + 1) * DH] = value[:, from_]
    theirs[:rows, 2 * half : 2 * half + side_width] = key_theirs[...]
    theirs[:rows, 2 * half + side_width :] = value_theirs[...]
    loads[4].wait()
    cosine, sine = cosine * (SCALE * LOG2E), sine * (SCALE * LOG2E)
    for i in range(half // DH):
        here = slice(i * DH, (i + 1) * DH)
        theirs[:rows, here] = rotate(query[:, here].astype(F32), cosine, sine).astype(BF16)
    loads[5].wait()
    valid[...] = jnp.where(places < limit, 1.0, 0.0)
    used_gate = jnp.where(places < limit, gate[...], 0.0)
    gate_mine[...] = used_gate
    theirs[rows:, :rows] = split_rows(used_gate, EXTRA)
    loads[6].wait()


def chosen(shape, ratio, dim):
    down = lax.broadcasted_iota(jnp.int32, shape, 0)
    along = lax.broadcasted_iota(jnp.int32, shape, 1)
    rows = shape[1 - dim]
    long, short = (down, along) if dim == 0 else (along, down)
    for _ in range(1, ratio):
        long = jnp.where(long >= rows, long - rows, long)
    return jnp.where(long == short, 1.0, 0.0).astype(BF16)


def chunks(low, high):
    return [slice(at, min(at + 256, high)) for at in range(low, high, 256)]


def used_slots(key, here):
    chip = lax.div(lax.axis_index("ctx"), 2)
    first = key[:, :DH].astype(F32)[:, :1]
    return jnp.broadcast_to(first, (key.shape[0], 256)) < jnp.where(chip >= here, UNUSED / 2, -UNUSED)


def local_kernel(
    key_mine, value_mine, query_in, cot_in, cos_ref, sin_ref, gate_mine, sib,
    keys, query, cot, gate, raws, grads, tops, sums, crosses, values, *, ratio
):
    rows = key_mine.shape[0]
    half_groups = keys.shape[0]
    wide = ratio * rows
    half = half_groups * ratio * DH
    core = core_of()
    spread = chosen((rows, wide), ratio, 1)
    key_sib = sib.at[:rows, 2 * half : 2 * half + half_groups * DH]
    value_sib = sib.at[:rows, 2 * half + half_groups * DH :]
    cosine, sine = cos_ref[...] * (SCALE * LOG2E), sin_ref[...] * (SCALE * LOG2E)
    for key, value, side in ((key_mine, value_mine, core), (key_sib, value_sib, 1 - core)):
        there = pl.ds(pl.multiple_of(side * rows, 16), rows)
        for i in range(half_groups):
            keys[i, there, :] = key[:, i * DH : (i + 1) * DH]
            values[i, there, :] = value[:, i * DH : (i + 1) * DH]
            for h in range(ratio):
                to = pl.ds(pl.multiple_of(side * wide + h * rows, 16), rows)
                at = (i * ratio + h) * DH
                if key is key_mine:
                    here = pl.ds(pl.multiple_of(core * half + at, DH), DH)
                    query[i, to, :] = rotate(query_in[:, here].astype(F32), cosine, sine).astype(BF16)
                    cot[i, to, :] = cot_in[:, here]
                else:
                    query[i, to, :] = sib[:rows, at : at + DH]
                    cot[i, to, :] = sib[:rows, half + at : half + at + DH]
    own = joined_row(dot(split_rows(gate_mine[...], EXTRA), spread, NN))
    other = joined_row(dot(sib[rows:, :rows], spread, NN))
    gate[:, :wide] = jnp.where(core == 0, own, other)
    gate[:, wide:] = jnp.where(core == 0, other, own)
    used = used_slots(keys[0, :rows, :], 0)
    for i in range(half_groups):
        for block in range(2):
            reach = (block + 1) * rows
            for here in chunks(block * wide, (block + 1) * wide):
                width = here.stop - here.start
                scores = dot(keys[i, :reach, :], query[i, here, :], NT)
                slot = lax.broadcasted_iota(jnp.int32, (rows, width), 0)
                lane = lax.broadcasted_iota(jnp.int32, (rows, width), 1) + (here.start - block * wide)
                for h in range(1, ratio):
                    lane = jnp.where(lane >= rows, lane - rows, lane)
                shown = jnp.where(slot <= lane, scores[block * rows :], HIDDEN)
                if block:
                    before = jnp.where(used[:, :width], scores[:rows], HIDDEN)
                    shown = jnp.concatenate([before, shown], axis=0)
                top = jnp.max(shown, axis=0, keepdims=True)
                raw = jnp.exp2(shown - top)
                prob_grad = dot(values[i, :reach, :], cot[i, here, :], NT)
                raws[i, :reach, here] = raw
                grads[i, :reach, here] = prob_grad
                tops[i, :, here] = top
                sums[i, :, here] = jnp.sum(raw, axis=0, keepdims=True)
                crosses[i, :, here] = jnp.sum(raw * prob_grad, axis=0, keepdims=True)


def part_of(weights, score_grads, query, cot, out_ref, i, there, lanes):
    key_part = dot(score_grads[i, there, lanes], query[i, lanes, :], NN) * LN2
    value_part = dot(weights[i, there, lanes], cot[i, lanes, :], NN)
    out_ref[:, 2 * i * DH : (2 * i + 1) * DH] = key_part.astype(out_ref.dtype)
    out_ref[:, (2 * i + 1) * DH : (2 * i + 2) * DH] = value_part.astype(out_ref.dtype)


def early_kernel(query, tops, sums, packet, raws, new_tops, new_sums):
    half_groups, lanes = query.shape[:2]
    alone = lax.axis_index("ctx") < 2

    @pl.when(alone)
    def _():
        new_tops[...] = tops[...]
        new_sums[...] = sums[...]

    @pl.when(jnp.logical_not(alone))
    def _():
        used = used_slots(packet, 1)
        for i in range(half_groups):
            key = packet[:, i * DH : (i + 1) * DH]
            for here in chunks(0, lanes):
                width = here.stop - here.start
                shown = jnp.where(used[:, :width], dot(key, query[i, here, :], NT), HIDDEN)
                old_top = tops[i, :, here]
                top = jnp.maximum(old_top, jnp.max(shown, axis=0, keepdims=True))
                raw = jnp.exp2(shown - top)
                raws[i, :, here] = raw
                new_tops[i, :, here] = top
                new_sums[i, :, here] = sums[i, :, here] * jnp.exp2(old_top - top) + jnp.sum(raw, axis=0, keepdims=True)


def far_keys_kernel(query, cot, gate, first_tops, early_raws, tops, sums, *refs, blocks):
    packets = refs[:blocks]
    far_keys, raws, factors, far_factors, shrinks, inverses = refs[blocks : blocks + 6]
    parts, weights = refs[blocks + 6 : -1], refs[-1]
    rows = packets[0].shape[0]
    half_groups, lanes = query.shape[:2]
    alone = lax.axis_index("ctx") < 2

    @pl.when(alone)
    def _():
        for i in range(half_groups):
            inverse = 1.0 / sums[i]
            factors[i] = inverse * gate[...]
            inverses[i] = inverse

    @pl.when(jnp.logical_not(alone))
    def _():
        for i in range(half_groups):
            for j, packet in enumerate(packets):
                far_keys[i, j * rows : (j + 1) * rows, :] = packet[:, i * DH : (i + 1) * DH]
        used = [used_slots(packets[j], j % (blocks // 2) + 1) for j in range(1, blocks)]
        for i in range(half_groups):
            for here in chunks(0, lanes):
                width = here.stop - here.start
                scores = dot(far_keys[i, rows:, :], query[i, here, :], NT)
                shown = [
                    jnp.where(used[j][:, :width], scores[j * rows : (j + 1) * rows], HIDDEN)
                    for j in range(blocks - 1)
                ]
                shown = jnp.concatenate(shown, axis=0)
                old_top = tops[i, :, here]
                top = jnp.maximum(old_top, jnp.max(shown, axis=0, keepdims=True))
                raw = jnp.exp2(shown - top)
                shrink = jnp.exp2(old_top - top)
                first_shrink = jnp.exp2(first_tops[i, :, here] - top)
                inverse = 1.0 / (sums[i, :, here] * shrink + jnp.sum(raw, axis=0, keepdims=True))
                factor = inverse * gate[:, here]
                factors[i, :, here] = factor * first_shrink
                far_factors[i, :, here] = factor
                shrinks[i, :, here] = first_shrink
                inverses[i, :, here] = inverse
                raws[i, rows:, here] = raw.astype(raws.dtype)
                weights[i, rows:, here] = (raw * factor).astype(BF16)
                raw = early_raws[i, :, here] * shrink
                raws[i, :rows, here] = raw.astype(raws.dtype)
                weights[i, :rows, here] = (raw * factor).astype(BF16)
            for j, out_ref in enumerate(parts):
                there = slice(j * rows, (j + 1) * rows)
                out_ref[:, i * DH : (i + 1) * DH] = dot(weights[i, there, :], cot[i], NN).astype(BF16)


def far_values_kernel(query, cot, raws, far_factors, shrinks, inverses, crosses, *refs, blocks):
    packets = refs[:blocks]
    score_grads, deltas = refs[blocks : blocks + 2]
    parts, far_values = refs[blocks + 2 : -1], refs[-1]
    rows = packets[0].shape[0]
    half_groups, lanes = query.shape[:2]
    alone = lax.axis_index("ctx") < 2

    @pl.when(alone)
    def _():
        for i in range(half_groups):
            deltas[i] = crosses[i] * inverses[i]

    @pl.when(jnp.logical_not(alone))
    def _():
        for i in range(half_groups):
            for j, packet in enumerate(packets):
                far_values[i, j * rows : (j + 1) * rows, :] = packet[:, i * DH : (i + 1) * DH]
        for i in range(half_groups):
            for here in chunks(0, lanes):
                raw = raws[i, :, here].astype(F32)
                prob_grad = dot(far_values[i], cot[i, here, :], NT)
                cross = jnp.sum(raw * prob_grad, axis=0, keepdims=True)
                delta = (crosses[i, :, here] * shrinks[i, :, here] + cross) * inverses[i, :, here]
                deltas[i, :, here] = delta
                score_grad = raw * far_factors[i, :, here] * (prob_grad - delta)
                score_grads[i, :, here] = score_grad.astype(BF16)
            key_parts(score_grads, query, parts, i, 0)


def key_parts(score_grads, query, parts, i, first):
    rows = parts[0].shape[0]
    for j, out_ref in enumerate(parts):
        there = slice((first + j) * rows, (first + j + 1) * rows)
        part = dot(score_grads[i, there, :], query[i], NN) * LN2
        out_ref[:, i * DH : (i + 1) * DH] = part.astype(BF16)


def far_rest_kernel(query, score_grads, *parts):
    @pl.when(lax.axis_index("ctx") >= 2)
    def _():
        for i in range(query.shape[0]):
            key_parts(score_grads, query, parts, i, len(parts))


def near_kernel(
    raws, grads, factors, deltas, keys, query, cot, far_keys, far_grads, cos_ref, sin_ref,
    part_mine, query_mine, gate_mine, theirs, weights, score_grads, parts, acc, turned,
    *, ratio
):
    rows = part_mine.shape[0]
    half_groups = keys.shape[0]
    wide = ratio * rows
    half = half_groups * ratio * DH
    for i in range(half_groups):
        for block in range(2):
            reach = (block + 1) * rows
            for here in chunks(block * wide, (block + 1) * wide):
                gated = raws[i, :reach, here] * factors[i, :, here]
                weights[i, :reach, here] = gated.astype(BF16)
                score_grads[i, :reach, here] = (gated * (grads[i, :reach, here] - deltas[i, :, here])).astype(BF16)
        for block in range(2):
            there, lanes = slice(block * rows, (block + 1) * rows), slice(block * wide, 2 * wide)
            part_of(weights, score_grads, query, cot, parts.at[block], i, there, lanes)
            reach, lanes = (block + 1) * rows, slice(block * wide, (block + 1) * wide)
            acc[i, :, lanes] = dot(keys[i, :reach, :], score_grads[i, :reach, lanes], TN)

    @pl.when(lax.axis_index("ctx") >= 2)
    def _():
        for i in range(half_groups):
            acc[i] += dot(far_keys[i], far_grads[i], TN)

    core = core_of()
    cosine, sine = cos_ref[...], -sin_ref[...]
    for i in range(half_groups):
        turned[...] = jnp.transpose(acc[i] * SCALE)
        for h in range(ratio):
            here = slice((i * ratio + h) * DH, (i * ratio + h + 1) * DH)
            own = turned[pl.ds(pl.multiple_of(core * wide + h * rows, 16), rows), :]
            query_mine[:, here] = rotate(own, cosine, sine).astype(BF16)
            other = turned[pl.ds(pl.multiple_of((1 - core) * wide + h * rows, 16), rows), :]
            theirs[:rows, here] = other.astype(BF16)
    part_mine[...] = parts[core]
    theirs[:rows, half:] = parts[1 - core].astype(BF16)
    summed = deltas[0]
    for i in range(1, half_groups):
        summed = summed + deltas[i]
    gates = []
    for block in range(2):
        own = split_rows(summed[:, block * wide : (block + 1) * wide], 16)
        gates.append(joined_row(dot(own, chosen((wide, rows), ratio, 0), NN)))
    gate_mine[...] = jnp.where(core == 0, gates[0], gates[1])
    theirs[rows:, :rows] = split_rows(jnp.where(core == 0, gates[1], gates[0]), EXTRA)


def sum_first_kernel(part_mine, *refs):
    got, (own, other) = refs[:-2], refs[-2:]
    total = got[0][...].astype(F32)
    for ref in got[2::2]:
        total = total + ref[...].astype(F32)
    other[...] = total
    for i in range(own.shape[1] // DH):
        here = slice(i * DH, (i + 1) * DH)
        value = part_mine[:, (2 * i + 1) * DH : (2 * i + 2) * DH]
        for ref in got[1::2]:
            value = value + ref[:, here].astype(F32)
        own[:, here] = value


def sum_middle_kernel(value_own, *refs):
    got, other = refs[:-1], refs[-1]
    total = got[0][...].astype(F32)
    for ref in got[1:]:
        total = total + ref[...].astype(F32)
    other[...] = total


def sum_rest_kernel(key_other, part_mine, *refs):
    got, own = refs[:-1], refs[-1]
    for i in range(own.shape[1] // DH):
        here = slice(i * DH, (i + 1) * DH)
        key = part_mine[:, 2 * i * DH : (2 * i + 1) * DH]
        for ref in got:
            key = key + ref[:, here].astype(F32)
        own[:, here] = key


def finish_kernel(
    back, query_mine, gate_mine, key_own, value_own, key_other, value_other, valid, cos_ref, sin_ref,
    query_grad, key_grad, value_grad, gate_grad
):
    rows, half = value_own.shape
    wide = query_mine.shape[1]
    core = core_of()
    side = lambda which, width, at=0, size=None: pl.ds(pl.multiple_of(which * width + at, DH), size or width)
    cosine, sine = cos_ref[...], -sin_ref[...]
    for i in range(half // DH):
        here = slice(i * DH, (i + 1) * DH)
        there = wide + 2 * i * DH
        other_key = key_other[:, here] + back[:rows, there : there + DH].astype(F32)
        other_value = value_other[:, here] + back[:rows, there + DH : there + 2 * DH].astype(F32)
        for key_sum, value_sum, which in (
            (key_own[:, here], value_own[:, here], core),
            (other_key, other_value, 1 - core),
        ):
            to = side(which, half, i * DH, DH)
            key_grad[:, to] = rotate(key_sum, cosine, sine).astype(BF16)
            value_grad[:, to] = value_sum.astype(BF16)
    query_grad[:, side(core, wide)] = query_mine[...]
    for i in range(wide // DH):
        turned = rotate(back[:rows, i * DH : (i + 1) * DH].astype(F32), cosine, sine)
        query_grad[:, side(1 - core, wide, i * DH, DH)] = turned.astype(BF16)
    gate = gate_mine[...] + joined_row(back[rows:, :rows])
    gate_grad[...] = jnp.where(valid[...] > 0.0, gate, 0.0)


def per_device(query_rows, key_rows, value_rows, cotangent, router_gate, positions):
    rows, heads_width = query_rows.shape[1:]
    group_width = key_rows.shape[2]
    groups = group_width // DH
    ratio = heads_width // group_width
    half_groups, half_width = groups // 2, heads_width // 2
    parts = lax.axis_size("ctx")
    chips = parts // 2
    limit = parts * LOCAL
    wide = ratio * rows
    params = pltpu.CompilerParams(vmem_limit_bytes=(16 + 4 * chips) * 1024 * 1024)

    def call(kernel, name, outs, *args, scratch=(), flops=10**6, in_hbm=False):
        if in_hbm:
            args = [pltpu.with_memory_space_constraint(arg, pltpu.HBM) for arg in args]
        spec = pl.BlockSpec(memory_space=pltpu.HBM if in_hbm else pltpu.VMEM)
        return pl.pallas_call(
            kernel,
            out_shape=[jax.ShapeDtypeStruct(*out) for out in outs],
            in_specs=[spec] * len(args),
            scratch_shapes=list(scratch),
            compiler_params=params,
            cost_estimate=pl.CostEstimate(flops=flops, bytes_accessed=1000, transcendentals=0),
            name=name,
        )(*args)

    index = np.arange(DH) % (DH // 2)
    freq = jnp.asarray((THETA ** (-2.0 * index / DH)).astype(np.float32))[None]
    packet = ((rows, group_width // 2), BF16)
    table = ((rows, DH), F32)
    line = ((1, rows), F32)
    theirs_shape = ((rows + EXTRA, heads_width + group_width), BF16)
    key_mine, key_theirs, value_mine, value_theirs, theirs, gate_mine, valid, cosine, sine = call(
        functools.partial(pack_kernel, limit=limit),
        "pack",
        [packet, packet, packet, packet, theirs_shape, line, line, table, table],
        key_rows[0],
        value_rows[0],
        query_rows[0],
        cotangent[0],
        router_gate,
        positions,
        freq,
        in_hbm=True,
        flops=5 * 10**9,
        scratch=[
            pltpu.VMEM((rows, group_width), BF16),
            pltpu.VMEM((rows, group_width), BF16),
            pltpu.VMEM((rows, half_width), BF16),
            pltpu.VMEM(*line),
            pltpu.VMEM((1, rows), jnp.int32),
            pltpu.VMEM((1, DH), F32),
            pltpu.SemaphoreType.DMA((7,)),
        ],
    )

    hop = [[(2 * x + k, 2 * (x + s) + k) for x in range(chips - s) for k in range(2)] for s in range(chips)]
    cross = [[(a, b + 1 - 2 * (b % 2)) for a, b in pairs] for pairs in hop]
    back_hop = [[(b, a) for a, b in pairs] for pairs in hop]
    back_cross = [[(b, a) for a, b in pairs] for pairs in cross]

    steps = range(1, chips)

    def send(sib, own, sib_pairs, own_pairs):
        sib = [lax.ppermute(sib[s - 1], "ctx", sib_pairs[s]) for s in steps]
        return sib, [lax.ppermute(own[s - 1], "ctx", own_pairs[s]) for s in steps]

    sib_keys, own_keys = send([key_theirs] * chips, [key_mine] * chips, cross, hop)
    sib_values, own_values = send([value_theirs] * chips, [value_mine] * chips, cross, hop)

    pairs = [[2 * x, 2 * x + 1] for x in range(chips)]
    swap = [pair for a, b in pairs for pair in ((a, b), (b, a))]
    sib = lax.ppermute(theirs, "ctx", swap)

    row = ((half_groups, 1, 2 * wide), F32)
    table = ((half_groups, 2 * rows, 2 * wide), F32)
    kv_table = ((half_groups, 2 * rows, DH), BF16)
    q_table = ((half_groups, 2 * wide, DH), BF16)
    keys, query, cot, gate_row, raws, grads, tops, sums, crosses = call(
        functools.partial(local_kernel, ratio=ratio),
        "local_scores",
        [kv_table, q_table, q_table, ((1, 2 * wide), F32), table, table, row, row, row],
        key_mine,
        value_mine,
        query_rows[0],
        cotangent[0],
        cosine,
        sine,
        gate_mine,
        sib,
        scratch=[pltpu.VMEM(*kv_table)],
        flops=3 * 10**6,
    )

    blocks = 2 * (chips - 1)
    far_rows = ((half_groups, blocks * rows, DH), BF16)
    far_low = ((half_groups, blocks * rows, 2 * wide), BF16)
    far_table = (far_low[0], F32 if chips == 2 else BF16)
    early_table = ((half_groups, rows, 2 * wide), F32)
    early_raws, early_tops, early_sums = call(
        early_kernel, "early_keys", [early_table, row, row], query, tops, sums, sib_keys[0]
    )
    far_keys, far_raws, factors, far_factors, shrinks, inverses, *parts = call(
        functools.partial(far_keys_kernel, blocks=blocks),
        "far_keys",
        [far_rows, far_table, row, row, row, row] + [packet] * blocks,
        query,
        cot,
        gate_row,
        tops,
        early_raws,
        early_tops,
        early_sums,
        *sib_keys,
        *own_keys,
        scratch=[pltpu.VMEM(*far_low)],
    )
    sib_value_got, own_value_got = send(parts[: chips - 1], parts[chips - 1 :], back_cross, back_hop)
    far_grads, deltas, *parts = call(
        functools.partial(far_values_kernel, blocks=blocks),
        "far_values",
        [far_low, row] + [packet] * (chips - 1),
        query,
        cot,
        far_raws,
        far_factors,
        shrinks,
        inverses,
        crosses,
        *sib_values,
        *own_values,
        scratch=[pltpu.VMEM(*far_rows)],
    )
    sib_key_got = [lax.ppermute(parts[s - 1], "ctx", back_cross[s]) for s in steps]
    parts = call(far_rest_kernel, "far_rest", [packet] * (chips - 1), query, far_grads)
    own_key_got = [lax.ppermute(parts[s - 1], "ctx", back_hop[s]) for s in steps]

    part_mine, query_mine, gate_part, theirs = call(
        functools.partial(near_kernel, ratio=ratio),
        "near_grads",
        [
            ((rows, group_width), F32),
            ((rows, half_width), BF16),
            ((1, rows), F32),
            ((rows + EXTRA, half_width + group_width), BF16),
        ],
        raws,
        grads,
        factors,
        deltas,
        keys,
        query,
        cot,
        far_keys,
        far_grads,
        cosine,
        sine,
        flops=4 * 10**6,
        scratch=[
            pltpu.VMEM((half_groups, 2 * rows, 2 * wide), BF16),
            pltpu.VMEM((half_groups, 2 * rows, 2 * wide), BF16),
            pltpu.VMEM((2, rows, group_width), F32),
            pltpu.VMEM((half_groups, DH, 2 * wide), F32),
            pltpu.VMEM((2 * wide, DH), F32),
        ],
    )
    back = lax.ppermute(theirs, "ctx", swap)
    total = ((rows, group_width // 2), F32)
    value_own, value_other = call(
        sum_first_kernel,
        "sum_first",
        [total, total],
        part_mine,
        *[part for pair in zip(sib_value_got, own_value_got) for part in pair],
        flops=3 * 10**8,
    )
    (key_other,) = call(sum_middle_kernel, "sum_middle", [total], value_own, *sib_key_got, flops=5 * 10**9)
    (key_own,) = call(sum_rest_kernel, "sum_rest", [total], key_other, part_mine, *own_key_got, flops=5 * 10**9)
    query_grad, key_grad, value_grad, gate_grad = call(
        finish_kernel,
        "finish",
        [((rows, heads_width), BF16)] + [((rows, group_width), BF16)] * 2 + [line],
        back,
        query_mine,
        gate_part,
        key_own,
        value_own,
        key_other,
        value_other,
        valid,
        cosine,
        sine,
    )
    return (query_grad[None], key_grad[None], value_grad[None], gate_grad)


def solution(mesh):
    wide = P(("group", "dp"), "ctx", None)
    narrow = P(("group", "dp"), "ctx")
    return jax.shard_map(
        per_device,
        mesh=mesh,
        in_specs=(wide, wide, wide, wide, narrow, narrow),
        out_specs=(wide, wide, wide, narrow),
        check_vma=False,
    )
```

```python
import functools
import math

import jax
import jax.numpy as jnp
import numpy as np
from jax import lax
from jax.experimental import pallas as pl
from jax.experimental.pallas import tpu as pltpu
from jax.sharding import PartitionSpec as P

DH = 128
LOCAL = 1024
THETA = 500000.0
EXTRA = 16
HIDDEN = -1e30
UNUSED = 2.0**14
SCALE = DH**-0.5
LOG2E = math.log2(math.e)
LN2 = math.log(2.0)

NT = (((1,), (1,)), ((), ()))
NN = (((1,), (0,)), ((), ()))
TN = (((0,), (0,)), ((), ()))
F32 = jnp.float32
BF16 = jnp.bfloat16


def few_bits(value, bits):
    unit = 2.0 ** (math.floor(math.log2(value)) + 1 - bits)
    return math.floor(value / unit) * unit


QUARTER_1 = few_bits(math.pi / 2, 10)
QUARTER_2 = few_bits(math.pi / 2 - QUARTER_1, 10)
QUARTER_3 = math.pi / 2 - QUARTER_1 - QUARTER_2


def dot(a, b, dims):
    return lax.dot_general(a, b, dims, preferred_element_type=F32)


def core_of():
    return lax.rem(lax.axis_index("ctx"), 2)


def rotate(values, cosine, sine):
    return values * cosine + pltpu.roll(values, DH // 2, 1) * sine


def sine_cosine(angle):
    turns = jnp.floor(angle * (2.0 / math.pi) + 0.5)
    rest = ((angle - turns * QUARTER_1) - turns * QUARTER_2) - turns * QUARTER_3
    square = rest * rest
    sine = ((-1.9515295891e-4 * square + 8.3321608736e-3) * square - 1.6666654611e-1) * square * rest + rest
    cosine = (2.443315711809948e-5 * square - 1.388731625493765e-3) * square + 4.166664568298827e-2
    cosine = cosine * square * square - 0.5 * square + 1.0
    quarter = turns.astype(jnp.int32)
    odd = (quarter & 1) == 1
    first, second = jnp.where(odd, cosine, sine), jnp.where(odd, sine, cosine)
    return (
        jnp.where((quarter & 2) == 2, -first, first),
        jnp.where(((quarter + 1) & 2) == 2, -second, second),
    )


def split_rows(row, height):
    high = row.astype(BF16).astype(F32)
    middle = (row - high).astype(BF16).astype(F32)
    low = row - high - middle
    line = lax.broadcasted_iota(jnp.int32, (height, row.shape[1]), 0)
    rows = jnp.where(line == 0, high, jnp.where(line == 1, middle, jnp.where(line == 2, low, 0.0)))
    return rows.astype(BF16)


def joined_row(rows):
    return jnp.sum(rows.astype(F32), axis=0, keepdims=True)


def pack_kernel(
    key_in, value_in, query_in, cot_in, gate_in, pos_in, freq_in,
    key_mine, key_theirs, value_mine, value_theirs, theirs, gate_mine, valid, cos_ref, sin_ref,
    key, value, query, gate, pos, freq, sems, *, limit
):
    rows, width = key.shape
    side_width = width // 2
    half = query.shape[1]
    core = core_of()
    there = pl.ds(pl.multiple_of((1 - core) * half, DH), half)
    loads = [(pos_in, pos), (freq_in, freq), (key_in, key), (value_in, value), (query_in.at[:, there], query)]
    loads += [(gate_in, gate), (cot_in.at[:, there], theirs.at[:rows, half : 2 * half])]
    loads = [pltpu.make_async_copy(source, target, sems.at[i]) for i, (source, target) in enumerate(loads)]
    for copy in loads:
        copy.start()
    down = lax.broadcasted_iota(jnp.int32, (rows, rows), 0)
    along = lax.broadcasted_iota(jnp.int32, (rows, rows), 1)
    lane = lax.broadcasted_iota(jnp.int32, (rows, DH), 1)
    loads[0].wait()
    loads[1].wait()
    places = pos[...]
    column = jnp.sum(jnp.where(down == along, places.astype(F32), 0.0), axis=1, keepdims=True)
    sine, cosine = sine_cosine(column * freq[...])
    sine = jnp.where(lane < DH // 2, -sine, sine)
    cos_ref[...] = cosine
    sin_ref[...] = sine
    used = jnp.broadcast_to(column, (rows, DH)) < limit
    loads[2].wait()
    loads[3].wait()
    for key_out, value_out, side in ((key_mine, value_mine, core), (key_theirs, value_theirs, 1 - core)):
        for i in range(side_width // DH):
            from_ = pl.ds(pl.multiple_of(side * side_width + i * DH, DH), DH)
            turned = jnp.where(used, rotate(key[:, from_].astype(F32), cosine, sine), UNUSED).astype(BF16)
            key_out[:, i * DH : (i + 1) * DH] = turned
            value_out[:, i * DH : (i + 1) * DH] = value[:, from_]
    theirs[:rows, 2 * half : 2 * half + side_width] = key_theirs[...]
    theirs[:rows, 2 * half + side_width :] = value_theirs[...]
    loads[4].wait()
    cosine, sine = cosine * (SCALE * LOG2E), sine * (SCALE * LOG2E)
    for i in range(half // DH):
        here = slice(i * DH, (i + 1) * DH)
        theirs[:rows, here] = rotate(query[:, here].astype(F32), cosine, sine).astype(BF16)
    loads[5].wait()
    valid[...] = jnp.where(places < limit, 1.0, 0.0)
    used_gate = jnp.where(places < limit, gate[...], 0.0)
    gate_mine[...] = used_gate
    theirs[rows:, :rows] = split_rows(used_gate, EXTRA)
    loads[6].wait()


def chosen(shape, ratio, dim):
    down = lax.broadcasted_iota(jnp.int32, shape, 0)
    along = lax.broadcasted_iota(jnp.int32, shape, 1)
    rows = shape[1 - dim]
    long, short = (down, along) if dim == 0 else (along, down)
    for _ in range(1, ratio):
        long = jnp.where(long >= rows, long - rows, long)
    return jnp.where(long == short, 1.0, 0.0).astype(BF16)


def chunks(low, high):
    return [slice(at, min(at + 256, high)) for at in range(low, high, 256)]


def used_slots(key, here):
    chip = lax.div(lax.axis_index("ctx"), 2)
    first = key[:, :DH].astype(F32)[:, :1]
    return jnp.broadcast_to(first, (key.shape[0], 256)) < jnp.where(chip >= here, UNUSED / 2, -UNUSED)


def local_kernel(
    key_mine, value_mine, query_in, cot_in, cos_ref, sin_ref, gate_mine, sib,
    keys, query, cot, gate, raws, grads, tops, sums, crosses, values, *, ratio
):
    rows = key_mine.shape[0]
    half_groups = keys.shape[0]
    wide = ratio * rows
    half = half_groups * ratio * DH
    core = core_of()
    spread = chosen((rows, wide), ratio, 1)
    key_sib = sib.at[:rows, 2 * half : 2 * half + half_groups * DH]
    value_sib = sib.at[:rows, 2 * half + half_groups * DH :]
    cosine, sine = cos_ref[...] * (SCALE * LOG2E), sin_ref[...] * (SCALE * LOG2E)
    for key, value, side in ((key_mine, value_mine, core), (key_sib, value_sib, 1 - core)):
        there = pl.ds(pl.multiple_of(side * rows, 16), rows)
        for i in range(half_groups):
            keys[i, there, :] = key[:, i * DH : (i + 1) * DH]
            values[i, there, :] = value[:, i * DH : (i + 1) * DH]
            for h in range(ratio):
                to = pl.ds(pl.multiple_of(side * wide + h * rows, 16), rows)
                at = (i * ratio + h) * DH
                if key is key_mine:
                    here = pl.ds(pl.multiple_of(core * half + at, DH), DH)
                    query[i, to, :] = rotate(query_in[:, here].astype(F32), cosine, sine).astype(BF16)
                    cot[i, to, :] = cot_in[:, here]
                else:
                    query[i, to, :] = sib[:rows, at : at + DH]
                    cot[i, to, :] = sib[:rows, half + at : half + at + DH]
    own = joined_row(dot(split_rows(gate_mine[...], EXTRA), spread, NN))
    other = joined_row(dot(sib[rows:, :rows], spread, NN))
    gate[:, :wide] = jnp.where(core == 0, own, other)
    gate[:, wide:] = jnp.where(core == 0, other, own)
    used = used_slots(keys[0, :rows, :], 0)
    for i in range(half_groups):
        for block in range(2):
            reach = (block + 1) * rows
            for here in chunks(block * wide, (block + 1) * wide):
                width = here.stop - here.start
                scores = dot(keys[i, :reach, :], query[i, here, :], NT)
                slot = lax.broadcasted_iota(jnp.int32, (rows, width), 0)
                lane = lax.broadcasted_iota(jnp.int32, (rows, width), 1) + (here.start - block * wide)
                for h in range(1, ratio):
                    lane = jnp.where(lane >= rows, lane - rows, lane)
                shown = jnp.where(slot <= lane, scores[block * rows :], HIDDEN)
                if block:
                    before = jnp.where(used[:, :width], scores[:rows], HIDDEN)
                    shown = jnp.concatenate([before, shown], axis=0)
                top = jnp.max(shown, axis=0, keepdims=True)
                raw = jnp.exp2(shown - top)
                prob_grad = dot(values[i, :reach, :], cot[i, here, :], NT)
                raws[i, :reach, here] = raw
                grads[i, :reach, here] = prob_grad
                tops[i, :, here] = top
                sums[i, :, here] = jnp.sum(raw, axis=0, keepdims=True)
                crosses[i, :, here] = jnp.sum(raw * prob_grad, axis=0, keepdims=True)


def part_of(weights, score_grads, query, cot, out_ref, i, there, lanes):
    key_part = dot(score_grads[i, there, lanes], query[i, lanes, :], NN) * LN2
    value_part = dot(weights[i, there, lanes], cot[i, lanes, :], NN)
    out_ref[:, 2 * i * DH : (2 * i + 1) * DH] = key_part.astype(out_ref.dtype)
    out_ref[:, (2 * i + 1) * DH : (2 * i + 2) * DH] = value_part.astype(out_ref.dtype)


def early_kernel(query, tops, sums, packet, raws, new_tops, new_sums):
    half_groups, lanes = query.shape[:2]
    alone = lax.axis_index("ctx") < 2

    @pl.when(alone)
    def _():
        new_tops[...] = tops[...]
        new_sums[...] = sums[...]

    @pl.when(jnp.logical_not(alone))
    def _():
        used = used_slots(packet, 1)
        for i in range(half_groups):
            key = packet[:, i * DH : (i + 1) * DH]
            for here in chunks(0, lanes):
                width = here.stop - here.start
                shown = jnp.where(used[:, :width], dot(key, query[i, here, :], NT), HIDDEN)
                old_top = tops[i, :, here]
                top = jnp.maximum(old_top, jnp.max(shown, axis=0, keepdims=True))
                raw = jnp.exp2(shown - top)
                raws[i, :, here] = raw
                new_tops[i, :, here] = top
                new_sums[i, :, here] = sums[i, :, here] * jnp.exp2(old_top - top) + jnp.sum(raw, axis=0, keepdims=True)


def far_keys_kernel(query, cot, gate, first_tops, early_raws, tops, sums, *refs, blocks):
    packets = refs[:blocks]
    far_keys, raws, factors, far_factors, shrinks, inverses = refs[blocks : blocks + 6]
    parts, weights = refs[blocks + 6 : -1], refs[-1]
    rows = packets[0].shape[0]
    half_groups, lanes = query.shape[:2]
    alone = lax.axis_index("ctx") < 2

    @pl.when(alone)
    def _():
        for i in range(half_groups):
            inverse = 1.0 / sums[i]
            factors[i] = inverse * gate[...]
            inverses[i] = inverse

    @pl.when(jnp.logical_not(alone))
    def _():
        for i in range(half_groups):
            for j, packet in enumerate(packets):
                far_keys[i, j * rows : (j + 1) * rows, :] = packet[:, i * DH : (i + 1) * DH]
        used = [used_slots(packets[j], j % (blocks // 2) + 1) for j in range(1, blocks)]
        for i in range(half_groups):
            for here in chunks(0, lanes):
                width = here.stop - here.start
                scores = dot(far_keys[i, rows:, :], query[i, here, :], NT)
                shown = [
                    jnp.where(used[j][:, :width], scores[j * rows : (j + 1) * rows], HIDDEN)
                    for j in range(blocks - 1)
                ]
                shown = jnp.concatenate(shown, axis=0)
                old_top = tops[i, :, here]
                top = jnp.maximum(old_top, jnp.max(shown, axis=0, keepdims=True))
                raw = jnp.exp2(shown - top)
                shrink = jnp.exp2(old_top - top)
                first_shrink = jnp.exp2(first_tops[i, :, here] - top)
                inverse = 1.0 / (sums[i, :, here] * shrink + jnp.sum(raw, axis=0, keepdims=True))
                factor = inverse * gate[:, here]
                factors[i, :, here] = factor * first_shrink
                far_factors[i, :, here] = factor
                shrinks[i, :, here] = first_shrink
                inverses[i, :, here] = inverse
                raws[i, rows:, here] = raw.astype(raws.dtype)
                weights[i, rows:, here] = (raw * factor).astype(BF16)
                raw = early_raws[i, :, here] * shrink
                raws[i, :rows, here] = raw.astype(raws.dtype)
                weights[i, :rows, here] = (raw * factor).astype(BF16)
            for j, out_ref in enumerate(parts):
                there = slice(j * rows, (j + 1) * rows)
                out_ref[:, i * DH : (i + 1) * DH] = dot(weights[i, there, :], cot[i], NN).astype(BF16)


def far_values_kernel(query, cot, raws, far_factors, shrinks, inverses, crosses, *refs, blocks):
    packets = refs[:blocks]
    score_grads, deltas = refs[blocks : blocks + 2]
    parts, far_values = refs[blocks + 2 : -1], refs[-1]
    rows = packets[0].shape[0]
    half_groups, lanes = query.shape[:2]
    alone = lax.axis_index("ctx") < 2

    @pl.when(alone)
    def _():
        for i in range(half_groups):
            deltas[i] = crosses[i] * inverses[i]

    @pl.when(jnp.logical_not(alone))
    def _():
        for i in range(half_groups):
            for j, packet in enumerate(packets):
                far_values[i, j * rows : (j + 1) * rows, :] = packet[:, i * DH : (i + 1) * DH]
        for i in range(half_groups):
            for here in chunks(0, lanes):
                raw = raws[i, :, here].astype(F32)
                prob_grad = dot(far_values[i], cot[i, here, :], NT)
                cross = jnp.sum(raw * prob_grad, axis=0, keepdims=True)
                delta = (crosses[i, :, here] * shrinks[i, :, here] + cross) * inverses[i, :, here]
                deltas[i, :, here] = delta
                score_grad = raw * far_factors[i, :, here] * (prob_grad - delta)
                score_grads[i, :, here] = score_grad.astype(BF16)
            key_parts(score_grads, query, parts, i, len(parts))


def key_parts(score_grads, query, parts, i, first):
    rows = parts[0].shape[0]
    for j, out_ref in enumerate(parts):
        there = slice((first + j) * rows, (first + j + 1) * rows)
        part = dot(score_grads[i, there, :], query[i], NN) * LN2
        out_ref[:, i * DH : (i + 1) * DH] = part.astype(BF16)


def far_rest_kernel(query, score_grads, *parts):
    @pl.when(lax.axis_index("ctx") >= 2)
    def _():
        for i in range(query.shape[0]):
            key_parts(score_grads, query, parts, i, 0)


def near_kernel(
    raws, grads, factors, deltas, keys, query, cot, far_keys, far_grads, cos_ref, sin_ref,
    part_mine, query_mine, gate_mine, theirs, weights, score_grads, parts, acc, turned,
    *, ratio
):
    rows = part_mine.shape[0]
    half_groups = keys.shape[0]
    wide = ratio * rows
    half = half_groups * ratio * DH
    for i in range(half_groups):
        for block in range(2):
            reach = (block + 1) * rows
            for here in chunks(block * wide, (block + 1) * wide):
                gated = raws[i, :reach, here] * factors[i, :, here]
                weights[i, :reach, here] = gated.astype(BF16)
                score_grads[i, :reach, here] = (gated * (grads[i, :reach, here] - deltas[i, :, here])).astype(BF16)
        for block in range(2):
            there, lanes = slice(block * rows, (block + 1) * rows), slice(block * wide, 2 * wide)
            part_of(weights, score_grads, query, cot, parts.at[block], i, there, lanes)
            reach, lanes = (block + 1) * rows, slice(block * wide, (block + 1) * wide)
            acc[i, :, lanes] = dot(keys[i, :reach, :], score_grads[i, :reach, lanes], TN)

    @pl.when(lax.axis_index("ctx") >= 2)
    def _():
        for i in range(half_groups):
            acc[i] += dot(far_keys[i], far_grads[i], TN)

    core = core_of()
    cosine, sine = cos_ref[...], -sin_ref[...]
    for i in range(half_groups):
        turned[...] = jnp.transpose(acc[i] * SCALE)
        for h in range(ratio):
            here = slice((i * ratio + h) * DH, (i * ratio + h + 1) * DH)
            own = turned[pl.ds(pl.multiple_of(core * wide + h * rows, 16), rows), :]
            query_mine[:, here] = rotate(own, cosine, sine).astype(BF16)
            other = turned[pl.ds(pl.multiple_of((1 - core) * wide + h * rows, 16), rows), :]
            theirs[:rows, here] = other.astype(BF16)
    part_mine[...] = parts[core]
    theirs[:rows, half:] = parts[1 - core].astype(BF16)
    summed = deltas[0]
    for i in range(1, half_groups):
        summed = summed + deltas[i]
    gates = []
    for block in range(2):
        own = split_rows(summed[:, block * wide : (block + 1) * wide], 16)
        gates.append(joined_row(dot(own, chosen((wide, rows), ratio, 0), NN)))
    gate_mine[...] = jnp.where(core == 0, gates[0], gates[1])
    theirs[rows:, :rows] = split_rows(jnp.where(core == 0, gates[1], gates[0]), EXTRA)


def sum_first_kernel(part_mine, *refs):
    got, (own, other) = refs[:-2], refs[-2:]
    total = got[0][...].astype(F32)
    for ref in got[2::2]:
        total = total + ref[...].astype(F32)
    other[...] = total
    for i in range(own.shape[1] // DH):
        here = slice(i * DH, (i + 1) * DH)
        value = part_mine[:, (2 * i + 1) * DH : (2 * i + 2) * DH]
        for ref in got[1::2]:
            value = value + ref[:, here].astype(F32)
        own[:, here] = value


def sum_middle_kernel(value_own, part_mine, *refs):
    got, own = refs[:-1], refs[-1]
    for i in range(own.shape[1] // DH):
        here = slice(i * DH, (i + 1) * DH)
        key = part_mine[:, 2 * i * DH : (2 * i + 1) * DH]
        for ref in got:
            key = key + ref[:, here].astype(F32)
        own[:, here] = key


def sum_rest_kernel(key_own, *refs):
    got, other = refs[:-1], refs[-1]
    total = got[0][...].astype(F32)
    for ref in got[1:]:
        total = total + ref[...].astype(F32)
    other[...] = total


def finish_kernel(
    back, query_mine, gate_mine, key_own, value_own, key_other, value_other, valid, cos_ref, sin_ref,
    query_grad, key_grad, value_grad, gate_grad
):
    rows, half = value_own.shape
    wide = query_mine.shape[1]
    core = core_of()
    side = lambda which, width, at=0, size=None: pl.ds(pl.multiple_of(which * width + at, DH), size or width)
    cosine, sine = cos_ref[...], -sin_ref[...]
    for i in range(half // DH):
        here = slice(i * DH, (i + 1) * DH)
        there = wide + 2 * i * DH
        other_key = key_other[:, here] + back[:rows, there : there + DH].astype(F32)
        other_value = value_other[:, here] + back[:rows, there + DH : there + 2 * DH].astype(F32)
        for key_sum, value_sum, which in (
            (key_own[:, here], value_own[:, here], core),
            (other_key, other_value, 1 - core),
        ):
            to = side(which, half, i * DH, DH)
            key_grad[:, to] = rotate(key_sum, cosine, sine).astype(BF16)
            value_grad[:, to] = value_sum.astype(BF16)
    query_grad[:, side(core, wide)] = query_mine[...]
    for i in range(wide // DH):
        turned = rotate(back[:rows, i * DH : (i + 1) * DH].astype(F32), cosine, sine)
        query_grad[:, side(1 - core, wide, i * DH, DH)] = turned.astype(BF16)
    gate = gate_mine[...] + joined_row(back[rows:, :rows])
    gate_grad[...] = jnp.where(valid[...] > 0.0, gate, 0.0)


def per_device(query_rows, key_rows, value_rows, cotangent, router_gate, positions):
    rows, heads_width = query_rows.shape[1:]
    group_width = key_rows.shape[2]
    groups = group_width // DH
    ratio = heads_width // group_width
    half_groups, half_width = groups // 2, heads_width // 2
    parts = lax.axis_size("ctx")
    chips = parts // 2
    limit = parts * LOCAL
    wide = ratio * rows
    params = pltpu.CompilerParams(vmem_limit_bytes=(16 + 4 * chips) * 1024 * 1024)

    def call(kernel, name, outs, *args, scratch=(), flops=10**6, in_hbm=False):
        if in_hbm:
            args = [pltpu.with_memory_space_constraint(arg, pltpu.HBM) for arg in args]
        spec = pl.BlockSpec(memory_space=pltpu.HBM if in_hbm else pltpu.VMEM)
        return pl.pallas_call(
            kernel,
            out_shape=[jax.ShapeDtypeStruct(*out) for out in outs],
            in_specs=[spec] * len(args),
            scratch_shapes=list(scratch),
            compiler_params=params,
            cost_estimate=pl.CostEstimate(flops=flops, bytes_accessed=1000, transcendentals=0),
            name=name,
        )(*args)

    index = np.arange(DH) % (DH // 2)
    freq = jnp.asarray((THETA ** (-2.0 * index / DH)).astype(np.float32))[None]
    packet = ((rows, group_width // 2), BF16)
    table = ((rows, DH), F32)
    line = ((1, rows), F32)
    theirs_shape = ((rows + EXTRA, heads_width + group_width), BF16)
    key_mine, key_theirs, value_mine, value_theirs, theirs, gate_mine, valid, cosine, sine = call(
        functools.partial(pack_kernel, limit=limit),
        "pack",
        [packet, packet, packet, packet, theirs_shape, line, line, table, table],
        key_rows[0],
        value_rows[0],
        query_rows[0],
        cotangent[0],
        router_gate,
        positions,
        freq,
        in_hbm=True,
        flops=5 * 10**9,
        scratch=[
            pltpu.VMEM((rows, group_width), BF16),
            pltpu.VMEM((rows, group_width), BF16),
            pltpu.VMEM((rows, half_width), BF16),
            pltpu.VMEM(*line),
            pltpu.VMEM((1, rows), jnp.int32),
            pltpu.VMEM((1, DH), F32),
            pltpu.SemaphoreType.DMA((7,)),
        ],
    )

    hop = [[(2 * x + k, 2 * (x + s) + k) for x in range(chips - s) for k in range(2)] for s in range(chips)]
    cross = [[(a, b + 1 - 2 * (b % 2)) for a, b in pairs] for pairs in hop]
    back_hop = [[(b, a) for a, b in pairs] for pairs in hop]
    back_cross = [[(b, a) for a, b in pairs] for pairs in cross]

    steps = range(1, chips)

    def send(sib, own, sib_pairs, own_pairs):
        sib = [lax.ppermute(sib[s - 1], "ctx", sib_pairs[s]) for s in steps]
        return sib, [lax.ppermute(own[s - 1], "ctx", own_pairs[s]) for s in steps]

    sib_keys, own_keys = send([key_theirs] * chips, [key_mine] * chips, cross, hop)
    sib_values, own_values = send([value_theirs] * chips, [value_mine] * chips, cross, hop)

    pairs = [[2 * x, 2 * x + 1] for x in range(chips)]
    swap = [pair for a, b in pairs for pair in ((a, b), (b, a))]
    sib = lax.ppermute(theirs, "ctx", swap)

    row = ((half_groups, 1, 2 * wide), F32)
    table = ((half_groups, 2 * rows, 2 * wide), F32)
    kv_table = ((half_groups, 2 * rows, DH), BF16)
    q_table = ((half_groups, 2 * wide, DH), BF16)
    keys, query, cot, gate_row, raws, grads, tops, sums, crosses = call(
        functools.partial(local_kernel, ratio=ratio),
        "local_scores",
        [kv_table, q_table, q_table, ((1, 2 * wide), F32), table, table, row, row, row],
        key_mine,
        value_mine,
        query_rows[0],
        cotangent[0],
        cosine,
        sine,
        gate_mine,
        sib,
        scratch=[pltpu.VMEM(*kv_table)],
        flops=3 * 10**6,
    )

    blocks = 2 * (chips - 1)
    far_rows = ((half_groups, blocks * rows, DH), BF16)
    far_low = ((half_groups, blocks * rows, 2 * wide), BF16)
    far_table = (far_low[0], F32 if chips == 2 else BF16)
    early_table = ((half_groups, rows, 2 * wide), F32)
    early_raws, early_tops, early_sums = call(
        early_kernel, "early_keys", [early_table, row, row], query, tops, sums, sib_keys[0]
    )
    far_keys, far_raws, factors, far_factors, shrinks, inverses, *parts = call(
        functools.partial(far_keys_kernel, blocks=blocks),
        "far_keys",
        [far_rows, far_table, row, row, row, row] + [packet] * blocks,
        query,
        cot,
        gate_row,
        tops,
        early_raws,
        early_tops,
        early_sums,
        *sib_keys,
        *own_keys,
        scratch=[pltpu.VMEM(*far_low)],
    )
    sib_value_got, own_value_got = send(parts[: chips - 1], parts[chips - 1 :], back_cross, back_hop)
    far_grads, deltas, *parts = call(
        functools.partial(far_values_kernel, blocks=blocks),
        "far_values",
        [far_low, row] + [packet] * (chips - 1),
        query,
        cot,
        far_raws,
        far_factors,
        shrinks,
        inverses,
        crosses,
        *sib_values,
        *own_values,
        scratch=[pltpu.VMEM(*far_rows)],
    )
    own_key_got = [lax.ppermute(parts[s - 1], "ctx", back_hop[s]) for s in steps]
    parts = call(far_rest_kernel, "far_rest", [packet] * (chips - 1), query, far_grads)
    sib_key_got = [lax.ppermute(parts[s - 1], "ctx", back_cross[s]) for s in steps]

    part_mine, query_mine, gate_part, theirs = call(
        functools.partial(near_kernel, ratio=ratio),
        "near_grads",
        [
            ((rows, group_width), F32),
            ((rows, half_width), BF16),
            ((1, rows), F32),
            ((rows + EXTRA, half_width + group_width), BF16),
        ],
        raws,
        grads,
        factors,
        deltas,
        keys,
        query,
        cot,
        far_keys,
        far_grads,
        cosine,
        sine,
        flops=4 * 10**6,
        scratch=[
            pltpu.VMEM((half_groups, 2 * rows, 2 * wide), BF16),
            pltpu.VMEM((half_groups, 2 * rows, 2 * wide), BF16),
            pltpu.VMEM((2, rows, group_width), F32),
            pltpu.VMEM((half_groups, DH, 2 * wide), F32),
            pltpu.VMEM((2 * wide, DH), F32),
        ],
    )
    back = lax.ppermute(theirs, "ctx", swap)
    total = ((rows, group_width // 2), F32)
    value_own, value_other = call(
        sum_first_kernel,
        "sum_first",
        [total, total],
        part_mine,
        *[part for pair in zip(sib_value_got, own_value_got) for part in pair],
        flops=3 * 10**8,
    )
    (key_own,) = call(sum_middle_kernel, "sum_middle", [total], value_own, part_mine, *own_key_got, flops=5 * 10**9)
    (key_other,) = call(sum_rest_kernel, "sum_rest", [total], key_own, *sib_key_got, flops=5 * 10**9)
    query_grad, key_grad, value_grad, gate_grad = call(
        finish_kernel,
        "finish",
        [((rows, heads_width), BF16)] + [((rows, group_width), BF16)] * 2 + [line],
        back,
        query_mine,
        gate_part,
        key_own,
        value_own,
        key_other,
        value_other,
        valid,
        cosine,
        sine,
    )
    return (query_grad[None], key_grad[None], value_grad[None], gate_grad)


def solution(mesh):
    wide = P(("group", "dp"), "ctx", None)
    narrow = P(("group", "dp"), "ctx")
    return jax.shard_map(
        per_device,
        mesh=mesh,
        in_specs=(wide, wide, wide, wide, narrow, narrow),
        out_specs=(wide, wide, wide, narrow),
        check_vma=False,
    )
```

```python
import functools
import math

import jax
import jax.numpy as jnp
import numpy as np
from jax import lax
from jax.experimental import pallas as pl
from jax.experimental.pallas import tpu as pltpu
from jax.sharding import PartitionSpec as P

DH = 128
LOCAL = 1024
THETA = 500000.0
EXTRA = 16
HIDDEN = -1e30
UNUSED = 2.0**14
SCALE = DH**-0.5
LOG2E = math.log2(math.e)
LN2 = math.log(2.0)

NT = (((1,), (1,)), ((), ()))
NN = (((1,), (0,)), ((), ()))
TN = (((0,), (0,)), ((), ()))
F32 = jnp.float32
BF16 = jnp.bfloat16


def few_bits(value, bits):
    unit = 2.0 ** (math.floor(math.log2(value)) + 1 - bits)
    return math.floor(value / unit) * unit


QUARTER_1 = few_bits(math.pi / 2, 10)
QUARTER_2 = few_bits(math.pi / 2 - QUARTER_1, 10)
QUARTER_3 = math.pi / 2 - QUARTER_1 - QUARTER_2


def dot(a, b, dims):
    return lax.dot_general(a, b, dims, preferred_element_type=F32)


def core_of():
    return lax.rem(lax.axis_index("ctx"), 2)


def rotate(values, cosine, sine):
    return values * cosine + pltpu.roll(values, DH // 2, 1) * sine


def sine_cosine(angle):
    turns = jnp.floor(angle * (2.0 / math.pi) + 0.5)
    rest = ((angle - turns * QUARTER_1) - turns * QUARTER_2) - turns * QUARTER_3
    square = rest * rest
    sine = ((-1.9515295891e-4 * square + 8.3321608736e-3) * square - 1.6666654611e-1) * square * rest + rest
    cosine = (2.443315711809948e-5 * square - 1.388731625493765e-3) * square + 4.166664568298827e-2
    cosine = cosine * square * square - 0.5 * square + 1.0
    quarter = turns.astype(jnp.int32)
    odd = (quarter & 1) == 1
    first, second = jnp.where(odd, cosine, sine), jnp.where(odd, sine, cosine)
    return (
        jnp.where((quarter & 2) == 2, -first, first),
        jnp.where(((quarter + 1) & 2) == 2, -second, second),
    )


def split_rows(row, height):
    high = row.astype(BF16).astype(F32)
    middle = (row - high).astype(BF16).astype(F32)
    low = row - high - middle
    line = lax.broadcasted_iota(jnp.int32, (height, row.shape[1]), 0)
    rows = jnp.where(line == 0, high, jnp.where(line == 1, middle, jnp.where(line == 2, low, 0.0)))
    return rows.astype(BF16)


def joined_row(rows):
    return jnp.sum(rows.astype(F32), axis=0, keepdims=True)


def pack_kernel(
    key_in, value_in, query_in, cot_in, gate_in, pos_in, freq_in,
    key_mine, key_theirs, value_mine, value_theirs, theirs, gate_mine, valid, cos_ref, sin_ref,
    key, value, query, gate, pos, freq, sems, *, limit
):
    rows, width = key.shape
    side_width = width // 2
    half = query.shape[1]
    core = core_of()
    there = pl.ds(pl.multiple_of((1 - core) * half, DH), half)
    loads = [(pos_in, pos), (freq_in, freq), (key_in, key), (value_in, value), (query_in.at[:, there], query)]
    loads += [(gate_in, gate), (cot_in.at[:, there], theirs.at[:rows, half : 2 * half])]
    loads = [pltpu.make_async_copy(source, target, sems.at[i]) for i, (source, target) in enumerate(loads)]
    for copy in loads:
        copy.start()
    down = lax.broadcasted_iota(jnp.int32, (rows, rows), 0)
    along = lax.broadcasted_iota(jnp.int32, (rows, rows), 1)
    lane = lax.broadcasted_iota(jnp.int32, (rows, DH), 1)
    loads[0].wait()
    loads[1].wait()
    places = pos[...]
    column = jnp.sum(jnp.where(down == along, places.astype(F32), 0.0), axis=1, keepdims=True)
    sine, cosine = sine_cosine(column * freq[...])
    sine = jnp.where(lane < DH // 2, -sine, sine)
    cos_ref[...] = cosine
    sin_ref[...] = sine
    used = jnp.broadcast_to(column, (rows, DH)) < limit
    loads[2].wait()
    loads[3].wait()
    for key_out, value_out, side in ((key_mine, value_mine, core), (key_theirs, value_theirs, 1 - core)):
        for i in range(side_width // DH):
            from_ = pl.ds(pl.multiple_of(side * side_width + i * DH, DH), DH)
            turned = jnp.where(used, rotate(key[:, from_].astype(F32), cosine, sine), UNUSED).astype(BF16)
            key_out[:, i * DH : (i + 1) * DH] = turned
            value_out[:, i * DH : (i + 1) * DH] = value[:, from_]
    theirs[:rows, 2 * half : 2 * half + side_width] = key_theirs[...]
    theirs[:rows, 2 * half + side_width :] = value_theirs[...]
    loads[4].wait()
    cosine, sine = cosine * (SCALE * LOG2E), sine * (SCALE * LOG2E)
    for i in range(half // DH):
        here = slice(i * DH, (i + 1) * DH)
        theirs[:rows, here] = rotate(query[:, here].astype(F32), cosine, sine).astype(BF16)
    loads[5].wait()
    valid[...] = jnp.where(places < limit, 1.0, 0.0)
    used_gate = jnp.where(places < limit, gate[...], 0.0)
    gate_mine[...] = used_gate
    theirs[rows:, :rows] = split_rows(used_gate, EXTRA)
    loads[6].wait()


def chosen(shape, ratio, dim):
    down = lax.broadcasted_iota(jnp.int32, shape, 0)
    along = lax.broadcasted_iota(jnp.int32, shape, 1)
    rows = shape[1 - dim]
    long, short = (down, along) if dim == 0 else (along, down)
    for _ in range(1, ratio):
        long = jnp.where(long >= rows, long - rows, long)
    return jnp.where(long == short, 1.0, 0.0).astype(BF16)


def chunks(low, high):
    return [slice(at, min(at + 256, high)) for at in range(low, high, 256)]


def used_slots(key, here):
    chip = lax.div(lax.axis_index("ctx"), 2)
    first = key[:, :DH].astype(F32)[:, :1]
    return jnp.broadcast_to(first, (key.shape[0], 256)) < jnp.where(chip >= here, UNUSED / 2, -UNUSED)


def local_kernel(
    key_mine, value_mine, query_in, cot_in, cos_ref, sin_ref, gate_mine, sib,
    keys, query, cot, gate, raws, grads, tops, sums, crosses, values, *, ratio
):
    rows = key_mine.shape[0]
    half_groups = keys.shape[0]
    wide = ratio * rows
    half = half_groups * ratio * DH
    core = core_of()
    spread = chosen((rows, wide), ratio, 1)
    key_sib = sib.at[:rows, 2 * half : 2 * half + half_groups * DH]
    value_sib = sib.at[:rows, 2 * half + half_groups * DH :]
    cosine, sine = cos_ref[...] * (SCALE * LOG2E), sin_ref[...] * (SCALE * LOG2E)
    for key, value, side in ((key_mine, value_mine, core), (key_sib, value_sib, 1 - core)):
        there = pl.ds(pl.multiple_of(side * rows, 16), rows)
        for i in range(half_groups):
            keys[i, there, :] = key[:, i * DH : (i + 1) * DH]
            values[i, there, :] = value[:, i * DH : (i + 1) * DH]
            for h in range(ratio):
                to = pl.ds(pl.multiple_of(side * wide + h * rows, 16), rows)
                at = (i * ratio + h) * DH
                if key is key_mine:
                    here = pl.ds(pl.multiple_of(core * half + at, DH), DH)
                    query[i, to, :] = rotate(query_in[:, here].astype(F32), cosine, sine).astype(BF16)
                    cot[i, to, :] = cot_in[:, here]
                else:
                    query[i, to, :] = sib[:rows, at : at + DH]
                    cot[i, to, :] = sib[:rows, half + at : half + at + DH]
    own = joined_row(dot(split_rows(gate_mine[...], EXTRA), spread, NN))
    other = joined_row(dot(sib[rows:, :rows], spread, NN))
    gate[:, :wide] = jnp.where(core == 0, own, other)
    gate[:, wide:] = jnp.where(core == 0, other, own)
    used = used_slots(keys[0, :rows, :], 0)
    for i in range(half_groups):
        for block in range(2):
            reach = (block + 1) * rows
            for here in chunks(block * wide, (block + 1) * wide):
                width = here.stop - here.start
                scores = dot(keys[i, :reach, :], query[i, here, :], NT)
                slot = lax.broadcasted_iota(jnp.int32, (rows, width), 0)
                lane = lax.broadcasted_iota(jnp.int32, (rows, width), 1) + (here.start - block * wide)
                for h in range(1, ratio):
                    lane = jnp.where(lane >= rows, lane - rows, lane)
                shown = jnp.where(slot <= lane, scores[block * rows :], HIDDEN)
                if block:
                    before = jnp.where(used[:, :width], scores[:rows], HIDDEN)
                    shown = jnp.concatenate([before, shown], axis=0)
                top = jnp.max(shown, axis=0, keepdims=True)
                raw = jnp.exp2(shown - top)
                prob_grad = dot(values[i, :reach, :], cot[i, here, :], NT)
                raws[i, :reach, here] = raw
                grads[i, :reach, here] = prob_grad
                tops[i, :, here] = top
                sums[i, :, here] = jnp.sum(raw, axis=0, keepdims=True)
                crosses[i, :, here] = jnp.sum(raw * prob_grad, axis=0, keepdims=True)


def part_of(weights, score_grads, query, cot, out_ref, i, there, lanes):
    key_part = dot(score_grads[i, there, lanes], query[i, lanes, :], NN) * LN2
    value_part = dot(weights[i, there, lanes], cot[i, lanes, :], NN)
    out_ref[:, 2 * i * DH : (2 * i + 1) * DH] = key_part.astype(out_ref.dtype)
    out_ref[:, (2 * i + 1) * DH : (2 * i + 2) * DH] = value_part.astype(out_ref.dtype)


def early_kernel(query, tops, sums, packet, raws, new_tops, new_sums):
    half_groups, lanes = query.shape[:2]
    alone = lax.axis_index("ctx") < 2

    @pl.when(alone)
    def _():
        new_tops[...] = tops[...]
        new_sums[...] = sums[...]

    @pl.when(jnp.logical_not(alone))
    def _():
        used = used_slots(packet, 1)
        for i in range(half_groups):
            key = packet[:, i * DH : (i + 1) * DH]
            for here in chunks(0, lanes):
                width = here.stop - here.start
                shown = jnp.where(used[:, :width], dot(key, query[i, here, :], NT), HIDDEN)
                old_top = tops[i, :, here]
                top = jnp.maximum(old_top, jnp.max(shown, axis=0, keepdims=True))
                raw = jnp.exp2(shown - top)
                raws[i, :, here] = raw
                new_tops[i, :, here] = top
                new_sums[i, :, here] = sums[i, :, here] * jnp.exp2(old_top - top) + jnp.sum(raw, axis=0, keepdims=True)


def far_keys_kernel(query, cot, gate, first_tops, early_raws, tops, sums, *refs, blocks):
    packets = refs[:blocks]
    far_keys, raws, factors, far_factors, shrinks, inverses = refs[blocks : blocks + 6]
    parts, weights = refs[blocks + 6 : -1], refs[-1]
    rows = packets[0].shape[0]
    half_groups, lanes = query.shape[:2]
    alone = lax.axis_index("ctx") < 2

    @pl.when(alone)
    def _():
        for i in range(half_groups):
            inverse = 1.0 / sums[i]
            factors[i] = inverse * gate[...]
            inverses[i] = inverse

    @pl.when(jnp.logical_not(alone))
    def _():
        for i in range(half_groups):
            for j, packet in enumerate(packets):
                far_keys[i, j * rows : (j + 1) * rows, :] = packet[:, i * DH : (i + 1) * DH]
        used = [used_slots(packets[j], j % (blocks // 2) + 1) for j in range(1, blocks)]
        for i in range(half_groups):
            for here in chunks(0, lanes):
                width = here.stop - here.start
                scores = dot(far_keys[i, rows:, :], query[i, here, :], NT)
                shown = [
                    jnp.where(used[j][:, :width], scores[j * rows : (j + 1) * rows], HIDDEN)
                    for j in range(blocks - 1)
                ]
                shown = jnp.concatenate(shown, axis=0)
                old_top = tops[i, :, here]
                top = jnp.maximum(old_top, jnp.max(shown, axis=0, keepdims=True))
                raw = jnp.exp2(shown - top)
                shrink = jnp.exp2(old_top - top)
                first_shrink = jnp.exp2(first_tops[i, :, here] - top)
                inverse = 1.0 / (sums[i, :, here] * shrink + jnp.sum(raw, axis=0, keepdims=True))
                factor = inverse * gate[:, here]
                factors[i, :, here] = factor * first_shrink
                far_factors[i, :, here] = factor
                shrinks[i, :, here] = first_shrink
                inverses[i, :, here] = inverse
                raws[i, rows:, here] = raw.astype(raws.dtype)
                weights[i, rows:, here] = (raw * factor).astype(BF16)
                raw = early_raws[i, :, here] * shrink
                raws[i, :rows, here] = raw.astype(raws.dtype)
                weights[i, :rows, here] = (raw * factor).astype(BF16)
            for j, out_ref in enumerate(parts):
                there = slice(j * rows, (j + 1) * rows)
                out_ref[:, i * DH : (i + 1) * DH] = dot(weights[i, there, :], cot[i], NN).astype(BF16)


def far_values_kernel(query, cot, raws, far_factors, shrinks, inverses, crosses, *refs, blocks):
    packets = refs[:blocks]
    score_grads, deltas = refs[blocks : blocks + 2]
    parts, far_values = refs[blocks + 2 : -1], refs[-1]
    rows = packets[0].shape[0]
    half_groups, lanes = query.shape[:2]
    alone = lax.axis_index("ctx") < 2

    @pl.when(alone)
    def _():
        for i in range(half_groups):
            deltas[i] = crosses[i] * inverses[i]

    @pl.when(jnp.logical_not(alone))
    def _():
        for i in range(half_groups):
            for j, packet in enumerate(packets):
                far_values[i, j * rows : (j + 1) * rows, :] = packet[:, i * DH : (i + 1) * DH]
        for i in range(half_groups):
            for here in chunks(0, lanes):
                raw = raws[i, :, here].astype(F32)
                prob_grad = dot(far_values[i], cot[i, here, :], NT)
                cross = jnp.sum(raw * prob_grad, axis=0, keepdims=True)
                delta = (crosses[i, :, here] * shrinks[i, :, here] + cross) * inverses[i, :, here]
                deltas[i, :, here] = delta
                score_grad = raw * far_factors[i, :, here] * (prob_grad - delta)
                score_grads[i, :, here] = score_grad.astype(BF16)
            key_parts(score_grads, query, parts, i, 0)


def key_parts(score_grads, query, parts, i, first):
    rows = parts[0].shape[0]
    for j, out_ref in enumerate(parts):
        there = slice((first + j) * rows, (first + j + 1) * rows)
        part = dot(score_grads[i, there, :], query[i], NN) * LN2
        out_ref[:, i * DH : (i + 1) * DH] = part.astype(BF16)


def far_rest_kernel(query, score_grads, *parts):
    @pl.when(lax.axis_index("ctx") >= 2)
    def _():
        for i in range(query.shape[0]):
            key_parts(score_grads, query, parts, i, len(parts))


def near_kernel(
    raws, grads, factors, deltas, keys, query, cot, far_keys, far_grads, cos_ref, sin_ref,
    part_mine, query_mine, gate_mine, theirs, weights, score_grads, parts, acc, turned,
    *, ratio
):
    rows = part_mine.shape[0]
    half_groups = keys.shape[0]
    wide = ratio * rows
    half = half_groups * ratio * DH
    for i in range(half_groups):
        for block in range(2):
            reach = (block + 1) * rows
            for here in chunks(block * wide, (block + 1) * wide):
                gated = raws[i, :reach, here] * factors[i, :, here]
                weights[i, :reach, here] = gated.astype(BF16)
                score_grads[i, :reach, here] = (gated * (grads[i, :reach, here] - deltas[i, :, here])).astype(BF16)
        for block in range(2):
            there, lanes = slice(block * rows, (block + 1) * rows), slice(block * wide, 2 * wide)
            part_of(weights, score_grads, query, cot, parts.at[block], i, there, lanes)
            reach, lanes = (block + 1) * rows, slice(block * wide, (block + 1) * wide)
            acc[i, :, lanes] = dot(keys[i, :reach, :], score_grads[i, :reach, lanes], TN)

    @pl.when(lax.axis_index("ctx") >= 2)
    def _():
        for i in range(half_groups):
            acc[i] += dot(far_keys[i], far_grads[i], TN)

    core = core_of()
    cosine, sine = cos_ref[...], -sin_ref[...]
    for i in range(half_groups):
        turned[...] = jnp.transpose(acc[i] * SCALE)
        for h in range(ratio):
            here = slice((i * ratio + h) * DH, (i * ratio + h + 1) * DH)
            own = turned[pl.ds(pl.multiple_of(core * wide + h * rows, 16), rows), :]
            query_mine[:, here] = rotate(own, cosine, sine).astype(BF16)
            other = turned[pl.ds(pl.multiple_of((1 - core) * wide + h * rows, 16), rows), :]
            theirs[:rows, here] = other.astype(BF16)
    part_mine[...] = parts[core]
    theirs[:rows, half:] = parts[1 - core].astype(BF16)
    summed = deltas[0]
    for i in range(1, half_groups):
        summed = summed + deltas[i]
    gates = []
    for block in range(2):
        own = split_rows(summed[:, block * wide : (block + 1) * wide], 16)
        gates.append(joined_row(dot(own, chosen((wide, rows), ratio, 0), NN)))
    gate_mine[...] = jnp.where(core == 0, gates[0], gates[1])
    theirs[rows:, :rows] = split_rows(jnp.where(core == 0, gates[1], gates[0]), EXTRA)


def sum_first_kernel(part_mine, *refs):
    got, (own, other) = refs[:-2], refs[-2:]
    total = got[0][...].astype(F32)
    for ref in got[2::2]:
        total = total + ref[...].astype(F32)
    other[...] = total
    for i in range(own.shape[1] // DH):
        here = slice(i * DH, (i + 1) * DH)
        value = part_mine[:, (2 * i + 1) * DH : (2 * i + 2) * DH]
        for ref in got[1::2]:
            value = value + ref[:, here].astype(F32)
        own[:, here] = value


def sum_middle_kernel(value_own, part_mine, *refs):
    got, own = refs[:-1], refs[-1]
    for i in range(own.shape[1] // DH):
        here = slice(i * DH, (i + 1) * DH)
        key = part_mine[:, 2 * i * DH : (2 * i + 1) * DH]
        for ref in got:
            key = key + ref[:, here].astype(F32)
        own[:, here] = key


def sum_rest_kernel(key_own, *refs):
    got, other = refs[:-1], refs[-1]
    total = got[0][...].astype(F32)
    for ref in got[1:]:
        total = total + ref[...].astype(F32)
    other[...] = total


def finish_kernel(
    back, query_mine, gate_mine, key_own, value_own, key_other, value_other, valid, cos_ref, sin_ref,
    query_grad, key_grad, value_grad, gate_grad
):
    rows, half = value_own.shape
    wide = query_mine.shape[1]
    core = core_of()
    side = lambda which, width, at=0, size=None: pl.ds(pl.multiple_of(which * width + at, DH), size or width)
    cosine, sine = cos_ref[...], -sin_ref[...]
    for i in range(half // DH):
        here = slice(i * DH, (i + 1) * DH)
        there = wide + 2 * i * DH
        other_key = key_other[:, here] + back[:rows, there : there + DH].astype(F32)
        other_value = value_other[:, here] + back[:rows, there + DH : there + 2 * DH].astype(F32)
        for key_sum, value_sum, which in (
            (key_own[:, here], value_own[:, here], core),
            (other_key, other_value, 1 - core),
        ):
            to = side(which, half, i * DH, DH)
            key_grad[:, to] = rotate(key_sum, cosine, sine).astype(BF16)
            value_grad[:, to] = value_sum.astype(BF16)
    query_grad[:, side(core, wide)] = query_mine[...]
    for i in range(wide // DH):
        turned = rotate(back[:rows, i * DH : (i + 1) * DH].astype(F32), cosine, sine)
        query_grad[:, side(1 - core, wide, i * DH, DH)] = turned.astype(BF16)
    gate = gate_mine[...] + joined_row(back[rows:, :rows])
    gate_grad[...] = jnp.where(valid[...] > 0.0, gate, 0.0)


def per_device(query_rows, key_rows, value_rows, cotangent, router_gate, positions):
    rows, heads_width = query_rows.shape[1:]
    group_width = key_rows.shape[2]
    groups = group_width // DH
    ratio = heads_width // group_width
    half_groups, half_width = groups // 2, heads_width // 2
    parts = lax.axis_size("ctx")
    chips = parts // 2
    limit = parts * LOCAL
    wide = ratio * rows
    params = pltpu.CompilerParams(vmem_limit_bytes=(16 + 4 * chips) * 1024 * 1024)

    def call(kernel, name, outs, *args, scratch=(), flops=10**6, in_hbm=False):
        if in_hbm:
            args = [pltpu.with_memory_space_constraint(arg, pltpu.HBM) for arg in args]
        spec = pl.BlockSpec(memory_space=pltpu.HBM if in_hbm else pltpu.VMEM)
        return pl.pallas_call(
            kernel,
            out_shape=[jax.ShapeDtypeStruct(*out) for out in outs],
            in_specs=[spec] * len(args),
            scratch_shapes=list(scratch),
            compiler_params=params,
            cost_estimate=pl.CostEstimate(flops=flops, bytes_accessed=1000, transcendentals=0),
            name=name,
        )(*args)

    index = np.arange(DH) % (DH // 2)
    freq = jnp.asarray((THETA ** (-2.0 * index / DH)).astype(np.float32))[None]
    packet = ((rows, group_width // 2), BF16)
    table = ((rows, DH), F32)
    line = ((1, rows), F32)
    theirs_shape = ((rows + EXTRA, heads_width + group_width), BF16)
    key_mine, key_theirs, value_mine, value_theirs, theirs, gate_mine, valid, cosine, sine = call(
        functools.partial(pack_kernel, limit=limit),
        "pack",
        [packet, packet, packet, packet, theirs_shape, line, line, table, table],
        key_rows[0],
        value_rows[0],
        query_rows[0],
        cotangent[0],
        router_gate,
        positions,
        freq,
        in_hbm=True,
        flops=5 * 10**9,
        scratch=[
            pltpu.VMEM((rows, group_width), BF16),
            pltpu.VMEM((rows, group_width), BF16),
            pltpu.VMEM((rows, half_width), BF16),
            pltpu.VMEM(*line),
            pltpu.VMEM((1, rows), jnp.int32),
            pltpu.VMEM((1, DH), F32),
            pltpu.SemaphoreType.DMA((7,)),
        ],
    )

    hop = [[(2 * x + k, 2 * (x + s) + k) for x in range(chips - s) for k in range(2)] for s in range(chips)]
    cross = [[(a, b + 1 - 2 * (b % 2)) for a, b in pairs] for pairs in hop]
    back_hop = [[(b, a) for a, b in pairs] for pairs in hop]
    back_cross = [[(b, a) for a, b in pairs] for pairs in cross]

    steps = range(1, chips)

    def send(sib, own, sib_pairs, own_pairs):
        sib = [lax.ppermute(sib[s - 1], "ctx", sib_pairs[s]) for s in steps]
        return sib, [lax.ppermute(own[s - 1], "ctx", own_pairs[s]) for s in steps]

    sib_keys, own_keys = send([key_theirs] * chips, [key_mine] * chips, cross, hop)
    sib_values, own_values = send([value_theirs] * chips, [value_mine] * chips, cross, hop)

    pairs = [[2 * x, 2 * x + 1] for x in range(chips)]
    swap = [pair for a, b in pairs for pair in ((a, b), (b, a))]
    sib = lax.ppermute(theirs, "ctx", swap)

    row = ((half_groups, 1, 2 * wide), F32)
    table = ((half_groups, 2 * rows, 2 * wide), F32)
    kv_table = ((half_groups, 2 * rows, DH), BF16)
    q_table = ((half_groups, 2 * wide, DH), BF16)
    keys, query, cot, gate_row, raws, grads, tops, sums, crosses = call(
        functools.partial(local_kernel, ratio=ratio),
        "local_scores",
        [kv_table, q_table, q_table, ((1, 2 * wide), F32), table, table, row, row, row],
        key_mine,
        value_mine,
        query_rows[0],
        cotangent[0],
        cosine,
        sine,
        gate_mine,
        sib,
        scratch=[pltpu.VMEM(*kv_table)],
        flops=3 * 10**6,
    )

    blocks = 2 * (chips - 1)
    far_rows = ((half_groups, blocks * rows, DH), BF16)
    far_low = ((half_groups, blocks * rows, 2 * wide), BF16)
    far_table = (far_low[0], F32 if chips == 2 else BF16)
    early_table = ((half_groups, rows, 2 * wide), F32)
    early_raws, early_tops, early_sums = call(
        early_kernel, "early_keys", [early_table, row, row], query, tops, sums, own_keys[0]
    )
    far_keys, far_raws, factors, far_factors, shrinks, inverses, *parts = call(
        functools.partial(far_keys_kernel, blocks=blocks),
        "far_keys",
        [far_rows, far_table, row, row, row, row] + [packet] * blocks,
        query,
        cot,
        gate_row,
        tops,
        early_raws,
        early_tops,
        early_sums,
        *own_keys,
        *sib_keys,
        scratch=[pltpu.VMEM(*far_low)],
    )
    sib_value_got, own_value_got = send(parts[chips - 1 :], parts[: chips - 1], back_cross, back_hop)
    far_grads, deltas, *parts = call(
        functools.partial(far_values_kernel, blocks=blocks),
        "far_values",
        [far_low, row] + [packet] * (chips - 1),
        query,
        cot,
        far_raws,
        far_factors,
        shrinks,
        inverses,
        crosses,
        *own_values,
        *sib_values,
        scratch=[pltpu.VMEM(*far_rows)],
    )
    own_key_got = [lax.ppermute(parts[s - 1], "ctx", back_hop[s]) for s in steps]
    parts = call(far_rest_kernel, "far_rest", [packet] * (chips - 1), query, far_grads)
    sib_key_got = [lax.ppermute(parts[s - 1], "ctx", back_cross[s]) for s in steps]

    part_mine, query_mine, gate_part, theirs = call(
        functools.partial(near_kernel, ratio=ratio),
        "near_grads",
        [
            ((rows, group_width), F32),
            ((rows, half_width), BF16),
            ((1, rows), F32),
            ((rows + EXTRA, half_width + group_width), BF16),
        ],
        raws,
        grads,
        factors,
        deltas,
        keys,
        query,
        cot,
        far_keys,
        far_grads,
        cosine,
        sine,
        flops=4 * 10**6,
        scratch=[
            pltpu.VMEM((half_groups, 2 * rows, 2 * wide), BF16),
            pltpu.VMEM((half_groups, 2 * rows, 2 * wide), BF16),
            pltpu.VMEM((2, rows, group_width), F32),
            pltpu.VMEM((half_groups, DH, 2 * wide), F32),
            pltpu.VMEM((2 * wide, DH), F32),
        ],
    )
    back = lax.ppermute(theirs, "ctx", swap)
    total = ((rows, group_width // 2), F32)
    value_own, value_other = call(
        sum_first_kernel,
        "sum_first",
        [total, total],
        part_mine,
        *[part for pair in zip(sib_value_got, own_value_got) for part in pair],
        flops=3 * 10**8,
    )
    (key_own,) = call(sum_middle_kernel, "sum_middle", [total], value_own, part_mine, *own_key_got, flops=5 * 10**9)
    (key_other,) = call(sum_rest_kernel, "sum_rest", [total], key_own, *sib_key_got, flops=5 * 10**9)
    query_grad, key_grad, value_grad, gate_grad = call(
        finish_kernel,
        "finish",
        [((rows, heads_width), BF16)] + [((rows, group_width), BF16)] * 2 + [line],
        back,
        query_mine,
        gate_part,
        key_own,
        value_own,
        key_other,
        value_other,
        valid,
        cosine,
        sine,
    )
    return (query_grad[None], key_grad[None], value_grad[None], gate_grad)


def solution(mesh):
    wide = P(("group", "dp"), "ctx", None)
    narrow = P(("group", "dp"), "ctx")
    return jax.shard_map(
        per_device,
        mesh=mesh,
        in_specs=(wide, wide, wide, wide, narrow, narrow),
        out_specs=(wide, wide, wide, narrow),
        check_vma=False,
    )
```

```python
import functools
import math

import jax
import jax.numpy as jnp
import numpy as np
from jax import lax
from jax.experimental import pallas as pl
from jax.experimental.pallas import tpu as pltpu
from jax.sharding import PartitionSpec as P

DH = 128
LOCAL = 1024
THETA = 500000.0
EXTRA = 16
HIDDEN = -1e30
UNUSED = 2.0**14
SCALE = DH**-0.5
LOG2E = math.log2(math.e)
LN2 = math.log(2.0)

NT = (((1,), (1,)), ((), ()))
NN = (((1,), (0,)), ((), ()))
TN = (((0,), (0,)), ((), ()))
F32 = jnp.float32
BF16 = jnp.bfloat16


def few_bits(value, bits):
    unit = 2.0 ** (math.floor(math.log2(value)) + 1 - bits)
    return math.floor(value / unit) * unit


QUARTER_1 = few_bits(math.pi / 2, 10)
QUARTER_2 = few_bits(math.pi / 2 - QUARTER_1, 10)
QUARTER_3 = math.pi / 2 - QUARTER_1 - QUARTER_2


def dot(a, b, dims):
    return lax.dot_general(a, b, dims, preferred_element_type=F32)


def core_of():
    return lax.rem(lax.axis_index("ctx"), 2)


def rotate(values, cosine, sine):
    return values * cosine + pltpu.roll(values, DH // 2, 1) * sine


def sine_cosine(angle):
    turns = jnp.floor(angle * (2.0 / math.pi) + 0.5)
    rest = ((angle - turns * QUARTER_1) - turns * QUARTER_2) - turns * QUARTER_3
    square = rest * rest
    sine = ((-1.9515295891e-4 * square + 8.3321608736e-3) * square - 1.6666654611e-1) * square * rest + rest
    cosine = (2.443315711809948e-5 * square - 1.388731625493765e-3) * square + 4.166664568298827e-2
    cosine = cosine * square * square - 0.5 * square + 1.0
    quarter = turns.astype(jnp.int32)
    odd = (quarter & 1) == 1
    first, second = jnp.where(odd, cosine, sine), jnp.where(odd, sine, cosine)
    return (
        jnp.where((quarter & 2) == 2, -first, first),
        jnp.where(((quarter + 1) & 2) == 2, -second, second),
    )


def split_rows(row, height):
    high = row.astype(BF16).astype(F32)
    middle = (row - high).astype(BF16).astype(F32)
    low = row - high - middle
    line = lax.broadcasted_iota(jnp.int32, (height, row.shape[1]), 0)
    rows = jnp.where(line == 0, high, jnp.where(line == 1, middle, jnp.where(line == 2, low, 0.0)))
    return rows.astype(BF16)


def joined_row(rows):
    return jnp.sum(rows.astype(F32), axis=0, keepdims=True)


def pack_kernel(
    key_in, value_in, query_in, cot_in, gate_in, pos_in, freq_in,
    key_mine, key_theirs, value_mine, value_theirs, theirs, gate_mine, valid, cos_ref, sin_ref,
    key, value, query, gate, pos, freq, sems, *, limit
):
    rows, width = key.shape
    side_width = width // 2
    half = query.shape[1]
    core = core_of()
    there = pl.ds(pl.multiple_of((1 - core) * half, DH), half)
    loads = [(pos_in, pos), (freq_in, freq), (key_in, key), (value_in, value), (query_in.at[:, there], query)]
    loads += [(gate_in, gate), (cot_in.at[:, there], theirs.at[:rows, half : 2 * half])]
    loads = [pltpu.make_async_copy(source, target, sems.at[i]) for i, (source, target) in enumerate(loads)]
    for copy in loads:
        copy.start()
    down = lax.broadcasted_iota(jnp.int32, (rows, rows), 0)
    along = lax.broadcasted_iota(jnp.int32, (rows, rows), 1)
    lane = lax.broadcasted_iota(jnp.int32, (rows, DH), 1)
    loads[0].wait()
    loads[1].wait()
    places = pos[...]
    column = jnp.sum(jnp.where(down == along, places.astype(F32), 0.0), axis=1, keepdims=True)
    sine, cosine = sine_cosine(column * freq[...])
    sine = jnp.where(lane < DH // 2, -sine, sine)
    cos_ref[...] = cosine
    sin_ref[...] = sine
    used = jnp.broadcast_to(column, (rows, DH)) < limit
    loads[2].wait()
    loads[3].wait()
    for key_out, value_out, side in ((key_mine, value_mine, core), (key_theirs, value_theirs, 1 - core)):
        for i in range(side_width // DH):
            from_ = pl.ds(pl.multiple_of(side * side_width + i * DH, DH), DH)
            turned = jnp.where(used, rotate(key[:, from_].astype(F32), cosine, sine), UNUSED).astype(BF16)
            key_out[:, i * DH : (i + 1) * DH] = turned
            value_out[:, i * DH : (i + 1) * DH] = value[:, from_]
    theirs[:rows, 2 * half : 2 * half + side_width] = key_theirs[...]
    theirs[:rows, 2 * half + side_width :] = value_theirs[...]
    loads[4].wait()
    cosine, sine = cosine * (SCALE * LOG2E), sine * (SCALE * LOG2E)
    for i in range(half // DH):
        here = slice(i * DH, (i + 1) * DH)
        theirs[:rows, here] = rotate(query[:, here].astype(F32), cosine, sine).astype(BF16)
    loads[5].wait()
    valid[...] = jnp.where(places < limit, 1.0, 0.0)
    used_gate = jnp.where(places < limit, gate[...], 0.0)
    gate_mine[...] = used_gate
    theirs[rows:, :rows] = split_rows(used_gate, EXTRA)
    loads[6].wait()


def chosen(shape, ratio, dim):
    down = lax.broadcasted_iota(jnp.int32, shape, 0)
    along = lax.broadcasted_iota(jnp.int32, shape, 1)
    rows = shape[1 - dim]
    long, short = (down, along) if dim == 0 else (along, down)
    for _ in range(1, ratio):
        long = jnp.where(long >= rows, long - rows, long)
    return jnp.where(long == short, 1.0, 0.0).astype(BF16)


def chunks(low, high):
    return [slice(at, min(at + 256, high)) for at in range(low, high, 256)]


def used_slots(key, here):
    chip = lax.div(lax.axis_index("ctx"), 2)
    first = key[:, :DH].astype(F32)[:, :1]
    return jnp.broadcast_to(first, (key.shape[0], 256)) < jnp.where(chip >= here, UNUSED / 2, -UNUSED)


def local_kernel(
    key_mine, value_mine, query_in, cot_in, cos_ref, sin_ref, gate_mine, sib,
    keys, query, cot, gate, raws, grads, tops, sums, crosses, values, *, ratio
):
    rows = key_mine.shape[0]
    half_groups = keys.shape[0]
    wide = ratio * rows
    half = half_groups * ratio * DH
    core = core_of()
    spread = chosen((rows, wide), ratio, 1)
    key_sib = sib.at[:rows, 2 * half : 2 * half + half_groups * DH]
    value_sib = sib.at[:rows, 2 * half + half_groups * DH :]
    cosine, sine = cos_ref[...] * (SCALE * LOG2E), sin_ref[...] * (SCALE * LOG2E)
    for key, value, side in ((key_mine, value_mine, core), (key_sib, value_sib, 1 - core)):
        there = pl.ds(pl.multiple_of(side * rows, 16), rows)
        for i in range(half_groups):
            keys[i, there, :] = key[:, i * DH : (i + 1) * DH]
            values[i, there, :] = value[:, i * DH : (i + 1) * DH]
            for h in range(ratio):
                to = pl.ds(pl.multiple_of(side * wide + h * rows, 16), rows)
                at = (i * ratio + h) * DH
                if key is key_mine:
                    here = pl.ds(pl.multiple_of(core * half + at, DH), DH)
                    query[i, to, :] = rotate(query_in[:, here].astype(F32), cosine, sine).astype(BF16)
                    cot[i, to, :] = cot_in[:, here]
                else:
                    query[i, to, :] = sib[:rows, at : at + DH]
                    cot[i, to, :] = sib[:rows, half + at : half + at + DH]
    own = joined_row(dot(split_rows(gate_mine[...], EXTRA), spread, NN))
    other = joined_row(dot(sib[rows:, :rows], spread, NN))
    gate[:, :wide] = jnp.where(core == 0, own, other)
    gate[:, wide:] = jnp.where(core == 0, other, own)
    used = used_slots(keys[0, :rows, :], 0)
    for i in range(half_groups):
        for block in range(2):
            reach = (block + 1) * rows
            for here in chunks(block * wide, (block + 1) * wide):
                width = here.stop - here.start
                scores = dot(keys[i, :reach, :], query[i, here, :], NT)
                slot = lax.broadcasted_iota(jnp.int32, (rows, width), 0)
                lane = lax.broadcasted_iota(jnp.int32, (rows, width), 1) + (here.start - block * wide)
                for h in range(1, ratio):
                    lane = jnp.where(lane >= rows, lane - rows, lane)
                shown = jnp.where(slot <= lane, scores[block * rows :], HIDDEN)
                if block:
                    before = jnp.where(used[:, :width], scores[:rows], HIDDEN)
                    shown = jnp.concatenate([before, shown], axis=0)
                top = jnp.max(shown, axis=0, keepdims=True)
                raw = jnp.exp2(shown - top)
                prob_grad = dot(values[i, :reach, :], cot[i, here, :], NT)
                raws[i, :reach, here] = raw
                grads[i, :reach, here] = prob_grad
                tops[i, :, here] = top
                sums[i, :, here] = jnp.sum(raw, axis=0, keepdims=True)
                crosses[i, :, here] = jnp.sum(raw * prob_grad, axis=0, keepdims=True)


def part_of(weights, score_grads, query, cot, out_ref, i, there, lanes):
    key_part = dot(score_grads[i, there, lanes], query[i, lanes, :], NN) * LN2
    value_part = dot(weights[i, there, lanes], cot[i, lanes, :], NN)
    out_ref[:, 2 * i * DH : (2 * i + 1) * DH] = key_part.astype(out_ref.dtype)
    out_ref[:, (2 * i + 1) * DH : (2 * i + 2) * DH] = value_part.astype(out_ref.dtype)


def early_kernel(query, tops, sums, packet, raws, new_tops, new_sums):
    half_groups, lanes = query.shape[:2]
    alone = lax.axis_index("ctx") < 2

    @pl.when(alone)
    def _():
        new_tops[...] = tops[...]
        new_sums[...] = sums[...]

    @pl.when(jnp.logical_not(alone))
    def _():
        used = used_slots(packet, 1)
        for i in range(half_groups):
            key = packet[:, i * DH : (i + 1) * DH]
            for here in chunks(0, lanes):
                width = here.stop - here.start
                shown = jnp.where(used[:, :width], dot(key, query[i, here, :], NT), HIDDEN)
                old_top = tops[i, :, here]
                top = jnp.maximum(old_top, jnp.max(shown, axis=0, keepdims=True))
                raw = jnp.exp2(shown - top)
                raws[i, :, here] = raw
                new_tops[i, :, here] = top
                new_sums[i, :, here] = sums[i, :, here] * jnp.exp2(old_top - top) + jnp.sum(raw, axis=0, keepdims=True)


def far_keys_kernel(query, cot, gate, first_tops, early_raws, tops, sums, *refs, blocks):
    packets = refs[:blocks]
    far_keys, raws, factors, far_factors, shrinks, inverses = refs[blocks : blocks + 6]
    parts, weights = refs[blocks + 6 : -1], refs[-1]
    rows = packets[0].shape[0]
    half_groups, lanes = query.shape[:2]
    alone = lax.axis_index("ctx") < 2

    @pl.when(alone)
    def _():
        for i in range(half_groups):
            inverse = 1.0 / sums[i]
            factors[i] = inverse * gate[...]
            inverses[i] = inverse

    @pl.when(jnp.logical_not(alone))
    def _():
        for i in range(half_groups):
            for j, packet in enumerate(packets):
                far_keys[i, j * rows : (j + 1) * rows, :] = packet[:, i * DH : (i + 1) * DH]
        used = [used_slots(packets[j], j % (blocks // 2) + 1) for j in range(1, blocks)]
        for i in range(half_groups):
            for here in chunks(0, lanes):
                width = here.stop - here.start
                scores = dot(far_keys[i, rows:, :], query[i, here, :], NT)
                shown = [
                    jnp.where(used[j][:, :width], scores[j * rows : (j + 1) * rows], HIDDEN)
                    for j in range(blocks - 1)
                ]
                shown = jnp.concatenate(shown, axis=0)
                old_top = tops[i, :, here]
                top = jnp.maximum(old_top, jnp.max(shown, axis=0, keepdims=True))
                raw = jnp.exp2(shown - top)
                shrink = jnp.exp2(old_top - top)
                first_shrink = jnp.exp2(first_tops[i, :, here] - top)
                inverse = 1.0 / (sums[i, :, here] * shrink + jnp.sum(raw, axis=0, keepdims=True))
                factor = inverse * gate[:, here]
                factors[i, :, here] = factor * first_shrink
                far_factors[i, :, here] = factor
                shrinks[i, :, here] = first_shrink
                inverses[i, :, here] = inverse
                raws[i, rows:, here] = raw.astype(raws.dtype)
                weights[i, rows:, here] = (raw * factor).astype(BF16)
                raw = early_raws[i, :, here] * shrink
                raws[i, :rows, here] = raw.astype(raws.dtype)
                weights[i, :rows, here] = (raw * factor).astype(BF16)
            for j, out_ref in enumerate(parts):
                there = slice(j * rows, (j + 1) * rows)
                out_ref[:, i * DH : (i + 1) * DH] = dot(weights[i, there, :], cot[i], NN).astype(BF16)


def far_values_kernel(query, cot, raws, far_factors, shrinks, inverses, crosses, *refs, blocks):
    packets = refs[:blocks]
    score_grads, deltas = refs[blocks : blocks + 2]
    parts, far_values = refs[blocks + 2 : -1], refs[-1]
    rows = packets[0].shape[0]
    half_groups, lanes = query.shape[:2]
    alone = lax.axis_index("ctx") < 2

    @pl.when(alone)
    def _():
        for i in range(half_groups):
            deltas[i] = crosses[i] * inverses[i]

    @pl.when(jnp.logical_not(alone))
    def _():
        for i in range(half_groups):
            for j, packet in enumerate(packets):
                far_values[i, j * rows : (j + 1) * rows, :] = packet[:, i * DH : (i + 1) * DH]
        for i in range(half_groups):
            for here in chunks(0, lanes):
                raw = raws[i, :, here].astype(F32)
                prob_grad = dot(far_values[i], cot[i, here, :], NT)
                cross = jnp.sum(raw * prob_grad, axis=0, keepdims=True)
                delta = (crosses[i, :, here] * shrinks[i, :, here] + cross) * inverses[i, :, here]
                deltas[i, :, here] = delta
                score_grad = raw * far_factors[i, :, here] * (prob_grad - delta)
                score_grads[i, :, here] = score_grad.astype(BF16)
            key_parts(score_grads, query, parts, i, 0)


def key_parts(score_grads, query, parts, i, first):
    rows = parts[0].shape[0]
    for j, out_ref in enumerate(parts):
        there = slice((first + j) * rows, (first + j + 1) * rows)
        part = dot(score_grads[i, there, :], query[i], NN) * LN2
        out_ref[:, i * DH : (i + 1) * DH] = part.astype(BF16)


def far_rest_kernel(query, score_grads, *parts):
    @pl.when(lax.axis_index("ctx") >= 2)
    def _():
        for i in range(query.shape[0]):
            key_parts(score_grads, query, parts, i, len(parts))


def near_kernel(
    raws, grads, factors, deltas, keys, query, cot, far_keys, far_grads, cos_ref, sin_ref,
    part_mine, query_mine, gate_mine, theirs, weights, score_grads, parts, acc, turned,
    *, ratio
):
    rows = part_mine.shape[0]
    half_groups = keys.shape[0]
    wide = ratio * rows
    half = half_groups * ratio * DH
    for i in range(half_groups):
        for block in range(2):
            reach = (block + 1) * rows
            for here in chunks(block * wide, (block + 1) * wide):
                gated = raws[i, :reach, here] * factors[i, :, here]
                weights[i, :reach, here] = gated.astype(BF16)
                score_grads[i, :reach, here] = (gated * (grads[i, :reach, here] - deltas[i, :, here])).astype(BF16)
        for block in range(2):
            there, lanes = slice(block * rows, (block + 1) * rows), slice(block * wide, 2 * wide)
            part_of(weights, score_grads, query, cot, parts.at[block], i, there, lanes)
            reach, lanes = (block + 1) * rows, slice(block * wide, (block + 1) * wide)
            acc[i, :, lanes] = dot(keys[i, :reach, :], score_grads[i, :reach, lanes], TN)

    @pl.when(lax.axis_index("ctx") >= 2)
    def _():
        for i in range(half_groups):
            acc[i] += dot(far_keys[i], far_grads[i], TN)

    core = core_of()
    cosine, sine = cos_ref[...], -sin_ref[...]
    for i in range(half_groups):
        turned[...] = jnp.transpose(acc[i] * SCALE)
        for h in range(ratio):
            here = slice((i * ratio + h) * DH, (i * ratio + h + 1) * DH)
            own = turned[pl.ds(pl.multiple_of(core * wide + h * rows, 16), rows), :]
            query_mine[:, here] = rotate(own, cosine, sine).astype(BF16)
            other = turned[pl.ds(pl.multiple_of((1 - core) * wide + h * rows, 16), rows), :]
            theirs[:rows, here] = other.astype(BF16)
    part_mine[...] = parts[core]
    theirs[:rows, half:] = parts[1 - core].astype(BF16)
    summed = deltas[0]
    for i in range(1, half_groups):
        summed = summed + deltas[i]
    gates = []
    for block in range(2):
        own = split_rows(summed[:, block * wide : (block + 1) * wide], 16)
        gates.append(joined_row(dot(own, chosen((wide, rows), ratio, 0), NN)))
    gate_mine[...] = jnp.where(core == 0, gates[0], gates[1])
    theirs[rows:, :rows] = split_rows(jnp.where(core == 0, gates[1], gates[0]), EXTRA)


def sum_first_kernel(part_mine, *refs):
    got, (own, other) = refs[:-2], refs[-2:]
    total = got[0][...].astype(F32)
    for ref in got[2::2]:
        total = total + ref[...].astype(F32)
    other[...] = total
    for i in range(own.shape[1] // DH):
        here = slice(i * DH, (i + 1) * DH)
        value = part_mine[:, (2 * i + 1) * DH : (2 * i + 2) * DH]
        for ref in got[1::2]:
            value = value + ref[:, here].astype(F32)
        own[:, here] = value


def sum_middle_kernel(value_own, part_mine, *refs):
    got, own = refs[:-1], refs[-1]
    for i in range(own.shape[1] // DH):
        here = slice(i * DH, (i + 1) * DH)
        key = part_mine[:, 2 * i * DH : (2 * i + 1) * DH]
        for ref in got:
            key = key + ref[:, here].astype(F32)
        own[:, here] = key


def sum_rest_kernel(key_own, *refs):
    got, other = refs[:-1], refs[-1]
    total = got[0][...].astype(F32)
    for ref in got[1:]:
        total = total + ref[...].astype(F32)
    other[...] = total


def finish_kernel(
    back, query_mine, gate_mine, key_own, value_own, key_other, value_other, valid, cos_ref, sin_ref,
    query_grad, key_grad, value_grad, gate_grad
):
    rows, half = value_own.shape
    wide = query_mine.shape[1]
    core = core_of()
    side = lambda which, width, at=0, size=None: pl.ds(pl.multiple_of(which * width + at, DH), size or width)
    cosine, sine = cos_ref[...], -sin_ref[...]
    for i in range(half // DH):
        here = slice(i * DH, (i + 1) * DH)
        there = wide + 2 * i * DH
        other_key = key_other[:, here] + back[:rows, there : there + DH].astype(F32)
        other_value = value_other[:, here] + back[:rows, there + DH : there + 2 * DH].astype(F32)
        for key_sum, value_sum, which in (
            (key_own[:, here], value_own[:, here], core),
            (other_key, other_value, 1 - core),
        ):
            to = side(which, half, i * DH, DH)
            key_grad[:, to] = rotate(key_sum, cosine, sine).astype(BF16)
            value_grad[:, to] = value_sum.astype(BF16)
    query_grad[:, side(core, wide)] = query_mine[...]
    for i in range(wide // DH):
        turned = rotate(back[:rows, i * DH : (i + 1) * DH].astype(F32), cosine, sine)
        query_grad[:, side(1 - core, wide, i * DH, DH)] = turned.astype(BF16)
    gate = gate_mine[...] + joined_row(back[rows:, :rows])
    gate_grad[...] = jnp.where(valid[...] > 0.0, gate, 0.0)


def per_device(query_rows, key_rows, value_rows, cotangent, router_gate, positions):
    rows, heads_width = query_rows.shape[1:]
    group_width = key_rows.shape[2]
    groups = group_width // DH
    ratio = heads_width // group_width
    half_groups, half_width = groups // 2, heads_width // 2
    parts = lax.axis_size("ctx")
    chips = parts // 2
    limit = parts * LOCAL
    wide = ratio * rows
    params = pltpu.CompilerParams(vmem_limit_bytes=(16 + 4 * chips) * 1024 * 1024)

    def call(kernel, name, outs, *args, scratch=(), flops=10**6, in_hbm=False):
        if in_hbm:
            args = [pltpu.with_memory_space_constraint(arg, pltpu.HBM) for arg in args]
        spec = pl.BlockSpec(memory_space=pltpu.HBM if in_hbm else pltpu.VMEM)
        return pl.pallas_call(
            kernel,
            out_shape=[jax.ShapeDtypeStruct(*out) for out in outs],
            in_specs=[spec] * len(args),
            scratch_shapes=list(scratch),
            compiler_params=params,
            cost_estimate=pl.CostEstimate(flops=flops, bytes_accessed=1000, transcendentals=0),
            name=name,
        )(*args)

    index = np.arange(DH) % (DH // 2)
    freq = jnp.asarray((THETA ** (-2.0 * index / DH)).astype(np.float32))[None]
    packet = ((rows, group_width // 2), BF16)
    table = ((rows, DH), F32)
    line = ((1, rows), F32)
    theirs_shape = ((rows + EXTRA, heads_width + group_width), BF16)
    key_mine, key_theirs, value_mine, value_theirs, theirs, gate_mine, valid, cosine, sine = call(
        functools.partial(pack_kernel, limit=limit),
        "pack",
        [packet, packet, packet, packet, theirs_shape, line, line, table, table],
        key_rows[0],
        value_rows[0],
        query_rows[0],
        cotangent[0],
        router_gate,
        positions,
        freq,
        in_hbm=True,
        flops=5 * 10**9,
        scratch=[
            pltpu.VMEM((rows, group_width), BF16),
            pltpu.VMEM((rows, group_width), BF16),
            pltpu.VMEM((rows, half_width), BF16),
            pltpu.VMEM(*line),
            pltpu.VMEM((1, rows), jnp.int32),
            pltpu.VMEM((1, DH), F32),
            pltpu.SemaphoreType.DMA((7,)),
        ],
    )

    hop = [[(2 * x + k, 2 * (x + s) + k) for x in range(chips - s) for k in range(2)] for s in range(chips)]
    cross = [[(a, b + 1 - 2 * (b % 2)) for a, b in pairs] for pairs in hop]
    back_hop = [[(b, a) for a, b in pairs] for pairs in hop]
    back_cross = [[(b, a) for a, b in pairs] for pairs in cross]

    steps = range(1, chips)

    def send(sib, own, sib_pairs, own_pairs):
        own = [lax.ppermute(own[s - 1], "ctx", own_pairs[s]) for s in steps]
        return [lax.ppermute(sib[s - 1], "ctx", sib_pairs[s]) for s in steps], own

    sib_keys, own_keys = send([key_theirs] * chips, [key_mine] * chips, cross, hop)
    sib_values, own_values = send([value_theirs] * chips, [value_mine] * chips, cross, hop)

    pairs = [[2 * x, 2 * x + 1] for x in range(chips)]
    swap = [pair for a, b in pairs for pair in ((a, b), (b, a))]
    sib = lax.ppermute(theirs, "ctx", swap)

    row = ((half_groups, 1, 2 * wide), F32)
    table = ((half_groups, 2 * rows, 2 * wide), F32)
    kv_table = ((half_groups, 2 * rows, DH), BF16)
    q_table = ((half_groups, 2 * wide, DH), BF16)
    keys, query, cot, gate_row, raws, grads, tops, sums, crosses = call(
        functools.partial(local_kernel, ratio=ratio),
        "local_scores",
        [kv_table, q_table, q_table, ((1, 2 * wide), F32), table, table, row, row, row],
        key_mine,
        value_mine,
        query_rows[0],
        cotangent[0],
        cosine,
        sine,
        gate_mine,
        sib,
        scratch=[pltpu.VMEM(*kv_table)],
        flops=3 * 10**6,
    )

    blocks = 2 * (chips - 1)
    far_rows = ((half_groups, blocks * rows, DH), BF16)
    far_low = ((half_groups, blocks * rows, 2 * wide), BF16)
    far_table = (far_low[0], F32 if chips == 2 else BF16)
    early_table = ((half_groups, rows, 2 * wide), F32)
    early_raws, early_tops, early_sums = call(
        early_kernel, "early_keys", [early_table, row, row], query, tops, sums, own_keys[0]
    )
    far_keys, far_raws, factors, far_factors, shrinks, inverses, *parts = call(
        functools.partial(far_keys_kernel, blocks=blocks),
        "far_keys",
        [far_rows, far_table, row, row, row, row] + [packet] * blocks,
        query,
        cot,
        gate_row,
        tops,
        early_raws,
        early_tops,
        early_sums,
        *own_keys,
        *sib_keys,
        scratch=[pltpu.VMEM(*far_low)],
    )
    sib_value_got, own_value_got = send(parts[chips - 1 :], parts[: chips - 1], back_cross, back_hop)
    far_grads, deltas, *parts = call(
        functools.partial(far_values_kernel, blocks=blocks),
        "far_values",
        [far_low, row] + [packet] * (chips - 1),
        query,
        cot,
        far_raws,
        far_factors,
        shrinks,
        inverses,
        crosses,
        *own_values,
        *sib_values,
        scratch=[pltpu.VMEM(*far_rows)],
    )
    own_key_got = [lax.ppermute(parts[s - 1], "ctx", back_hop[s]) for s in steps]
    parts = call(far_rest_kernel, "far_rest", [packet] * (chips - 1), query, far_grads)
    sib_key_got = [lax.ppermute(parts[s - 1], "ctx", back_cross[s]) for s in steps]

    part_mine, query_mine, gate_part, theirs = call(
        functools.partial(near_kernel, ratio=ratio),
        "near_grads",
        [
            ((rows, group_width), F32),
            ((rows, half_width), BF16),
            ((1, rows), F32),
            ((rows + EXTRA, half_width + group_width), BF16),
        ],
        raws,
        grads,
        factors,
        deltas,
        keys,
        query,
        cot,
        far_keys,
        far_grads,
        cosine,
        sine,
        flops=4 * 10**6,
        scratch=[
            pltpu.VMEM((half_groups, 2 * rows, 2 * wide), BF16),
            pltpu.VMEM((half_groups, 2 * rows, 2 * wide), BF16),
            pltpu.VMEM((2, rows, group_width), F32),
            pltpu.VMEM((half_groups, DH, 2 * wide), F32),
            pltpu.VMEM((2 * wide, DH), F32),
        ],
    )
    back = lax.ppermute(theirs, "ctx", swap)
    total = ((rows, group_width // 2), F32)
    value_own, value_other = call(
        sum_first_kernel,
        "sum_first",
        [total, total],
        part_mine,
        *[part for pair in zip(sib_value_got, own_value_got) for part in pair],
        flops=3 * 10**8,
    )
    (key_own,) = call(sum_middle_kernel, "sum_middle", [total], value_own, part_mine, *own_key_got, flops=5 * 10**9)
    (key_other,) = call(sum_rest_kernel, "sum_rest", [total], key_own, *sib_key_got, flops=5 * 10**9)
    query_grad, key_grad, value_grad, gate_grad = call(
        finish_kernel,
        "finish",
        [((rows, heads_width), BF16)] + [((rows, group_width), BF16)] * 2 + [line],
        back,
        query_mine,
        gate_part,
        key_own,
        value_own,
        key_other,
        value_other,
        valid,
        cosine,
        sine,
    )
    return (query_grad[None], key_grad[None], value_grad[None], gate_grad)


def solution(mesh):
    wide = P(("group", "dp"), "ctx", None)
    narrow = P(("group", "dp"), "ctx")
    return jax.shard_map(
        per_device,
        mesh=mesh,
        in_specs=(wide, wide, wide, wide, narrow, narrow),
        out_specs=(wide, wide, wide, narrow),
        check_vma=False,
    )
```
